32 devices in a mesh: grp: 2 (over y), comp: 8 (over z, x), tile: 2 (over core).
Axes of the slice: x: 2, y: 2, z: 4, core: 2. Of those that a mesh axis runs over, the one named last changes fastest.
Arguments:
- energy: float32 [1152, 512, 256], P('comp', ('grp', 'tile')), parts along dimension 1, may hold values from 0.2 to 2
- sea_mask: int32 [512, 256], P('grp'), parts along dimension 0, may hold values from 0 to 1, as said below
- current_u: float32 [512, 256], P('grp'), parts along dimension 0, may hold values from -0.15 to 0.15
- current_v: float32 [512, 256], P('grp'), parts along dimension 0, may hold values from -0.15 to 0.15
- wind_forcing: float32 [512, 256], P('grp'), parts along dimension 0, may hold values from 0.3 to 3
- refraction: float32 [512, 256], P('grp'), parts along dimension 0, may hold values from -0.3 to 0.3
- group_speed: float32 [32], replicated, may hold values from 0.15 to 0.35
- growth: float32 [1152], replicated, may hold values from 0.03 to 0.3
- damping: float32 [1152], replicated, may hold values from 0.03 to 0.3
- coupling: float32 [1152], replicated, may hold values from 0.01 to 0.1
- dia_index: int32 [4, 1152], replicated, may hold values from 0 to 1151, as said below
Outputs:
- energy_out: float32 [1152, 512, 256], P('comp', ('grp', 'tile')), parts along dimension 1
The draws below stay inside these ranges and needn't reach their ends.
There are 2 independent parts, one for each index of `grp`. The reference program is written for one: setup_inputs(seed, part) draws one part's arguments, and reference() takes and returns one part's arrays. A program takes and returns all parts, laid end to end along the dimension named above; an argument that names none is the same for every part. Nothing has to cross between parts.
Inputs may be any that keep to these rules, and one draw needn't show every extreme that they name: `sea_mask`: each tile's block of 128 x 256 cells holds at most 16384 sea cells, and one tile holds exactly that many. `dia_index`: partners of a component lie one or two frequency bins above (plus) or below (minus), clamped to the range, with direction offsets that depend only on the frequency.
All inputs are finite; a program needn't handle non-finite values.
Results may differ from the reference program's by a relative error of at most 0.0025.
Values sent between devices are 32-bit elements; how exact they have to be, the bound alone decides.
No kernel may reach another device: no remote copies, remote signals or barrier semaphores. Data moves between devices by JAX's collectives and lax.ppermute only.
A program may use at most 320 MiB of HBM per device.

```python
import math
import jax
import jax.numpy as jnp
from jax import lax

NTH = 36
NF = 32
GX = 128
NY = 256
K = 1152
NX = 256
SEA_MAX = 16384


def draw_sea_mask(key, part):
    key = jax.random.fold_in(key, 11)
    counts_key, fullest_key, order_key = jax.random.split(key, 3)
    tile_count = NX // GX
    cell_count = GX * NY
    counts = jax.random.randint(counts_key, (tile_count,), 3 * SEA_MAX // 4, SEA_MAX + 1)
    fullest = jax.random.randint(fullest_key, (), 0, tile_count)
    counts = jnp.where(jnp.arange(tile_count) == fullest, SEA_MAX, counts)
    rank_table = jax.vmap(lambda sub_key: jax.random.permutation(sub_key, cell_count))(jax.random.split(order_key, tile_count))
    sea_cells = (rank_table < counts[:, None]).astype(jnp.int32)
    return sea_cells.reshape(tile_count * GX, NY)


def draw_dia_index(key, part):
    key = jax.random.fold_in(key, 23)
    sub_keys = jax.random.split(key, 4)
    comp_ids = jnp.arange(NF * NTH)
    frequency = comp_ids // NTH
    direction = comp_ids % NTH
    freq_up = jax.random.randint(sub_keys[0], (NF,), 1, 3)
    freq_down = jax.random.randint(sub_keys[1], (NF,), 1, 3)
    turn_plus = jax.random.randint(sub_keys[2], (NF,), 1, 5)
    turn_minus = jax.random.randint(sub_keys[3], (NF,), 2, 7)
    freq_plus = jnp.minimum(frequency + freq_up[frequency], NF - 1)
    freq_minus = jnp.maximum(frequency - freq_down[frequency], 0)
    pattern = [freq_plus * NTH + (direction + turn_plus[frequency]) % NTH, freq_minus * NTH + (direction - turn_minus[frequency]) % NTH, freq_plus * NTH + (direction - turn_plus[frequency]) % NTH, freq_minus * NTH + (direction + turn_minus[frequency]) % NTH]
    return jnp.stack(pattern).astype(jnp.int32)


def level_of(own_key, dims, shards, smallest, largest):
    level = 1.0
    for axis_at, blocks in shards:
        draws = jax.random.uniform(jax.random.fold_in(jax.random.fold_in(own_key, 6), axis_at), (blocks,), jnp.float32, smallest / len(shards), largest / len(shards))
        level = level * jnp.repeat(jnp.exp(draws), dims[axis_at] // blocks).reshape((-1,) + (1,) * (len(dims) - 1 - axis_at))
    return level


def setup_inputs(seed: int = 0, part: int = 0) -> dict:
    splits = jax.random.split(jax.random.key(seed), 12)
    own_keys = jax.random.split(jax.random.fold_in(splits[11], part), 12)
    energy = jnp.clip(jnp.exp(math.log(2.0) - 2.3025851 * jax.random.uniform(own_keys[0], (K, NX, NY), jnp.float32) ** level_of(own_keys[0], (K, NX, NY), ((0, 8), (1, 2)), -0.2, 0.2)), 0.2, 2.0)
    sea_mask = draw_sea_mask(jax.random.fold_in(jax.random.fold_in(splits[11], part), 71), part)
    current_u = jnp.clip(jax.random.uniform(own_keys[2], (NX, NY), jnp.float32, -0.15, 0.15), -0.15, 0.15)
    current_v = jnp.clip(jax.random.uniform(own_keys[3], (NX, NY), jnp.float32, -0.15, 0.15), -0.15, 0.15)
    wind_forcing = jnp.clip(jnp.exp(jax.random.uniform(own_keys[4], (NX, NY), jnp.float32, math.log(0.3), math.log(3.0))), 0.3, 3.0)
    refraction = jnp.clip(jax.random.uniform(own_keys[5], (NX, NY), jnp.float32, -0.3, 0.3), -0.3, 0.3)
    group_speed = jnp.clip(jax.random.uniform(splits[6], (NF,), jnp.float32, 0.15, 0.35), 0.15, 0.35)
    growth = jnp.clip(jnp.exp(jax.random.uniform(splits[7], (K,), jnp.float32, math.log(0.03), math.log(0.3))), 0.03, 0.3)
    damping = jnp.clip(jnp.exp(jax.random.uniform(splits[8], (K,), jnp.float32, math.log(0.03), math.log(0.3))), 0.03, 0.3)
    coupling = jnp.clip(jnp.exp(jax.random.uniform(splits[9], (K,), jnp.float32, math.log(0.01), math.log(0.1))), 0.01, 0.1)
    dia_index = draw_dia_index(jax.random.fold_in(splits[11], 71), part)
    return {"energy": energy, "sea_mask": sea_mask, "current_u": current_u, "current_v": current_v, "wind_forcing": wind_forcing, "refraction": refraction, "group_speed": group_speed, "growth": growth, "damping": damping, "coupling": coupling, "dia_index": dia_index}


weight_plus = 0.4096
weight_minus = 3.1605
weight_cross = 1.2945


def quick_flux(far_left, left_cell, right_cell, far_right, courant):
    centre = 0.5 * (left_cell + right_cell) - 0.5 * courant * (right_cell - left_cell)
    curvature = (1.0 - courant * courant) / 6.0
    upward = centre - curvature * (right_cell - 2.0 * left_cell + far_left)
    downward = centre - curvature * (left_cell - 2.0 * right_cell + far_right)
    return courant * jnp.where(courant > 0.0, upward, downward)


def flux_change(padded, speed, current, sea_pad, axis):
    cell_count = padded.shape[axis] - 4

    def take_part(source, first, which_axis):
        return lax.slice_in_dim(source, first, first + cell_count + 1, axis=which_axis)

    face_current = 0.5 * (take_part(current, 0, axis - 1) + take_part(current, 1, axis - 1))
    courant = speed[:, None, None] + face_current[None]
    open_face = (take_part(sea_pad, 0, axis - 1) * take_part(sea_pad, 1, axis - 1))[None]
    face_flux = quick_flux(take_part(padded, 0, axis), take_part(padded, 1, axis),
                           take_part(padded, 2, axis), take_part(padded, 3, axis), courant) * open_face
    return lax.slice_in_dim(face_flux, 1, cell_count + 1, axis=axis) - lax.slice_in_dim(face_flux, 0, cell_count, axis=axis)


def source_terms(energy_block, wind, turning, growth, damping, coupling, lookup, spread):
    cell_count = energy_block.shape[1]
    spectrum = energy_block.reshape(NF, NTH, cell_count)
    turn_rate = turning[None, None, :]
    next_dir = jnp.roll(spectrum, -1, axis=1)
    forward = jnp.maximum(turn_rate, 0.0)
    backward = jnp.minimum(turn_rate, 0.0)
    upper_flux = forward * spectrum + backward * next_dir
    lower_flux = jnp.roll(upper_flux, 1, axis=1)
    turned = (spectrum - upper_flux + lower_flux).reshape(energy_block.shape)
    rounded = lax.optimization_barrier(turned.astype(jnp.bfloat16))
    plus_first, minus_first, plus_second, minus_second = lookup(rounded)
    couple_rate = coupling[:, None]
    delta_first = couple_rate * (turned * turned * (weight_plus * plus_first + weight_minus * minus_first)
                                 - 2.0 * weight_cross * turned * plus_first * minus_first)
    delta_second = couple_rate * (turned * turned * (weight_plus * plus_second + weight_minus * minus_second)
                                  - 2.0 * weight_cross * turned * plus_second * minus_second)
    moved = spread(delta_first.astype(jnp.bfloat16), delta_second.astype(jnp.bfloat16))
    mean_level = jnp.sum(turned, axis=0) / energy_block.shape[0]
    return (turned + growth[:, None] * wind[None] * turned - damping[:, None] * mean_level[None] * turned
            - 2.0 * (delta_first + delta_second) + moved)


def reference(energy, sea_mask, current_u, current_v, wind_forcing, refraction, group_speed, growth, damping, coupling, dia_index):
    comp_total = NTH * NF
    angles = (2.0 * math.pi / NTH) * (jnp.arange(comp_total) % NTH).astype(jnp.float32)
    speeds = jnp.repeat(group_speed, NTH)
    speed_east = speeds * jnp.cos(angles)
    speed_north = speeds * jnp.sin(angles)
    sea_cells = sea_mask.astype(jnp.float32)
    sea_pad = jnp.pad(sea_cells, 1)
    east_pad = jnp.pad(current_u, 1)
    north_pad = jnp.pad(current_v, 1)
    masked = energy * sea_cells[None]
    along_east = flux_change(jnp.pad(masked, ((0, 0), (2, 2), (0, 0))), speed_east, east_pad[:, 1:-1], sea_pad[:, 1:-1], 1)
    along_north = flux_change(jnp.pad(masked, ((0, 0), (0, 0), (2, 2))), speed_north, north_pad[1:-1, :], sea_pad[1:-1, :], 2)
    propagated = sea_cells[None] * (masked - along_east - along_north)

    def lookup(rounded):
        return tuple(jnp.take(rounded, dia_index[slot_row], axis=0).astype(jnp.float32) for slot_row in range(4))

    def spread(first_terms, second_terms):
        summed = jnp.zeros((comp_total, first_terms.shape[1]), jnp.float32)
        summed = summed.at[dia_index[0]].add(first_terms.astype(jnp.float32))
        summed = summed.at[dia_index[1]].add(first_terms.astype(jnp.float32))
        summed = summed.at[dia_index[2]].add(second_terms.astype(jnp.float32))
        summed = summed.at[dia_index[3]].add(second_terms.astype(jnp.float32))
        return summed

    def one_row(inputs):
        energy_row, wind_row, turn_row = inputs
        return source_terms(energy_row, wind_row, turn_row, growth, damping, coupling, lookup, spread)

    by_rows = jnp.moveaxis(propagated, 1, 0)
    result = lax.map(one_row, (by_rows, wind_forcing, refraction))
    return jnp.moveaxis(result, 0, 1)
```

```python
import functools
import math

import jax
import jax.numpy as jnp
from jax import lax
from jax.experimental import pallas as pl
from jax.experimental.pallas import tpu as pltpu
from jax.sharding import PartitionSpec as P

NTH = 36
NF = 32


weight_plus = 0.4096
weight_minus = 3.1605
weight_cross = 1.2945


def with_halo(block, sides, width):
    for axis, dim in sides:
        count = lax.axis_size(axis)
        forward = [(i, i + 1) for i in range(count - 1)]
        backward = [(target, source) for source, target in forward]
        low = lax.ppermute(
            lax.slice_in_dim(block, block.shape[dim] - width, None, axis=dim), axis, forward
        )
        high = lax.ppermute(lax.slice_in_dim(block, 0, width, axis=dim), axis, backward)
        block = jnp.concatenate([low, block, high], axis=dim)
    return block


def quick_flux(far_left, left_cell, right_cell, far_right, courant):
    centre = 0.5 * (left_cell + right_cell) - 0.5 * courant * (right_cell - left_cell)
    curvature = (1.0 - courant * courant) / 6.0
    upward = centre - curvature * (right_cell - 2.0 * left_cell + far_left)
    downward = centre - curvature * (left_cell - 2.0 * right_cell + far_right)
    return courant * jnp.where(courant > 0.0, upward, downward)


def flux_change(padded, speed, current, sea_pad, axis):
    cell_count = padded.shape[axis] - 4

    def take_part(source, first, which_axis):
        return lax.slice_in_dim(source, first, first + cell_count + 1, axis=which_axis)

    face_current = 0.5 * (take_part(current, 0, axis - 1) + take_part(current, 1, axis - 1))
    courant = speed[:, None, None] + face_current[None]
    open_face = (take_part(sea_pad, 0, axis - 1) * take_part(sea_pad, 1, axis - 1))[None]
    face_flux = (
        quick_flux(
            take_part(padded, 0, axis),
            take_part(padded, 1, axis),
            take_part(padded, 2, axis),
            take_part(padded, 3, axis),
            courant,
        )
        * open_face
    )
    return lax.slice_in_dim(face_flux, 1, cell_count + 1, axis=axis) - lax.slice_in_dim(
        face_flux, 0, cell_count, axis=axis
    )


def source_terms(energy_block, wind, turning, growth, damping, coupling, lookup, spread):
    cell_count = energy_block.shape[1]
    spectrum = energy_block.reshape(NF, NTH, cell_count)
    turn_rate = turning[None, None, :]
    next_dir = jnp.roll(spectrum, -1, axis=1)
    forward = jnp.maximum(turn_rate, 0.0)
    backward = jnp.minimum(turn_rate, 0.0)
    upper_flux = forward * spectrum + backward * next_dir
    lower_flux = jnp.roll(upper_flux, 1, axis=1)
    turned = (spectrum - upper_flux + lower_flux).reshape(energy_block.shape)
    rounded = turned.astype(jnp.bfloat16)
    plus_first, minus_first, plus_second, minus_second = lookup(rounded)
    couple_rate = coupling[:, None]
    delta_first = couple_rate * (
        turned * turned * (weight_plus * plus_first + weight_minus * minus_first)
        - 2.0 * weight_cross * turned * plus_first * minus_first
    )
    delta_second = couple_rate * (
        turned * turned * (weight_plus * plus_second + weight_minus * minus_second)
        - 2.0 * weight_cross * turned * plus_second * minus_second
    )
    moved = spread(delta_first.astype(jnp.bfloat16), delta_second.astype(jnp.bfloat16))
    mean_level = jnp.sum(turned, axis=0) / energy_block.shape[0]
    return (
        turned
        + growth[:, None] * wind[None] * turned
        - damping[:, None] * mean_level[None] * turned
        - 2.0 * (delta_first + delta_second)
        + moved
    )


def shards(
    energy,
    sea_mask,
    current_u,
    current_v,
    wind_forcing,
    refraction,
    group_speed,
    growth,
    damping,
    coupling,
    dia_index,
):
    comp_count = lax.axis_size("comp")
    comp_pos = lax.axis_index("comp")
    tile_pos = lax.axis_index("tile")
    local_comps, row_count, col_count = energy.shape
    first_row = tile_pos * row_count
    first_comp = comp_pos * local_comps
    comp_total = NTH * NF
    angles = 2.0 * math.pi / NTH * (jnp.arange(comp_total) % NTH).astype(jnp.float32)
    speeds = jnp.repeat(group_speed, NTH)
    speed_east = lax.dynamic_slice_in_dim(speeds * jnp.cos(angles), first_comp, local_comps)
    speed_north = lax.dynamic_slice_in_dim(speeds * jnp.sin(angles), first_comp, local_comps)
    window = (row_count + 2, col_count + 2)
    sea_pad = lax.dynamic_slice(jnp.pad(sea_mask.astype(jnp.float32), 1), (first_row, 0), window)
    east_pad = lax.dynamic_slice(jnp.pad(current_u, 1), (first_row, 0), window)
    north_pad = lax.dynamic_slice(jnp.pad(current_v, 1), (first_row, 0), window)
    sea_tile = sea_pad[1:-1, 1:-1]
    masked = energy * sea_tile[None]
    padded_east = with_halo(masked, (("tile", 1),), 2)
    along_east = flux_change(padded_east, speed_east, east_pad[:, 1:-1], sea_pad[:, 1:-1], 1)
    along_north = flux_change(
        jnp.pad(masked, ((0, 0), (0, 0), (2, 2))),
        speed_north,
        north_pad[1:-1, :],
        sea_pad[1:-1, :],
        2,
    )
    propagated = (sea_tile[None] * (masked - along_east - along_north)).reshape(
        local_comps, row_count * col_count
    )
    tile_wind = lax.dynamic_slice(wind_forcing, (first_row, 0), (row_count, col_count)).reshape(-1)
    tile_turn = lax.dynamic_slice(refraction, (first_row, 0), (row_count, col_count)).reshape(-1)
    comp_ids = jnp.arange(comp_total)
    tables = [
        (dia_index[slot_row][:, None] == comp_ids[None, :]).astype(jnp.bfloat16)
        for slot_row in range(4)
    ]

    def lookup(rounded):
        return tuple(
            (
                jnp.dot(tables[slot_row], rounded, preferred_element_type=jnp.float32)
                for slot_row in range(4)
            )
        )

    def scatter_back(table, terms):
        return lax.dot_general(
            table, terms, (((0,), (0,)), ((), ())), preferred_element_type=jnp.float32
        )

    def spread(first_terms, second_terms):
        return (
            scatter_back(tables[0], first_terms)
            + scatter_back(tables[1], first_terms)
            + scatter_back(tables[2], second_terms)
            + scatter_back(tables[3], second_terms)
        )

    share_size = row_count * col_count // comp_count
    point_field = lax.all_to_all(propagated, "comp", split_axis=1, concat_axis=0, tiled=True)
    first_point = comp_pos * share_size
    own_wind = lax.dynamic_slice_in_dim(tile_wind, first_point, share_size)
    own_turn = lax.dynamic_slice_in_dim(tile_turn, first_point, share_size)
    result = source_terms(
        point_field, own_wind, own_turn, growth, damping, coupling, lookup, spread
    )
    returned_field = lax.all_to_all(result, "comp", split_axis=0, concat_axis=1, tiled=True)
    return returned_field.reshape(local_comps, row_count, col_count)


BLOCK = 128
GROUP = 24
CELL_CHUNKS = 4
MIB = 1024 * 1024


def row_of(ref, row):
    return ref[row : row + 1, :]


def upwind(courant, here, ahead, slope_here, bend_here, bend_ahead):
    square = courant * courant
    bend = jnp.where(courant > 0.0, bend_here, bend_ahead)
    return courant * ((here + ahead) - courant * slope_here - (1.0 / 3.0 - square * (1.0 / 3.0)) * bend)


def pack_block(block, index, offset, spill, tile, out_ref, rows, held):
    lanes = lax.broadcasted_iota(jnp.int32, block.shape, 1)
    moved = jnp.take_along_axis(block, jnp.broadcast_to(index, block.shape), axis=1)
    merged = jnp.where(lanes >= offset, moved, held)
    out_ref[rows, pl.ds(pl.multiple_of(tile * BLOCK, BLOCK), BLOCK)] = merged
    return jnp.where(spill > 0, moved, merged)


def pack_fields_kernel(row_count, table_ref, fields_ref, index_ref, out_ref, wide_ref):
    halves = fields_ref.shape[2] // BLOCK
    group = 8 // halves

    def step(i, held):
        index_rows = index_ref[pl.ds(pl.multiple_of(8 * i, 8), 8), :]
        for r in range(group):
            row = fields_ref[i * group + r]
            for h in range(halves):
                at = r * halves + h
                b = i * 8 + at
                held = pack_block(
                    row[:, h * BLOCK : (h + 1) * BLOCK], index_rows[at : at + 1, :],
                    table_ref[1, b], table_ref[2, b], table_ref[0, b], wide_ref, slice(None), held,
                )
        return held

    held = lax.fori_loop(0, row_count // group, step, jnp.zeros((8, BLOCK), jnp.float32))
    last = table_ref[0, row_count * halves]
    wide_ref[:, pl.ds(pl.multiple_of(last * BLOCK, BLOCK), BLOCK)] = held
    out_ref[...] = wide_ref[:, : out_ref.shape[1]]


def propagate_kernel(steps, table_ref, energy_ref, low_ref, high_ref, coef_ref, index_ref, east_ref, north_ref,
                     fields_ref, *refs):
    wide_ref, sum_ref, outs = refs[-1], refs[-2], refs[:-2]
    step_id = pl.program_id(0)
    row_count, col_count = energy_ref.shape[1:]
    halves = col_count // BLOCK
    lane = lax.broadcasted_iota(jnp.int32, (8, col_count), 1)
    first_lane, last_lane = lane == 0, lane == col_count - 1

    def cell_row(at, coef, index_rows, first, fresh, state, east, north, rows):
        here, ahead, bend_here, flux_low, held = state
        new = fresh * row_of(coef, 0)
        slope = ahead - here
        bend_ahead = (new - ahead) - slope
        flux = upwind(east * row_of(coef, 1) + row_of(coef, 2), here, ahead, slope, bend_here, bend_ahead)
        right = jnp.where(last_lane, 0.0, pltpu.roll(here, col_count - 1, 1))
        left = jnp.where(first_lane, 0.0, pltpu.roll(here, 1, 1))
        slope_right = right - here
        bend = slope_right - (here - left)
        cross = upwind(north * row_of(coef, 3) + row_of(coef, 4), here, right, slope_right, bend,
                       pltpu.roll(bend, col_count - 1, 1))
        moved = row_of(coef, 5) * ((here + here) - (flux - flux_low) - (cross - pltpu.roll(cross, 1, 1)))
        for h in range(halves):
            b = first + at * halves + h
            held = pack_block(
                moved[:, h * BLOCK : (h + 1) * BLOCK], index_rows[at * halves + h],
                table_ref[1, b], table_ref[2, b], table_ref[0, b], wide_ref, rows, held,
            )
        return ahead, new, bend_ahead, flux, held

    @pl.loop(0, GROUP // 8)
    def _(g):
        local = pl.ds(pl.multiple_of(g * 8, 8), 8)
        rows = pl.ds(pl.multiple_of(step_id * GROUP + g * 8, 8), 8)
        east = jnp.broadcast_to(east_ref[local, :], (8, col_count))
        north = jnp.broadcast_to(north_ref[local, :], (8, col_count))
        here = low_ref[0, local, :] * coef_ref[row_count + 2, 0:1, :]
        ahead = low_ref[1, local, :] * coef_ref[row_count + 3, 0:1, :]
        zero = jnp.zeros_like(here)
        state = (here, ahead, zero, zero, jnp.zeros((8, BLOCK), jnp.float32))

        def eight(i, state):
            fresh = jnp.swapaxes(energy_ref[local, pl.ds(pl.multiple_of(8 * i, 8), 8), :], 0, 1)
            picks = index_ref[pl.ds(pl.multiple_of(8 * halves * i, 8), 8 * halves), :]
            index_rows = [picks[b : b + 1, :] for b in range(8 * halves)]
            for at in range(8):
                state = cell_row(at, coef_ref.at[8 * i + at], index_rows, 8 * halves * i, fresh[at], state,
                                 east, north, rows)
            return state

        state = lax.fori_loop(0, row_count // 8, eight, state)
        first = row_count * halves
        index_rows = [index_ref[first + b : first + b + 1, :] for b in range(2 * halves)]
        for at in range(2):
            state = cell_row(at, coef_ref.at[row_count + at], index_rows, first, high_ref[at, local, :], state,
                             east, north, rows)
        last = table_ref[0, first + 2 * halves]
        wide_ref[rows, pl.ds(pl.multiple_of(last * BLOCK, BLOCK), BLOCK)] = state[-1]

    @pl.when(step_id == steps - 1)
    def _():
        comps, width = outs[0].shape
        tile_width = 2 * BLOCK
        comp_row = lax.broadcasted_iota(jnp.int32, (comps, tile_width), 0)
        circle_row = comp_row % NTH
        for o, out_ref in enumerate(outs):

            @pl.loop(0, width // tile_width)
            def _(i):
                source = pl.ds(pl.multiple_of(o * width + i * tile_width, tile_width), tile_width)
                target = pl.ds(pl.multiple_of(i * tile_width, tile_width), tile_width)
                level = wide_ref[:, source]
                rate = fields_ref[1:2, source]
                forward = jnp.maximum(rate, 0.0)
                backward = jnp.minimum(rate, 0.0)
                after = pltpu.roll(level, comps - 1, 0)
                before = pltpu.roll(level, 1, 0)
                for start in range(0, comps, NTH):
                    end = start + NTH - 1
                    after = jnp.where(comp_row == end, level[start : start + 1, :], after)
                    before = jnp.where(comp_row == start, level[end : end + 1, :], before)
                turned = (1.0 - forward + backward) * level - backward * after + forward * before
                out_ref[:, target] = turned
                sum_ref[:, source] = jnp.sum(turned, axis=0, keepdims=True)


def interact_kernel(table_ref, spread_ref, coupling_ref, *refs):
    window, own_ref, back_ref, delta_ref = refs[:8], refs[8], refs[9], refs[10]
    comps = window[0].shape[0]
    kept = []
    for j in range(1, 7):
        level = window[j][...]
        around = jnp.concatenate([window[j - 1][...], level, window[j + 1][...]], axis=0).astype(jnp.bfloat16)
        partner = jnp.dot(table_ref[j - 1], around, preferred_element_type=jnp.float32)
        rate = coupling_ref[(j - 1) * comps : j * comps, :] * level
        plus_part = weight_plus * level
        minus_part = weight_minus * level
        deltas = []
        for pair in range(2):
            plus = partner[2 * pair * comps : (2 * pair + 1) * comps, :]
            minus = partner[(2 * pair + 1) * comps : (2 * pair + 2) * comps, :]
            deltas.append(rate * (plus * (plus_part - (2.0 * weight_cross) * minus) + minus_part * minus))
        both = jnp.concatenate(deltas, axis=0).astype(jnp.bfloat16)
        delta_ref[(j - 1) * 2 * comps : j * 2 * comps, :] = both
        if 2 <= j <= 5:
            part = -2.0 * (deltas[0] + deltas[1])
            target = own_ref if j <= 3 else back_ref
            at = (j % 2) * comps
            target[at : at + comps, :] = part
    spread = jnp.dot(spread_ref[...], delta_ref[...], preferred_element_type=jnp.float32)
    own_ref[...] += spread[: 2 * comps, :]
    back_ref[...] += spread[2 * comps :, :]


def finish_kernel(chunks, table_ref, place_ref, mean_ref, fields_ref, growth_ref, damping_ref, *refs):
    turned, own, back = refs[: 2 * chunks], refs[2 * chunks : 3 * chunks], refs[3 * chunks : 4 * chunks]
    out_ref, wide_ref = refs[-2], refs[-1]
    width = own[0].shape[1]
    col_count = out_ref.shape[2]
    halves = col_count // BLOCK
    tile_width = 2 * BLOCK
    for o in range(2 * chunks):
        extra = own[o] if o < chunks else back[o - chunks]

        @pl.loop(0, width // tile_width)
        def _(i):
            source = pl.ds(pl.multiple_of(i * tile_width, tile_width), tile_width)
            target = pl.ds(pl.multiple_of(o * width + i * tile_width, tile_width), tile_width)
            scale = 1.0 + growth_ref[...] * fields_ref[0:1, target] - damping_ref[...] * mean_ref[0:1, target]
            wide_ref[:, target] = turned[o][:, source] * scale + extra[:, source]

    @pl.loop(0, GROUP // 8)
    def _(g):
        local = pl.ds(pl.multiple_of(g * 8, 8), 8)

        @pl.loop(0, out_ref.shape[1] // 8)
        def _(i):
            places = place_ref[pl.ds(pl.multiple_of(8 * halves * i, 8), 8 * halves), :]
            grid_rows = []
            for r in range(8):
                parts = []
                for h in range(halves):
                    at = r * halves + h
                    b = 8 * halves * i + at
                    place = jnp.broadcast_to(places[at : at + 1, :], (8, BLOCK))
                    lane = jnp.bitwise_and(place, BLOCK - 1)
                    low = wide_ref[local, pl.ds(pl.multiple_of(table_ref[1, b] * BLOCK, BLOCK), BLOCK)]
                    high = wide_ref[local, pl.ds(pl.multiple_of(table_ref[2, b] * BLOCK, BLOCK), BLOCK)]
                    low = jnp.take_along_axis(low, lane, axis=1)
                    high = jnp.take_along_axis(high, lane, axis=1)
                    parts.append(jnp.where(place >= BLOCK, high, jnp.where(place >= 0, low, 0.0)))
                grid_rows.append(jnp.concatenate(parts, axis=1))
            out_ref[local, pl.ds(pl.multiple_of(8 * i, 8), 8), :] = jnp.swapaxes(jnp.stack(grid_rows), 0, 1)


def params(limit):
    return pltpu.CompilerParams(vmem_limit_bytes=limit * MIB)


def packed_shards(energy, sea_mask, current_u, current_v, wind_forcing, refraction, group_speed, growth, damping,
                  coupling, dia_index):
    comp_count = lax.axis_size("comp")
    comp_pos = lax.axis_index("comp")
    tile_pos = lax.axis_index("tile")
    odd = lax.rem(comp_pos, 2)
    pair_pos = comp_pos // 2
    local_comps, row_count, col_count = energy.shape
    comps = local_comps // 2
    comp_total = NTH * NF
    first_row = tile_pos * row_count
    first_comp = comp_pos * local_comps
    cells = row_count * col_count // 2
    half = cells // 2
    width = half // CELL_CHUNKS
    halves = col_count // BLOCK
    blocks = row_count * halves
    tiles = cells // BLOCK
    f32, i32 = jnp.float32, jnp.int32

    low, high = [], []
    tile_count = lax.axis_size("tile")
    forward = [(i, i + 1) for i in range(tile_count - 1)]
    backward = [(target, source) for source, target in forward]
    low = lax.ppermute(jnp.swapaxes(energy[:, -2:, :], 0, 1), "tile", forward)
    high = lax.ppermute(jnp.swapaxes(energy[:, :2, :], 0, 1), "tile", backward)

    window = (row_count + 4, col_count)

    def rows_of(field):
        return lax.dynamic_slice(jnp.pad(field, ((2, 2), (0, 0))), (first_row, 0), window)

    sea = rows_of(sea_mask.astype(f32))
    east = rows_of(current_u)
    north = rows_of(current_v)
    sea_up = jnp.pad(sea[1:], ((0, 1), (0, 0)))
    east_up = jnp.pad(east[1:], ((0, 1), (0, 0)))
    open_east = sea * sea_up
    flow_east = open_east * (0.5 * (east + east_up))
    open_north = sea * jnp.pad(sea[:, 1:], ((0, 0), (0, 1)))
    flow_north = open_north * (0.5 * (north + jnp.pad(north[:, 1:], ((0, 0), (0, 1)))))
    sea_new = jnp.concatenate([sea[2:], sea[:2]], axis=0)
    coef = jnp.stack([sea_new, open_east, flow_east, open_north, flow_north, 0.5 * sea, sea, sea], axis=1)

    sea_blocks = sea[2:-2].reshape(blocks, BLOCK)
    lane = jnp.arange(BLOCK)
    earlier = (lane[:, None] < lane[None, :]).astype(jnp.bfloat16)
    rank = jnp.dot(sea_blocks.astype(jnp.bfloat16), earlier, preferred_element_type=f32).astype(i32)
    number = jnp.sum(sea_blocks, axis=1).astype(i32)
    block_ids = jnp.arange(blocks + 1)
    start = jnp.sum(jnp.where(block_ids[None, :blocks] < block_ids[:, None], number[None, :], 0), axis=1)
    offset = start % BLOCK
    tile_of = start // BLOCK
    is_sea = sea_blocks > 0.0
    place = jnp.where(is_sea, rank + offset[:blocks, None], -1)
    slot = jnp.where(is_sea, place % BLOCK, -1)
    index = jnp.sum(jnp.where(slot[:, :, None] == lane[None, None, :], lane[None, :, None], 0), axis=1)

    def turned_tile(tile):
        return jnp.where(tile >= tiles, tiles, (tile + odd * (tiles // 2)) % tiles)

    put = turned_tile(tile_of)
    put = put.at[blocks].set(jnp.where(offset[blocks] == 0, tiles, put[blocks]))
    spill = (offset[:blocks] + number >= BLOCK).astype(i32)
    get_low = jnp.minimum(put[:blocks], tiles - 1)
    get_high = jnp.minimum(turned_tile(tile_of[:blocks] + 1), tiles - 1)
    table = jnp.stack([put, offset, jnp.pad(spill, (0, 1))])
    edge = 2 * halves
    table_wide = jnp.concatenate(
        [jnp.broadcast_to(jnp.array([[tiles], [0], [0]], i32), (3, edge)), table], axis=1
    )
    index_wide = jnp.pad(index, ((edge, edge), (0, 0)))
    table_back = jnp.stack([put[:blocks], get_low, get_high])

    tile_wind = lax.dynamic_slice(wind_forcing, (first_row, 0), (row_count, col_count))
    tile_turn = lax.dynamic_slice(refraction, (first_row, 0), (row_count, col_count))
    fields = jnp.stack([tile_wind, tile_turn] * 4, axis=1)
    packed_fields = pl.pallas_call(
        functools.partial(pack_fields_kernel, row_count),
        grid_spec=pltpu.PrefetchScalarGridSpec(
            num_scalar_prefetch=1,
            grid=(),
            in_specs=[pl.BlockSpec(memory_space=pltpu.VMEM)] * 2,
            out_specs=pl.BlockSpec(memory_space=pltpu.VMEM),
            scratch_shapes=[pltpu.VMEM((8, cells + BLOCK), f32)],
        ),
        out_shape=jax.ShapeDtypeStruct((8, cells), f32),
        name="pack_fields",
        compiler_params=params(16),
    )(table, fields, index)

    angles = (2.0 * math.pi / NTH) * (jnp.arange(comp_total) % NTH).astype(f32)
    speeds = jnp.repeat(group_speed, NTH)
    speed_east = lax.dynamic_slice_in_dim(speeds * jnp.cos(angles), first_comp, local_comps)[:, None]
    speed_north = lax.dynamic_slice_in_dim(speeds * jnp.sin(angles), first_comp, local_comps)[:, None]
    own_growth = lax.dynamic_slice_in_dim(growth, first_comp, local_comps)[:, None]
    own_damping = lax.dynamic_slice_in_dim(damping, first_comp, local_comps)[:, None]

    steps = comps // GROUP

    def group_at(part, tables):
        return (part + tables[0, tables.shape[1] - 1] * (1 - 2 * part)) * steps

    def with_odd(tables):
        return jnp.concatenate([tables, jnp.broadcast_to(odd, (tables.shape[0], 1)).astype(i32)], axis=1)

    table_wide = with_odd(table_wide)
    table_back = with_odd(table_back)

    def propagate(part):
        whole = lambda shape: pl.BlockSpec(shape, lambda s, t: (0,) * len(shape))
        column = pl.BlockSpec((GROUP, 1), lambda s, t: (group_at(part, t) + s, 0))
        halo = pl.BlockSpec((2, GROUP, col_count), lambda s, t: (0, group_at(part, t) + s, 0))
        out_chunk = jax.ShapeDtypeStruct((comps, width), f32)
        outs = pl.pallas_call(
            functools.partial(propagate_kernel, steps),
            grid_spec=pltpu.PrefetchScalarGridSpec(
                num_scalar_prefetch=1,
                grid=(steps,),
                in_specs=[
                    pl.BlockSpec((GROUP, row_count, col_count), lambda s, t: (group_at(part, t) + s, 0, 0)),
                    halo, halo, whole(coef.shape), whole(index_wide.shape), column, column,
                    whole(packed_fields.shape),
                ],
                out_specs=[whole((comps, width))] * (2 * CELL_CHUNKS) + [whole((1, cells))],
                scratch_shapes=[pltpu.VMEM((comps, cells + BLOCK), f32)],
            ),
            out_shape=[out_chunk] * (2 * CELL_CHUNKS) + [jax.ShapeDtypeStruct((1, cells), f32)],
            name="propagate_chunk",
            compiler_params=params(44),
            cost_estimate=pl.CostEstimate(
                flops=60 * comps * row_count * col_count,
                bytes_accessed=4 * comps * (row_count * col_count + cells), transcendentals=0,
            ),
        )(table_wide, energy, low, high, coef, index_wide, speed_east, speed_north, packed_fields)
        return outs[:CELL_CHUNKS], outs[CELL_CHUNKS : 2 * CELL_CHUNKS], outs[-1]

    pairs = [(i, i ^ 1) for i in range(comp_count)]
    apart = [(i, i - 2 if i % 2 == 0 else i + 2) for i in range(comp_count)]
    apart = [(a, b) for a, b in apart if 0 <= b < comp_count]
    across = [(b, a) for a, b in apart]
    own, other, received, sums = [], [], [], []
    from_own, from_received = [], []
    for part in range(2):
        kept, sent, level_sum = propagate(part)
        got = [lax.ppermute(piece, "comp", pairs) for piece in sent]
        own.append(kept)
        other.append(sent)
        received.append(got)
        sums.append(level_sum)
        from_own.append([lax.ppermute(piece, "comp", apart) for piece in kept])
        from_received.append([lax.ppermute(piece, "comp", across) for piece in got])

    def swap(levels):
        return jnp.where(odd > 0, jnp.roll(levels, half, axis=1), levels)

    mean_level = swap(lax.psum(swap(sums[0] + sums[1]), "comp")) / comp_total

    dia_index, coupling, _ = lax.optimization_barrier((dia_index, coupling, sums[0]))
    chunk_ids = jnp.arange(8)
    even_first = 8 * pair_pos - 4 + 2 * chunk_ids
    odd_first = 8 * pair_pos + 10 - 2 * chunk_ids
    chunk_first = NTH * jnp.where(odd > 0, odd_first, even_first)
    margin = 8 * NTH
    dia_pad = jnp.pad(dia_index, ((0, 0), (margin, margin)), constant_values=-1)
    coupling_pad = jnp.pad(coupling, (margin, margin))
    own_ids = jnp.arange(comps)
    targets, rates = [], []
    for j in range(1, 7):
        targets.append(lax.dynamic_slice(dia_pad, (0, chunk_first[j] + margin), (4, comps)))
        rates.append(lax.dynamic_slice_in_dim(coupling_pad, chunk_first[j] + margin, comps))
    lookup = []
    for j in range(1, 7):
        ids = jnp.concatenate([chunk_first[j + d] + own_ids for d in (-1, 0, 1)])
        lookup.append((targets[j - 1].reshape(4 * comps)[:, None] == ids[None, :]).astype(jnp.bfloat16))
    lookup = jnp.stack(lookup)
    out_ids = jnp.concatenate([chunk_first[j] + own_ids for j in range(2, 6)])
    spread = []
    for j in range(1, 7):
        for pair in range(2):
            hits = [
                (out_ids[:, None] == targets[j - 1][2 * pair + q][None, :]).astype(f32) for q in range(2)
            ]
            spread.append(hits[0] + hits[1])
    spread = jnp.concatenate(spread, axis=1).astype(jnp.bfloat16)
    rates = jnp.concatenate(rates)[:, None]

    lanes = 512 if width % 512 == 0 else width
    own_parts, back_parts = [], []
    for c in range(CELL_CHUNKS):
        levels = [
            from_received[1][c], from_received[0][c], own[0][c], own[1][c],
            received[1][c], received[0][c], from_own[0][c], from_own[1][c],
        ]
        own_part, back_part = pl.pallas_call(
            interact_kernel,
            grid=(width // lanes,),
            in_specs=[
                pl.BlockSpec(lookup.shape, lambda s: (0, 0, 0)),
                pl.BlockSpec(spread.shape, lambda s: (0, 0)),
                pl.BlockSpec(rates.shape, lambda s: (0, 0)),
            ] + [pl.BlockSpec((comps, lanes), lambda s: (0, s))] * 8,
            out_specs=[pl.BlockSpec((2 * comps, lanes), lambda s: (0, s))] * 2,
            out_shape=[jax.ShapeDtypeStruct((2 * comps, width), f32)] * 2,
            scratch_shapes=[pltpu.VMEM((12 * comps, lanes), jnp.bfloat16)],
            name="interact_cells",
            compiler_params=params(32),
            cost_estimate=pl.CostEstimate(
                flops=2 * width * comps * comps * (6 * 12 + 48),
                bytes_accessed=4 * comps * width * 12, transcendentals=0,
            ),
        )(lookup, spread, rates, *levels)
        own_parts.append(own_part)
        back_parts.append(lax.ppermute(back_part, "comp", pairs))

    def finish(part, so_far):
        whole = lambda shape: pl.BlockSpec(shape, lambda s, t: (0,) * len(shape))
        column = pl.BlockSpec((GROUP, 1), lambda s, t: (group_at(part, t) + s, 0))
        piece = pl.BlockSpec((GROUP, width), lambda s, t: (s, 0))
        own_piece = pl.BlockSpec((GROUP, width), lambda s, t: (part * steps + s, 0))
        back_piece = pl.BlockSpec((GROUP, width), lambda s, t: ((1 - part) * steps + s, 0))
        inputs = [place, mean_level, packed_fields, own_growth, own_damping]
        specs = [whole(place.shape), whole(mean_level.shape), whole(packed_fields.shape), column, column]
        inputs += list(own[part]) + list(other[part]) + own_parts + back_parts
        specs += [piece] * (2 * CELL_CHUNKS) + [own_piece] * CELL_CHUNKS + [back_piece] * CELL_CHUNKS
        aliases = {}
        if so_far is not None:
            inputs.append(so_far)
            specs.append(pl.BlockSpec(memory_space=pl.ANY))
            aliases = {len(inputs): 0}
        return pl.pallas_call(
            functools.partial(finish_kernel, CELL_CHUNKS),
            grid_spec=pltpu.PrefetchScalarGridSpec(
                num_scalar_prefetch=1,
                grid=(steps,),
                in_specs=specs,
                out_specs=pl.BlockSpec((GROUP, row_count, col_count), lambda s, t: (group_at(part, t) + s, 0, 0)),
                scratch_shapes=[pltpu.VMEM((GROUP, cells), f32)],
            ),
            out_shape=jax.ShapeDtypeStruct(energy.shape, f32),
            input_output_aliases=aliases,
            name="finish_chunk",
            compiler_params=params(40),
            cost_estimate=pl.CostEstimate(
                flops=20 * comps * row_count * col_count,
                bytes_accessed=4 * comps * (row_count * col_count + 2 * cells), transcendentals=0,
            ),
        )(table_back, *inputs)

    return finish(1, finish(0, None))


def choose_shards(energy, *rest):
    local_comps, row_count, col_count = energy.shape
    fits = (
        local_comps == 4 * NTH and lax.axis_size("comp") % 2 == 0
        and lax.axis_size("comp") * local_comps == NTH * NF
        and row_count % 8 == 0 and col_count == 2 * BLOCK
    )
    return packed_shards(energy, *rest) if fits else shards(energy, *rest)


def solution(mesh):
    placed = (
        P("comp", ("grp", "tile"), None),
        P("grp", None),
        P("grp", None),
        P("grp", None),
        P("grp", None),
        P("grp", None),
        P(),
        P(),
        P(),
        P(),
        P(),
    )
    return jax.shard_map(
        choose_shards,
        mesh=mesh,
        in_specs=placed,
        out_specs=P("comp", ("grp", "tile"), None),
        check_vma=False,
    )
```

```python
import functools
import math

import jax
import jax.numpy as jnp
import numpy as np
from jax import lax
from jax.experimental import pallas as pl
from jax.experimental.pallas import tpu as pltpu
from jax.sharding import PartitionSpec as P

NTH = 36
NF = 32


weight_plus = 0.4096
weight_minus = 3.1605
weight_cross = 1.2945


def with_halo(block, sides, width):
    for axis, dim in sides:
        count = lax.axis_size(axis)
        forward = [(i, i + 1) for i in range(count - 1)]
        backward = [(target, source) for source, target in forward]
        low = lax.ppermute(
            lax.slice_in_dim(block, block.shape[dim] - width, None, axis=dim), axis, forward
        )
        high = lax.ppermute(lax.slice_in_dim(block, 0, width, axis=dim), axis, backward)
        block = jnp.concatenate([low, block, high], axis=dim)
    return block


def quick_flux(far_left, left_cell, right_cell, far_right, courant):
    centre = 0.5 * (left_cell + right_cell) - 0.5 * courant * (right_cell - left_cell)
    curvature = (1.0 - courant * courant) / 6.0
    upward = centre - curvature * (right_cell - 2.0 * left_cell + far_left)
    downward = centre - curvature * (left_cell - 2.0 * right_cell + far_right)
    return courant * jnp.where(courant > 0.0, upward, downward)


def flux_change(padded, speed, current, sea_pad, axis):
    cell_count = padded.shape[axis] - 4

    def take_part(source, first, which_axis):
        return lax.slice_in_dim(source, first, first + cell_count + 1, axis=which_axis)

    face_current = 0.5 * (take_part(current, 0, axis - 1) + take_part(current, 1, axis - 1))
    courant = speed[:, None, None] + face_current[None]
    open_face = (take_part(sea_pad, 0, axis - 1) * take_part(sea_pad, 1, axis - 1))[None]
    face_flux = (
        quick_flux(
            take_part(padded, 0, axis),
            take_part(padded, 1, axis),
            take_part(padded, 2, axis),
            take_part(padded, 3, axis),
            courant,
        )
        * open_face
    )
    return lax.slice_in_dim(face_flux, 1, cell_count + 1, axis=axis) - lax.slice_in_dim(
        face_flux, 0, cell_count, axis=axis
    )


def source_terms(energy_block, wind, turning, growth, damping, coupling, lookup, spread):
    cell_count = energy_block.shape[1]
    spectrum = energy_block.reshape(NF, NTH, cell_count)
    turn_rate = turning[None, None, :]
    next_dir = jnp.roll(spectrum, -1, axis=1)
    forward = jnp.maximum(turn_rate, 0.0)
    backward = jnp.minimum(turn_rate, 0.0)
    upper_flux = forward * spectrum + backward * next_dir
    lower_flux = jnp.roll(upper_flux, 1, axis=1)
    turned = (spectrum - upper_flux + lower_flux).reshape(energy_block.shape)
    rounded = turned.astype(jnp.bfloat16)
    plus_first, minus_first, plus_second, minus_second = lookup(rounded)
    couple_rate = coupling[:, None]
    delta_first = couple_rate * (
        turned * turned * (weight_plus * plus_first + weight_minus * minus_first)
        - 2.0 * weight_cross * turned * plus_first * minus_first
    )
    delta_second = couple_rate * (
        turned * turned * (weight_plus * plus_second + weight_minus * minus_second)
        - 2.0 * weight_cross * turned * plus_second * minus_second
    )
    moved = spread(delta_first.astype(jnp.bfloat16), delta_second.astype(jnp.bfloat16))
    mean_level = jnp.sum(turned, axis=0) / energy_block.shape[0]
    return (
        turned
        + growth[:, None] * wind[None] * turned
        - damping[:, None] * mean_level[None] * turned
        - 2.0 * (delta_first + delta_second)
        + moved
    )


def shards(
    energy,
    sea_mask,
    current_u,
    current_v,
    wind_forcing,
    refraction,
    group_speed,
    growth,
    damping,
    coupling,
    dia_index,
):
    comp_count = lax.axis_size("comp")
    comp_pos = lax.axis_index("comp")
    tile_pos = lax.axis_index("tile")
    local_comps, row_count, col_count = energy.shape
    first_row = tile_pos * row_count
    first_comp = comp_pos * local_comps
    comp_total = NTH * NF
    angles = 2.0 * math.pi / NTH * (jnp.arange(comp_total) % NTH).astype(jnp.float32)
    speeds = jnp.repeat(group_speed, NTH)
    speed_east = lax.dynamic_slice_in_dim(speeds * jnp.cos(angles), first_comp, local_comps)
    speed_north = lax.dynamic_slice_in_dim(speeds * jnp.sin(angles), first_comp, local_comps)
    window = (row_count + 2, col_count + 2)
    sea_pad = lax.dynamic_slice(jnp.pad(sea_mask.astype(jnp.float32), 1), (first_row, 0), window)
    east_pad = lax.dynamic_slice(jnp.pad(current_u, 1), (first_row, 0), window)
    north_pad = lax.dynamic_slice(jnp.pad(current_v, 1), (first_row, 0), window)
    sea_tile = sea_pad[1:-1, 1:-1]
    masked = energy * sea_tile[None]
    padded_east = with_halo(masked, (("tile", 1),), 2)
    along_east = flux_change(padded_east, speed_east, east_pad[:, 1:-1], sea_pad[:, 1:-1], 1)
    along_north = flux_change(
        jnp.pad(masked, ((0, 0), (0, 0), (2, 2))),
        speed_north,
        north_pad[1:-1, :],
        sea_pad[1:-1, :],
        2,
    )
    propagated = (sea_tile[None] * (masked - along_east - along_north)).reshape(
        local_comps, row_count * col_count
    )
    tile_wind = lax.dynamic_slice(wind_forcing, (first_row, 0), (row_count, col_count)).reshape(-1)
    tile_turn = lax.dynamic_slice(refraction, (first_row, 0), (row_count, col_count)).reshape(-1)
    comp_ids = jnp.arange(comp_total)
    tables = [
        (dia_index[slot_row][:, None] == comp_ids[None, :]).astype(jnp.bfloat16)
        for slot_row in range(4)
    ]

    def lookup(rounded):
        return tuple(
            (
                jnp.dot(tables[slot_row], rounded, preferred_element_type=jnp.float32)
                for slot_row in range(4)
            )
        )

    def scatter_back(table, terms):
        return lax.dot_general(
            table, terms, (((0,), (0,)), ((), ())), preferred_element_type=jnp.float32
        )

    def spread(first_terms, second_terms):
        return (
            scatter_back(tables[0], first_terms)
            + scatter_back(tables[1], first_terms)
            + scatter_back(tables[2], second_terms)
            + scatter_back(tables[3], second_terms)
        )

    share_size = row_count * col_count // comp_count
    point_field = lax.all_to_all(propagated, "comp", split_axis=1, concat_axis=0, tiled=True)
    first_point = comp_pos * share_size
    own_wind = lax.dynamic_slice_in_dim(tile_wind, first_point, share_size)
    own_turn = lax.dynamic_slice_in_dim(tile_turn, first_point, share_size)
    result = source_terms(
        point_field, own_wind, own_turn, growth, damping, coupling, lookup, spread
    )
    returned_field = lax.all_to_all(result, "comp", split_axis=0, concat_axis=1, tiled=True)
    return returned_field.reshape(local_comps, row_count, col_count)


BLOCK = 128
GROUP = 24
CELL_CHUNKS = 4
MIB = 1024 * 1024
EDGE = 2
SEA, OPEN_EAST, FLOW_EAST, OPEN_NORTH, FLOW_NORTH, HALF_SEA, WIND, TURN = range(8)
PUT, OFFSET, SPILL, NEXT = range(4)


def row_of(ref, row):
    return ref[row : row + 1, :]


def upwind(courant, here, ahead, slope_here, bend_here, bend_ahead):
    square = courant * courant
    bend = jnp.where(courant > 0.0, bend_here, bend_ahead)
    return courant * ((here + ahead) - courant * slope_here - (1.0 / 3.0 - square * (1.0 / 3.0)) * bend)


def pack_block(block, index, offset, spill, tile, out_ref, rows, held):
    lanes = lax.broadcasted_iota(jnp.int32, block.shape, 1)
    moved = jnp.take_along_axis(block, jnp.broadcast_to(index, block.shape), axis=1)
    merged = jnp.where(lanes >= offset, moved, held)
    out_ref[rows, pl.ds(pl.multiple_of(tile * BLOCK, BLOCK), BLOCK)] = merged
    return jnp.where(spill > 0, moved, merged)


def prepare_kernel(places, base_ref, speed_ref, sea_ref, east_ref, north_ref, wind_ref, turn_ref, cos_ref, sin_ref,
                   coef_ref, index_ref, place_ref, table_ref, speed_east_ref, speed_north_ref, field_ref, pick_ref):
    first_row, odd, first_freq = base_ref[0], base_ref[1], base_ref[2]
    all_rows, col_count = sea_ref.shape
    row_count = place_ref.shape[1]
    tiles = places // BLOCK
    sea = sea_ref[...].astype(jnp.float32)
    row = lax.broadcasted_iota(jnp.int32, sea.shape, 0)
    col = lax.broadcasted_iota(jnp.int32, sea.shape, 1)

    def next_row(field):
        return jnp.where(row == all_rows - 1, 0.0, pltpu.roll(field, all_rows - 1, 0))

    def next_col(field):
        return jnp.where(col == col_count - 1, 0.0, pltpu.roll(field, col_count - 1, 1))

    open_east, open_north = sea * next_row(sea), sea * next_col(sea)
    east, north = east_ref[...], north_ref[...]
    field_ref[SEA] = sea
    field_ref[OPEN_EAST] = open_east
    field_ref[FLOW_EAST] = open_east * (0.5 * (east + next_row(east)))
    field_ref[OPEN_NORTH] = open_north
    field_ref[FLOW_NORTH] = open_north * (0.5 * (north + next_col(north)))
    field_ref[HALF_SEA] = 0.5 * sea
    field_ref[WIND] = wind_ref[...]
    field_ref[TURN] = turn_ref[...]
    coef_ref[0:EDGE] = jnp.zeros((EDGE, 8, col_count), jnp.float32)
    coef_ref[EDGE + all_rows :] = jnp.zeros((EDGE, 8, col_count), jnp.float32)

    @pl.loop(0, all_rows // 8)
    def _(i):
        rows = field_ref[:, pl.ds(pl.multiple_of(8 * i, 8), 8), :]
        coef_ref[pl.ds(8 * i + EDGE, 8)] = jnp.swapaxes(rows, 0, 1)

    freqs = cos_ref.shape[0] // NTH
    for f in range(freqs):
        circle = slice(f * NTH, (f + 1) * NTH)
        speed_east_ref[circle, :] = cos_ref[circle, :] * speed_ref[first_freq + f]
        speed_north_ref[circle, :] = sin_ref[circle, :] * speed_ref[first_freq + f]

    bf16, f32 = jnp.bfloat16, jnp.float32
    tile_sea = sea_ref[pl.ds(pl.multiple_of(first_row, 8), row_count), :].astype(f32)
    square = (BLOCK, BLOCK)
    down, over = lax.broadcasted_iota(jnp.int32, square, 0), lax.broadcasted_iota(jnp.int32, square, 1)
    before = (down < over).astype(f32).astype(bf16)
    ones = jnp.ones(square, bf16)
    row_square = (row_count, row_count)
    above = lax.broadcasted_iota(jnp.int32, row_square, 1) < lax.broadcasted_iota(jnp.int32, row_square, 0)
    above = above.astype(f32).astype(bf16)
    parts = [tile_sea[:, :BLOCK], tile_sea[:, BLOCK:]]
    numbers = [jnp.dot(p.astype(bf16), ones, preferred_element_type=f32) for p in parts]
    in_row = numbers[0] + numbers[1]
    starts = [jnp.dot(above, in_row.astype(bf16), preferred_element_type=f32)]
    starts.append(starts[0] + numbers[0])
    total = jnp.sum(in_row, axis=0, keepdims=True).astype(jnp.int32)

    def turned_tile(tile):
        return jnp.where(tile >= tiles, tiles, jnp.bitwise_and(tile + odd * (tiles // 2), tiles - 1))

    index_ref[...] = jnp.zeros(index_ref.shape, jnp.int32)
    wide = (8, 2 * BLOCK)
    wide_lane = lax.broadcasted_iota(jnp.int32, wide, 1)
    wide_row = lax.broadcasted_iota(jnp.int32, wide, 0)
    columns = []
    for h in range(2):
        rank = jnp.dot(parts[h].astype(bf16), before, preferred_element_type=f32).astype(jnp.int32)
        start = starts[h].astype(jnp.int32)
        offset = jnp.bitwise_and(start, BLOCK - 1)
        is_sea = parts[h] > 0.0
        place = jnp.where(is_sea, rank + offset, -1)
        place_ref[h] = place
        slot = jnp.where(is_sea, jnp.bitwise_and(place, BLOCK - 1), -1).astype(f32).T
        from_lane = down[:, :row_count].astype(f32)

        @pl.loop(0, BLOCK // 8)
        def _(i):
            found = []
            for k in range(8):
                lane = (8 * i + k).astype(f32)
                found.append(jnp.sum(jnp.where(slot == lane, from_lane, 0.0), axis=0, keepdims=True))
            pick_ref[pl.ds(pl.multiple_of(8 * i, 8), 8), :] = jnp.concatenate(found, axis=0)

        index_ref[h, EDGE : EDGE + row_count, :] = pick_ref[...].T.astype(jnp.int32)
        start_row = starts[h].T[0:8, :].astype(jnp.int32)
        end_row = (starts[h] + numbers[h]).T[0:8, :].astype(jnp.int32)
        tile = lax.shift_right_logical(start_row, 7)
        offset_row = jnp.bitwise_and(start_row, BLOCK - 1)
        spill = jnp.where(offset_row + (end_row - start_row) >= BLOCK, 1, 0)
        columns += [turned_tile(tile), offset_row, spill, jnp.minimum(turned_tile(tile + 1), tiles - 1)]
    empty = jnp.where(jnp.bitwise_and(wide_row, 3) == PUT, tiles, 0)
    merged = jnp.zeros((8, row_count), jnp.int32)
    for k, column in enumerate(columns):
        merged = jnp.where(wide_row[:, :row_count] == k, column, merged)
    merged = jnp.concatenate([merged, jnp.zeros((8, 2 * BLOCK - row_count), jnp.int32)], axis=1)
    merged = pltpu.roll(merged, EDGE, 1)
    inside = (wide_lane >= EDGE) & (wide_lane < EDGE + row_count)
    end_offset = jnp.bitwise_and(total, BLOCK - 1)
    end_tile = jnp.where(end_offset == 0, tiles, turned_tile(lax.shift_right_logical(total, 7)))
    end_tile = jnp.concatenate([end_tile, end_tile], axis=1)
    result = jnp.where(inside, merged, empty)
    table_ref[...] = jnp.where((wide_lane == EDGE + row_count + EDGE) & (wide_row == PUT), end_tile, result)


def pack_fields_kernel(row_count, base_ref, table_ref, coef_ref, index_ref, out_ref, wide_ref):
    def some_rows(first, count, held):
        picks = [index_ref[h, pl.ds(first, count), :] for h in range(2)]
        for at in range(count):
            row = first + at
            fields = coef_ref[base_ref[0] + row]
            for h in range(2):
                held = pack_block(
                    fields[:, h * BLOCK : (h + 1) * BLOCK], picks[h][at : at + 1, :], table_ref[4 * h + OFFSET, row],
                    table_ref[4 * h + SPILL, row], table_ref[4 * h + PUT, row], wide_ref, slice(None), held,
                )
        return held

    held = jnp.zeros((8, BLOCK), jnp.float32)
    held = lax.fori_loop(
        0, row_count // 8, lambda i, held: some_rows(pl.multiple_of(8 * i, 8), 8, held), held
    )
    held = some_rows(row_count, EDGE, held)
    last = table_ref[PUT, row_count + 2 * EDGE]
    wide_ref[:, pl.ds(pl.multiple_of(last * BLOCK, BLOCK), BLOCK)] = held
    out_ref[...] = wide_ref[:, : out_ref.shape[1]]


def propagate_kernel(part, steps, base_ref, table_ref, energy_ref, low_ref, high_ref, coef_ref, index_ref, east_ref,
                     north_ref, fields_ref, *refs):
    wide_ref, rows_ref, sems = refs[-3:]
    sum_ref, outs = refs[-4], refs[:-4]
    step_id = pl.program_id(0)
    row_count, col_count = energy_ref.shape[1:]
    first_row = base_ref[0]
    first_comp = (part + base_ref[1] * (1 - 2 * part)) * steps * GROUP
    lane = lax.broadcasted_iota(jnp.int32, (8, col_count), 1)
    first_lane, last_lane = lane == 0, lane == col_count - 1

    def fetch(step):
        comps = pl.ds(first_comp + step * GROUP, GROUP)

        @pl.loop(0, row_count, unroll=4)
        def _(r):
            pltpu.make_async_copy(energy_ref.at[comps, r, :], rows_ref.at[step % 2, r], sems.at[step % 2]).start()

    @pl.when(step_id == 0)
    def _():
        fetch(0)

    @pl.when(step_id + 1 < steps)
    def _():
        fetch(step_id + 1)

    slot = step_id % 2
    pltpu.make_async_copy(rows_ref.at[slot], rows_ref.at[slot], sems.at[slot]).wait()

    def cell_row(row, picks, fresh, state, east, north, rows):
        here, ahead, bend_here, flux_low, held = state
        coef = coef_ref.at[first_row + row]
        new = fresh * row_of(coef_ref.at[first_row + row + EDGE], SEA)
        slope = ahead - here
        bend_ahead = (new - ahead) - slope
        flux = upwind(east * row_of(coef, OPEN_EAST) + row_of(coef, FLOW_EAST), here, ahead, slope, bend_here,
                      bend_ahead)
        right = jnp.where(last_lane, 0.0, pltpu.roll(here, col_count - 1, 1))
        left = jnp.where(first_lane, 0.0, pltpu.roll(here, 1, 1))
        slope_right = right - here
        bend = slope_right - (here - left)
        cross = upwind(north * row_of(coef, OPEN_NORTH) + row_of(coef, FLOW_NORTH), here, right, slope_right, bend,
                       pltpu.roll(bend, col_count - 1, 1))
        moved = row_of(coef, HALF_SEA) * ((here + here) - (flux - flux_low) - (cross - pltpu.roll(cross, 1, 1)))
        for h in range(2):
            held = pack_block(
                moved[:, h * BLOCK : (h + 1) * BLOCK], picks[h], table_ref[4 * h + OFFSET, row],
                table_ref[4 * h + SPILL, row], table_ref[4 * h + PUT, row], wide_ref, rows, held,
            )
        return ahead, new, bend_ahead, flux, held

    @pl.loop(0, GROUP // 8)
    def _(g):
        local = pl.ds(pl.multiple_of(g * 8, 8), 8)
        rows = pl.ds(pl.multiple_of(step_id * GROUP + g * 8, 8), 8)
        east = jnp.concatenate([east_ref[local, :]] * 2, axis=1)
        north = jnp.concatenate([north_ref[local, :]] * 2, axis=1)
        here = low_ref[0, local, :] * row_of(coef_ref.at[first_row], SEA)
        ahead = low_ref[1, local, :] * row_of(coef_ref.at[first_row + 1], SEA)
        zero = jnp.zeros_like(here)
        state = (here, ahead, zero, zero, jnp.zeros((8, BLOCK), jnp.float32))

        def eight(i, state):
            picks = [index_ref[h, pl.ds(pl.multiple_of(8 * i, 8), 8), :] for h in range(2)]
            for at in range(8):
                state = cell_row(8 * i + at, [p[at : at + 1, :] for p in picks],
                                 rows_ref[slot, 8 * i + at, local, :], state, east, north, rows)
            return state

        state = lax.fori_loop(0, row_count // 8, eight, state)
        picks = [index_ref[h, row_count : row_count + EDGE, :] for h in range(2)]
        for at in range(EDGE):
            state = cell_row(row_count + at, [p[at : at + 1, :] for p in picks], high_ref[at, local, :], state,
                             east, north, rows)
        last = table_ref[PUT, row_count + 2 * EDGE]
        wide_ref[rows, pl.ds(pl.multiple_of(last * BLOCK, BLOCK), BLOCK)] = state[-1]

    @pl.when(step_id == steps - 1)
    def _():
        comps, width = outs[0].shape
        tile_width = 2 * BLOCK
        comp_row = lax.broadcasted_iota(jnp.int32, (comps, tile_width), 0)
        circle_row = comp_row % NTH
        for o, out_ref in enumerate(outs):

            @pl.loop(0, width // tile_width)
            def _(i):
                source = pl.ds(pl.multiple_of(o * width + i * tile_width, tile_width), tile_width)
                target = pl.ds(pl.multiple_of(i * tile_width, tile_width), tile_width)
                level = wide_ref[:, source]
                rate = fields_ref[TURN : TURN + 1, source]
                forward = jnp.maximum(rate, 0.0)
                backward = jnp.minimum(rate, 0.0)
                after = pltpu.roll(level, comps - 1, 0)
                before = pltpu.roll(level, 1, 0)
                for start in range(0, comps, NTH):
                    end = start + NTH - 1
                    after = jnp.where(comp_row == end, level[start : start + 1, :], after)
                    before = jnp.where(comp_row == start, level[end : end + 1, :], before)
                turned = (1.0 - forward + backward) * level - backward * after + forward * before
                out_ref[:, target] = turned
                sum_ref[:, source] = jnp.sum(turned, axis=0, keepdims=True)


def interact_kernel(table_ref, spread_ref, coupling_ref, *refs):
    window, own_ref, back_ref, delta_ref = refs[:8], refs[8], refs[9], refs[10]
    comps = window[0].shape[0]
    kept = []
    for j in range(1, 7):
        level = window[j][...]
        around = jnp.concatenate([window[j - 1][...], level, window[j + 1][...]], axis=0).astype(jnp.bfloat16)
        partner = jnp.dot(table_ref[j - 1], around, preferred_element_type=jnp.float32)
        rate = coupling_ref[(j - 1) * comps : j * comps, :] * level
        plus_part = weight_plus * level
        minus_part = weight_minus * level
        deltas = []
        for pair in range(2):
            plus = partner[2 * pair * comps : (2 * pair + 1) * comps, :]
            minus = partner[(2 * pair + 1) * comps : (2 * pair + 2) * comps, :]
            deltas.append(rate * (plus * (plus_part - (2.0 * weight_cross) * minus) + minus_part * minus))
        both = jnp.concatenate(deltas, axis=0).astype(jnp.bfloat16)
        delta_ref[(j - 1) * 2 * comps : j * 2 * comps, :] = both
        if 2 <= j <= 5:
            part = -2.0 * (deltas[0] + deltas[1])
            target = own_ref if j <= 3 else back_ref
            at = (j % 2) * comps
            target[at : at + comps, :] = part
    spread = jnp.dot(spread_ref[...], delta_ref[...], preferred_element_type=jnp.float32)
    own_ref[...] += spread[: 2 * comps, :]
    back_ref[...] += spread[2 * comps :, :]


def finish_kernel(chunks, base_ref, table_ref, place_ref, mean_ref, fields_ref, growth_ref, damping_ref, *refs):
    turned, own, back = refs[: 2 * chunks], refs[2 * chunks : 3 * chunks], refs[3 * chunks : 4 * chunks]
    out_ref, wide_ref = refs[-2], refs[-1]
    width = own[0].shape[1]
    tiles = wide_ref.shape[1] // BLOCK
    tile_width = 2 * BLOCK
    for o in range(2 * chunks):
        extra = own[o] if o < chunks else back[o - chunks]

        @pl.loop(0, width // tile_width)
        def _(i):
            source = pl.ds(pl.multiple_of(i * tile_width, tile_width), tile_width)
            target = pl.ds(pl.multiple_of(o * width + i * tile_width, tile_width), tile_width)
            scale = (1.0 + growth_ref[...] * fields_ref[WIND : WIND + 1, target]
                     - damping_ref[...] * mean_ref[0:1, target])
            wide_ref[:, target] = turned[o][:, source] * scale + extra[:, source]

    lane = lax.broadcasted_iota(jnp.int32, (8, BLOCK), 1)

    @pl.loop(0, GROUP // 8)
    def _(g):
        local = pl.ds(pl.multiple_of(g * 8, 8), 8)

        @pl.loop(0, out_ref.shape[1] // 8)
        def _(i):
            places = [place_ref[h, pl.ds(pl.multiple_of(8 * i, 8), 8), :] for h in range(2)]
            grid_rows = []
            for r in range(8):
                parts = []
                for h in range(2):
                    row = 8 * i + r + EDGE
                    place = jnp.broadcast_to(places[h][r : r + 1, :], (8, BLOCK))
                    first = jnp.minimum(table_ref[4 * h + PUT, row], tiles - 1)
                    second = table_ref[4 * h + NEXT, row]
                    low = wide_ref[local, pl.ds(pl.multiple_of(first * BLOCK, BLOCK), BLOCK)]
                    high = wide_ref[local, pl.ds(pl.multiple_of(second * BLOCK, BLOCK), BLOCK)]
                    near = jnp.where(lane >= table_ref[4 * h + OFFSET, row], low, high)
                    level = jnp.take_along_axis(near, jnp.bitwise_and(place, BLOCK - 1), axis=1)
                    parts.append(jnp.where(place >= 0, level, 0.0))
                grid_rows.append(jnp.concatenate(parts, axis=1))
            out_ref[local, pl.ds(pl.multiple_of(8 * i, 8), 8), :] = jnp.swapaxes(jnp.stack(grid_rows), 0, 1)


def params(limit):
    return pltpu.CompilerParams(vmem_limit_bytes=limit * MIB)


def after(value, *others):
    return lax.optimization_barrier((value,) + others)[0]


def packed_shards(energy, sea_mask, current_u, current_v, wind_forcing, refraction, group_speed, growth, damping,
                  coupling, dia_index):
    comp_count = lax.axis_size("comp")
    comp_pos = lax.axis_index("comp")
    tile_pos = lax.axis_index("tile")
    odd = lax.rem(comp_pos, 2)
    pair_pos = comp_pos // 2
    local_comps, row_count, col_count = energy.shape
    comps = local_comps // 2
    comp_total = NTH * NF
    first_row = tile_pos * row_count
    first_comp = comp_pos * local_comps
    cells = row_count * col_count // 2
    half = cells // 2
    width = half // CELL_CHUNKS
    f32, i32 = jnp.float32, jnp.int32
    base = jnp.stack([first_row, odd, comp_pos * (local_comps // NTH)]).astype(i32)

    tile_count = lax.axis_size("tile")
    forward = [(i, i + 1) for i in range(tile_count - 1)]
    backward = [(target, source) for source, target in forward]
    low = lax.ppermute(jnp.swapaxes(energy[:, -EDGE:, :], 0, 1), "tile", forward)
    high = lax.ppermute(jnp.swapaxes(energy[:, :EDGE, :], 0, 1), "tile", backward)

    all_rows = sea_mask.shape[0]
    angles = np.float32(2.0 * math.pi / NTH) * (np.arange(local_comps) % NTH).astype(np.float32)
    cosines = np.broadcast_to(np.cos(angles)[:, None], (local_comps, BLOCK)).astype(np.float32)
    sines = np.broadcast_to(np.sin(angles)[:, None], (local_comps, BLOCK)).astype(np.float32)
    vmem = pl.BlockSpec(memory_space=pltpu.VMEM)
    padded_rows = row_count + 8
    coef, index, place, table, speed_east, speed_north = pl.pallas_call(
        functools.partial(prepare_kernel, cells),
        grid_spec=pltpu.PrefetchScalarGridSpec(
            num_scalar_prefetch=2,
            grid=(),
            in_specs=[vmem] * 7,
            out_specs=[vmem] * 6,
            scratch_shapes=[pltpu.VMEM((8, all_rows, col_count), f32), pltpu.VMEM((BLOCK, row_count), f32)],
        ),
        out_shape=[
            jax.ShapeDtypeStruct((all_rows + 2 * EDGE, 8, col_count), f32),
            jax.ShapeDtypeStruct((2, padded_rows, BLOCK), i32),
            jax.ShapeDtypeStruct((2, row_count, BLOCK), i32),
            jax.ShapeDtypeStruct((8, 2 * BLOCK), i32),
            jax.ShapeDtypeStruct((local_comps, BLOCK), f32),
            jax.ShapeDtypeStruct((local_comps, BLOCK), f32),
        ],
        name="prepare",
        compiler_params=params(24),
    )(base, group_speed, sea_mask, current_u, current_v, wind_forcing, refraction, cosines, sines)
    packed_fields = pl.pallas_call(
        functools.partial(pack_fields_kernel, row_count),
        grid_spec=pltpu.PrefetchScalarGridSpec(
            num_scalar_prefetch=2,
            grid=(),
            in_specs=[vmem] * 2,
            out_specs=vmem,
            scratch_shapes=[pltpu.VMEM((8, cells + BLOCK), f32)],
        ),
        out_shape=jax.ShapeDtypeStruct((8, cells), f32),
        name="pack_fields",
        compiler_params=params(16),
    )(base, table, coef, index)

    steps = comps // GROUP

    def group_at(part, base_ref):
        return (part + base_ref[1] * (1 - 2 * part)) * steps

    def whole(shape):
        return pl.BlockSpec(shape, lambda s, b, t: (0,) * len(shape))

    def column(part, lanes):
        return pl.BlockSpec((GROUP, lanes), lambda s, b, t: (group_at(part, b) + s, 0))

    def propagate(part, table):
        halo = pl.BlockSpec((EDGE, GROUP, col_count), lambda s, b, t: (0, group_at(part, b) + s, 0))
        out_chunk = jax.ShapeDtypeStruct((comps, width), f32)
        outs = pl.pallas_call(
            functools.partial(propagate_kernel, part, steps),
            grid_spec=pltpu.PrefetchScalarGridSpec(
                num_scalar_prefetch=2,
                grid=(steps,),
                in_specs=[
                    pl.BlockSpec(memory_space=pl.ANY), halo, halo, whole(coef.shape), whole(index.shape),
                    column(part, BLOCK), column(part, BLOCK), whole(packed_fields.shape),
                ],
                out_specs=[whole((comps, width))] * (2 * CELL_CHUNKS) + [whole((1, cells))],
                scratch_shapes=[
                    pltpu.VMEM((comps, cells + BLOCK), f32),
                    pltpu.VMEM((2, row_count, GROUP, col_count), f32),
                    pltpu.SemaphoreType.DMA((2,)),
                ],
            ),
            out_shape=[out_chunk] * (2 * CELL_CHUNKS) + [jax.ShapeDtypeStruct((1, cells), f32)],
            name="propagate_chunk",
            compiler_params=params(44),
            cost_estimate=pl.CostEstimate(
                flops=60 * comps * row_count * col_count, bytes_accessed=100 * MIB, transcendentals=0,
            ),
        )(base, table, energy, low, high, coef, index, speed_east, speed_north, packed_fields)
        return list(outs[:CELL_CHUNKS]), list(outs[CELL_CHUNKS : 2 * CELL_CHUNKS]), outs[-1]

    pairs = [(i, i ^ 1) for i in range(comp_count)]
    apart = [(i, i - 2 if i % 2 == 0 else i + 2) for i in range(comp_count)]
    apart = [(a, b) for a, b in apart if 0 <= b < comp_count]
    across = [(b, a) for a, b in apart]
    chunk_range = range(CELL_CHUNKS)
    kept_0, sent_0, sums_0 = propagate(0, table)
    got_0 = [lax.ppermute(piece, "comp", pairs) for piece in sent_0]
    from_own_0 = [lax.ppermute(piece, "comp", apart) for piece in kept_0]
    kept_1, sent_1, sums_1 = propagate(1, after(table, sums_0))
    from_got_0 = [lax.ppermute(piece, "comp", across) for piece in got_0]
    got_1, from_own_1 = [], []
    for c in chunk_range:
        waits = [got_0[c]] + ([got_1[c - 2]] if c >= 2 else [])
        got_1.append(lax.ppermute(after(sent_1[c], *waits), "comp", pairs))
        from_own_1.append(lax.ppermute(after(kept_1[c], from_own_0[c]), "comp", apart))

    def swap(levels):
        return jnp.where(odd > 0, jnp.roll(levels, half, axis=1), levels)

    mean_level = swap(lax.psum(swap(sums_0 + sums_1), "comp")) / comp_total

    dia_index, coupling, growth, damping, _ = lax.optimization_barrier(
        (dia_index, coupling, growth, damping, sums_0)
    )
    own_growth = lax.dynamic_slice_in_dim(growth, first_comp, local_comps)[:, None]
    own_damping = lax.dynamic_slice_in_dim(damping, first_comp, local_comps)[:, None]
    chunk_ids = jnp.arange(8)
    even_first = 8 * pair_pos - 4 + 2 * chunk_ids
    odd_first = 8 * pair_pos + 10 - 2 * chunk_ids
    chunk_first = NTH * jnp.where(odd > 0, odd_first, even_first)
    margin = 8 * NTH
    dia_pad = jnp.pad(dia_index, ((0, 0), (margin, margin)), constant_values=-1)
    coupling_pad = jnp.pad(coupling, (margin, margin))
    own_ids = jnp.arange(comps)
    targets, rates = [], []
    for j in range(1, 7):
        targets.append(lax.dynamic_slice(dia_pad, (0, chunk_first[j] + margin), (4, comps)))
        rates.append(lax.dynamic_slice_in_dim(coupling_pad, chunk_first[j] + margin, comps))
    lookup = []
    for j in range(1, 7):
        ids = jnp.concatenate([chunk_first[j + d] + own_ids for d in (-1, 0, 1)])
        lookup.append((targets[j - 1].reshape(4 * comps)[:, None] == ids[None, :]).astype(jnp.bfloat16))
    lookup = jnp.stack(lookup)
    out_ids = jnp.concatenate([chunk_first[j] + own_ids for j in range(2, 6)])
    spread = []
    for j in range(1, 7):
        for pair in range(2):
            hits = [
                (out_ids[:, None] == targets[j - 1][2 * pair + q][None, :]).astype(f32) for q in range(2)
            ]
            spread.append(hits[0] + hits[1])
    spread = jnp.concatenate(spread, axis=1).astype(jnp.bfloat16)
    rates = jnp.concatenate(rates)[:, None]

    lanes = 512 if width % 512 == 0 else width
    own_parts, back_parts = [], []
    for c in chunk_range:
        from_got_1 = lax.ppermute(after(got_1[c], *own_parts[c - 2 : c - 1]) if c >= 2 else got_1[c], "comp", across)
        levels = [
            from_got_1, from_got_0[c], kept_0[c], kept_1[c], got_1[c], got_0[c], from_own_0[c], from_own_1[c],
        ]
        own_part, back_part = pl.pallas_call(
            interact_kernel,
            grid=(width // lanes,),
            in_specs=[
                pl.BlockSpec(lookup.shape, lambda s: (0, 0, 0)),
                pl.BlockSpec(spread.shape, lambda s: (0, 0)),
                pl.BlockSpec(rates.shape, lambda s: (0, 0)),
            ] + [pl.BlockSpec((comps, lanes), lambda s: (0, s))] * 8,
            out_specs=[pl.BlockSpec((2 * comps, lanes), lambda s: (0, s))] * 2,
            out_shape=[jax.ShapeDtypeStruct((2 * comps, width), f32)] * 2,
            scratch_shapes=[pltpu.VMEM((12 * comps, lanes), jnp.bfloat16)],
            name="interact_cells",
            compiler_params=params(32),
            cost_estimate=pl.CostEstimate(
                flops=2 * width * comps * comps * (6 * 12 + 48),
                bytes_accessed=20 * MIB, transcendentals=0,
            ),
        )(lookup, spread, rates, *levels)
        own_parts.append(own_part)
        wait = got_1[c + 2] if c + 2 < CELL_CHUNKS else back_parts[c - 2]
        back_parts.append(lax.ppermute(after(back_part, wait), "comp", pairs))

    def finish(part, so_far):
        piece = pl.BlockSpec((GROUP, width), lambda s, b, t: (s, 0))
        own_piece = pl.BlockSpec((GROUP, width), lambda s, b, t: (part * steps + s, 0))
        back_piece = pl.BlockSpec((GROUP, width), lambda s, b, t: ((1 - part) * steps + s, 0))
        inputs = [place, mean_level, packed_fields, own_growth, own_damping]
        specs = [whole(place.shape), whole(mean_level.shape), whole(packed_fields.shape), column(part, 1),
                 column(part, 1)]
        inputs += [kept_0, kept_1][part] + [sent_0, sent_1][part] + own_parts + back_parts
        specs += [piece] * (2 * CELL_CHUNKS) + [own_piece] * CELL_CHUNKS + [back_piece] * CELL_CHUNKS
        aliases = {}
        if so_far is not None:
            inputs.append(so_far)
            specs.append(pl.BlockSpec(memory_space=pl.ANY))
            aliases = {len(inputs) + 1: 0}
        return pl.pallas_call(
            functools.partial(finish_kernel, CELL_CHUNKS),
            grid_spec=pltpu.PrefetchScalarGridSpec(
                num_scalar_prefetch=2,
                grid=(steps,),
                in_specs=specs,
                out_specs=pl.BlockSpec((GROUP, row_count, col_count), lambda s, b, t: (group_at(part, b) + s, 0, 0)),
                scratch_shapes=[pltpu.VMEM((GROUP, cells), f32)],
            ),
            out_shape=jax.ShapeDtypeStruct(energy.shape, f32),
            input_output_aliases=aliases,
            name="finish_chunk",
            compiler_params=params(40),
            cost_estimate=pl.CostEstimate(
                flops=20 * comps * row_count * col_count,
                bytes_accessed=100 * MIB, transcendentals=0,
            ),
        )(base, table, *inputs)

    return finish(1, finish(0, None))


def choose_shards(energy, *rest):
    local_comps, row_count, col_count = energy.shape
    fits = (
        local_comps == 4 * NTH and lax.axis_size("comp") % 2 == 0
        and lax.axis_size("comp") * local_comps == NTH * NF
        and row_count % 8 == 0 and col_count == 2 * BLOCK
    )
    return packed_shards(energy, *rest) if fits else shards(energy, *rest)


def solution(mesh):
    placed = (
        P("comp", ("grp", "tile"), None),
        P("grp", None),
        P("grp", None),
        P("grp", None),
        P("grp", None),
        P("grp", None),
        P(),
        P(),
        P(),
        P(),
        P(),
    )
    return jax.shard_map(
        choose_shards,
        mesh=mesh,
        in_specs=placed,
        out_specs=P("comp", ("grp", "tile"), None),
        check_vma=False,
    )
```

```python
import functools
import math

import jax
import jax.numpy as jnp
import numpy as np
from jax import lax
from jax.experimental import pallas as pl
from jax.experimental.pallas import tpu as pltpu
from jax.sharding import PartitionSpec as P

NTH = 36
NF = 32


weight_plus = 0.4096
weight_minus = 3.1605
weight_cross = 1.2945


def with_halo(block, sides, width):
    for axis, dim in sides:
        count = lax.axis_size(axis)
        forward = [(i, i + 1) for i in range(count - 1)]
        backward = [(target, source) for source, target in forward]
        low = lax.ppermute(
            lax.slice_in_dim(block, block.shape[dim] - width, None, axis=dim), axis, forward
        )
        high = lax.ppermute(lax.slice_in_dim(block, 0, width, axis=dim), axis, backward)
        block = jnp.concatenate([low, block, high], axis=dim)
    return block


def quick_flux(far_left, left_cell, right_cell, far_right, courant):
    centre = 0.5 * (left_cell + right_cell) - 0.5 * courant * (right_cell - left_cell)
    curvature = (1.0 - courant * courant) / 6.0
    upward = centre - curvature * (right_cell - 2.0 * left_cell + far_left)
    downward = centre - curvature * (left_cell - 2.0 * right_cell + far_right)
    return courant * jnp.where(courant > 0.0, upward, downward)


def flux_change(padded, speed, current, sea_pad, axis):
    cell_count = padded.shape[axis] - 4

    def take_part(source, first, which_axis):
        return lax.slice_in_dim(source, first, first + cell_count + 1, axis=which_axis)

    face_current = 0.5 * (take_part(current, 0, axis - 1) + take_part(current, 1, axis - 1))
    courant = speed[:, None, None] + face_current[None]
    open_face = (take_part(sea_pad, 0, axis - 1) * take_part(sea_pad, 1, axis - 1))[None]
    face_flux = (
        quick_flux(
            take_part(padded, 0, axis),
            take_part(padded, 1, axis),
            take_part(padded, 2, axis),
            take_part(padded, 3, axis),
            courant,
        )
        * open_face
    )
    return lax.slice_in_dim(face_flux, 1, cell_count + 1, axis=axis) - lax.slice_in_dim(
        face_flux, 0, cell_count, axis=axis
    )


def source_terms(energy_block, wind, turning, growth, damping, coupling, lookup, spread):
    cell_count = energy_block.shape[1]
    spectrum = energy_block.reshape(NF, NTH, cell_count)
    turn_rate = turning[None, None, :]
    next_dir = jnp.roll(spectrum, -1, axis=1)
    forward = jnp.maximum(turn_rate, 0.0)
    backward = jnp.minimum(turn_rate, 0.0)
    upper_flux = forward * spectrum + backward * next_dir
    lower_flux = jnp.roll(upper_flux, 1, axis=1)
    turned = (spectrum - upper_flux + lower_flux).reshape(energy_block.shape)
    rounded = turned.astype(jnp.bfloat16)
    plus_first, minus_first, plus_second, minus_second = lookup(rounded)
    couple_rate = coupling[:, None]
    delta_first = couple_rate * (
        turned * turned * (weight_plus * plus_first + weight_minus * minus_first)
        - 2.0 * weight_cross * turned * plus_first * minus_first
    )
    delta_second = couple_rate * (
        turned * turned * (weight_plus * plus_second + weight_minus * minus_second)
        - 2.0 * weight_cross * turned * plus_second * minus_second
    )
    moved = spread(delta_first.astype(jnp.bfloat16), delta_second.astype(jnp.bfloat16))
    mean_level = jnp.sum(turned, axis=0) / energy_block.shape[0]
    return (
        turned
        + growth[:, None] * wind[None] * turned
        - damping[:, None] * mean_level[None] * turned
        - 2.0 * (delta_first + delta_second)
        + moved
    )


def shards(
    energy,
    sea_mask,
    current_u,
    current_v,
    wind_forcing,
    refraction,
    group_speed,
    growth,
    damping,
    coupling,
    dia_index,
):
    comp_count = lax.axis_size("comp")
    comp_pos = lax.axis_index("comp")
    tile_pos = lax.axis_index("tile")
    local_comps, row_count, col_count = energy.shape
    first_row = tile_pos * row_count
    first_comp = comp_pos * local_comps
    comp_total = NTH * NF
    angles = 2.0 * math.pi / NTH * (jnp.arange(comp_total) % NTH).astype(jnp.float32)
    speeds = jnp.repeat(group_speed, NTH)
    speed_east = lax.dynamic_slice_in_dim(speeds * jnp.cos(angles), first_comp, local_comps)
    speed_north = lax.dynamic_slice_in_dim(speeds * jnp.sin(angles), first_comp, local_comps)
    window = (row_count + 2, col_count + 2)
    sea_pad = lax.dynamic_slice(jnp.pad(sea_mask.astype(jnp.float32), 1), (first_row, 0), window)
    east_pad = lax.dynamic_slice(jnp.pad(current_u, 1), (first_row, 0), window)
    north_pad = lax.dynamic_slice(jnp.pad(current_v, 1), (first_row, 0), window)
    sea_tile = sea_pad[1:-1, 1:-1]
    masked = energy * sea_tile[None]
    padded_east = with_halo(masked, (("tile", 1),), 2)
    along_east = flux_change(padded_east, speed_east, east_pad[:, 1:-1], sea_pad[:, 1:-1], 1)
    along_north = flux_change(
        jnp.pad(masked, ((0, 0), (0, 0), (2, 2))),
        speed_north,
        north_pad[1:-1, :],
        sea_pad[1:-1, :],
        2,
    )
    propagated = (sea_tile[None] * (masked - along_east - along_north)).reshape(
        local_comps, row_count * col_count
    )
    tile_wind = lax.dynamic_slice(wind_forcing, (first_row, 0), (row_count, col_count)).reshape(-1)
    tile_turn = lax.dynamic_slice(refraction, (first_row, 0), (row_count, col_count)).reshape(-1)
    comp_ids = jnp.arange(comp_total)
    tables = [
        (dia_index[slot_row][:, None] == comp_ids[None, :]).astype(jnp.bfloat16)
        for slot_row in range(4)
    ]

    def lookup(rounded):
        return tuple(
            (
                jnp.dot(tables[slot_row], rounded, preferred_element_type=jnp.float32)
                for slot_row in range(4)
            )
        )

    def scatter_back(table, terms):
        return lax.dot_general(
            table, terms, (((0,), (0,)), ((), ())), preferred_element_type=jnp.float32
        )

    def spread(first_terms, second_terms):
        return (
            scatter_back(tables[0], first_terms)
            + scatter_back(tables[1], first_terms)
            + scatter_back(tables[2], second_terms)
            + scatter_back(tables[3], second_terms)
        )

    share_size = row_count * col_count // comp_count
    point_field = lax.all_to_all(propagated, "comp", split_axis=1, concat_axis=0, tiled=True)
    first_point = comp_pos * share_size
    own_wind = lax.dynamic_slice_in_dim(tile_wind, first_point, share_size)
    own_turn = lax.dynamic_slice_in_dim(tile_turn, first_point, share_size)
    result = source_terms(
        point_field, own_wind, own_turn, growth, damping, coupling, lookup, spread
    )
    returned_field = lax.all_to_all(result, "comp", split_axis=0, concat_axis=1, tiled=True)
    return returned_field.reshape(local_comps, row_count, col_count)


BLOCK = 128
GROUP = 24
CELL_CHUNKS = 4
MIB = 1024 * 1024
VMEM_MIB = 60
EDGE = 2
SEA, OPEN_EAST, FLOW_EAST, OPEN_NORTH, FLOW_NORTH, HALF_SEA, WIND, TURN = range(8)
KEEP, SPILL, IS_SEA = BLOCK, 2 * BLOCK, 2 * BLOCK


def row_of(ref, row):
    return ref[row : row + 1, :]


def upwind(courant, here, ahead, slope_here, bend_here, bend_ahead):
    square = courant * courant
    bend = jnp.where(courant > 0.0, bend_here, bend_ahead)
    return courant * ((here + ahead) - courant * slope_here - (1.0 / 3.0 - square * (1.0 / 3.0)) * bend)


def pick_lanes(block, index):
    return jnp.take_along_axis(block, index, axis=1, mode="promise_in_bounds")


def tile_at(tile):
    return pl.ds(pl.multiple_of(tile * BLOCK, BLOCK), BLOCK)


def has(code, flag):
    return jnp.bitwise_and(code, flag) != 0


def pack_block(blocks, code, tile, out_ref, firsts, held):
    code = jnp.broadcast_to(code, (8, BLOCK))
    index = jnp.bitwise_and(code, BLOCK - 1)
    keep, spill = has(code, KEEP), has(code, SPILL)
    result = []
    for block, first, old in zip(blocks, firsts, held):
        moved = pick_lanes(block, index)
        merged = jnp.where(keep, moved, old)
        out_ref[pl.ds(first, 8), tile_at(tile)] = merged
        result.append(jnp.where(spill, moved, merged))
    return tuple(result)


def prepare_kernel(places, base_ref, speed_ref, sea_ref, east_ref, north_ref, wind_ref, turn_ref, cos_ref, sin_ref,
                   coef_ref, index_ref, place_ref, table_ref, speed_east_ref, speed_north_ref, field_ref, pick_ref):
    first_row, odd, first_freq = base_ref[0], base_ref[1], base_ref[2]
    all_rows, col_count = sea_ref.shape
    row_count = place_ref.shape[1]
    tiles = places // BLOCK
    sea = sea_ref[...].astype(jnp.float32)
    row = lax.broadcasted_iota(jnp.int32, sea.shape, 0)
    col = lax.broadcasted_iota(jnp.int32, sea.shape, 1)

    def next_row(field):
        return jnp.where(row == all_rows - 1, 0.0, pltpu.roll(field, all_rows - 1, 0))

    def next_col(field):
        return jnp.where(col == col_count - 1, 0.0, pltpu.roll(field, col_count - 1, 1))

    open_east, open_north = sea * next_row(sea), sea * next_col(sea)
    east, north = east_ref[...], north_ref[...]
    field_ref[SEA] = sea
    field_ref[OPEN_EAST] = open_east
    field_ref[FLOW_EAST] = open_east * (0.5 * (east + next_row(east)))
    field_ref[OPEN_NORTH] = open_north
    field_ref[FLOW_NORTH] = open_north * (0.5 * (north + next_col(north)))
    field_ref[HALF_SEA] = 0.5 * sea
    field_ref[WIND] = wind_ref[...]
    field_ref[TURN] = turn_ref[...]
    coef_ref[0:EDGE] = jnp.zeros((EDGE, 8, col_count), jnp.float32)
    coef_ref[EDGE + all_rows :] = jnp.zeros((EDGE, 8, col_count), jnp.float32)

    @pl.loop(0, all_rows // 8)
    def _(i):
        rows = field_ref[:, pl.ds(pl.multiple_of(8 * i, 8), 8), :]
        coef_ref[pl.ds(8 * i + EDGE, 8)] = jnp.swapaxes(rows, 0, 1)

    freqs = cos_ref.shape[0] // NTH
    for f in range(freqs):
        circle = slice(f * NTH, (f + 1) * NTH)
        speed_east_ref[circle, :] = cos_ref[circle, :] * speed_ref[first_freq + f]
        speed_north_ref[circle, :] = sin_ref[circle, :] * speed_ref[first_freq + f]

    bf16, f32 = jnp.bfloat16, jnp.float32
    tile_sea = sea_ref[pl.ds(pl.multiple_of(first_row, 8), row_count), :].astype(f32)
    square = (BLOCK, BLOCK)
    down, over = lax.broadcasted_iota(jnp.int32, square, 0), lax.broadcasted_iota(jnp.int32, square, 1)
    before = (down < over).astype(f32).astype(bf16)
    ones = jnp.ones(square, bf16)
    row_square = (row_count, row_count)
    above = lax.broadcasted_iota(jnp.int32, row_square, 1) < lax.broadcasted_iota(jnp.int32, row_square, 0)
    above = above.astype(f32).astype(bf16)
    parts = [tile_sea[:, :BLOCK], tile_sea[:, BLOCK:]]
    numbers = [jnp.dot(p.astype(bf16), ones, preferred_element_type=f32) for p in parts]
    in_row = numbers[0] + numbers[1]
    starts = [jnp.dot(above, in_row.astype(bf16), preferred_element_type=f32)]
    starts.append(starts[0] + numbers[0])
    total = jnp.sum(in_row, axis=0, keepdims=True).astype(jnp.int32)

    def turned_tile(tile):
        return jnp.where(tile >= tiles, tiles, jnp.bitwise_and(tile + odd * (tiles // 2), tiles - 1))

    columns = []
    for h in range(2):
        rank = jnp.dot(parts[h].astype(bf16), before, preferred_element_type=f32).astype(jnp.int32)
        start = starts[h].astype(jnp.int32)
        offset = jnp.bitwise_and(start, BLOCK - 1)
        keep = jnp.where(over[:row_count] >= offset, KEEP, 0)
        slot = jnp.bitwise_and(rank + offset, BLOCK - 1)
        is_sea = parts[h] > 0.0
        place_ref[h] = slot + keep + jnp.where(is_sea, IS_SEA, 0)
        slot = jnp.where(is_sea, slot, -1).astype(f32).T
        from_lane = down[:, :row_count].astype(f32)

        @pl.loop(0, BLOCK // 8)
        def _(i):
            found = []
            for k in range(8):
                lane = (8 * i + k).astype(f32)
                found.append(jnp.sum(jnp.where(slot == lane, from_lane, 0.0), axis=0, keepdims=True))
            pick_ref[pl.ds(pl.multiple_of(8 * i, 8), 8), :] = jnp.concatenate(found, axis=0)

        spill = jnp.where(offset + numbers[h].astype(jnp.int32) >= BLOCK, SPILL, 0)
        index_ref[h] = pick_ref[...].T.astype(jnp.int32) + keep + spill
        columns.append(turned_tile(lax.shift_right_logical(starts[h].T[0:8, :].astype(jnp.int32), 7)))
    row_id = lax.broadcasted_iota(jnp.int32, (8, row_count), 0)
    end_tile = jnp.where(
        jnp.bitwise_and(total, BLOCK - 1) == 0, tiles, turned_tile(lax.shift_right_logical(total, 7))
    )
    end_tile = jnp.broadcast_to(end_tile, (8, BLOCK))
    table_ref[...] = jnp.concatenate([jnp.where(row_id == 0, columns[0], columns[1]), end_tile], axis=1)


def pack_fields_kernel(row_count, base_ref, table_ref, coef_ref, index_ref, out_ref, wide_ref):
    def eight(i, held):
        codes = [index_ref[h, pl.ds(pl.multiple_of(8 * i, 8), 8), :] for h in range(2)]
        for at in range(8):
            row = 8 * i + at
            fields = coef_ref[base_ref[0] + EDGE + row]
            for h in range(2):
                block = fields[:, h * BLOCK : (h + 1) * BLOCK]
                held = pack_block([block], codes[h][at : at + 1, :], table_ref[h, row], wide_ref, [0], held)
        return held

    held = lax.fori_loop(0, row_count // 8, eight, (jnp.zeros((8, BLOCK), jnp.float32),))
    wide_ref[:, tile_at(table_ref[0, row_count])] = held[0]
    out_ref[...] = wide_ref[:, : out_ref.shape[1]]


def propagate_kernel(part, steps, base_ref, table_ref, energy_ref, halo_ref, coef_ref, index_ref, east_ref,
                     north_ref, fields_ref, *refs):
    wide_ref, rows_ref, sems = refs[-3:]
    sum_ref, outs = refs[-4], refs[:-4]
    step_id = pl.program_id(0)
    row_count, col_count = energy_ref.shape[1:]
    first_row = base_ref[0]
    first_comp = (part + base_ref[1] * (1 - 2 * part)) * steps * GROUP
    lane = lax.broadcasted_iota(jnp.int32, (8, BLOCK), 1)
    first_lane, last_lane = lane == 0, lane == BLOCK - 1

    def fetch(step):
        comps = pl.ds(first_comp + step * GROUP, GROUP)

        @pl.loop(0, row_count, unroll=4)
        def _(r):
            pltpu.make_async_copy(energy_ref.at[comps, r, :], rows_ref.at[step % 2, r], sems.at[step % 2]).start()

    @pl.when(step_id == 0)
    def _():
        fetch(0)

    @pl.when(step_id + 1 < steps)
    def _():
        fetch(step_id + 1)

    slot = step_id % 2
    pltpu.make_async_copy(rows_ref.at[slot], rows_ref.at[slot], sems.at[slot]).wait()

    def halves(row):
        return row[:, :BLOCK], row[:, BLOCK:]

    def masked(row, at):
        sea_row = halves(coef_ref.at[first_row + at][SEA : SEA + 1, :])
        return tuple(part * sea for part, sea in zip(halves(row), sea_row))

    def cell_row(at, new, state, east, north):
        here, ahead, bend_here, flux_low = state
        coef = [halves(row_of(coef_ref.at[first_row + at], k)) for k in range(HALF_SEA + 1)]
        to_right = [pltpu.roll(part, BLOCK - 1, 1) for part in here]
        to_left = [pltpu.roll(part, 1, 1) for part in here]
        right = (jnp.where(last_lane, to_right[1], to_right[0]), jnp.where(last_lane, 0.0, to_right[1]))
        left = (jnp.where(first_lane, 0.0, to_left[0]), jnp.where(first_lane, to_left[0], to_left[1]))
        slope_right = [right[h] - here[h] for h in range(2)]
        bend = [slope_right[h] - (here[h] - left[h]) for h in range(2)]
        bend_roll = [pltpu.roll(part, BLOCK - 1, 1) for part in bend]
        bend_right = (jnp.where(last_lane, bend_roll[1], bend_roll[0]), bend_roll[1])
        cross, flux, bend_ahead = [], [], []
        for h in range(2):
            cross.append(upwind(north * coef[OPEN_NORTH][h] + coef[FLOW_NORTH][h], here[h], right[h],
                                slope_right[h], bend[h], bend_right[h]))
            slope = ahead[h] - here[h]
            bend_ahead.append((new[h] - ahead[h]) - slope)
            flux.append(upwind(east * coef[OPEN_EAST][h] + coef[FLOW_EAST][h], here[h], ahead[h], slope,
                               bend_here[h], bend_ahead[h]))
        cross_roll = [pltpu.roll(part, 1, 1) for part in cross]
        cross_low = (jnp.where(first_lane, cross_roll[1], cross_roll[0]),
                     jnp.where(first_lane, cross_roll[0], cross_roll[1]))
        moved = [
            coef[HALF_SEA][h] * ((here[h] + here[h]) - (flux[h] - flux_low[h]) - (cross[h] - cross_low[h]))
            for h in range(2)
        ]
        return (ahead, new, tuple(bend_ahead), tuple(flux)), jnp.concatenate(moved, axis=1)

    @pl.loop(0, GROUP // 8)
    def _(g):
        local = pl.ds(pl.multiple_of(g * 8, 8), 8)
        east, north = east_ref[local, :], north_ref[local, :]
        zero = (jnp.zeros((8, BLOCK), jnp.float32),) * 2
        state = (masked(halo_ref[local, 0, :], 0), masked(halo_ref[local, 1, :], 1), zero, zero)

        def eight(i, state):
            fresh = [rows_ref[slot, 8 * i + k, local, :] for k in range(8)]
            done = []
            for k in range(8):
                new = masked(fresh[k], 8 * i + k + EDGE)
                state, moved = cell_row(8 * i + k, new, state, east, north)
                done.append(moved)
            for k in range(8):
                rows_ref[slot, jnp.maximum(8 * i + k - EDGE, 0), local, :] = done[k]
            return state

        state = lax.fori_loop(0, row_count // 8, eight, state)
        for k in range(EDGE):
            new = masked(halo_ref[local, k, :], row_count + EDGE + k)
            state, moved = cell_row(row_count + k, new, state, east, north)
            rows_ref[slot, row_count - EDGE + k, local, :] = moved

    group_rows = [pl.multiple_of(step_id * GROUP + 8 * k, 8) for k in range(GROUP // 8)]

    def pack_eight(i, held):
        codes = [index_ref[h, pl.ds(pl.multiple_of(8 * i, 8), 8), :] for h in range(2)]
        for k in range(8):
            for h in range(2):
                lanes = slice(h * BLOCK, (h + 1) * BLOCK)
                blocks = [rows_ref[slot, 8 * i + k, 8 * n : 8 * n + 8, lanes] for n in range(GROUP // 8)]
                held = pack_block(blocks, codes[h][k : k + 1, :], table_ref[h, 8 * i + k], wide_ref, group_rows, held)
        return held

    empty = (jnp.zeros((8, BLOCK), jnp.float32),) * (GROUP // 8)
    held = lax.fori_loop(0, row_count // 8, pack_eight, empty)
    for first, block in zip(group_rows, held):
        wide_ref[pl.ds(first, 8), tile_at(table_ref[0, row_count])] = block

    @pl.when(step_id == steps - 1)
    def _():
        comps, width = outs[0].shape
        tile_width = 2 * BLOCK
        comp_row = lax.broadcasted_iota(jnp.int32, (comps, tile_width), 0)
        circle_row = comp_row % NTH
        for o, out_ref in enumerate(outs):

            @pl.loop(0, width // tile_width)
            def _(i):
                source = pl.ds(pl.multiple_of(o * width + i * tile_width, tile_width), tile_width)
                target = pl.ds(pl.multiple_of(i * tile_width, tile_width), tile_width)
                level = wide_ref[:, source]
                rate = fields_ref[TURN : TURN + 1, source]
                forward = jnp.maximum(rate, 0.0)
                backward = jnp.minimum(rate, 0.0)
                after = pltpu.roll(level, comps - 1, 0)
                before = pltpu.roll(level, 1, 0)
                for start in range(0, comps, NTH):
                    end = start + NTH - 1
                    after = jnp.where(comp_row == end, level[start : start + 1, :], after)
                    before = jnp.where(comp_row == start, level[end : end + 1, :], before)
                turned = (1.0 - forward + backward) * level - backward * after + forward * before
                out_ref[:, target] = turned
                sum_ref[:, source] = jnp.sum(turned, axis=0, keepdims=True)


def interact_kernel(table_ref, spread_ref, coupling_ref, *refs):
    window, (own_ref, back_0_ref, back_1_ref, delta_ref) = refs[:8], refs[8:]
    comps = window[0].shape[0]
    kept = []
    for j in range(1, 7):
        level = window[j][...]
        around = jnp.concatenate([window[j - 1][...], level, window[j + 1][...]], axis=0).astype(jnp.bfloat16)
        partner = jnp.dot(table_ref[j - 1], around, preferred_element_type=jnp.float32)
        rate = coupling_ref[(j - 1) * comps : j * comps, :] * level
        plus_part = weight_plus * level
        minus_part = weight_minus * level
        deltas = []
        for pair in range(2):
            plus = partner[2 * pair * comps : (2 * pair + 1) * comps, :]
            minus = partner[(2 * pair + 1) * comps : (2 * pair + 2) * comps, :]
            deltas.append(rate * (plus * (plus_part - (2.0 * weight_cross) * minus) + minus_part * minus))
        both = jnp.concatenate(deltas, axis=0).astype(jnp.bfloat16)
        delta_ref[(j - 1) * 2 * comps : j * 2 * comps, :] = both
        if 2 <= j <= 5:
            part = -2.0 * (deltas[0] + deltas[1])
            if j <= 3:
                own_ref[(j - 2) * comps : (j - 1) * comps, :] = part
            elif j == 4:
                back_1_ref[...] = part
            else:
                back_0_ref[...] = part
    spread = jnp.dot(spread_ref[...], delta_ref[...], preferred_element_type=jnp.float32)
    own_ref[...] += spread[: 2 * comps, :]
    back_1_ref[...] += spread[2 * comps : 3 * comps, :]
    back_0_ref[...] += spread[3 * comps :, :]


def finish_kernel(chunks, base_ref, table_ref, place_ref, mean_ref, fields_ref, growth_ref, damping_ref, *refs):
    turned, own, back = refs[: 2 * chunks], refs[2 * chunks : 3 * chunks], refs[3 * chunks : 4 * chunks]
    out_ref, wide_ref = refs[-2], refs[-1]
    width = own[0].shape[1]
    tiles = wide_ref.shape[1] // BLOCK
    tile_width = 2 * BLOCK
    growth = jnp.broadcast_to(growth_ref[...], (GROUP, tile_width))
    damping = jnp.broadcast_to(damping_ref[...], (GROUP, tile_width))
    for o in range(2 * chunks):
        extra = own[o] if o < chunks else back[o - chunks]

        @pl.loop(0, width // tile_width)
        def _(i):
            source = pl.ds(pl.multiple_of(i * tile_width, tile_width), tile_width)
            target = pl.ds(pl.multiple_of(o * width + i * tile_width, tile_width), tile_width)
            scale = 1.0 + growth * fields_ref[WIND : WIND + 1, target] - damping * mean_ref[0:1, target]
            wide_ref[:, target] = turned[o][:, source] * scale + extra[:, source]

    @pl.loop(0, out_ref.shape[1] // 8)
    def _(i):
        codes = [place_ref[h, pl.ds(pl.multiple_of(8 * i, 8), 8), :] for h in range(2)]
        done = [[] for _ in range(GROUP // 8)]
        for r in range(8):
            parts = [[] for _ in range(GROUP // 8)]
            for h in range(2):
                code = jnp.broadcast_to(codes[h][r : r + 1, :], (8, BLOCK))
                index = jnp.bitwise_and(code, BLOCK - 1)
                keep, is_sea = has(code, KEEP), has(code, IS_SEA)
                tile = table_ref[h, 8 * i + r]
                first, second = jnp.minimum(tile, tiles - 1), jnp.bitwise_and(tile + 1, tiles - 1)
                for k in range(GROUP // 8):
                    rows = slice(8 * k, 8 * k + 8)
                    near = jnp.where(keep, wide_ref[rows, tile_at(first)], wide_ref[rows, tile_at(second)])
                    parts[k].append(jnp.where(is_sea, pick_lanes(near, index), 0.0))
            for k in range(GROUP // 8):
                done[k].append(jnp.concatenate(parts[k], axis=1))
        for k in range(GROUP // 8):
            out_ref[8 * k : 8 * k + 8, pl.ds(pl.multiple_of(8 * i, 8), 8), :] = jnp.swapaxes(jnp.stack(done[k]), 0, 1)


def params(limit):
    return pltpu.CompilerParams(vmem_limit_bytes=limit * MIB)


def after(value, *others):
    return lax.optimization_barrier((value,) + others)[0]


def packed_shards(energy, sea_mask, current_u, current_v, wind_forcing, refraction, group_speed, growth, damping,
                  coupling, dia_index):
    comp_count = lax.axis_size("comp")
    comp_pos = lax.axis_index("comp")
    tile_pos = lax.axis_index("tile")
    odd = lax.rem(comp_pos, 2)
    pair_pos = comp_pos // 2
    local_comps, row_count, col_count = energy.shape
    comps = local_comps // 2
    comp_total = NTH * NF
    first_row = tile_pos * row_count
    first_comp = comp_pos * local_comps
    cells = row_count * col_count // 2
    half = cells // 2
    width = half // CELL_CHUNKS
    f32, i32 = jnp.float32, jnp.int32
    base = jnp.stack([first_row, odd, comp_pos * (local_comps // NTH)]).astype(i32)

    edge_first = jnp.where(tile_pos == 0, row_count - EDGE, 0)
    edge_rows = lax.dynamic_slice_in_dim(energy, edge_first, EDGE, axis=1)
    halo_rows = lax.ppermute(edge_rows, "tile", [(0, 1), (1, 0)])

    all_rows = sea_mask.shape[0]
    angles = np.float32(2.0 * math.pi / NTH) * (np.arange(local_comps) % NTH).astype(np.float32)
    cosines = np.broadcast_to(np.cos(angles)[:, None], (local_comps, BLOCK)).astype(np.float32)
    sines = np.broadcast_to(np.sin(angles)[:, None], (local_comps, BLOCK)).astype(np.float32)
    vmem = pl.BlockSpec(memory_space=pltpu.VMEM)
    coef, index, place, table, speed_east, speed_north = pl.pallas_call(
        functools.partial(prepare_kernel, cells),
        grid_spec=pltpu.PrefetchScalarGridSpec(
            num_scalar_prefetch=2,
            grid=(),
            in_specs=[vmem] * 7,
            out_specs=[vmem] * 6,
            scratch_shapes=[pltpu.VMEM((8, all_rows, col_count), f32), pltpu.VMEM((BLOCK, row_count), f32)],
        ),
        out_shape=[
            jax.ShapeDtypeStruct((all_rows + 2 * EDGE, 8, col_count), f32),
            jax.ShapeDtypeStruct((2, row_count, BLOCK), i32),
            jax.ShapeDtypeStruct((2, row_count, BLOCK), i32),
            jax.ShapeDtypeStruct((8, 2 * BLOCK), i32),
            jax.ShapeDtypeStruct((local_comps, BLOCK), f32),
            jax.ShapeDtypeStruct((local_comps, BLOCK), f32),
        ],
        name="prepare",
        compiler_params=params(VMEM_MIB),
    )(base, group_speed, sea_mask, current_u, current_v, wind_forcing, refraction, cosines, sines)
    packed_fields = pl.pallas_call(
        functools.partial(pack_fields_kernel, row_count),
        grid_spec=pltpu.PrefetchScalarGridSpec(
            num_scalar_prefetch=2,
            grid=(),
            in_specs=[vmem] * 2,
            out_specs=vmem,
            scratch_shapes=[pltpu.VMEM((8, cells + BLOCK), f32)],
        ),
        out_shape=jax.ShapeDtypeStruct((8, cells), f32),
        name="pack_fields",
        compiler_params=params(VMEM_MIB),
    )(base, table, coef, index)

    steps = comps // GROUP

    def group_at(part, base_ref):
        return (part + base_ref[1] * (1 - 2 * part)) * steps

    def whole(shape):
        return pl.BlockSpec(shape, lambda s, b, t: (0,) * len(shape))

    def column(part, lanes):
        return pl.BlockSpec((GROUP, lanes), lambda s, b, t: (group_at(part, b) + s, 0))

    def propagate(part, table):
        halo = pl.BlockSpec((GROUP, EDGE, col_count), lambda s, b, t: (group_at(part, b) + s, 0, 0))
        out_chunk = jax.ShapeDtypeStruct((comps, width), f32)
        outs = pl.pallas_call(
            functools.partial(propagate_kernel, part, steps),
            grid_spec=pltpu.PrefetchScalarGridSpec(
                num_scalar_prefetch=2,
                grid=(steps,),
                in_specs=[
                    pl.BlockSpec(memory_space=pl.ANY), halo, whole(coef.shape), whole(index.shape),
                    column(part, BLOCK), column(part, BLOCK), whole(packed_fields.shape),
                ],
                out_specs=[whole((comps, width))] * (2 * CELL_CHUNKS) + [whole((1, cells))],
                scratch_shapes=[
                    pltpu.VMEM((comps, cells + BLOCK), f32),
                    pltpu.VMEM((2, row_count, GROUP, col_count), f32),
                    pltpu.SemaphoreType.DMA((2,)),
                ],
            ),
            out_shape=[out_chunk] * (2 * CELL_CHUNKS) + [jax.ShapeDtypeStruct((1, cells), f32)],
            name="propagate_chunk",
            compiler_params=params(VMEM_MIB),
            cost_estimate=pl.CostEstimate(
                flops=60 * comps * row_count * col_count, bytes_accessed=100 * MIB, transcendentals=0,
            ),
        )(base, table, energy, halo_rows, coef, index, speed_east, speed_north, packed_fields)
        return list(outs[:CELL_CHUNKS]), list(outs[CELL_CHUNKS : 2 * CELL_CHUNKS]), outs[-1]

    pairs = [(i, i ^ 1) for i in range(comp_count)]
    apart = [(i, i - 2 if i % 2 == 0 else i + 2) for i in range(comp_count)]
    apart = [(a, b) for a, b in apart if 0 <= b < comp_count]
    across = [(b, a) for a, b in apart]
    chunk_range = range(CELL_CHUNKS)
    kept_0, sent_0, sums_0 = propagate(0, table)
    got_0 = [lax.ppermute(piece, "comp", pairs) for piece in sent_0]
    from_own_0 = [lax.ppermute(piece, "comp", apart) for piece in kept_0]
    kept_1, sent_1, sums_1 = propagate(1, after(table, sums_0))
    from_got_0 = [lax.ppermute(piece, "comp", across) for piece in got_0]
    sums = sums_0 + sums_1
    partner_sums = lax.ppermute(sums, "comp", pairs)
    partner_sums = jnp.roll(partner_sums, half, axis=1)
    got_1, from_own_1 = [], []
    for c in chunk_range:
        waits = [got_0[c]] + ([got_1[c - 2]] if c >= 2 else []) + ([partner_sums] if c == 2 else [])
        got_1.append(lax.ppermute(after(sent_1[c], *waits), "comp", pairs))
        from_own_1.append(lax.ppermute(after(kept_1[c], from_own_0[c]), "comp", apart))
    sums = sums + partner_sums
    sums = sums_two = sums + lax.ppermute(sums, "comp", [(i, i ^ 2) for i in range(comp_count)])
    sums = sums + lax.ppermute(sums, "comp", [(i, i ^ 4) for i in range(comp_count)])
    mean_level = sums / comp_total

    dia_index, coupling, growth, damping, late_odd, late_pair, _ = lax.optimization_barrier(
        (dia_index, coupling, growth, damping, odd, pair_pos, sums_0)
    )
    own_growth = lax.dynamic_slice_in_dim(growth, first_comp, local_comps)[:, None]
    own_damping = lax.dynamic_slice_in_dim(damping, first_comp, local_comps)[:, None]
    chunk_first = [
        NTH * jnp.where(late_odd > 0, 8 * late_pair + 10 - 2 * j, 8 * late_pair - 4 + 2 * j) for j in range(8)
    ]
    margin = 8 * NTH
    dia_pad = jnp.pad(dia_index, ((0, 0), (margin, margin)), constant_values=-1)
    coupling_pad = jnp.pad(coupling, (margin, margin))
    own_ids = jnp.arange(comps)
    targets, rates = [], []
    for j in range(1, 7):
        targets.append(lax.dynamic_slice(dia_pad, (0, chunk_first[j] + margin), (4, comps)))
        rates.append(lax.dynamic_slice_in_dim(coupling_pad, chunk_first[j] + margin, comps))
    lookup = []
    for j in range(1, 7):
        ids = jnp.concatenate([chunk_first[j + d] + own_ids for d in (-1, 0, 1)])
        lookup.append((targets[j - 1].reshape(4 * comps)[:, None] == ids[None, :]).astype(jnp.bfloat16))
    lookup = jnp.stack(lookup)
    out_ids = jnp.concatenate([chunk_first[j] + own_ids for j in range(2, 6)])
    spread = []
    for j in range(1, 7):
        for pair in range(2):
            hits = [
                (out_ids[:, None] == targets[j - 1][2 * pair + q][None, :]).astype(f32) for q in range(2)
            ]
            spread.append(hits[0] + hits[1])
    spread = jnp.concatenate(spread, axis=1).astype(jnp.bfloat16)
    rates = jnp.concatenate(rates)[:, None]

    lanes = 512 if width % 512 == 0 else width
    own_parts, parts_0, parts_1 = [], [], []
    for c in chunk_range:
        from_got_1 = lax.ppermute(after(got_1[c], *own_parts[c - 2 : c - 1]) if c >= 2 else got_1[c], "comp", across)
        levels = [
            from_got_1, from_got_0[c], kept_0[c], kept_1[c], got_1[c], got_0[c], from_own_0[c], from_own_1[c],
        ]
        own_part, part_0, part_1 = pl.pallas_call(
            interact_kernel,
            grid=(width // lanes,),
            in_specs=[
                pl.BlockSpec(lookup.shape, lambda s: (0, 0, 0)),
                pl.BlockSpec(spread.shape, lambda s: (0, 0)),
                pl.BlockSpec(rates.shape, lambda s: (0, 0)),
            ] + [pl.BlockSpec((comps, lanes), lambda s: (0, s))] * 8,
            out_specs=[pl.BlockSpec((n * comps, lanes), lambda s: (0, s)) for n in (2, 1, 1)],
            out_shape=[jax.ShapeDtypeStruct((n * comps, width), f32) for n in (2, 1, 1)],
            scratch_shapes=[pltpu.VMEM((12 * comps, lanes), jnp.bfloat16)],
            name="interact_cells",
            compiler_params=params(VMEM_MIB),
            cost_estimate=pl.CostEstimate(
                flops=2 * width * comps * comps * (6 * 12 + 48),
                bytes_accessed=20 * MIB, transcendentals=0,
            ),
        )(lookup, spread, rates, *levels)
        own_parts.append(own_part)
        parts_0.append(part_0)
        parts_1.append(part_1)

    def send_back(piece, *waits):
        return lax.ppermute(after(piece, *waits), "comp", pairs)

    back = [[None] * CELL_CHUNKS for _ in range(2)]
    back[0][0] = send_back(parts_0[0], got_1[2], sums_two)
    back[1][0] = send_back(parts_1[0], got_1[3])
    back[0][1] = send_back(parts_0[1], back[0][0], sums)
    back[0][2] = send_back(parts_0[2], back[1][0])
    back[0][3] = send_back(parts_0[3], back[0][1])
    for c in range(1, CELL_CHUNKS):
        back[1][c] = send_back(parts_1[c], back[0][2])

    def finish(part, so_far):
        piece = pl.BlockSpec((GROUP, width), lambda s, b, t: (s, 0))
        own_piece = pl.BlockSpec((GROUP, width), lambda s, b, t: (part * steps + s, 0))
        inputs = [place, mean_level, packed_fields, own_growth, own_damping]
        specs = [whole(place.shape), whole(mean_level.shape), whole(packed_fields.shape), column(part, 1),
                 column(part, 1)]
        inputs += [kept_0, kept_1][part] + [sent_0, sent_1][part] + own_parts + back[part]
        specs += [piece] * (2 * CELL_CHUNKS) + [own_piece] * CELL_CHUNKS + [piece] * CELL_CHUNKS
        aliases = {}
        if so_far is not None:
            inputs.append(so_far)
            specs.append(pl.BlockSpec(memory_space=pl.ANY))
            aliases = {len(inputs) + 1: 0}
        return pl.pallas_call(
            functools.partial(finish_kernel, CELL_CHUNKS),
            grid_spec=pltpu.PrefetchScalarGridSpec(
                num_scalar_prefetch=2,
                grid=(steps,),
                in_specs=specs,
                out_specs=pl.BlockSpec((GROUP, row_count, col_count), lambda s, b, t: (group_at(part, b) + s, 0, 0)),
                scratch_shapes=[pltpu.VMEM((GROUP, cells), f32)],
            ),
            out_shape=jax.ShapeDtypeStruct(energy.shape, f32),
            input_output_aliases=aliases,
            name="finish_chunk",
            compiler_params=params(VMEM_MIB),
            cost_estimate=pl.CostEstimate(
                flops=20 * comps * row_count * col_count,
                bytes_accessed=100 * MIB, transcendentals=0,
            ),
        )(base, table, *inputs)

    return finish(1, finish(0, None))


def choose_shards(energy, *rest):
    local_comps, row_count, col_count = energy.shape
    fits = (
        local_comps == 4 * NTH and lax.axis_size("comp") == 8 and local_comps * 8 == NTH * NF
        and lax.axis_size("tile") == 2 and row_count == BLOCK and col_count == 2 * BLOCK
    )
    return packed_shards(energy, *rest) if fits else shards(energy, *rest)


def solution(mesh):
    placed = (
        P("comp", ("grp", "tile"), None),
        P("grp", None),
        P("grp", None),
        P("grp", None),
        P("grp", None),
        P("grp", None),
        P(),
        P(),
        P(),
        P(),
        P(),
    )
    return jax.shard_map(
        choose_shards,
        mesh=mesh,
        in_specs=placed,
        out_specs=P("comp", ("grp", "tile"), None),
        check_vma=False,
    )
```

```python
import functools
import math

import jax
import jax.numpy as jnp
import numpy as np
from jax import lax
from jax.experimental import pallas as pl
from jax.experimental.pallas import tpu as pltpu
from jax.sharding import PartitionSpec as P

NTH = 36
NF = 32


weight_plus = 0.4096
weight_minus = 3.1605
weight_cross = 1.2945


def with_halo(block, sides, width):
    for axis, dim in sides:
        count = lax.axis_size(axis)
        forward = [(i, i + 1) for i in range(count - 1)]
        backward = [(target, source) for source, target in forward]
        low = lax.ppermute(
            lax.slice_in_dim(block, block.shape[dim] - width, None, axis=dim), axis, forward
        )
        high = lax.ppermute(lax.slice_in_dim(block, 0, width, axis=dim), axis, backward)
        block = jnp.concatenate([low, block, high], axis=dim)
    return block


def quick_flux(far_left, left_cell, right_cell, far_right, courant):
    centre = 0.5 * (left_cell + right_cell) - 0.5 * courant * (right_cell - left_cell)
    curvature = (1.0 - courant * courant) / 6.0
    upward = centre - curvature * (right_cell - 2.0 * left_cell + far_left)
    downward = centre - curvature * (left_cell - 2.0 * right_cell + far_right)
    return courant * jnp.where(courant > 0.0, upward, downward)


def flux_change(padded, speed, current, sea_pad, axis):
    cell_count = padded.shape[axis] - 4

    def take_part(source, first, which_axis):
        return lax.slice_in_dim(source, first, first + cell_count + 1, axis=which_axis)

    face_current = 0.5 * (take_part(current, 0, axis - 1) + take_part(current, 1, axis - 1))
    courant = speed[:, None, None] + face_current[None]
    open_face = (take_part(sea_pad, 0, axis - 1) * take_part(sea_pad, 1, axis - 1))[None]
    face_flux = (
        quick_flux(
            take_part(padded, 0, axis),
            take_part(padded, 1, axis),
            take_part(padded, 2, axis),
            take_part(padded, 3, axis),
            courant,
        )
        * open_face
    )
    return lax.slice_in_dim(face_flux, 1, cell_count + 1, axis=axis) - lax.slice_in_dim(
        face_flux, 0, cell_count, axis=axis
    )


def source_terms(energy_block, wind, turning, growth, damping, coupling, lookup, spread):
    cell_count = energy_block.shape[1]
    spectrum = energy_block.reshape(NF, NTH, cell_count)
    turn_rate = turning[None, None, :]
    next_dir = jnp.roll(spectrum, -1, axis=1)
    forward = jnp.maximum(turn_rate, 0.0)
    backward = jnp.minimum(turn_rate, 0.0)
    upper_flux = forward * spectrum + backward * next_dir
    lower_flux = jnp.roll(upper_flux, 1, axis=1)
    turned = (spectrum - upper_flux + lower_flux).reshape(energy_block.shape)
    rounded = turned.astype(jnp.bfloat16)
    plus_first, minus_first, plus_second, minus_second = lookup(rounded)
    couple_rate = coupling[:, None]
    delta_first = couple_rate * (
        turned * turned * (weight_plus * plus_first + weight_minus * minus_first)
        - 2.0 * weight_cross * turned * plus_first * minus_first
    )
    delta_second = couple_rate * (
        turned * turned * (weight_plus * plus_second + weight_minus * minus_second)
        - 2.0 * weight_cross * turned * plus_second * minus_second
    )
    moved = spread(delta_first.astype(jnp.bfloat16), delta_second.astype(jnp.bfloat16))
    mean_level = jnp.sum(turned, axis=0) / energy_block.shape[0]
    return (
        turned
        + growth[:, None] * wind[None] * turned
        - damping[:, None] * mean_level[None] * turned
        - 2.0 * (delta_first + delta_second)
        + moved
    )


def shards(
    energy,
    sea_mask,
    current_u,
    current_v,
    wind_forcing,
    refraction,
    group_speed,
    growth,
    damping,
    coupling,
    dia_index,
):
    comp_count = lax.axis_size("comp")
    comp_pos = lax.axis_index("comp")
    tile_pos = lax.axis_index("tile")
    local_comps, row_count, col_count = energy.shape
    first_row = tile_pos * row_count
    first_comp = comp_pos * local_comps
    comp_total = NTH * NF
    angles = 2.0 * math.pi / NTH * (jnp.arange(comp_total) % NTH).astype(jnp.float32)
    speeds = jnp.repeat(group_speed, NTH)
    speed_east = lax.dynamic_slice_in_dim(speeds * jnp.cos(angles), first_comp, local_comps)
    speed_north = lax.dynamic_slice_in_dim(speeds * jnp.sin(angles), first_comp, local_comps)
    window = (row_count + 2, col_count + 2)
    sea_pad = lax.dynamic_slice(jnp.pad(sea_mask.astype(jnp.float32), 1), (first_row, 0), window)
    east_pad = lax.dynamic_slice(jnp.pad(current_u, 1), (first_row, 0), window)
    north_pad = lax.dynamic_slice(jnp.pad(current_v, 1), (first_row, 0), window)
    sea_tile = sea_pad[1:-1, 1:-1]
    masked = energy * sea_tile[None]
    padded_east = with_halo(masked, (("tile", 1),), 2)
    along_east = flux_change(padded_east, speed_east, east_pad[:, 1:-1], sea_pad[:, 1:-1], 1)
    along_north = flux_change(
        jnp.pad(masked, ((0, 0), (0, 0), (2, 2))),
        speed_north,
        north_pad[1:-1, :],
        sea_pad[1:-1, :],
        2,
    )
    propagated = (sea_tile[None] * (masked - along_east - along_north)).reshape(
        local_comps, row_count * col_count
    )
    tile_wind = lax.dynamic_slice(wind_forcing, (first_row, 0), (row_count, col_count)).reshape(-1)
    tile_turn = lax.dynamic_slice(refraction, (first_row, 0), (row_count, col_count)).reshape(-1)
    comp_ids = jnp.arange(comp_total)
    tables = [
        (dia_index[slot_row][:, None] == comp_ids[None, :]).astype(jnp.bfloat16)
        for slot_row in range(4)
    ]

    def lookup(rounded):
        return tuple(
            (
                jnp.dot(tables[slot_row], rounded, preferred_element_type=jnp.float32)
                for slot_row in range(4)
            )
        )

    def scatter_back(table, terms):
        return lax.dot_general(
            table, terms, (((0,), (0,)), ((), ())), preferred_element_type=jnp.float32
        )

    def spread(first_terms, second_terms):
        return (
            scatter_back(tables[0], first_terms)
            + scatter_back(tables[1], first_terms)
            + scatter_back(tables[2], second_terms)
            + scatter_back(tables[3], second_terms)
        )

    share_size = row_count * col_count // comp_count
    point_field = lax.all_to_all(propagated, "comp", split_axis=1, concat_axis=0, tiled=True)
    first_point = comp_pos * share_size
    own_wind = lax.dynamic_slice_in_dim(tile_wind, first_point, share_size)
    own_turn = lax.dynamic_slice_in_dim(tile_turn, first_point, share_size)
    result = source_terms(
        point_field, own_wind, own_turn, growth, damping, coupling, lookup, spread
    )
    returned_field = lax.all_to_all(result, "comp", split_axis=0, concat_axis=1, tiled=True)
    return returned_field.reshape(local_comps, row_count, col_count)


BLOCK = 128
GROUP = 24
EARLY = 40
CELL_CHUNKS = 4
MIB = 1024 * 1024
VMEM_MIB = 60
EDGE = 2
SEA, OPEN_EAST, FLOW_EAST, OPEN_NORTH, FLOW_NORTH, HALF_SEA, WIND, TURN = range(8)
KEEP, SPILL, IS_SEA = BLOCK, 2 * BLOCK, 2 * BLOCK


def row_of(ref, row):
    return ref[row : row + 1, :]


def upwind(courant, total, slope, bend_here, bend_ahead):
    bend = jnp.where(courant > 0.0, bend_here, bend_ahead)
    return courant * ((total - bend) - courant * (slope - courant * bend))


def pick_lanes(block, index):
    return jnp.take_along_axis(block, index, axis=1, mode="promise_in_bounds")


def tile_at(tile):
    return pl.ds(pl.multiple_of(tile * BLOCK, BLOCK), BLOCK)


def has(code, flag):
    return jnp.bitwise_and(code, flag) != 0


def pack_block(blocks, code, tile, out_ref, firsts, held):
    code = jnp.broadcast_to(code, (8, BLOCK))
    index = jnp.bitwise_and(code, BLOCK - 1)
    keep, spill = has(code, KEEP), has(code, SPILL)
    result = []
    for block, first, old in zip(blocks, firsts, held):
        moved = pick_lanes(block, index)
        merged = jnp.where(keep, moved, old)
        out_ref[pl.ds(first, 8), tile_at(tile)] = merged
        result.append(jnp.where(spill, moved, merged))
    return tuple(result)


def prepare_kernel(places, base_ref, speed_ref, sea_ref, east_ref, north_ref, wind_ref, turn_ref, cos_ref, sin_ref,
                   coef_ref, index_ref, place_ref, table_ref, speed_east_ref, speed_north_ref, field_ref, pick_ref):
    first_row, odd, first_freq = base_ref[0], base_ref[1], base_ref[2]
    all_rows, col_count = sea_ref.shape
    row_count = place_ref.shape[1]
    tiles = places // BLOCK
    sea = sea_ref[...].astype(jnp.float32)
    row = lax.broadcasted_iota(jnp.int32, sea.shape, 0)
    col = lax.broadcasted_iota(jnp.int32, sea.shape, 1)

    def next_row(field):
        return jnp.where(row == all_rows - 1, 0.0, pltpu.roll(field, all_rows - 1, 0))

    def next_col(field):
        return jnp.where(col == col_count - 1, 0.0, pltpu.roll(field, col_count - 1, 1))

    open_east, open_north = sea * next_row(sea), sea * next_col(sea)
    east, north = east_ref[...], north_ref[...]
    field_ref[SEA] = sea
    field_ref[OPEN_EAST] = open_east
    field_ref[FLOW_EAST] = open_east * (0.5 * (east + next_row(east)))
    field_ref[OPEN_NORTH] = open_north
    field_ref[FLOW_NORTH] = open_north * (0.5 * (north + next_col(north)))
    field_ref[HALF_SEA] = 0.5 * sea
    field_ref[WIND] = wind_ref[...]
    field_ref[TURN] = turn_ref[...]
    coef_ref[0:EDGE] = jnp.zeros((EDGE, 8, col_count), jnp.float32)
    coef_ref[EDGE + all_rows :] = jnp.zeros((EDGE, 8, col_count), jnp.float32)

    @pl.loop(0, all_rows // 8)
    def _(i):
        rows = field_ref[:, pl.ds(pl.multiple_of(8 * i, 8), 8), :]
        coef_ref[pl.ds(8 * i + EDGE, 8)] = jnp.swapaxes(rows, 0, 1)

    freqs = cos_ref.shape[0] // NTH
    for f in range(freqs):
        circle = slice(f * NTH, (f + 1) * NTH)
        speed_east_ref[circle, :] = cos_ref[circle, :] * speed_ref[first_freq + f]
        speed_north_ref[circle, :] = sin_ref[circle, :] * speed_ref[first_freq + f]

    bf16, f32 = jnp.bfloat16, jnp.float32
    tile_sea = sea_ref[pl.ds(pl.multiple_of(first_row, 8), row_count), :].astype(f32)
    square = (BLOCK, BLOCK)
    down, over = lax.broadcasted_iota(jnp.int32, square, 0), lax.broadcasted_iota(jnp.int32, square, 1)
    before = (down < over).astype(f32).astype(bf16)
    ones = jnp.ones(square, bf16)
    row_square = (row_count, row_count)
    above = lax.broadcasted_iota(jnp.int32, row_square, 1) < lax.broadcasted_iota(jnp.int32, row_square, 0)
    above = above.astype(f32).astype(bf16)
    parts = [tile_sea[:, :BLOCK], tile_sea[:, BLOCK:]]
    numbers = [jnp.dot(p.astype(bf16), ones, preferred_element_type=f32) for p in parts]
    in_row = numbers[0] + numbers[1]
    starts = [jnp.dot(above, in_row.astype(bf16), preferred_element_type=f32)]
    starts.append(starts[0] + numbers[0])
    total = jnp.sum(in_row, axis=0, keepdims=True).astype(jnp.int32)

    def turned_tile(tile):
        return jnp.where(tile >= tiles, tiles, jnp.bitwise_and(tile + odd * (tiles // 2), tiles - 1))

    columns = []
    for h in range(2):
        rank = jnp.dot(parts[h].astype(bf16), before, preferred_element_type=f32).astype(jnp.int32)
        start = starts[h].astype(jnp.int32)
        offset = jnp.bitwise_and(start, BLOCK - 1)
        keep = jnp.where(over[:row_count] >= offset, KEEP, 0)
        slot = jnp.bitwise_and(rank + offset, BLOCK - 1)
        is_sea = parts[h] > 0.0
        place_ref[h] = slot + keep + jnp.where(is_sea, IS_SEA, 0)
        slot = jnp.where(is_sea, slot, -1).astype(f32).T
        from_lane = down[:, :row_count].astype(f32)

        @pl.loop(0, BLOCK // 8)
        def _(i):
            found = []
            for k in range(8):
                lane = (8 * i + k).astype(f32)
                found.append(jnp.sum(jnp.where(slot == lane, from_lane, 0.0), axis=0, keepdims=True))
            pick_ref[pl.ds(pl.multiple_of(8 * i, 8), 8), :] = jnp.concatenate(found, axis=0)

        spill = jnp.where(offset + numbers[h].astype(jnp.int32) >= BLOCK, SPILL, 0)
        index_ref[h] = pick_ref[...].T.astype(jnp.int32) + keep + spill
        columns.append(turned_tile(lax.shift_right_logical(starts[h].T[0:8, :].astype(jnp.int32), 7)))
    row_id = lax.broadcasted_iota(jnp.int32, (8, row_count), 0)
    end_tile = jnp.where(
        jnp.bitwise_and(total, BLOCK - 1) == 0, tiles, turned_tile(lax.shift_right_logical(total, 7))
    )
    end_tile = jnp.broadcast_to(end_tile, (8, BLOCK))
    table_ref[...] = jnp.concatenate([jnp.where(row_id == 0, columns[0], columns[1]), end_tile], axis=1)


def propagate_kernel(part, late, pieces, base_ref, table_ref, energy_ref, halo_ref, coef_ref, index_ref, east_ref,
                     north_ref, *refs):
    refs = list(refs)
    with_fields = part == 0 and not late
    fields_ref = None if with_fields else refs.pop(0)
    seam_ref = refs.pop(0) if late else None
    if late:
        refs.pop(0)
    piece_refs = [refs.pop(0) for _ in range(2 * pieces)]
    sum_ref, full_ref = refs.pop(0), refs.pop(0)
    seam_out_ref = None if late else refs.pop(0)
    fields_out_ref = refs.pop(0) if with_fields else None
    rows_ref, wide_ref, result_ref, row_sems, out_sems = refs
    row_count, comp_count, col_count = rows_ref.shape
    strips = comp_count // 8
    sent_rows = piece_refs[0].shape[0]
    cells = result_ref.shape[1]
    first_row = base_ref[0]
    first_comp = pl.multiple_of((part + base_ref[1] * (1 - 2 * part)) * 2 * NTH + late * EARLY, 8)
    lane = lax.broadcasted_iota(jnp.int32, (8, BLOCK), 1)
    first_lane, last_lane = lane == 0, lane == BLOCK - 1
    third = 1.0 / 3.0

    @pl.loop(0, row_count // 8)
    def _(i):
        for k in range(8):
            row = 8 * i + k
            source = energy_ref.at[pl.ds(first_comp, comp_count), row, :]
            pltpu.make_async_copy(source, rows_ref.at[row], row_sems.at[i]).start()

    def halves(row):
        return row[:, :BLOCK], row[:, BLOCK:]

    def masked(row, at):
        sea_row = halves(coef_ref.at[first_row + at][SEA : SEA + 1, :])
        return tuple(part * sea for part, sea in zip(halves(row), sea_row))

    def cell_row(at, new, state, east, north):
        here, ahead, slope_ahead, bend_here, flux_low = state
        coef = [halves(row_of(coef_ref.at[first_row + at], k)) for k in range(HALF_SEA + 1)]
        to_right = [pltpu.roll(part, BLOCK - 1, 1) for part in here]
        right = (jnp.where(last_lane, to_right[1], to_right[0]), jnp.where(last_lane, 0.0, to_right[1]))
        slope = [right[h] - here[h] for h in range(2)]
        slope_roll = [pltpu.roll(part, 1, 1) for part in slope]
        slope_left = (jnp.where(first_lane, here[0], slope_roll[0]),
                      jnp.where(first_lane, slope_roll[0], slope_roll[1]))
        bend = [third * (slope[h] - slope_left[h]) for h in range(2)]
        bend_roll = [pltpu.roll(part, BLOCK - 1, 1) for part in bend]
        bend_right = (jnp.where(last_lane, bend_roll[1], bend_roll[0]), bend_roll[1])
        cross, flux, slope_next, bend_ahead = [], [], [], []
        for h in range(2):
            cross.append(upwind(north * coef[OPEN_NORTH][h] + coef[FLOW_NORTH][h], here[h] + right[h], slope[h],
                                bend[h], bend_right[h]))
            slope_next.append(new[h] - ahead[h])
            bend_ahead.append(third * (slope_next[h] - slope_ahead[h]))
            flux.append(upwind(east * coef[OPEN_EAST][h] + coef[FLOW_EAST][h], here[h] + ahead[h], slope_ahead[h],
                               bend_here[h], bend_ahead[h]))
        cross_roll = [pltpu.roll(part, 1, 1) for part in cross]
        cross_low = (jnp.where(first_lane, cross_roll[1], cross_roll[0]),
                     jnp.where(first_lane, cross_roll[0], cross_roll[1]))
        moved = [
            coef[HALF_SEA][h] * (((here[h] + here[h]) + (flux_low[h] + cross_low[h])) - (flux[h] + cross[h]))
            for h in range(2)
        ]
        return (ahead, new, tuple(slope_next), tuple(bend_ahead), tuple(flux)), jnp.concatenate(moved, axis=1)

    def strip(g, arrive):
        local = pl.ds(pl.multiple_of(g * 8, 8), 8)
        comps = pl.ds(pl.multiple_of(first_comp + g * 8, 8), 8)
        east, north = east_ref[comps, :], north_ref[comps, :]
        zero = (jnp.zeros((8, BLOCK), jnp.float32),) * 2
        here, ahead = masked(halo_ref[comps, 0, :], 0), masked(halo_ref[comps, 1, :], 1)
        state = (here, ahead, tuple(b - a for a, b in zip(here, ahead)), zero, zero)

        def eight(i, state):
            if arrive:
                block = rows_ref.at[pl.ds(8 * i, 8)]
                pltpu.make_async_copy(block, block, row_sems.at[i]).wait()
            fresh = [rows_ref[8 * i + k, local, :] for k in range(8)]
            done = []
            for k in range(8):
                new = masked(fresh[k], 8 * i + k + EDGE)
                state, moved = cell_row(8 * i + k, new, state, east, north)
                done.append(moved)
            for k in range(8):
                rows_ref[jnp.maximum(8 * i + k - EDGE, 0), local, :] = done[k]
            return state

        state = lax.fori_loop(0, row_count // 8, eight, state)
        for k in range(EDGE):
            new = masked(halo_ref[comps, k, :], row_count + EDGE + k)
            state, moved = cell_row(row_count + k, new, state, east, north)
            rows_ref[row_count - EDGE + k, local, :] = moved

    strip(0, True)

    @pl.loop(1, strips)
    def _(g):
        strip(g, False)

    group_rows = [8 * n for n in range(strips + with_fields)]

    def pack_eight(i, held):
        codes = [index_ref[h, pl.ds(pl.multiple_of(8 * i, 8), 8), :] for h in range(2)]
        for k in range(8):
            row = 8 * i + k
            for h in range(2):
                lanes = slice(h * BLOCK, (h + 1) * BLOCK)
                blocks = [rows_ref[row, 8 * n : 8 * n + 8, lanes] for n in range(strips)]
                if with_fields:
                    blocks.append(coef_ref[first_row + EDGE + row, :, lanes])
                held = pack_block(blocks, codes[h][k : k + 1, :], table_ref[h, row], wide_ref, group_rows, held)
        return held

    empty = (jnp.zeros((8, BLOCK), jnp.float32),) * len(group_rows)
    held = lax.fori_loop(0, row_count // 8, pack_eight, empty)
    for first, block in zip(group_rows, held):
        wide_ref[pl.ds(first, 8), tile_at(table_ref[0, row_count])] = block
    if with_fields:
        fields_out_ref[...] = wide_ref[comp_count:, :cells]

    tile_width = 2 * BLOCK
    height = result_ref.shape[0]
    comp_row = lax.broadcasted_iota(jnp.int32, (height, tile_width), 0)
    start = height - NTH if late else 0
    end = start + NTH - 1
    in_circle = (comp_row >= start) & (comp_row <= end)

    @pl.loop(0, cells // tile_width)
    def _(i):
        source = pl.ds(pl.multiple_of(i * tile_width, tile_width), tile_width)
        level = wide_ref[:comp_count, source]
        if late:
            level = jnp.concatenate([seam_ref[:, source], level], axis=0)
        if with_fields:
            rate = wide_ref[comp_count + TURN : comp_count + TURN + 1, source]
        else:
            rate = fields_ref[TURN : TURN + 1, source]
        forward = jnp.maximum(rate, 0.0)
        backward = jnp.minimum(rate, 0.0)
        above = jnp.where(comp_row == end, level[start : start + 1, :], pltpu.roll(level, height - 1, 0))
        below = jnp.where(comp_row == start, level[end : end + 1, :], pltpu.roll(level, 1, 0))
        turned = (1.0 - forward + backward) * level - backward * above + forward * below
        result_ref[:, source] = jnp.where(in_circle, turned, level)
        sum_ref[:, source] = jnp.sum(jnp.where(in_circle, turned, 0.0), axis=0, keepdims=True)

    if not late:
        seam_out_ref[...] = result_ref[sent_rows:, :]
    width = cells // (2 * pieces)
    copies = []
    for n, piece in enumerate(piece_refs):
        source = result_ref.at[:sent_rows, n * width : (n + 1) * width]
        copies.append(pltpu.make_async_copy(source, piece, out_sems.at[n]))
    rows = pl.ds(EARLY - 8 if late else 0, sent_rows)
    copies.append(pltpu.make_async_copy(result_ref.at[:sent_rows, :], full_ref.at[rows, :], out_sems.at[2 * pieces]))
    for copy in copies:
        copy.start()
    for copy in copies:
        copy.wait()


def interact_kernel(table_ref, spread_ref, coupling_ref, *refs):
    own_ref, back_0_ref, back_1_ref, delta_ref = refs[16:]
    window = [jnp.concatenate([refs[2 * j][...], refs[2 * j + 1][...]], axis=0) for j in range(8)]
    comps = window[0].shape[0]
    for j in range(1, 7):
        level = window[j]
        around = jnp.concatenate([window[j - 1], level, window[j + 1]], axis=0).astype(jnp.bfloat16)
        partner = jnp.dot(table_ref[j - 1], around, preferred_element_type=jnp.float32)
        rate = coupling_ref[(j - 1) * comps : j * comps, :] * level
        plus_part = weight_plus * level
        minus_part = weight_minus * level
        deltas = []
        for pair in range(2):
            plus = partner[2 * pair * comps : (2 * pair + 1) * comps, :]
            minus = partner[(2 * pair + 1) * comps : (2 * pair + 2) * comps, :]
            deltas.append(rate * (plus * (plus_part - (2.0 * weight_cross) * minus) + minus_part * minus))
        both = jnp.concatenate(deltas, axis=0).astype(jnp.bfloat16)
        delta_ref[(j - 1) * 2 * comps : j * 2 * comps, :] = both
        if 2 <= j <= 5:
            part = -2.0 * (deltas[0] + deltas[1])
            if j <= 3:
                own_ref[(j - 2) * comps : (j - 1) * comps, :] = part
            elif j == 4:
                back_1_ref[...] = part
            else:
                back_0_ref[...] = part
    spread = jnp.dot(spread_ref[...], delta_ref[...], preferred_element_type=jnp.float32)
    own_ref[...] += spread[: 2 * comps, :]
    back_1_ref[...] += spread[2 * comps : 3 * comps, :]
    back_0_ref[...] += spread[3 * comps :, :]


def finish_kernel(chunks, base_ref, table_ref, place_ref, mean_ref, fields_ref, growth_ref, damping_ref, *refs):
    turned_ref, own, back = refs[0], refs[1 : 1 + chunks], refs[1 + chunks : 1 + 2 * chunks]
    out_ref, wide_ref = refs[-2], refs[-1]
    width = own[0].shape[1]
    tiles = wide_ref.shape[1] // BLOCK
    tile_width = 2 * BLOCK
    growth = jnp.broadcast_to(growth_ref[...], (GROUP, tile_width))
    damping = jnp.broadcast_to(damping_ref[...], (GROUP, tile_width))
    for o in range(2 * chunks):
        extra = own[o] if o < chunks else back[o - chunks]

        @pl.loop(0, width // tile_width)
        def _(i):
            source = pl.ds(pl.multiple_of(i * tile_width, tile_width), tile_width)
            target = pl.ds(pl.multiple_of(o * width + i * tile_width, tile_width), tile_width)
            scale = 1.0 + growth * fields_ref[WIND : WIND + 1, target] - damping * mean_ref[0:1, target]
            wide_ref[:, target] = turned_ref[:, target] * scale + extra[:, source]

    @pl.loop(0, out_ref.shape[1] // 8)
    def _(i):
        codes = [place_ref[h, pl.ds(pl.multiple_of(8 * i, 8), 8), :] for h in range(2)]
        done = [[] for _ in range(GROUP // 8)]
        for r in range(8):
            parts = [[] for _ in range(GROUP // 8)]
            for h in range(2):
                code = jnp.broadcast_to(codes[h][r : r + 1, :], (8, BLOCK))
                index = jnp.bitwise_and(code, BLOCK - 1)
                keep, is_sea = has(code, KEEP), has(code, IS_SEA)
                tile = table_ref[h, 8 * i + r]
                first, second = jnp.minimum(tile, tiles - 1), jnp.bitwise_and(tile + 1, tiles - 1)
                for k in range(GROUP // 8):
                    rows = slice(8 * k, 8 * k + 8)
                    near = jnp.where(keep, wide_ref[rows, tile_at(first)], wide_ref[rows, tile_at(second)])
                    parts[k].append(jnp.where(is_sea, pick_lanes(near, index), 0.0))
            for k in range(GROUP // 8):
                done[k].append(jnp.concatenate(parts[k], axis=1))
        for k in range(GROUP // 8):
            out_ref[8 * k : 8 * k + 8, pl.ds(pl.multiple_of(8 * i, 8), 8), :] = jnp.swapaxes(jnp.stack(done[k]), 0, 1)


def params(limit):
    return pltpu.CompilerParams(vmem_limit_bytes=limit * MIB)


def after(value, *others):
    return lax.optimization_barrier((value,) + others)[0]


def packed_shards(energy, sea_mask, current_u, current_v, wind_forcing, refraction, group_speed, growth, damping,
                  coupling, dia_index):
    comp_count = lax.axis_size("comp")
    comp_pos = lax.axis_index("comp")
    tile_pos = lax.axis_index("tile")
    odd = lax.rem(comp_pos, 2)
    pair_pos = comp_pos // 2
    local_comps, row_count, col_count = energy.shape
    comps = local_comps // 2
    comp_total = NTH * NF
    first_row = tile_pos * row_count
    first_comp = comp_pos * local_comps
    cells = row_count * col_count // 2
    half = cells // 2
    width = half // CELL_CHUNKS
    f32, i32 = jnp.float32, jnp.int32
    base = jnp.stack([first_row, odd, comp_pos * (local_comps // NTH)]).astype(i32)

    edge_first = jnp.where(tile_pos == 0, row_count - EDGE, 0)
    edge_rows = lax.dynamic_slice_in_dim(energy, edge_first, EDGE, axis=1)
    halo_rows = lax.ppermute(edge_rows, "tile", [(0, 1), (1, 0)])

    all_rows = sea_mask.shape[0]
    angles = np.float32(2.0 * math.pi / NTH) * (np.arange(local_comps) % NTH).astype(np.float32)
    cosines = np.broadcast_to(np.cos(angles)[:, None], (local_comps, BLOCK)).astype(np.float32)
    sines = np.broadcast_to(np.sin(angles)[:, None], (local_comps, BLOCK)).astype(np.float32)
    vmem = pl.BlockSpec(memory_space=pltpu.VMEM)
    coef, index, place, table, speed_east, speed_north = pl.pallas_call(
        functools.partial(prepare_kernel, cells),
        grid_spec=pltpu.PrefetchScalarGridSpec(
            num_scalar_prefetch=2,
            grid=(),
            in_specs=[vmem] * 7,
            out_specs=[vmem] * 6,
            scratch_shapes=[pltpu.VMEM((8, all_rows, col_count), f32), pltpu.VMEM((BLOCK, row_count), f32)],
        ),
        out_shape=[
            jax.ShapeDtypeStruct((all_rows + 2 * EDGE, 8, col_count), f32),
            jax.ShapeDtypeStruct((2, row_count, BLOCK), i32),
            jax.ShapeDtypeStruct((2, row_count, BLOCK), i32),
            jax.ShapeDtypeStruct((8, 2 * BLOCK), i32),
            jax.ShapeDtypeStruct((local_comps, BLOCK), f32),
            jax.ShapeDtypeStruct((local_comps, BLOCK), f32),
        ],
        name="prepare",
        compiler_params=params(VMEM_MIB),
    )(base, group_speed, sea_mask, current_u, current_v, wind_forcing, refraction, cosines, sines)
    steps = comps // GROUP

    def group_at(part, base_ref):
        return (part + base_ref[1] * (1 - 2 * part)) * steps

    def whole(shape):
        return pl.BlockSpec(shape, lambda s, b, t: (0,) * len(shape))

    def column(part, lanes):
        return pl.BlockSpec((GROUP, lanes), lambda s, b, t: (group_at(part, b) + s, 0))

    def propagate(part, late, table, fields=None, seam=None, full=None):
        pieces = CELL_CHUNKS if part and late else 1
        comp_rows = comps - EARLY if late else EARLY
        sent_rows = comps - EARLY + 8 if late else EARLY - 8
        height = EARLY
        anywhere = pl.BlockSpec(memory_space=pl.ANY)
        with_fields = fields is None
        inputs = [energy, halo_rows, coef, index, speed_east, speed_north]
        in_specs = [anywhere] + [vmem] * 5
        aliases = {}
        if not with_fields:
            inputs.append(fields)
            in_specs.append(vmem)
        if late:
            inputs += [seam, full]
            in_specs += [vmem, anywhere]
            aliases = {len(inputs) + 1: 2 * pieces + 1}
        shapes = [(sent_rows, half // pieces)] * (2 * pieces) + [(1, cells), (comps, cells)]
        out_specs = [anywhere] * (2 * pieces) + [vmem, anywhere]
        if not late:
            shapes.append((8, cells))
            out_specs.append(vmem)
        if with_fields:
            shapes.append((8, cells))
            out_specs.append(vmem)
        outs = pl.pallas_call(
            functools.partial(propagate_kernel, part, late, pieces),
            grid_spec=pltpu.PrefetchScalarGridSpec(
                num_scalar_prefetch=2,
                grid=(),
                in_specs=in_specs,
                out_specs=out_specs,
                scratch_shapes=[
                    pltpu.VMEM((row_count, comp_rows, col_count), f32),
                    pltpu.VMEM((comp_rows + (8 if with_fields else 0), cells + BLOCK), f32),
                    pltpu.VMEM((height, cells), f32),
                    pltpu.SemaphoreType.DMA((row_count // 8,)),
                    pltpu.SemaphoreType.DMA((2 * pieces + 1,)),
                ],
            ),
            out_shape=[jax.ShapeDtypeStruct(shape, f32) for shape in shapes],
            input_output_aliases=aliases,
            name="propagate_late" if late else "propagate_early",
            compiler_params=params(VMEM_MIB),
            cost_estimate=pl.CostEstimate(
                flops=60 * comp_rows * row_count * col_count, bytes_accessed=60 * MIB, transcendentals=0,
            ),
        )(base, table, *inputs)
        return list(outs[:pieces]), list(outs[pieces : 2 * pieces]), outs[2 * pieces :]

    pairs = [(i, i ^ 1) for i in range(comp_count)]
    apart = [(i, i - 2 if i % 2 == 0 else i + 2) for i in range(comp_count)]
    apart = [(a, b) for a, b in apart if 0 <= b < comp_count]
    across = [(b, a) for a, b in apart]
    chunk_range = range(CELL_CHUNKS)

    def send(pieces, route, waits):
        return [lax.ppermute(after(piece, *wait), "comp", route) for piece, wait in zip(pieces, waits)]

    stages = [(0, 0), (0, 1), (1, 0), (1, 1)]
    kept, sent, got, from_own, from_got, level_sums, full = {}, {}, {}, {}, {}, [], {}
    fields = seam = before = None
    part_table = table
    for stage in stages:
        part, late = stage
        kept[stage], sent[stage], extra = propagate(part, late, part_table, fields, seam, full.get(part))
        level_sums.append(extra[0])
        full[part] = extra[1]
        seam = None if late else extra[2]
        fields = extra[3] if fields is None else fields
        if stage == stages[-1]:
            break
        got[stage] = send(sent[stage], pairs, [[]])
        from_own[stage] = send(kept[stage], apart, [[]])
        waits = [from_got[before][0]] if stage == stages[2] else []
        from_got[stage] = send(got[stage], across, [waits])
        done = [extra[0]]
        if before is not None:
            done.append(got[before][0])
            if stage == stages[2]:
                done += [from_got[stages[0]][0], from_own[stages[1]][0]]
        part_table = after(table, *done)
        before = stage
    packed_fields = fields
    sums_0 = level_sums[0]

    sums = level_sums[0] + level_sums[1] + level_sums[2] + level_sums[3]
    partner_sums = lax.ppermute(sums, "comp", pairs)
    partner_sums = jnp.roll(partner_sums, half, axis=1)
    last, got_1, from_own_1 = stages[-1], [], []
    for c in chunk_range:
        waits = [got[before][0]] + ([got_1[c - 2]] if c >= 2 else []) + ([partner_sums] if c == 2 else [])
        got_1.append(lax.ppermute(after(sent[last][c], *waits), "comp", pairs))
        from_own_1.append(lax.ppermute(after(kept[last][c], from_own[before][0]), "comp", apart))
    got[last], from_own[last], from_got[last] = got_1, from_own_1, []
    sums = sums + partner_sums
    sums = sums_two = sums + lax.ppermute(sums, "comp", [(i, i ^ 2) for i in range(comp_count)])
    sums = sums + lax.ppermute(sums, "comp", [(i, i ^ 4) for i in range(comp_count)])
    mean_level = sums / comp_total

    dia_index, coupling, growth, damping, late_odd, late_pair, _ = lax.optimization_barrier(
        (dia_index, coupling, growth, damping, odd, pair_pos, sums_0)
    )
    own_growth = lax.dynamic_slice_in_dim(growth, first_comp, local_comps)[:, None]
    own_damping = lax.dynamic_slice_in_dim(damping, first_comp, local_comps)[:, None]
    chunk_first = [
        NTH * jnp.where(late_odd > 0, 8 * late_pair + 10 - 2 * j, 8 * late_pair - 4 + 2 * j) for j in range(8)
    ]
    margin = 8 * NTH
    dia_pad = jnp.pad(dia_index, ((0, 0), (margin, margin)), constant_values=-1)
    coupling_pad = jnp.pad(coupling, (margin, margin))
    own_ids = jnp.arange(comps)
    targets, rates = [], []
    for j in range(1, 7):
        targets.append(lax.dynamic_slice(dia_pad, (0, chunk_first[j] + margin), (4, comps)))
        rates.append(lax.dynamic_slice_in_dim(coupling_pad, chunk_first[j] + margin, comps))
    lookup = []
    for j in range(1, 7):
        ids = jnp.concatenate([chunk_first[j + d] + own_ids for d in (-1, 0, 1)])
        lookup.append((targets[j - 1].reshape(4 * comps)[:, None] == ids[None, :]).astype(jnp.bfloat16))
    lookup = jnp.stack(lookup)
    out_ids = jnp.concatenate([chunk_first[j] + own_ids for j in range(2, 6)])
    spread = []
    for j in range(1, 7):
        for pair in range(2):
            hits = [
                (out_ids[:, None] == targets[j - 1][2 * pair + q][None, :]).astype(f32) for q in range(2)
            ]
            spread.append(hits[0] + hits[1])
    spread = jnp.concatenate(spread, axis=1).astype(jnp.bfloat16)
    rates = jnp.concatenate(rates)[:, None]

    lanes = 512 if width % 512 == 0 else width
    own_parts, parts_0, parts_1 = [], [], []
    groups = [(from_got, 1), (from_got, 0), (kept, 0), (kept, 1), (got, 1), (got, 0), (from_own, 0), (from_own, 1)]
    for c in chunk_range:
        waits = [from_got[before][0]] + ([from_got[last][c - 2]] if c >= 2 else [])
        from_got[last].append(lax.ppermute(after(got_1[c], *waits), "comp", across))
        levels, level_specs = [], []
        for group, part in groups:
            for late in range(2):
                pieces = group[part, late]
                single = len(pieces) == 1
                levels.append(pieces[0 if single else c])
                skipped = c * (width // lanes) if single else 0
                level_specs.append(
                    pl.BlockSpec((levels[-1].shape[0], lanes), functools.partial(lambda n, s: (0, n + s), skipped))
                )
        own_part, part_0, part_1 = pl.pallas_call(
            interact_kernel,
            grid=(width // lanes,),
            in_specs=[
                pl.BlockSpec(lookup.shape, lambda s: (0, 0, 0)),
                pl.BlockSpec(spread.shape, lambda s: (0, 0)),
                pl.BlockSpec(rates.shape, lambda s: (0, 0)),
            ] + level_specs,
            out_specs=[pl.BlockSpec((n * comps, lanes), lambda s: (0, s)) for n in (2, 1, 1)],
            out_shape=[jax.ShapeDtypeStruct((n * comps, width), f32) for n in (2, 1, 1)],
            scratch_shapes=[pltpu.VMEM((12 * comps, lanes), jnp.bfloat16)],
            name="interact_cells",
            compiler_params=params(VMEM_MIB),
            cost_estimate=pl.CostEstimate(
                flops=2 * width * comps * comps * (6 * 12 + 48),
                bytes_accessed=20 * MIB, transcendentals=0,
            ),
        )(lookup, spread, rates, *levels)
        own_parts.append(own_part)
        parts_0.append(part_0)
        parts_1.append(part_1)

    def send_back(piece, *waits):
        return lax.ppermute(after(piece, *waits), "comp", pairs)

    back = [[None] * CELL_CHUNKS for _ in range(2)]
    back[0][0] = send_back(parts_0[0], got_1[2], sums_two)
    back[1][0] = send_back(parts_1[0], got_1[3])
    back[0][1] = send_back(parts_0[1], back[0][0], sums)
    back[0][2] = send_back(parts_0[2], back[1][0])
    back[0][3] = send_back(parts_0[3], back[0][1])
    for c in range(1, CELL_CHUNKS):
        back[1][c] = send_back(parts_1[c], back[0][2])

    def finish(part, so_far):
        piece = pl.BlockSpec((GROUP, width), lambda s, b, t: (s, 0))
        own_piece = pl.BlockSpec((GROUP, width), lambda s, b, t: (part * steps + s, 0))
        inputs = [place, mean_level, packed_fields, own_growth, own_damping]
        specs = [whole(place.shape), whole(mean_level.shape), whole(packed_fields.shape), column(part, 1),
                 column(part, 1)]
        inputs += [full[part]] + own_parts + back[part]
        specs.append(pl.BlockSpec((GROUP, cells), lambda s, b, t: (s, 0)))
        specs += [own_piece] * CELL_CHUNKS + [piece] * CELL_CHUNKS
        aliases = {}
        if so_far is not None:
            inputs.append(so_far)
            specs.append(pl.BlockSpec(memory_space=pl.ANY))
            aliases = {len(inputs) + 1: 0}
        return pl.pallas_call(
            functools.partial(finish_kernel, CELL_CHUNKS),
            grid_spec=pltpu.PrefetchScalarGridSpec(
                num_scalar_prefetch=2,
                grid=(steps,),
                in_specs=specs,
                out_specs=pl.BlockSpec((GROUP, row_count, col_count), lambda s, b, t: (group_at(part, b) + s, 0, 0)),
                scratch_shapes=[pltpu.VMEM((GROUP, cells), f32)],
            ),
            out_shape=jax.ShapeDtypeStruct(energy.shape, f32),
            input_output_aliases=aliases,
            name="finish_chunk",
            compiler_params=params(VMEM_MIB),
            cost_estimate=pl.CostEstimate(
                flops=20 * comps * row_count * col_count,
                bytes_accessed=100 * MIB, transcendentals=0,
            ),
        )(base, table, *inputs)

    return finish(1, finish(0, None))


def choose_shards(energy, *rest):
    local_comps, row_count, col_count = energy.shape
    fits = (
        local_comps == 4 * NTH and lax.axis_size("comp") == 8 and local_comps * 8 == NTH * NF
        and lax.axis_size("tile") == 2 and row_count == BLOCK and col_count == 2 * BLOCK
    )
    return packed_shards(energy, *rest) if fits else shards(energy, *rest)


def solution(mesh):
    placed = (
        P("comp", ("grp", "tile"), None),
        P("grp", None),
        P("grp", None),
        P("grp", None),
        P("grp", None),
        P("grp", None),
        P(),
        P(),
        P(),
        P(),
        P(),
    )
    return jax.shard_map(
        choose_shards,
        mesh=mesh,
        in_specs=placed,
        out_specs=P("comp", ("grp", "tile"), None),
        check_vma=False,
    )
```

```python
import functools
import math

import jax
import jax.numpy as jnp
import numpy as np
from jax import lax
from jax.experimental import pallas as pl
from jax.experimental.pallas import tpu as pltpu
from jax.sharding import PartitionSpec as P

NTH = 36
NF = 32


weight_plus = 0.4096
weight_minus = 3.1605
weight_cross = 1.2945


def with_halo(block, sides, width):
    for axis, dim in sides:
        count = lax.axis_size(axis)
        forward = [(i, i + 1) for i in range(count - 1)]
        backward = [(target, source) for source, target in forward]
        low = lax.ppermute(
            lax.slice_in_dim(block, block.shape[dim] - width, None, axis=dim), axis, forward
        )
        high = lax.ppermute(lax.slice_in_dim(block, 0, width, axis=dim), axis, backward)
        block = jnp.concatenate([low, block, high], axis=dim)
    return block


def quick_flux(far_left, left_cell, right_cell, far_right, courant):
    centre = 0.5 * (left_cell + right_cell) - 0.5 * courant * (right_cell - left_cell)
    curvature = (1.0 - courant * courant) / 6.0
    upward = centre - curvature * (right_cell - 2.0 * left_cell + far_left)
    downward = centre - curvature * (left_cell - 2.0 * right_cell + far_right)
    return courant * jnp.where(courant > 0.0, upward, downward)


def flux_change(padded, speed, current, sea_pad, axis):
    cell_count = padded.shape[axis] - 4

    def take_part(source, first, which_axis):
        return lax.slice_in_dim(source, first, first + cell_count + 1, axis=which_axis)

    face_current = 0.5 * (take_part(current, 0, axis - 1) + take_part(current, 1, axis - 1))
    courant = speed[:, None, None] + face_current[None]
    open_face = (take_part(sea_pad, 0, axis - 1) * take_part(sea_pad, 1, axis - 1))[None]
    face_flux = (
        quick_flux(
            take_part(padded, 0, axis),
            take_part(padded, 1, axis),
            take_part(padded, 2, axis),
            take_part(padded, 3, axis),
            courant,
        )
        * open_face
    )
    return lax.slice_in_dim(face_flux, 1, cell_count + 1, axis=axis) - lax.slice_in_dim(
        face_flux, 0, cell_count, axis=axis
    )


def source_terms(energy_block, wind, turning, growth, damping, coupling, lookup, spread):
    cell_count = energy_block.shape[1]
    spectrum = energy_block.reshape(NF, NTH, cell_count)
    turn_rate = turning[None, None, :]
    next_dir = jnp.roll(spectrum, -1, axis=1)
    forward = jnp.maximum(turn_rate, 0.0)
    backward = jnp.minimum(turn_rate, 0.0)
    upper_flux = forward * spectrum + backward * next_dir
    lower_flux = jnp.roll(upper_flux, 1, axis=1)
    turned = (spectrum - upper_flux + lower_flux).reshape(energy_block.shape)
    rounded = turned.astype(jnp.bfloat16)
    plus_first, minus_first, plus_second, minus_second = lookup(rounded)
    couple_rate = coupling[:, None]
    delta_first = couple_rate * (
        turned * turned * (weight_plus * plus_first + weight_minus * minus_first)
        - 2.0 * weight_cross * turned * plus_first * minus_first
    )
    delta_second = couple_rate * (
        turned * turned * (weight_plus * plus_second + weight_minus * minus_second)
        - 2.0 * weight_cross * turned * plus_second * minus_second
    )
    moved = spread(delta_first.astype(jnp.bfloat16), delta_second.astype(jnp.bfloat16))
    mean_level = jnp.sum(turned, axis=0) / energy_block.shape[0]
    return (
        turned
        + growth[:, None] * wind[None] * turned
        - damping[:, None] * mean_level[None] * turned
        - 2.0 * (delta_first + delta_second)
        + moved
    )


def shards(
    energy,
    sea_mask,
    current_u,
    current_v,
    wind_forcing,
    refraction,
    group_speed,
    growth,
    damping,
    coupling,
    dia_index,
):
    comp_count = lax.axis_size("comp")
    comp_pos = lax.axis_index("comp")
    tile_pos = lax.axis_index("tile")
    local_comps, row_count, col_count = energy.shape
    first_row = tile_pos * row_count
    first_comp = comp_pos * local_comps
    comp_total = NTH * NF
    angles = 2.0 * math.pi / NTH * (jnp.arange(comp_total) % NTH).astype(jnp.float32)
    speeds = jnp.repeat(group_speed, NTH)
    speed_east = lax.dynamic_slice_in_dim(speeds * jnp.cos(angles), first_comp, local_comps)
    speed_north = lax.dynamic_slice_in_dim(speeds * jnp.sin(angles), first_comp, local_comps)
    window = (row_count + 2, col_count + 2)
    sea_pad = lax.dynamic_slice(jnp.pad(sea_mask.astype(jnp.float32), 1), (first_row, 0), window)
    east_pad = lax.dynamic_slice(jnp.pad(current_u, 1), (first_row, 0), window)
    north_pad = lax.dynamic_slice(jnp.pad(current_v, 1), (first_row, 0), window)
    sea_tile = sea_pad[1:-1, 1:-1]
    masked = energy * sea_tile[None]
    padded_east = with_halo(masked, (("tile", 1),), 2)
    along_east = flux_change(padded_east, speed_east, east_pad[:, 1:-1], sea_pad[:, 1:-1], 1)
    along_north = flux_change(
        jnp.pad(masked, ((0, 0), (0, 0), (2, 2))),
        speed_north,
        north_pad[1:-1, :],
        sea_pad[1:-1, :],
        2,
    )
    propagated = (sea_tile[None] * (masked - along_east - along_north)).reshape(
        local_comps, row_count * col_count
    )
    tile_wind = lax.dynamic_slice(wind_forcing, (first_row, 0), (row_count, col_count)).reshape(-1)
    tile_turn = lax.dynamic_slice(refraction, (first_row, 0), (row_count, col_count)).reshape(-1)
    comp_ids = jnp.arange(comp_total)
    tables = [
        (dia_index[slot_row][:, None] == comp_ids[None, :]).astype(jnp.bfloat16)
        for slot_row in range(4)
    ]

    def lookup(rounded):
        return tuple(
            (
                jnp.dot(tables[slot_row], rounded, preferred_element_type=jnp.float32)
                for slot_row in range(4)
            )
        )

    def scatter_back(table, terms):
        return lax.dot_general(
            table, terms, (((0,), (0,)), ((), ())), preferred_element_type=jnp.float32
        )

    def spread(first_terms, second_terms):
        return (
            scatter_back(tables[0], first_terms)
            + scatter_back(tables[1], first_terms)
            + scatter_back(tables[2], second_terms)
            + scatter_back(tables[3], second_terms)
        )

    share_size = row_count * col_count // comp_count
    point_field = lax.all_to_all(propagated, "comp", split_axis=1, concat_axis=0, tiled=True)
    first_point = comp_pos * share_size
    own_wind = lax.dynamic_slice_in_dim(tile_wind, first_point, share_size)
    own_turn = lax.dynamic_slice_in_dim(tile_turn, first_point, share_size)
    result = source_terms(
        point_field, own_wind, own_turn, growth, damping, coupling, lookup, spread
    )
    returned_field = lax.all_to_all(result, "comp", split_axis=0, concat_axis=1, tiled=True)
    return returned_field.reshape(local_comps, row_count, col_count)


BLOCK = 128
GROUP = 24
EARLY = 40
CELL_CHUNKS = 4
MIB = 1024 * 1024
VMEM_MIB = 60
EDGE = 2
SEA, OPEN_EAST, FLOW_EAST, OPEN_NORTH, FLOW_NORTH, HALF_SEA, WIND, TURN = range(8)
KEEP, SPILL, IS_SEA = BLOCK, 2 * BLOCK, 2 * BLOCK


def upwind(courant, total, slope, bend_here, bend_ahead):
    bend = jnp.where(courant > 0.0, bend_here, bend_ahead)
    return courant * ((total - bend) - courant * (slope - courant * bend))


def pick_lanes(block, index):
    return jnp.take_along_axis(block, index, axis=1, mode="promise_in_bounds")


def tile_at(tile):
    return pl.ds(pl.multiple_of(tile * BLOCK, BLOCK), BLOCK)


def has(code, flag):
    return jnp.bitwise_and(code, flag) != 0


def pack_block(blocks, code, tile, out_ref, firsts, held):
    code = jnp.broadcast_to(code, (8, BLOCK))
    index = jnp.bitwise_and(code, BLOCK - 1)
    keep, spill = has(code, KEEP), has(code, SPILL)
    result = []
    for block, first, old in zip(blocks, firsts, held):
        moved = pick_lanes(block, index)
        merged = jnp.where(keep, moved, old)
        out_ref[pl.ds(first, 8), tile_at(tile)] = merged
        result.append(jnp.where(spill, moved, merged))
    return tuple(result)


def prepare_kernel(places, base_ref, speed_ref, sea_ref, east_ref, north_ref, wind_ref, turn_ref, cos_ref, sin_ref,
                   coef_ref, index_ref, place_ref, table_ref, speed_east_ref, speed_north_ref, field_ref, pick_ref):
    first_row, odd, first_freq = base_ref[0], base_ref[1], base_ref[2]
    all_rows, col_count = sea_ref.shape
    row_count = place_ref.shape[1]
    tiles = places // BLOCK
    sea = sea_ref[...].astype(jnp.float32)
    row = lax.broadcasted_iota(jnp.int32, sea.shape, 0)
    col = lax.broadcasted_iota(jnp.int32, sea.shape, 1)

    def next_row(field):
        return jnp.where(row == all_rows - 1, 0.0, pltpu.roll(field, all_rows - 1, 0))

    def next_col(field):
        return jnp.where(col == col_count - 1, 0.0, pltpu.roll(field, col_count - 1, 1))

    open_east, open_north = sea * next_row(sea), sea * next_col(sea)
    east, north = east_ref[...], north_ref[...]
    field_ref[SEA] = sea
    field_ref[OPEN_EAST] = open_east
    field_ref[FLOW_EAST] = open_east * (0.5 * (east + next_row(east)))
    field_ref[OPEN_NORTH] = open_north
    field_ref[FLOW_NORTH] = open_north * (0.5 * (north + next_col(north)))
    field_ref[HALF_SEA] = 0.5 * sea
    field_ref[WIND] = wind_ref[...]
    field_ref[TURN] = turn_ref[...]
    coef_ref[0:EDGE] = jnp.zeros((EDGE, 8, col_count), jnp.float32)
    coef_ref[EDGE + all_rows :] = jnp.zeros((EDGE, 8, col_count), jnp.float32)

    @pl.loop(0, all_rows // 8)
    def _(i):
        rows = field_ref[:, pl.ds(pl.multiple_of(8 * i, 8), 8), :]
        coef_ref[pl.ds(8 * i + EDGE, 8)] = jnp.swapaxes(rows, 0, 1)

    freqs = cos_ref.shape[0] // NTH
    for f in range(freqs):
        circle = slice(f * NTH, (f + 1) * NTH)
        speed_east_ref[circle, :] = cos_ref[circle, :] * speed_ref[first_freq + f]
        speed_north_ref[circle, :] = sin_ref[circle, :] * speed_ref[first_freq + f]

    bf16, f32 = jnp.bfloat16, jnp.float32
    tile_sea = sea_ref[pl.ds(pl.multiple_of(first_row, 8), row_count), :].astype(f32)
    square = (BLOCK, BLOCK)
    down, over = lax.broadcasted_iota(jnp.int32, square, 0), lax.broadcasted_iota(jnp.int32, square, 1)
    before = (down < over).astype(f32).astype(bf16)
    ones = jnp.ones(square, bf16)
    row_square = (row_count, row_count)
    above = lax.broadcasted_iota(jnp.int32, row_square, 1) < lax.broadcasted_iota(jnp.int32, row_square, 0)
    above = above.astype(f32).astype(bf16)
    parts = [tile_sea[:, :BLOCK], tile_sea[:, BLOCK:]]
    numbers = [jnp.dot(p.astype(bf16), ones, preferred_element_type=f32) for p in parts]
    in_row = numbers[0] + numbers[1]
    starts = [jnp.dot(above, in_row.astype(bf16), preferred_element_type=f32)]
    starts.append(starts[0] + numbers[0])
    total = jnp.sum(in_row, axis=0, keepdims=True).astype(jnp.int32)

    def turned_tile(tile):
        return jnp.where(tile >= tiles, tiles, jnp.bitwise_and(tile + odd * (tiles // 2), tiles - 1))

    columns = []
    for h in range(2):
        rank = jnp.dot(parts[h].astype(bf16), before, preferred_element_type=f32).astype(jnp.int32)
        start = starts[h].astype(jnp.int32)
        offset = jnp.bitwise_and(start, BLOCK - 1)
        keep = jnp.where(over[:row_count] >= offset, KEEP, 0)
        slot = jnp.bitwise_and(rank + offset, BLOCK - 1)
        is_sea = parts[h] > 0.0
        place_ref[h] = slot + keep + jnp.where(is_sea, IS_SEA, 0)
        slot = jnp.where(is_sea, slot, -1).astype(f32).T
        from_lane = down[:, :row_count].astype(f32)

        @pl.loop(0, BLOCK // 8)
        def _(i):
            found = []
            for k in range(8):
                lane = (8 * i + k).astype(f32)
                found.append(jnp.sum(jnp.where(slot == lane, from_lane, 0.0), axis=0, keepdims=True))
            pick_ref[pl.ds(pl.multiple_of(8 * i, 8), 8), :] = jnp.concatenate(found, axis=0)

        spill = jnp.where(offset + numbers[h].astype(jnp.int32) >= BLOCK, SPILL, 0)
        index_ref[h] = pick_ref[...].T.astype(jnp.int32) + keep + spill
        columns.append(turned_tile(lax.shift_right_logical(starts[h].T[0:8, :].astype(jnp.int32), 7)))
    row_id = lax.broadcasted_iota(jnp.int32, (8, row_count), 0)
    end_tile = jnp.where(
        jnp.bitwise_and(total, BLOCK - 1) == 0, tiles, turned_tile(lax.shift_right_logical(total, 7))
    )
    end_tile = jnp.broadcast_to(end_tile, (8, BLOCK))
    table_ref[...] = jnp.concatenate([jnp.where(row_id == 0, columns[0], columns[1]), end_tile], axis=1)


def propagate_kernel(part, late, pieces, base_ref, table_ref, energy_ref, halo_ref, coef_ref, index_ref, east_ref,
                     north_ref, *refs):
    refs = list(refs)
    with_fields = part == 0 and not late
    fields_ref = None if with_fields else refs.pop(0)
    seam_ref = refs.pop(0) if late else None
    if late:
        refs.pop(0)
    piece_refs = [refs.pop(0) for _ in range(2 * pieces)]
    sum_ref, full_ref = refs.pop(0), refs.pop(0)
    seam_out_ref = None if late else refs.pop(0)
    fields_out_ref = refs.pop(0) if with_fields else None
    rows_ref, spread_ref, wide_ref, result_ref, row_sems, out_sems = refs
    row_count, comp_count, col_count = rows_ref.shape
    strips = comp_count // 8
    sent_rows = piece_refs[0].shape[0]
    cells = result_ref.shape[1]
    first_row = base_ref[0]
    first_comp = pl.multiple_of((part + base_ref[1] * (1 - 2 * part)) * 2 * NTH + late * EARLY, 8)
    lane = lax.broadcasted_iota(jnp.int32, (8, BLOCK), 1)
    first_lane, last_lane = lane == 0, lane == BLOCK - 1
    third = 1.0 / 3.0

    @pl.loop(0, row_count // 8)
    def _(i):
        for k in range(8):
            row = 8 * i + k
            source = energy_ref.at[pl.ds(first_comp, comp_count), row, :]
            pltpu.make_async_copy(source, rows_ref.at[row], row_sems.at[i]).start()

    def halves(row):
        return row[:, :BLOCK], row[:, BLOCK:]

    @pl.loop(0, row_count + 2 * EDGE)
    def _(r):
        coef = coef_ref[first_row + r]
        for k in range(HALF_SEA + 1):
            spread_ref[r, k] = jnp.broadcast_to(coef[k : k + 1, :], coef.shape)

    def masked(row, at):
        return tuple(part * sea for part, sea in zip(halves(row), halves(spread_ref[at, SEA])))

    def cell_row(at, new, state, east, north):
        here, ahead, slope_ahead, bend_here, flux_low = state
        coef = [None] + [halves(spread_ref[at, k]) for k in range(1, HALF_SEA + 1)]
        to_right = [pltpu.roll(part, BLOCK - 1, 1) for part in here]
        right = (jnp.where(last_lane, to_right[1], to_right[0]), jnp.where(last_lane, 0.0, to_right[1]))
        slope = [right[h] - here[h] for h in range(2)]
        slope_roll = [pltpu.roll(part, 1, 1) for part in slope]
        slope_left = (jnp.where(first_lane, here[0], slope_roll[0]),
                      jnp.where(first_lane, slope_roll[0], slope_roll[1]))
        bend = [third * (slope[h] - slope_left[h]) for h in range(2)]
        bend_roll = [pltpu.roll(part, BLOCK - 1, 1) for part in bend]
        bend_right = (jnp.where(last_lane, bend_roll[1], bend_roll[0]), bend_roll[1])
        cross, flux, slope_next, bend_ahead = [], [], [], []
        for h in range(2):
            cross.append(upwind(north * coef[OPEN_NORTH][h] + coef[FLOW_NORTH][h], here[h] + right[h], slope[h],
                                bend[h], bend_right[h]))
            slope_next.append(new[h] - ahead[h])
            bend_ahead.append(third * (slope_next[h] - slope_ahead[h]))
            flux.append(upwind(east * coef[OPEN_EAST][h] + coef[FLOW_EAST][h], here[h] + ahead[h], slope_ahead[h],
                               bend_here[h], bend_ahead[h]))
        cross_roll = [pltpu.roll(part, 1, 1) for part in cross]
        cross_low = (jnp.where(first_lane, cross_roll[1], cross_roll[0]),
                     jnp.where(first_lane, cross_roll[0], cross_roll[1]))
        moved = [
            coef[HALF_SEA][h] * (((here[h] + here[h]) + (flux_low[h] + cross_low[h])) - (flux[h] + cross[h]))
            for h in range(2)
        ]
        return (ahead, new, tuple(slope_next), tuple(bend_ahead), tuple(flux)), jnp.concatenate(moved, axis=1)

    def strip(g, arrive):
        local = pl.ds(pl.multiple_of(g * 8, 8), 8)
        comps = pl.ds(pl.multiple_of(first_comp + g * 8, 8), 8)
        east, north = east_ref[comps, :], north_ref[comps, :]
        zero = (jnp.zeros((8, BLOCK), jnp.float32),) * 2
        here, ahead = masked(halo_ref[comps, 0, :], 0), masked(halo_ref[comps, 1, :], 1)
        state = (here, ahead, tuple(b - a for a, b in zip(here, ahead)), zero, zero)

        def eight(i, state):
            if arrive:
                block = rows_ref.at[pl.ds(8 * i, 8)]
                pltpu.make_async_copy(block, block, row_sems.at[i]).wait()
            fresh = [rows_ref[8 * i + k, local, :] for k in range(8)]
            done = []
            for k in range(8):
                new = masked(fresh[k], 8 * i + k + EDGE)
                state, moved = cell_row(8 * i + k, new, state, east, north)
                done.append(moved)
            for k in range(8):
                rows_ref[jnp.maximum(8 * i + k - EDGE, 0), local, :] = done[k]
            return state

        state = lax.fori_loop(0, row_count // 8, eight, state)
        for k in range(EDGE):
            new = masked(halo_ref[comps, k, :], row_count + EDGE + k)
            state, moved = cell_row(row_count + k, new, state, east, north)
            rows_ref[row_count - EDGE + k, local, :] = moved

    strip(0, True)

    @pl.loop(1, strips)
    def _(g):
        strip(g, False)

    group_rows = [8 * n for n in range(strips + with_fields)]

    def pack_eight(i, held):
        codes = [index_ref[h, pl.ds(pl.multiple_of(8 * i, 8), 8), :] for h in range(2)]
        for k in range(8):
            row = 8 * i + k
            for h in range(2):
                lanes = slice(h * BLOCK, (h + 1) * BLOCK)
                blocks = [rows_ref[row, 8 * n : 8 * n + 8, lanes] for n in range(strips)]
                if with_fields:
                    blocks.append(coef_ref[first_row + EDGE + row, :, lanes])
                held = pack_block(blocks, codes[h][k : k + 1, :], table_ref[h, row], wide_ref, group_rows, held)
        return held

    empty = (jnp.zeros((8, BLOCK), jnp.float32),) * len(group_rows)
    held = lax.fori_loop(0, row_count // 8, pack_eight, empty)
    for first, block in zip(group_rows, held):
        wide_ref[pl.ds(first, 8), tile_at(table_ref[0, row_count])] = block
    if with_fields:
        fields_out_ref[...] = wide_ref[comp_count:, :cells]

    tile_width = 2 * BLOCK
    height = result_ref.shape[0]
    comp_row = lax.broadcasted_iota(jnp.int32, (height, tile_width), 0)
    start = height - NTH if late else 0
    end = start + NTH - 1
    mixed = slice(0, 8) if late else slice(height - 8, height)
    mixed_row = comp_row[mixed]
    in_circle = (mixed_row >= start) & (mixed_row <= end)

    @pl.loop(0, cells // tile_width)
    def _(i):
        source = pl.ds(pl.multiple_of(i * tile_width, tile_width), tile_width)
        level = wide_ref[:comp_count, source]
        if late:
            level = jnp.concatenate([seam_ref[:, source], level], axis=0)
        if with_fields:
            rate = wide_ref[comp_count + TURN : comp_count + TURN + 1, source]
        else:
            rate = fields_ref[TURN : TURN + 1, source]
        forward = jnp.maximum(rate, 0.0)
        backward = jnp.minimum(rate, 0.0)
        stay = (1.0 - forward) + backward
        above = pltpu.roll(level, height - 1, 0)
        below = pltpu.roll(level, 1, 0)

        def with_row(rolled, row, value):
            tile = slice(row - row % 8, row - row % 8 + 8)
            fixed = jnp.where(comp_row[tile] == row, value, rolled[tile])
            parts = [rolled[: tile.start], fixed, rolled[tile.stop :]]
            return jnp.concatenate([part for part in parts if part.shape[0]], axis=0)

        above = with_row(above, end, level[start : start + 1, :])
        below = with_row(below, start, level[end : end + 1, :])
        turned = stay * level - backward * above + forward * below
        partial = jnp.where(in_circle, turned[mixed], 0.0)
        for first in range(0, height, 8):
            rows = slice(first, first + 8)
            if first == mixed.start:
                result_ref[rows, source] = jnp.where(in_circle, turned[rows], level[rows])
            else:
                result_ref[rows, source] = turned[rows]
                partial += turned[rows]
        sum_ref[:, source] = jnp.sum(partial, axis=0, keepdims=True)

    if not late:
        seam_out_ref[...] = result_ref[sent_rows:, :]
    width = cells // (2 * pieces)
    copies = []
    for n, piece in enumerate(piece_refs):
        source = result_ref.at[:sent_rows, n * width : (n + 1) * width]
        copies.append(pltpu.make_async_copy(source, piece, out_sems.at[n]))
    rows = pl.ds(EARLY - 8 if late else 0, sent_rows)
    copies.append(pltpu.make_async_copy(result_ref.at[:sent_rows, :], full_ref.at[rows, :], out_sems.at[2 * pieces]))
    for copy in copies:
        copy.start()
    for copy in copies:
        copy.wait()


def interact_kernel(table_ref, spread_ref, coupling_ref, *refs):
    own_ref, back_0_ref, back_1_ref, delta_ref = refs[16:]
    window = [jnp.concatenate([refs[2 * j][...], refs[2 * j + 1][...]], axis=0) for j in range(8)]
    comps = window[0].shape[0]
    for j in range(1, 7):
        level = window[j]
        around = jnp.concatenate([window[j - 1], level, window[j + 1]], axis=0).astype(jnp.bfloat16)
        partner = jnp.dot(table_ref[j - 1], around, preferred_element_type=jnp.float32)
        rate = coupling_ref[(j - 1) * comps : j * comps, :] * level
        plus_part = weight_plus * level
        minus_part = weight_minus * level
        deltas = []
        for pair in range(2):
            plus = partner[2 * pair * comps : (2 * pair + 1) * comps, :]
            minus = partner[(2 * pair + 1) * comps : (2 * pair + 2) * comps, :]
            deltas.append(rate * (plus * (plus_part - (2.0 * weight_cross) * minus) + minus_part * minus))
        both = jnp.concatenate(deltas, axis=0).astype(jnp.bfloat16)
        delta_ref[(j - 1) * 2 * comps : j * 2 * comps, :] = both
        if 2 <= j <= 5:
            part = -2.0 * (deltas[0] + deltas[1])
            if j <= 3:
                own_ref[(j - 2) * comps : (j - 1) * comps, :] = part
            elif j == 4:
                back_1_ref[...] = part
            else:
                back_0_ref[...] = part
    spread = jnp.dot(spread_ref[...], delta_ref[...], preferred_element_type=jnp.float32)
    own_ref[...] += spread[: 2 * comps, :]
    back_1_ref[...] += spread[2 * comps : 3 * comps, :]
    back_0_ref[...] += spread[3 * comps :, :]


def finish_kernel(chunks, base_ref, table_ref, place_ref, mean_ref, fields_ref, growth_ref, damping_ref, *refs):
    turned_ref, own, back = refs[0], refs[1 : 1 + chunks], refs[1 + chunks : 1 + 2 * chunks]
    out_ref, wide_ref = refs[-2], refs[-1]
    width = own[0].shape[1]
    tiles = wide_ref.shape[1] // BLOCK
    tile_width = 2 * BLOCK
    growth = jnp.broadcast_to(growth_ref[...], (GROUP, tile_width))
    damping = jnp.broadcast_to(damping_ref[...], (GROUP, tile_width))
    for o in range(2 * chunks):
        extra = own[o] if o < chunks else back[o - chunks]

        @pl.loop(0, width // tile_width)
        def _(i):
            source = pl.ds(pl.multiple_of(i * tile_width, tile_width), tile_width)
            target = pl.ds(pl.multiple_of(o * width + i * tile_width, tile_width), tile_width)
            scale = 1.0 + growth * fields_ref[WIND : WIND + 1, target] - damping * mean_ref[0:1, target]
            wide_ref[:, target] = turned_ref[:, target] * scale + extra[:, source]

    @pl.loop(0, out_ref.shape[1] // 8)
    def _(i):
        codes = [place_ref[h, pl.ds(pl.multiple_of(8 * i, 8), 8), :] for h in range(2)]
        done = [[] for _ in range(GROUP // 8)]
        for r in range(8):
            parts = [[] for _ in range(GROUP // 8)]
            for h in range(2):
                code = jnp.broadcast_to(codes[h][r : r + 1, :], (8, BLOCK))
                index = jnp.bitwise_and(code, BLOCK - 1)
                keep, is_sea = has(code, KEEP), has(code, IS_SEA)
                tile = table_ref[h, 8 * i + r]
                first, second = jnp.minimum(tile, tiles - 1), jnp.bitwise_and(tile + 1, tiles - 1)
                for k in range(GROUP // 8):
                    rows = slice(8 * k, 8 * k + 8)
                    near = jnp.where(keep, wide_ref[rows, tile_at(first)], wide_ref[rows, tile_at(second)])
                    parts[k].append(jnp.where(is_sea, pick_lanes(near, index), 0.0))
            for k in range(GROUP // 8):
                done[k].append(jnp.concatenate(parts[k], axis=1))
        for k in range(GROUP // 8):
            out_ref[8 * k : 8 * k + 8, pl.ds(pl.multiple_of(8 * i, 8), 8), :] = jnp.swapaxes(jnp.stack(done[k]), 0, 1)


def params(limit):
    return pltpu.CompilerParams(vmem_limit_bytes=limit * MIB)


def after(value, *others):
    return lax.optimization_barrier((value,) + others)[0]


def packed_shards(energy, sea_mask, current_u, current_v, wind_forcing, refraction, group_speed, growth, damping,
                  coupling, dia_index):
    comp_count = lax.axis_size("comp")
    comp_pos = lax.axis_index("comp")
    tile_pos = lax.axis_index("tile")
    odd = lax.rem(comp_pos, 2)
    pair_pos = comp_pos // 2
    local_comps, row_count, col_count = energy.shape
    comps = local_comps // 2
    comp_total = NTH * NF
    first_row = tile_pos * row_count
    first_comp = comp_pos * local_comps
    cells = row_count * col_count // 2
    half = cells // 2
    width = half // CELL_CHUNKS
    f32, i32 = jnp.float32, jnp.int32
    base = jnp.stack([first_row, odd, comp_pos * (local_comps // NTH)]).astype(i32)

    edge_first = jnp.where(tile_pos == 0, row_count - EDGE, 0)
    edge_rows = lax.dynamic_slice_in_dim(energy, edge_first, EDGE, axis=1)
    halo_rows = lax.ppermute(edge_rows, "tile", [(0, 1), (1, 0)])

    all_rows = sea_mask.shape[0]
    angles = np.float32(2.0 * math.pi / NTH) * (np.arange(local_comps) % NTH).astype(np.float32)
    cosines = np.broadcast_to(np.cos(angles)[:, None], (local_comps, BLOCK)).astype(np.float32)
    sines = np.broadcast_to(np.sin(angles)[:, None], (local_comps, BLOCK)).astype(np.float32)
    vmem = pl.BlockSpec(memory_space=pltpu.VMEM)
    coef, index, place, table, speed_east, speed_north = pl.pallas_call(
        functools.partial(prepare_kernel, cells),
        grid_spec=pltpu.PrefetchScalarGridSpec(
            num_scalar_prefetch=2,
            grid=(),
            in_specs=[vmem] * 7,
            out_specs=[vmem] * 6,
            scratch_shapes=[pltpu.VMEM((8, all_rows, col_count), f32), pltpu.VMEM((BLOCK, row_count), f32)],
        ),
        out_shape=[
            jax.ShapeDtypeStruct((all_rows + 2 * EDGE, 8, col_count), f32),
            jax.ShapeDtypeStruct((2, row_count, BLOCK), i32),
            jax.ShapeDtypeStruct((2, row_count, BLOCK), i32),
            jax.ShapeDtypeStruct((8, 2 * BLOCK), i32),
            jax.ShapeDtypeStruct((local_comps, BLOCK), f32),
            jax.ShapeDtypeStruct((local_comps, BLOCK), f32),
        ],
        name="prepare",
        compiler_params=params(VMEM_MIB),
    )(base, group_speed, sea_mask, current_u, current_v, wind_forcing, refraction, cosines, sines)
    steps = comps // GROUP

    def group_at(part, base_ref):
        return (part + base_ref[1] * (1 - 2 * part)) * steps

    def whole(shape):
        return pl.BlockSpec(shape, lambda s, b, t: (0,) * len(shape))

    def column(part, lanes):
        return pl.BlockSpec((GROUP, lanes), lambda s, b, t: (group_at(part, b) + s, 0))

    def propagate(part, late, table, fields=None, seam=None, full=None):
        pieces = CELL_CHUNKS if part and late else 1
        comp_rows = comps - EARLY if late else EARLY
        sent_rows = comps - EARLY + 8 if late else EARLY - 8
        height = EARLY
        anywhere = pl.BlockSpec(memory_space=pl.ANY)
        with_fields = fields is None
        inputs = [energy, halo_rows, coef, index, speed_east, speed_north]
        in_specs = [anywhere] + [vmem] * 5
        aliases = {}
        if not with_fields:
            inputs.append(fields)
            in_specs.append(vmem)
        if late:
            inputs += [seam, full]
            in_specs += [vmem, anywhere]
            aliases = {len(inputs) + 1: 2 * pieces + 1}
        shapes = [(sent_rows, half // pieces)] * (2 * pieces) + [(1, cells), (comps, cells)]
        out_specs = [anywhere] * (2 * pieces) + [vmem, anywhere]
        if not late:
            shapes.append((8, cells))
            out_specs.append(vmem)
        if with_fields:
            shapes.append((8, cells))
            out_specs.append(vmem)
        outs = pl.pallas_call(
            functools.partial(propagate_kernel, part, late, pieces),
            grid_spec=pltpu.PrefetchScalarGridSpec(
                num_scalar_prefetch=2,
                grid=(),
                in_specs=in_specs,
                out_specs=out_specs,
                scratch_shapes=[
                    pltpu.VMEM((row_count, comp_rows, col_count), f32),
                    pltpu.VMEM((row_count + 2 * EDGE, HALF_SEA + 1, 8, col_count), f32),
                    pltpu.VMEM((comp_rows + (8 if with_fields else 0), cells + BLOCK), f32),
                    pltpu.VMEM((height, cells), f32),
                    pltpu.SemaphoreType.DMA((row_count // 8,)),
                    pltpu.SemaphoreType.DMA((2 * pieces + 1,)),
                ],
            ),
            out_shape=[jax.ShapeDtypeStruct(shape, f32) for shape in shapes],
            input_output_aliases=aliases,
            name="propagate_late" if late else "propagate_early",
            compiler_params=params(VMEM_MIB),
            cost_estimate=pl.CostEstimate(
                flops=60 * comp_rows * row_count * col_count, bytes_accessed=60 * MIB, transcendentals=0,
            ),
        )(base, table, *inputs)
        return list(outs[:pieces]), list(outs[pieces : 2 * pieces]), outs[2 * pieces :]

    pairs = [(i, i ^ 1) for i in range(comp_count)]
    apart = [(i, i - 2 if i % 2 == 0 else i + 2) for i in range(comp_count)]
    apart = [(a, b) for a, b in apart if 0 <= b < comp_count]
    across = [(b, a) for a, b in apart]
    chunk_range = range(CELL_CHUNKS)

    def send(pieces, route, waits):
        return [lax.ppermute(after(piece, *wait), "comp", route) for piece, wait in zip(pieces, waits)]

    stages = [(0, 0), (0, 1), (1, 0), (1, 1)]
    kept, sent, got, from_own, from_got, level_sums, full = {}, {}, {}, {}, {}, [], {}
    fields = seam = before = None
    part_table = table
    for stage in stages:
        part, late = stage
        kept[stage], sent[stage], extra = propagate(part, late, part_table, fields, seam, full.get(part))
        level_sums.append(extra[0])
        full[part] = extra[1]
        seam = None if late else extra[2]
        fields = extra[3] if fields is None else fields
        if stage == stages[-1]:
            break
        got[stage] = send(sent[stage], pairs, [[]])
        from_own[stage] = send(kept[stage], apart, [[]])
        waits = [from_got[before][0]] if stage == stages[2] else []
        from_got[stage] = send(got[stage], across, [waits])
        done = [extra[0]]
        if before is not None:
            done.append(got[before][0])
            if stage == stages[2]:
                done += [from_got[stages[0]][0], from_own[stages[1]][0]]
        part_table = after(table, *done)
        before = stage
    packed_fields = fields
    sums_0 = level_sums[0]

    sums = level_sums[0] + level_sums[1] + level_sums[2] + level_sums[3]
    partner_sums = lax.ppermute(sums, "comp", pairs)
    partner_sums = jnp.roll(partner_sums, half, axis=1)
    last, got_1, from_own_1 = stages[-1], [], []
    for c in chunk_range:
        waits = [got[before][0]] + ([got_1[c - 2]] if c >= 2 else []) + ([partner_sums] if c == 2 else [])
        got_1.append(lax.ppermute(after(sent[last][c], *waits), "comp", pairs))
        from_own_1.append(lax.ppermute(after(kept[last][c], from_own[before][0]), "comp", apart))
    got[last], from_own[last], from_got[last] = got_1, from_own_1, []
    sums = sums + partner_sums
    sums = sums_two = sums + lax.ppermute(sums, "comp", [(i, i ^ 2) for i in range(comp_count)])
    sums = sums + lax.ppermute(sums, "comp", [(i, i ^ 4) for i in range(comp_count)])
    mean_level = sums / comp_total

    dia_index, coupling, growth, damping, late_odd, late_pair, _ = lax.optimization_barrier(
        (dia_index, coupling, growth, damping, odd, pair_pos, sums_0)
    )
    own_growth = lax.dynamic_slice_in_dim(growth, first_comp, local_comps)[:, None]
    own_damping = lax.dynamic_slice_in_dim(damping, first_comp, local_comps)[:, None]
    chunk_first = [
        NTH * jnp.where(late_odd > 0, 8 * late_pair + 10 - 2 * j, 8 * late_pair - 4 + 2 * j) for j in range(8)
    ]
    margin = 8 * NTH
    dia_pad = jnp.pad(dia_index, ((0, 0), (margin, margin)), constant_values=-1)
    coupling_pad = jnp.pad(coupling, (margin, margin))
    own_ids = jnp.arange(comps)
    targets, rates = [], []
    for j in range(1, 7):
        targets.append(lax.dynamic_slice(dia_pad, (0, chunk_first[j] + margin), (4, comps)))
        rates.append(lax.dynamic_slice_in_dim(coupling_pad, chunk_first[j] + margin, comps))
    lookup = []
    for j in range(1, 7):
        ids = jnp.concatenate([chunk_first[j + d] + own_ids for d in (-1, 0, 1)])
        lookup.append((targets[j - 1].reshape(4 * comps)[:, None] == ids[None, :]).astype(jnp.bfloat16))
    lookup = jnp.stack(lookup)
    out_ids = jnp.concatenate([chunk_first[j] + own_ids for j in range(2, 6)])
    spread = []
    for j in range(1, 7):
        for pair in range(2):
            hits = [
                (out_ids[:, None] == targets[j - 1][2 * pair + q][None, :]).astype(f32) for q in range(2)
            ]
            spread.append(hits[0] + hits[1])
    spread = jnp.concatenate(spread, axis=1).astype(jnp.bfloat16)
    rates = jnp.concatenate(rates)[:, None]

    lanes = 512 if width % 512 == 0 else width
    own_parts, parts_0, parts_1 = [], [], []
    groups = [(from_got, 1), (from_got, 0), (kept, 0), (kept, 1), (got, 1), (got, 0), (from_own, 0), (from_own, 1)]
    for c in chunk_range:
        waits = [from_got[before][0]] + ([from_got[last][c - 2]] if c >= 2 else [])
        from_got[last].append(lax.ppermute(after(got_1[c], *waits), "comp", across))
        levels, level_specs = [], []
        for group, part in groups:
            for late in range(2):
                pieces = group[part, late]
                single = len(pieces) == 1
                levels.append(pieces[0 if single else c])
                skipped = c * (width // lanes) if single else 0
                level_specs.append(
                    pl.BlockSpec((levels[-1].shape[0], lanes), functools.partial(lambda n, s: (0, n + s), skipped))
                )
        own_part, part_0, part_1 = pl.pallas_call(
            interact_kernel,
            grid=(width // lanes,),
            in_specs=[
                pl.BlockSpec(lookup.shape, lambda s: (0, 0, 0)),
                pl.BlockSpec(spread.shape, lambda s: (0, 0)),
                pl.BlockSpec(rates.shape, lambda s: (0, 0)),
            ] + level_specs,
            out_specs=[pl.BlockSpec((n * comps, lanes), lambda s: (0, s)) for n in (2, 1, 1)],
            out_shape=[jax.ShapeDtypeStruct((n * comps, width), f32) for n in (2, 1, 1)],
            scratch_shapes=[pltpu.VMEM((12 * comps, lanes), jnp.bfloat16)],
            name="interact_cells",
            compiler_params=params(VMEM_MIB),
            cost_estimate=pl.CostEstimate(
                flops=2 * width * comps * comps * (6 * 12 + 48),
                bytes_accessed=20 * MIB, transcendentals=0,
            ),
        )(lookup, spread, rates, *levels)
        own_parts.append(own_part)
        parts_0.append(part_0)
        parts_1.append(part_1)

    def send_back(piece, *waits):
        return lax.ppermute(after(piece, *waits), "comp", pairs)

    back = [[None] * CELL_CHUNKS for _ in range(2)]
    back[0][0] = send_back(parts_0[0], got_1[2], sums_two)
    back[1][0] = send_back(parts_1[0], got_1[3])
    back[0][1] = send_back(parts_0[1], back[0][0], sums)
    back[0][2] = send_back(parts_0[2], back[1][0])
    back[0][3] = send_back(parts_0[3], back[0][1])
    for c in range(1, CELL_CHUNKS):
        back[1][c] = send_back(parts_1[c], back[0][2])

    def finish(part, so_far):
        piece = pl.BlockSpec((GROUP, width), lambda s, b, t: (s, 0))
        own_piece = pl.BlockSpec((GROUP, width), lambda s, b, t: (part * steps + s, 0))
        inputs = [place, mean_level, packed_fields, own_growth, own_damping]
        specs = [whole(place.shape), whole(mean_level.shape), whole(packed_fields.shape), column(part, 1),
                 column(part, 1)]
        inputs += [full[part]] + own_parts + back[part]
        specs.append(pl.BlockSpec((GROUP, cells), lambda s, b, t: (s, 0)))
        specs += [own_piece] * CELL_CHUNKS + [piece] * CELL_CHUNKS
        aliases = {}
        if so_far is not None:
            inputs.append(so_far)
            specs.append(pl.BlockSpec(memory_space=pl.ANY))
            aliases = {len(inputs) + 1: 0}
        return pl.pallas_call(
            functools.partial(finish_kernel, CELL_CHUNKS),
            grid_spec=pltpu.PrefetchScalarGridSpec(
                num_scalar_prefetch=2,
                grid=(steps,),
                in_specs=specs,
                out_specs=pl.BlockSpec((GROUP, row_count, col_count), lambda s, b, t: (group_at(part, b) + s, 0, 0)),
                scratch_shapes=[pltpu.VMEM((GROUP, cells), f32)],
            ),
            out_shape=jax.ShapeDtypeStruct(energy.shape, f32),
            input_output_aliases=aliases,
            name="finish_chunk",
            compiler_params=params(VMEM_MIB),
            cost_estimate=pl.CostEstimate(
                flops=20 * comps * row_count * col_count,
                bytes_accessed=100 * MIB, transcendentals=0,
            ),
        )(base, table, *inputs)

    return finish(1, finish(0, None))


def choose_shards(energy, *rest):
    local_comps, row_count, col_count = energy.shape
    fits = (
        local_comps == 4 * NTH and lax.axis_size("comp") == 8 and local_comps * 8 == NTH * NF
        and lax.axis_size("tile") == 2 and row_count == BLOCK and col_count == 2 * BLOCK
    )
    return packed_shards(energy, *rest) if fits else shards(energy, *rest)


def solution(mesh):
    placed = (
        P("comp", ("grp", "tile"), None),
        P("grp", None),
        P("grp", None),
        P("grp", None),
        P("grp", None),
        P("grp", None),
        P(),
        P(),
        P(),
        P(),
        P(),
    )
    return jax.shard_map(
        choose_shards,
        mesh=mesh,
        in_specs=placed,
        out_specs=P("comp", ("grp", "tile"), None),
        check_vma=False,
    )
```

```python
import functools
import math

import jax
import jax.numpy as jnp
import numpy as np
from jax import lax
from jax.experimental import pallas as pl
from jax.experimental.pallas import tpu as pltpu
from jax.sharding import PartitionSpec as P

NTH = 36
NF = 32


weight_plus = 0.4096
weight_minus = 3.1605
weight_cross = 1.2945


def with_halo(block, sides, width):
    for axis, dim in sides:
        count = lax.axis_size(axis)
        forward = [(i, i + 1) for i in range(count - 1)]
        backward = [(target, source) for source, target in forward]
        low = lax.ppermute(
            lax.slice_in_dim(block, block.shape[dim] - width, None, axis=dim), axis, forward
        )
        high = lax.ppermute(lax.slice_in_dim(block, 0, width, axis=dim), axis, backward)
        block = jnp.concatenate([low, block, high], axis=dim)
    return block


def quick_flux(far_left, left_cell, right_cell, far_right, courant):
    centre = 0.5 * (left_cell + right_cell) - 0.5 * courant * (right_cell - left_cell)
    curvature = (1.0 - courant * courant) / 6.0
    upward = centre - curvature * (right_cell - 2.0 * left_cell + far_left)
    downward = centre - curvature * (left_cell - 2.0 * right_cell + far_right)
    return courant * jnp.where(courant > 0.0, upward, downward)


def flux_change(padded, speed, current, sea_pad, axis):
    cell_count = padded.shape[axis] - 4

    def take_part(source, first, which_axis):
        return lax.slice_in_dim(source, first, first + cell_count + 1, axis=which_axis)

    face_current = 0.5 * (take_part(current, 0, axis - 1) + take_part(current, 1, axis - 1))
    courant = speed[:, None, None] + face_current[None]
    open_face = (take_part(sea_pad, 0, axis - 1) * take_part(sea_pad, 1, axis - 1))[None]
    face_flux = (
        quick_flux(
            take_part(padded, 0, axis),
            take_part(padded, 1, axis),
            take_part(padded, 2, axis),
            take_part(padded, 3, axis),
            courant,
        )
        * open_face
    )
    return lax.slice_in_dim(face_flux, 1, cell_count + 1, axis=axis) - lax.slice_in_dim(
        face_flux, 0, cell_count, axis=axis
    )


def source_terms(energy_block, wind, turning, growth, damping, coupling, lookup, spread):
    cell_count = energy_block.shape[1]
    spectrum = energy_block.reshape(NF, NTH, cell_count)
    turn_rate = turning[None, None, :]
    next_dir = jnp.roll(spectrum, -1, axis=1)
    forward = jnp.maximum(turn_rate, 0.0)
    backward = jnp.minimum(turn_rate, 0.0)
    upper_flux = forward * spectrum + backward * next_dir
    lower_flux = jnp.roll(upper_flux, 1, axis=1)
    turned = (spectrum - upper_flux + lower_flux).reshape(energy_block.shape)
    rounded = turned.astype(jnp.bfloat16)
    plus_first, minus_first, plus_second, minus_second = lookup(rounded)
    couple_rate = coupling[:, None]
    delta_first = couple_rate * (
        turned * turned * (weight_plus * plus_first + weight_minus * minus_first)
        - 2.0 * weight_cross * turned * plus_first * minus_first
    )
    delta_second = couple_rate * (
        turned * turned * (weight_plus * plus_second + weight_minus * minus_second)
        - 2.0 * weight_cross * turned * plus_second * minus_second
    )
    moved = spread(delta_first.astype(jnp.bfloat16), delta_second.astype(jnp.bfloat16))
    mean_level = jnp.sum(turned, axis=0) / energy_block.shape[0]
    return (
        turned
        + growth[:, None] * wind[None] * turned
        - damping[:, None] * mean_level[None] * turned
        - 2.0 * (delta_first + delta_second)
        + moved
    )


def shards(
    energy,
    sea_mask,
    current_u,
    current_v,
    wind_forcing,
    refraction,
    group_speed,
    growth,
    damping,
    coupling,
    dia_index,
):
    comp_count = lax.axis_size("comp")
    comp_pos = lax.axis_index("comp")
    tile_pos = lax.axis_index("tile")
    local_comps, row_count, col_count = energy.shape
    first_row = tile_pos * row_count
    first_comp = comp_pos * local_comps
    comp_total = NTH * NF
    angles = 2.0 * math.pi / NTH * (jnp.arange(comp_total) % NTH).astype(jnp.float32)
    speeds = jnp.repeat(group_speed, NTH)
    speed_east = lax.dynamic_slice_in_dim(speeds * jnp.cos(angles), first_comp, local_comps)
    speed_north = lax.dynamic_slice_in_dim(speeds * jnp.sin(angles), first_comp, local_comps)
    window = (row_count + 2, col_count + 2)
    sea_pad = lax.dynamic_slice(jnp.pad(sea_mask.astype(jnp.float32), 1), (first_row, 0), window)
    east_pad = lax.dynamic_slice(jnp.pad(current_u, 1), (first_row, 0), window)
    north_pad = lax.dynamic_slice(jnp.pad(current_v, 1), (first_row, 0), window)
    sea_tile = sea_pad[1:-1, 1:-1]
    masked = energy * sea_tile[None]
    padded_east = with_halo(masked, (("tile", 1),), 2)
    along_east = flux_change(padded_east, speed_east, east_pad[:, 1:-1], sea_pad[:, 1:-1], 1)
    along_north = flux_change(
        jnp.pad(masked, ((0, 0), (0, 0), (2, 2))),
        speed_north,
        north_pad[1:-1, :],
        sea_pad[1:-1, :],
        2,
    )
    propagated = (sea_tile[None] * (masked - along_east - along_north)).reshape(
        local_comps, row_count * col_count
    )
    tile_wind = lax.dynamic_slice(wind_forcing, (first_row, 0), (row_count, col_count)).reshape(-1)
    tile_turn = lax.dynamic_slice(refraction, (first_row, 0), (row_count, col_count)).reshape(-1)
    comp_ids = jnp.arange(comp_total)
    tables = [
        (dia_index[slot_row][:, None] == comp_ids[None, :]).astype(jnp.bfloat16)
        for slot_row in range(4)
    ]

    def lookup(rounded):
        return tuple(
            (
                jnp.dot(tables[slot_row], rounded, preferred_element_type=jnp.float32)
                for slot_row in range(4)
            )
        )

    def scatter_back(table, terms):
        return lax.dot_general(
            table, terms, (((0,), (0,)), ((), ())), preferred_element_type=jnp.float32
        )

    def spread(first_terms, second_terms):
        return (
            scatter_back(tables[0], first_terms)
            + scatter_back(tables[1], first_terms)
            + scatter_back(tables[2], second_terms)
            + scatter_back(tables[3], second_terms)
        )

    share_size = row_count * col_count // comp_count
    point_field = lax.all_to_all(propagated, "comp", split_axis=1, concat_axis=0, tiled=True)
    first_point = comp_pos * share_size
    own_wind = lax.dynamic_slice_in_dim(tile_wind, first_point, share_size)
    own_turn = lax.dynamic_slice_in_dim(tile_turn, first_point, share_size)
    result = source_terms(
        point_field, own_wind, own_turn, growth, damping, coupling, lookup, spread
    )
    returned_field = lax.all_to_all(result, "comp", split_axis=0, concat_axis=1, tiled=True)
    return returned_field.reshape(local_comps, row_count, col_count)


BLOCK = 128
GROUP = 24
EARLY = 40
BATCH = 4
CELL_CHUNKS = 4
MIB = 1024 * 1024
VMEM_MIB = 60
EDGE = 2
SEA, OPEN_EAST, FLOW_EAST, OPEN_NORTH, FLOW_NORTH, HALF_SEA, WIND, TURN = range(8)
KEEP, SPILL, IS_SEA = BLOCK, 2 * BLOCK, 2 * BLOCK


def upwind(courant, total, slope, bend_here, bend_ahead):
    bend = jnp.where(courant > 0.0, bend_here, bend_ahead)
    return courant * ((total - bend) - courant * (slope - courant * bend))


def pick_lanes(block, index):
    return jnp.take_along_axis(block, index, axis=1, mode="promise_in_bounds")


def tile_at(tile):
    return pl.ds(pl.multiple_of(tile * BLOCK, BLOCK), BLOCK)


def has(code, flag):
    return jnp.bitwise_and(code, flag) != 0


def pack_block(blocks, code, tile, out_ref, firsts, held):
    code = jnp.broadcast_to(code, (8, BLOCK))
    index = jnp.bitwise_and(code, BLOCK - 1)
    keep, spill = has(code, KEEP), has(code, SPILL)
    result = []
    for block, first, old in zip(blocks, firsts, held):
        moved = pick_lanes(block, index)
        merged = jnp.where(keep, moved, old)
        out_ref[pl.ds(first, 8), tile_at(tile)] = merged
        result.append(jnp.where(spill, moved, merged))
    return tuple(result)


def prepare_kernel(places, base_ref, speed_ref, sea_ref, east_ref, north_ref, wind_ref, turn_ref, cos_ref, sin_ref,
                   coef_ref, index_ref, place_ref, table_ref, speed_east_ref, speed_north_ref, field_ref, pick_ref):
    first_row, odd, first_freq = base_ref[0], base_ref[1], base_ref[2]
    all_rows, col_count = sea_ref.shape
    row_count = place_ref.shape[1]
    tiles = places // BLOCK
    sea = sea_ref[...].astype(jnp.float32)
    row = lax.broadcasted_iota(jnp.int32, sea.shape, 0)
    col = lax.broadcasted_iota(jnp.int32, sea.shape, 1)

    def next_row(field):
        return jnp.where(row == all_rows - 1, 0.0, pltpu.roll(field, all_rows - 1, 0))

    def next_col(field):
        return jnp.where(col == col_count - 1, 0.0, pltpu.roll(field, col_count - 1, 1))

    open_east, open_north = sea * next_row(sea), sea * next_col(sea)
    east, north = east_ref[...], north_ref[...]
    field_ref[SEA] = sea
    field_ref[OPEN_EAST] = open_east
    field_ref[FLOW_EAST] = open_east * (0.5 * (east + next_row(east)))
    field_ref[OPEN_NORTH] = open_north
    field_ref[FLOW_NORTH] = open_north * (0.5 * (north + next_col(north)))
    field_ref[HALF_SEA] = 0.5 * sea
    field_ref[WIND] = wind_ref[...]
    field_ref[TURN] = turn_ref[...]
    coef_ref[0:EDGE] = jnp.zeros((EDGE, 8, col_count), jnp.float32)
    coef_ref[EDGE + all_rows :] = jnp.zeros((EDGE, 8, col_count), jnp.float32)

    @pl.loop(0, all_rows // 8)
    def _(i):
        rows = field_ref[:, pl.ds(pl.multiple_of(8 * i, 8), 8), :]
        coef_ref[pl.ds(8 * i + EDGE, 8)] = jnp.swapaxes(rows, 0, 1)

    freqs = cos_ref.shape[0] // NTH
    for f in range(freqs):
        circle = slice(f * NTH, (f + 1) * NTH)
        speed_east_ref[circle, :] = cos_ref[circle, :] * speed_ref[first_freq + f]
        speed_north_ref[circle, :] = sin_ref[circle, :] * speed_ref[first_freq + f]

    bf16, f32 = jnp.bfloat16, jnp.float32
    tile_sea = sea_ref[pl.ds(pl.multiple_of(first_row, 8), row_count), :].astype(f32)
    square = (BLOCK, BLOCK)
    down, over = lax.broadcasted_iota(jnp.int32, square, 0), lax.broadcasted_iota(jnp.int32, square, 1)
    before = (down < over).astype(f32).astype(bf16)
    ones = jnp.ones(square, bf16)
    row_square = (row_count, row_count)
    above = lax.broadcasted_iota(jnp.int32, row_square, 1) < lax.broadcasted_iota(jnp.int32, row_square, 0)
    above = above.astype(f32).astype(bf16)
    parts = [tile_sea[:, :BLOCK], tile_sea[:, BLOCK:]]
    numbers = [jnp.dot(p.astype(bf16), ones, preferred_element_type=f32) for p in parts]
    in_row = numbers[0] + numbers[1]
    starts = [jnp.dot(above, in_row.astype(bf16), preferred_element_type=f32)]
    starts.append(starts[0] + numbers[0])
    total = jnp.sum(in_row, axis=0, keepdims=True).astype(jnp.int32)

    def turned_tile(tile):
        return jnp.where(tile >= tiles, tiles, jnp.bitwise_and(tile + odd * (tiles // 2), tiles - 1))

    columns = []
    for h in range(2):
        rank = jnp.dot(parts[h].astype(bf16), before, preferred_element_type=f32).astype(jnp.int32)
        start = starts[h].astype(jnp.int32)
        offset = jnp.bitwise_and(start, BLOCK - 1)
        keep = jnp.where(over[:row_count] >= offset, KEEP, 0)
        slot = jnp.bitwise_and(rank + offset, BLOCK - 1)
        is_sea = parts[h] > 0.0
        place_ref[h] = slot + keep + jnp.where(is_sea, IS_SEA, 0)
        slot = jnp.where(is_sea, slot, -1).astype(f32).T
        from_lane = down[:, :row_count].astype(f32)

        @pl.loop(0, BLOCK // 8)
        def _(i):
            found = []
            for k in range(8):
                lane = (8 * i + k).astype(f32)
                found.append(jnp.sum(jnp.where(slot == lane, from_lane, 0.0), axis=0, keepdims=True))
            pick_ref[pl.ds(pl.multiple_of(8 * i, 8), 8), :] = jnp.concatenate(found, axis=0)

        spill = jnp.where(offset + numbers[h].astype(jnp.int32) >= BLOCK, SPILL, 0)
        index_ref[h] = pick_ref[...].T.astype(jnp.int32) + keep + spill
        columns.append(turned_tile(lax.shift_right_logical(starts[h].T[0:8, :].astype(jnp.int32), 7)))
    row_id = lax.broadcasted_iota(jnp.int32, (8, row_count), 0)
    end_tile = jnp.where(
        jnp.bitwise_and(total, BLOCK - 1) == 0, tiles, turned_tile(lax.shift_right_logical(total, 7))
    )
    end_tile = jnp.broadcast_to(end_tile, (8, BLOCK))
    table_ref[...] = jnp.concatenate([jnp.where(row_id == 0, columns[0], columns[1]), end_tile], axis=1)


def propagate_kernel(part, late, pieces, base_ref, table_ref, energy_ref, halo_ref, coef_ref, index_ref, east_ref,
                     north_ref, *refs):
    refs = list(refs)
    with_fields = part == 0 and not late
    fields_ref = None if with_fields else refs.pop(0)
    seam_ref = refs.pop(0) if late else None
    if late:
        refs.pop(0)
    piece_refs = [refs.pop(0) for _ in range(2 * pieces)]
    sum_ref, full_ref = refs.pop(0), refs.pop(0)
    seam_out_ref = None if late else refs.pop(0)
    fields_out_ref = refs.pop(0) if with_fields else None
    rows_ref, spread_ref, wide_ref, result_ref, row_sems, out_sems = refs
    row_count, comp_count, col_count = rows_ref.shape
    strips = comp_count // 8
    sent_rows = piece_refs[0].shape[0]
    cells = result_ref.shape[1]
    first_row = base_ref[0]
    first_comp = pl.multiple_of((part + base_ref[1] * (1 - 2 * part)) * 2 * NTH + late * EARLY, 8)
    lane = lax.broadcasted_iota(jnp.int32, (8, BLOCK), 1)
    first_lane, last_lane, last_lanes = lane == 0, lane == BLOCK - 1, lane >= BLOCK - 2
    third = 1.0 / 3.0

    @pl.loop(0, row_count // 8)
    def _(i):
        for k in range(8):
            row = 8 * i + k
            source = energy_ref.at[pl.ds(first_comp, comp_count), row, :]
            pltpu.make_async_copy(source, rows_ref.at[row], row_sems.at[i]).start()

    def halves(row):
        return row[:, :BLOCK], row[:, BLOCK:]

    @pl.loop(0, row_count + 2 * EDGE, unroll=4)
    def _(r):
        coef = coef_ref[first_row + r]
        for k in range(HALF_SEA + 1):
            spread_ref[r, k] = jnp.broadcast_to(coef[k : k + 1, :], coef.shape)

    def masked(row, at):
        return tuple(part * sea for part, sea in zip(halves(row), halves(spread_ref[at, SEA])))

    def cell_rows(first, fresh, state, east, north):
        here, ahead, slope_here, bend_here, flux_low = state
        count, sides = len(fresh), range(2)
        level = [here, ahead] + [masked(row, first + k + EDGE) for k, row in enumerate(fresh)]
        rows = range(count)
        coef = [[None] + [halves(spread_ref[first + k, f]) for f in range(1, HALF_SEA + 1)] for k in rows]
        one_right = [[pltpu.roll(part, BLOCK - 1, 1) for part in level[k]] for k in rows]
        one_left = [[pltpu.roll(part, 1, 1) for part in level[k]] for k in rows]
        two_right = [[pltpu.roll(part, BLOCK - 2, 1) for part in level[k]] for k in rows]
        cross = []
        for k in rows:
            right = (jnp.where(last_lane, one_right[k][1], one_right[k][0]), jnp.where(last_lane, 0.0, one_right[k][1]))
            left = (jnp.where(first_lane, 0.0, one_left[k][0]), jnp.where(first_lane, one_left[k][0], one_left[k][1]))
            next_right = (jnp.where(last_lanes, two_right[k][1], two_right[k][0]),
                          jnp.where(last_lanes, 0.0, two_right[k][1]))
            parts = []
            for h in sides:
                mid = level[k][h]
                slope = right[h] - mid
                bend = third * (slope - (mid - left[h]))
                bend_right = third * ((next_right[h] - right[h]) - slope)
                parts.append(upwind(north * coef[k][OPEN_NORTH][h] + coef[k][FLOW_NORTH][h], mid + right[h], slope,
                                    bend, bend_right))
            cross.append(parts)
        cross_roll = [[pltpu.roll(part, 1, 1) for part in cross[k]] for k in rows]
        slopes = [slope_here] + [tuple(level[k + 1][h] - level[k][h] for h in sides) for k in range(1, count + 1)]
        bends = [bend_here] + [
            tuple(third * (slopes[k][h] - slopes[k - 1][h]) for h in sides) for k in range(1, count + 1)
        ]
        flux = [flux_low]
        for k in rows:
            flux.append(tuple(
                upwind(east * coef[k][OPEN_EAST][h] + coef[k][FLOW_EAST][h], level[k][h] + level[k + 1][h],
                       slopes[k][h], bends[k][h], bends[k + 1][h])
                for h in sides
            ))
        done = []
        for k in rows:
            cross_low = (jnp.where(first_lane, cross_roll[k][1], cross_roll[k][0]),
                         jnp.where(first_lane, cross_roll[k][0], cross_roll[k][1]))
            done.append([
                coef[k][HALF_SEA][h] * (((level[k][h] + level[k][h]) + (flux[k][h] + cross_low[h]))
                                        - (flux[k + 1][h] + cross[k][h]))
                for h in sides
            ])
        return (level[count], level[count + 1], slopes[count], bends[count], flux[count]), done

    def store_row(row, local, parts):
        for h in range(2):
            rows_ref[row, local, h * BLOCK : (h + 1) * BLOCK] = parts[h]

    def strip(g, arrive):
        local = pl.ds(pl.multiple_of(g * 8, 8), 8)
        comps = pl.ds(pl.multiple_of(first_comp + g * 8, 8), 8)
        east, north = east_ref[comps, :], north_ref[comps, :]
        zero = (jnp.zeros((8, BLOCK), jnp.float32),) * 2
        here, ahead = masked(halo_ref[comps, 0, :], 0), masked(halo_ref[comps, 1, :], 1)
        state = (here, ahead, tuple(b - a for a, b in zip(here, ahead)), zero, zero)

        def eight(i, state):
            if arrive:
                block = rows_ref.at[pl.ds(8 * i, 8)]
                pltpu.make_async_copy(block, block, row_sems.at[i]).wait()
            for first in range(0, 8, BATCH):
                fresh = [rows_ref[8 * i + first + k, local, :] for k in range(BATCH)]
                state, done = cell_rows(8 * i + first, fresh, state, east, north)
                for k in range(BATCH):
                    store_row(jnp.maximum(8 * i + first + k - EDGE, 0), local, done[k])
            return state

        state = lax.fori_loop(0, row_count // 8, eight, state)
        fresh = [halo_ref[comps, k, :] for k in range(EDGE)]
        state, done = cell_rows(row_count, fresh, state, east, north)
        for k in range(EDGE):
            store_row(row_count - EDGE + k, local, done[k])

    strip(0, True)

    @pl.loop(1, strips)
    def _(g):
        strip(g, False)

    group_rows = [8 * n for n in range(strips + with_fields)]

    def pack_eight(i, held):
        codes = [index_ref[h, pl.ds(pl.multiple_of(8 * i, 8), 8), :] for h in range(2)]
        for k in range(8):
            row = 8 * i + k
            for h in range(2):
                lanes = slice(h * BLOCK, (h + 1) * BLOCK)
                blocks = [rows_ref[row, 8 * n : 8 * n + 8, lanes] for n in range(strips)]
                if with_fields:
                    blocks.append(coef_ref[first_row + EDGE + row, :, lanes])
                held = pack_block(blocks, codes[h][k : k + 1, :], table_ref[h, row], wide_ref, group_rows, held)
        return held

    empty = (jnp.zeros((8, BLOCK), jnp.float32),) * len(group_rows)
    held = lax.fori_loop(0, row_count // 8, pack_eight, empty)
    for first, block in zip(group_rows, held):
        wide_ref[pl.ds(first, 8), tile_at(table_ref[0, row_count])] = block
    if with_fields:
        fields_out_ref[...] = wide_ref[comp_count:, :cells]

    tile_width = 2 * BLOCK
    height = result_ref.shape[0]
    comp_row = lax.broadcasted_iota(jnp.int32, (height, tile_width), 0)
    start = height - NTH if late else 0
    end = start + NTH - 1
    mixed = slice(0, 8) if late else slice(height - 8, height)
    mixed_row = comp_row[mixed]
    in_circle = (mixed_row >= start) & (mixed_row <= end)

    @pl.loop(0, cells // tile_width, unroll=2)
    def _(i):
        source = pl.ds(pl.multiple_of(i * tile_width, tile_width), tile_width)
        level = wide_ref[:comp_count, source]
        if late:
            level = jnp.concatenate([seam_ref[:, source], level], axis=0)
        if with_fields:
            rate = wide_ref[comp_count + TURN : comp_count + TURN + 1, source]
        else:
            rate = fields_ref[TURN : TURN + 1, source]
        forward = jnp.maximum(rate, 0.0)
        backward = jnp.minimum(rate, 0.0)
        stay = (1.0 - forward) + backward
        above = pltpu.roll(level, height - 1, 0)
        below = pltpu.roll(level, 1, 0)

        def with_row(rolled, row, value):
            tile = slice(row - row % 8, row - row % 8 + 8)
            fixed = jnp.where(comp_row[tile] == row, value, rolled[tile])
            parts = [rolled[: tile.start], fixed, rolled[tile.stop :]]
            return jnp.concatenate([part for part in parts if part.shape[0]], axis=0)

        above = with_row(above, end, level[start : start + 1, :])
        below = with_row(below, start, level[end : end + 1, :])
        turned = stay * level - backward * above + forward * below
        partial = jnp.where(in_circle, turned[mixed], 0.0)
        for first in range(0, height, 8):
            rows = slice(first, first + 8)
            if first == mixed.start:
                result_ref[rows, source] = jnp.where(in_circle, turned[rows], level[rows])
            else:
                result_ref[rows, source] = turned[rows]
                partial += turned[rows]
        sum_ref[:, source] = jnp.sum(partial, axis=0, keepdims=True)

    if not late:
        seam_out_ref[...] = result_ref[sent_rows:, :]
    width = cells // (2 * pieces)
    copies = []
    for n, piece in enumerate(piece_refs):
        source = result_ref.at[:sent_rows, n * width : (n + 1) * width]
        copies.append(pltpu.make_async_copy(source, piece, out_sems.at[n]))
    rows = pl.ds(EARLY - 8 if late else 0, sent_rows)
    copies.append(pltpu.make_async_copy(result_ref.at[:sent_rows, :], full_ref.at[rows, :], out_sems.at[2 * pieces]))
    for copy in copies:
        copy.start()
    for copy in copies:
        copy.wait()


def interact_kernel(table_ref, spread_ref, coupling_ref, *refs):
    own_ref, back_0_ref, back_1_ref, delta_ref = refs[16:]
    window = [jnp.concatenate([refs[2 * j][...], refs[2 * j + 1][...]], axis=0) for j in range(8)]
    comps = window[0].shape[0]
    for j in range(1, 7):
        level = window[j]
        around = jnp.concatenate([window[j - 1], level, window[j + 1]], axis=0).astype(jnp.bfloat16)
        partner = jnp.dot(table_ref[j - 1], around, preferred_element_type=jnp.float32)
        rate = coupling_ref[(j - 1) * comps : j * comps, :] * level
        plus_part = weight_plus * level
        minus_part = weight_minus * level
        deltas = []
        for pair in range(2):
            plus = partner[2 * pair * comps : (2 * pair + 1) * comps, :]
            minus = partner[(2 * pair + 1) * comps : (2 * pair + 2) * comps, :]
            deltas.append(rate * (plus * (plus_part - (2.0 * weight_cross) * minus) + minus_part * minus))
        both = jnp.concatenate(deltas, axis=0).astype(jnp.bfloat16)
        delta_ref[(j - 1) * 2 * comps : j * 2 * comps, :] = both
        if 2 <= j <= 5:
            part = -2.0 * (deltas[0] + deltas[1])
            if j <= 3:
                own_ref[(j - 2) * comps : (j - 1) * comps, :] = part
            elif j == 4:
                back_1_ref[...] = part
            else:
                back_0_ref[...] = part
    spread = jnp.dot(spread_ref[...], delta_ref[...], preferred_element_type=jnp.float32)
    own_ref[...] += spread[: 2 * comps, :]
    back_1_ref[...] += spread[2 * comps : 3 * comps, :]
    back_0_ref[...] += spread[3 * comps :, :]


def finish_kernel(chunks, base_ref, table_ref, place_ref, mean_ref, fields_ref, growth_ref, damping_ref, *refs):
    turned_ref, own, back = refs[0], refs[1 : 1 + chunks], refs[1 + chunks : 1 + 2 * chunks]
    out_ref, wide_ref = refs[-2], refs[-1]
    width = own[0].shape[1]
    tiles = wide_ref.shape[1] // BLOCK
    tile_width = 2 * BLOCK
    growth = jnp.broadcast_to(growth_ref[...], (GROUP, tile_width))
    damping = jnp.broadcast_to(damping_ref[...], (GROUP, tile_width))
    for o in range(2 * chunks):
        extra = own[o] if o < chunks else back[o - chunks]

        @pl.loop(0, width // tile_width, unroll=2)
        def _(i):
            source = pl.ds(pl.multiple_of(i * tile_width, tile_width), tile_width)
            target = pl.ds(pl.multiple_of(o * width + i * tile_width, tile_width), tile_width)
            scale = 1.0 + growth * fields_ref[WIND : WIND + 1, target] - damping * mean_ref[0:1, target]
            wide_ref[:, target] = turned_ref[:, target] * scale + extra[:, source]

    @pl.loop(0, out_ref.shape[1] // 8)
    def _(i):
        codes = [place_ref[h, pl.ds(pl.multiple_of(8 * i, 8), 8), :] for h in range(2)]
        done = [[] for _ in range(GROUP // 8)]
        for r in range(8):
            parts = [[] for _ in range(GROUP // 8)]
            for h in range(2):
                code = jnp.broadcast_to(codes[h][r : r + 1, :], (8, BLOCK))
                index = jnp.bitwise_and(code, BLOCK - 1)
                keep, is_sea = has(code, KEEP), has(code, IS_SEA)
                tile = table_ref[h, 8 * i + r]
                first, second = jnp.minimum(tile, tiles - 1), jnp.bitwise_and(tile + 1, tiles - 1)
                for k in range(GROUP // 8):
                    rows = slice(8 * k, 8 * k + 8)
                    near = jnp.where(keep, wide_ref[rows, tile_at(first)], wide_ref[rows, tile_at(second)])
                    parts[k].append(jnp.where(is_sea, pick_lanes(near, index), 0.0))
            for k in range(GROUP // 8):
                done[k].append(jnp.concatenate(parts[k], axis=1))
        for k in range(GROUP // 8):
            out_ref[8 * k : 8 * k + 8, pl.ds(pl.multiple_of(8 * i, 8), 8), :] = jnp.swapaxes(jnp.stack(done[k]), 0, 1)


def params(limit):
    return pltpu.CompilerParams(vmem_limit_bytes=limit * MIB)


def after(value, *others):
    return lax.optimization_barrier((value,) + others)[0]


def packed_shards(energy, sea_mask, current_u, current_v, wind_forcing, refraction, group_speed, growth, damping,
                  coupling, dia_index):
    comp_count = lax.axis_size("comp")
    comp_pos = lax.axis_index("comp")
    tile_pos = lax.axis_index("tile")
    odd = lax.rem(comp_pos, 2)
    pair_pos = comp_pos // 2
    local_comps, row_count, col_count = energy.shape
    comps = local_comps // 2
    comp_total = NTH * NF
    first_row = tile_pos * row_count
    first_comp = comp_pos * local_comps
    cells = row_count * col_count // 2
    half = cells // 2
    width = half // CELL_CHUNKS
    f32, i32 = jnp.float32, jnp.int32
    base = jnp.stack([first_row, odd, comp_pos * (local_comps // NTH)]).astype(i32)

    edge_first = jnp.where(tile_pos == 0, row_count - EDGE, 0)
    edge_rows = lax.dynamic_slice_in_dim(energy, edge_first, EDGE, axis=1)
    halo_rows = lax.ppermute(edge_rows, "tile", [(0, 1), (1, 0)])

    all_rows = sea_mask.shape[0]
    angles = np.float32(2.0 * math.pi / NTH) * (np.arange(local_comps) % NTH).astype(np.float32)
    cosines = np.broadcast_to(np.cos(angles)[:, None], (local_comps, BLOCK)).astype(np.float32)
    sines = np.broadcast_to(np.sin(angles)[:, None], (local_comps, BLOCK)).astype(np.float32)
    vmem = pl.BlockSpec(memory_space=pltpu.VMEM)
    coef, index, place, table, speed_east, speed_north = pl.pallas_call(
        functools.partial(prepare_kernel, cells),
        grid_spec=pltpu.PrefetchScalarGridSpec(
            num_scalar_prefetch=2,
            grid=(),
            in_specs=[vmem] * 7,
            out_specs=[vmem] * 6,
            scratch_shapes=[pltpu.VMEM((8, all_rows, col_count), f32), pltpu.VMEM((BLOCK, row_count), f32)],
        ),
        out_shape=[
            jax.ShapeDtypeStruct((all_rows + 2 * EDGE, 8, col_count), f32),
            jax.ShapeDtypeStruct((2, row_count, BLOCK), i32),
            jax.ShapeDtypeStruct((2, row_count, BLOCK), i32),
            jax.ShapeDtypeStruct((8, 2 * BLOCK), i32),
            jax.ShapeDtypeStruct((local_comps, BLOCK), f32),
            jax.ShapeDtypeStruct((local_comps, BLOCK), f32),
        ],
        name="prepare",
        compiler_params=params(VMEM_MIB),
    )(base, group_speed, sea_mask, current_u, current_v, wind_forcing, refraction, cosines, sines)
    steps = comps // GROUP

    def group_at(part, base_ref):
        return (part + base_ref[1] * (1 - 2 * part)) * steps

    def whole(shape):
        return pl.BlockSpec(shape, lambda s, b, t: (0,) * len(shape))

    def column(part, lanes):
        return pl.BlockSpec((GROUP, lanes), lambda s, b, t: (group_at(part, b) + s, 0))

    def propagate(part, late, table, fields=None, seam=None, full=None):
        pieces = CELL_CHUNKS if part and late else 1
        comp_rows = comps - EARLY if late else EARLY
        sent_rows = comps - EARLY + 8 if late else EARLY - 8
        height = EARLY
        anywhere = pl.BlockSpec(memory_space=pl.ANY)
        with_fields = fields is None
        inputs = [energy, halo_rows, coef, index, speed_east, speed_north]
        in_specs = [anywhere] + [vmem] * 5
        aliases = {}
        if not with_fields:
            inputs.append(fields)
            in_specs.append(vmem)
        if late:
            inputs += [seam, full]
            in_specs += [vmem, anywhere]
            aliases = {len(inputs) + 1: 2 * pieces + 1}
        shapes = [(sent_rows, half // pieces)] * (2 * pieces) + [(1, cells), (comps, cells)]
        out_specs = [anywhere] * (2 * pieces) + [vmem, anywhere]
        if not late:
            shapes.append((8, cells))
            out_specs.append(vmem)
        if with_fields:
            shapes.append((8, cells))
            out_specs.append(vmem)
        outs = pl.pallas_call(
            functools.partial(propagate_kernel, part, late, pieces),
            grid_spec=pltpu.PrefetchScalarGridSpec(
                num_scalar_prefetch=2,
                grid=(),
                in_specs=in_specs,
                out_specs=out_specs,
                scratch_shapes=[
                    pltpu.VMEM((row_count, comp_rows, col_count), f32),
                    pltpu.VMEM((row_count + 2 * EDGE, HALF_SEA + 1, 8, col_count), f32),
                    pltpu.VMEM((comp_rows + (8 if with_fields else 0), cells + BLOCK), f32),
                    pltpu.VMEM((height, cells), f32),
                    pltpu.SemaphoreType.DMA((row_count // 8,)),
                    pltpu.SemaphoreType.DMA((2 * pieces + 1,)),
                ],
            ),
            out_shape=[jax.ShapeDtypeStruct(shape, f32) for shape in shapes],
            input_output_aliases=aliases,
            name="propagate_late" if late else "propagate_early",
            compiler_params=params(VMEM_MIB),
            cost_estimate=pl.CostEstimate(
                flops=60 * comp_rows * row_count * col_count, bytes_accessed=60 * MIB, transcendentals=0,
            ),
        )(base, table, *inputs)
        return list(outs[:pieces]), list(outs[pieces : 2 * pieces]), outs[2 * pieces :]

    pairs = [(i, i ^ 1) for i in range(comp_count)]
    apart = [(i, i - 2 if i % 2 == 0 else i + 2) for i in range(comp_count)]
    apart = [(a, b) for a, b in apart if 0 <= b < comp_count]
    across = [(b, a) for a, b in apart]
    chunk_range = range(CELL_CHUNKS)

    def send(pieces, route, waits):
        return [lax.ppermute(after(piece, *wait), "comp", route) for piece, wait in zip(pieces, waits)]

    stages = [(0, 0), (0, 1), (1, 0), (1, 1)]
    kept, sent, got, from_own, from_got, level_sums, full = {}, {}, {}, {}, {}, [], {}
    fields = seam = before = None
    part_table = table
    for stage in stages:
        part, late = stage
        kept[stage], sent[stage], extra = propagate(part, late, part_table, fields, seam, full.get(part))
        level_sums.append(extra[0])
        full[part] = extra[1]
        seam = None if late else extra[2]
        fields = extra[3] if fields is None else fields
        if stage == stages[-1]:
            break
        got[stage] = send(sent[stage], pairs, [[]])
        from_own[stage] = send(kept[stage], apart, [[]])
        waits = [from_got[before][0]] if stage == stages[2] else []
        from_got[stage] = send(got[stage], across, [waits])
        done = [extra[0]]
        if before is not None:
            done.append(got[before][0])
            if stage == stages[2]:
                done += [from_got[stages[0]][0], from_own[stages[1]][0]]
        part_table = after(table, *done)
        before = stage
    packed_fields = fields
    sums_0 = level_sums[0]

    sums = level_sums[0] + level_sums[1] + level_sums[2] + level_sums[3]
    partner_sums = lax.ppermute(sums, "comp", pairs)
    partner_sums = jnp.roll(partner_sums, half, axis=1)
    last, got_1, from_own_1 = stages[-1], [], []
    for c in chunk_range:
        waits = [got[before][0]] + ([got_1[c - 2]] if c >= 2 else []) + ([partner_sums] if c == 2 else [])
        got_1.append(lax.ppermute(after(sent[last][c], *waits), "comp", pairs))
        from_own_1.append(lax.ppermute(after(kept[last][c], from_own[before][0]), "comp", apart))
    got[last], from_own[last], from_got[last] = got_1, from_own_1, []
    sums = sums + partner_sums
    sums = sums_two = sums + lax.ppermute(sums, "comp", [(i, i ^ 2) for i in range(comp_count)])
    sums = sums + lax.ppermute(sums, "comp", [(i, i ^ 4) for i in range(comp_count)])
    mean_level = sums / comp_total

    dia_index, coupling, growth, damping, late_odd, late_pair, _ = lax.optimization_barrier(
        (dia_index, coupling, growth, damping, odd, pair_pos, sums_0)
    )
    own_growth = lax.dynamic_slice_in_dim(growth, first_comp, local_comps)[:, None]
    own_damping = lax.dynamic_slice_in_dim(damping, first_comp, local_comps)[:, None]
    chunk_first = [
        NTH * jnp.where(late_odd > 0, 8 * late_pair + 10 - 2 * j, 8 * late_pair - 4 + 2 * j) for j in range(8)
    ]
    margin = 8 * NTH
    dia_pad = jnp.pad(dia_index, ((0, 0), (margin, margin)), constant_values=-1)
    coupling_pad = jnp.pad(coupling, (margin, margin))
    own_ids = jnp.arange(comps)
    targets, rates = [], []
    for j in range(1, 7):
        targets.append(lax.dynamic_slice(dia_pad, (0, chunk_first[j] + margin), (4, comps)))
        rates.append(lax.dynamic_slice_in_dim(coupling_pad, chunk_first[j] + margin, comps))
    lookup = []
    for j in range(1, 7):
        ids = jnp.concatenate([chunk_first[j + d] + own_ids for d in (-1, 0, 1)])
        lookup.append((targets[j - 1].reshape(4 * comps)[:, None] == ids[None, :]).astype(jnp.bfloat16))
    lookup = jnp.stack(lookup)
    out_ids = jnp.concatenate([chunk_first[j] + own_ids for j in range(2, 6)])
    spread = []
    for j in range(1, 7):
        for pair in range(2):
            hits = [
                (out_ids[:, None] == targets[j - 1][2 * pair + q][None, :]).astype(f32) for q in range(2)
            ]
            spread.append(hits[0] + hits[1])
    spread = jnp.concatenate(spread, axis=1).astype(jnp.bfloat16)
    rates = jnp.concatenate(rates)[:, None]

    lanes = 512 if width % 512 == 0 else width
    own_parts, parts_0, parts_1 = [], [], []
    groups = [(from_got, 1), (from_got, 0), (kept, 0), (kept, 1), (got, 1), (got, 0), (from_own, 0), (from_own, 1)]
    for c in chunk_range:
        waits = [from_got[before][0]] + ([from_got[last][c - 2]] if c >= 2 else [])
        from_got[last].append(lax.ppermute(after(got_1[c], *waits), "comp", across))
        levels, level_specs = [], []
        for group, part in groups:
            for late in range(2):
                pieces = group[part, late]
                single = len(pieces) == 1
                levels.append(pieces[0 if single else c])
                skipped = c * (width // lanes) if single else 0
                level_specs.append(
                    pl.BlockSpec((levels[-1].shape[0], lanes), functools.partial(lambda n, s: (0, n + s), skipped))
                )
        own_part, part_0, part_1 = pl.pallas_call(
            interact_kernel,
            grid=(width // lanes,),
            in_specs=[
                pl.BlockSpec(lookup.shape, lambda s: (0, 0, 0)),
                pl.BlockSpec(spread.shape, lambda s: (0, 0)),
                pl.BlockSpec(rates.shape, lambda s: (0, 0)),
            ] + level_specs,
            out_specs=[pl.BlockSpec((n * comps, lanes), lambda s: (0, s)) for n in (2, 1, 1)],
            out_shape=[jax.ShapeDtypeStruct((n * comps, width), f32) for n in (2, 1, 1)],
            scratch_shapes=[pltpu.VMEM((12 * comps, lanes), jnp.bfloat16)],
            name="interact_cells",
            compiler_params=params(VMEM_MIB),
            cost_estimate=pl.CostEstimate(
                flops=2 * width * comps * comps * (6 * 12 + 48),
                bytes_accessed=20 * MIB, transcendentals=0,
            ),
        )(lookup, spread, rates, *levels)
        own_parts.append(own_part)
        parts_0.append(part_0)
        parts_1.append(part_1)

    def send_back(piece, *waits):
        return lax.ppermute(after(piece, *waits), "comp", pairs)

    back = [[None] * CELL_CHUNKS for _ in range(2)]
    back[0][0] = send_back(parts_0[0], got_1[2], sums_two)
    back[1][0] = send_back(parts_1[0], got_1[3])
    back[0][1] = send_back(parts_0[1], back[0][0], sums)
    back[0][2] = send_back(parts_0[2], back[1][0])
    back[0][3] = send_back(parts_0[3], back[0][1])
    for c in range(1, CELL_CHUNKS):
        back[1][c] = send_back(parts_1[c], back[0][2])

    def finish(part, so_far):
        piece = pl.BlockSpec((GROUP, width), lambda s, b, t: (s, 0))
        own_piece = pl.BlockSpec((GROUP, width), lambda s, b, t: (part * steps + s, 0))
        inputs = [place, mean_level, packed_fields, own_growth, own_damping]
        specs = [whole(place.shape), whole(mean_level.shape), whole(packed_fields.shape), column(part, 1),
                 column(part, 1)]
        inputs += [full[part]] + own_parts + back[part]
        specs.append(pl.BlockSpec((GROUP, cells), lambda s, b, t: (s, 0)))
        specs += [own_piece] * CELL_CHUNKS + [piece] * CELL_CHUNKS
        aliases = {}
        if so_far is not None:
            inputs.append(so_far)
            specs.append(pl.BlockSpec(memory_space=pl.ANY))
            aliases = {len(inputs) + 1: 0}
        return pl.pallas_call(
            functools.partial(finish_kernel, CELL_CHUNKS),
            grid_spec=pltpu.PrefetchScalarGridSpec(
                num_scalar_prefetch=2,
                grid=(steps,),
                in_specs=specs,
                out_specs=pl.BlockSpec((GROUP, row_count, col_count), lambda s, b, t: (group_at(part, b) + s, 0, 0)),
                scratch_shapes=[pltpu.VMEM((GROUP, cells), f32)],
            ),
            out_shape=jax.ShapeDtypeStruct(energy.shape, f32),
            input_output_aliases=aliases,
            name="finish_chunk",
            compiler_params=params(VMEM_MIB),
            cost_estimate=pl.CostEstimate(
                flops=20 * comps * row_count * col_count,
                bytes_accessed=100 * MIB, transcendentals=0,
            ),
        )(base, table, *inputs)

    return finish(1, finish(0, None))


def choose_shards(energy, *rest):
    local_comps, row_count, col_count = energy.shape
    fits = (
        local_comps == 4 * NTH and lax.axis_size("comp") == 8 and local_comps * 8 == NTH * NF
        and lax.axis_size("tile") == 2 and row_count == BLOCK and col_count == 2 * BLOCK
    )
    return packed_shards(energy, *rest) if fits else shards(energy, *rest)


def solution(mesh):
    placed = (
        P("comp", ("grp", "tile"), None),
        P("grp", None),
        P("grp", None),
        P("grp", None),
        P("grp", None),
        P("grp", None),
        P(),
        P(),
        P(),
        P(),
        P(),
    )
    return jax.shard_map(
        choose_shards,
        mesh=mesh,
        in_specs=placed,
        out_specs=P("comp", ("grp", "tile"), None),
        check_vma=False,
    )
```

```python
import functools
import math

import jax
import jax.numpy as jnp
import numpy as np
from jax import lax
from jax.experimental import pallas as pl
from jax.experimental.pallas import tpu as pltpu
from jax.sharding import PartitionSpec as P

NTH = 36
NF = 32


weight_plus = 0.4096
weight_minus = 3.1605
weight_cross = 1.2945


def with_halo(block, sides, width):
    for axis, dim in sides:
        count = lax.axis_size(axis)
        forward = [(i, i + 1) for i in range(count - 1)]
        backward = [(target, source) for source, target in forward]
        low = lax.ppermute(
            lax.slice_in_dim(block, block.shape[dim] - width, None, axis=dim), axis, forward
        )
        high = lax.ppermute(lax.slice_in_dim(block, 0, width, axis=dim), axis, backward)
        block = jnp.concatenate([low, block, high], axis=dim)
    return block


def quick_flux(far_left, left_cell, right_cell, far_right, courant):
    centre = 0.5 * (left_cell + right_cell) - 0.5 * courant * (right_cell - left_cell)
    curvature = (1.0 - courant * courant) / 6.0
    upward = centre - curvature * (right_cell - 2.0 * left_cell + far_left)
    downward = centre - curvature * (left_cell - 2.0 * right_cell + far_right)
    return courant * jnp.where(courant > 0.0, upward, downward)


def flux_change(padded, speed, current, sea_pad, axis):
    cell_count = padded.shape[axis] - 4

    def take_part(source, first, which_axis):
        return lax.slice_in_dim(source, first, first + cell_count + 1, axis=which_axis)

    face_current = 0.5 * (take_part(current, 0, axis - 1) + take_part(current, 1, axis - 1))
    courant = speed[:, None, None] + face_current[None]
    open_face = (take_part(sea_pad, 0, axis - 1) * take_part(sea_pad, 1, axis - 1))[None]
    face_flux = (
        quick_flux(
            take_part(padded, 0, axis),
            take_part(padded, 1, axis),
            take_part(padded, 2, axis),
            take_part(padded, 3, axis),
            courant,
        )
        * open_face
    )
    return lax.slice_in_dim(face_flux, 1, cell_count + 1, axis=axis) - lax.slice_in_dim(
        face_flux, 0, cell_count, axis=axis
    )


def source_terms(energy_block, wind, turning, growth, damping, coupling, lookup, spread):
    cell_count = energy_block.shape[1]
    spectrum = energy_block.reshape(NF, NTH, cell_count)
    turn_rate = turning[None, None, :]
    next_dir = jnp.roll(spectrum, -1, axis=1)
    forward = jnp.maximum(turn_rate, 0.0)
    backward = jnp.minimum(turn_rate, 0.0)
    upper_flux = forward * spectrum + backward * next_dir
    lower_flux = jnp.roll(upper_flux, 1, axis=1)
    turned = (spectrum - upper_flux + lower_flux).reshape(energy_block.shape)
    rounded = turned.astype(jnp.bfloat16)
    plus_first, minus_first, plus_second, minus_second = lookup(rounded)
    couple_rate = coupling[:, None]
    delta_first = couple_rate * (
        turned * turned * (weight_plus * plus_first + weight_minus * minus_first)
        - 2.0 * weight_cross * turned * plus_first * minus_first
    )
    delta_second = couple_rate * (
        turned * turned * (weight_plus * plus_second + weight_minus * minus_second)
        - 2.0 * weight_cross * turned * plus_second * minus_second
    )
    moved = spread(delta_first.astype(jnp.bfloat16), delta_second.astype(jnp.bfloat16))
    mean_level = jnp.sum(turned, axis=0) / energy_block.shape[0]
    return (
        turned
        + growth[:, None] * wind[None] * turned
        - damping[:, None] * mean_level[None] * turned
        - 2.0 * (delta_first + delta_second)
        + moved
    )


def shards(
    energy,
    sea_mask,
    current_u,
    current_v,
    wind_forcing,
    refraction,
    group_speed,
    growth,
    damping,
    coupling,
    dia_index,
):
    comp_count = lax.axis_size("comp")
    comp_pos = lax.axis_index("comp")
    tile_pos = lax.axis_index("tile")
    local_comps, row_count, col_count = energy.shape
    first_row = tile_pos * row_count
    first_comp = comp_pos * local_comps
    comp_total = NTH * NF
    angles = 2.0 * math.pi / NTH * (jnp.arange(comp_total) % NTH).astype(jnp.float32)
    speeds = jnp.repeat(group_speed, NTH)
    speed_east = lax.dynamic_slice_in_dim(speeds * jnp.cos(angles), first_comp, local_comps)
    speed_north = lax.dynamic_slice_in_dim(speeds * jnp.sin(angles), first_comp, local_comps)
    window = (row_count + 2, col_count + 2)
    sea_pad = lax.dynamic_slice(jnp.pad(sea_mask.astype(jnp.float32), 1), (first_row, 0), window)
    east_pad = lax.dynamic_slice(jnp.pad(current_u, 1), (first_row, 0), window)
    north_pad = lax.dynamic_slice(jnp.pad(current_v, 1), (first_row, 0), window)
    sea_tile = sea_pad[1:-1, 1:-1]
    masked = energy * sea_tile[None]
    padded_east = with_halo(masked, (("tile", 1),), 2)
    along_east = flux_change(padded_east, speed_east, east_pad[:, 1:-1], sea_pad[:, 1:-1], 1)
    along_north = flux_change(
        jnp.pad(masked, ((0, 0), (0, 0), (2, 2))),
        speed_north,
        north_pad[1:-1, :],
        sea_pad[1:-1, :],
        2,
    )
    propagated = (sea_tile[None] * (masked - along_east - along_north)).reshape(
        local_comps, row_count * col_count
    )
    tile_wind = lax.dynamic_slice(wind_forcing, (first_row, 0), (row_count, col_count)).reshape(-1)
    tile_turn = lax.dynamic_slice(refraction, (first_row, 0), (row_count, col_count)).reshape(-1)
    comp_ids = jnp.arange(comp_total)
    tables = [
        (dia_index[slot_row][:, None] == comp_ids[None, :]).astype(jnp.bfloat16)
        for slot_row in range(4)
    ]

    def lookup(rounded):
        return tuple(
            (
                jnp.dot(tables[slot_row], rounded, preferred_element_type=jnp.float32)
                for slot_row in range(4)
            )
        )

    def scatter_back(table, terms):
        return lax.dot_general(
            table, terms, (((0,), (0,)), ((), ())), preferred_element_type=jnp.float32
        )

    def spread(first_terms, second_terms):
        return (
            scatter_back(tables[0], first_terms)
            + scatter_back(tables[1], first_terms)
            + scatter_back(tables[2], second_terms)
            + scatter_back(tables[3], second_terms)
        )

    share_size = row_count * col_count // comp_count
    point_field = lax.all_to_all(propagated, "comp", split_axis=1, concat_axis=0, tiled=True)
    first_point = comp_pos * share_size
    own_wind = lax.dynamic_slice_in_dim(tile_wind, first_point, share_size)
    own_turn = lax.dynamic_slice_in_dim(tile_turn, first_point, share_size)
    result = source_terms(
        point_field, own_wind, own_turn, growth, damping, coupling, lookup, spread
    )
    returned_field = lax.all_to_all(result, "comp", split_axis=0, concat_axis=1, tiled=True)
    return returned_field.reshape(local_comps, row_count, col_count)


BLOCK = 128
GROUP = 24
EARLY = 40
BATCH = 4
CELL_CHUNKS = 4
MIB = 1024 * 1024
VMEM_MIB = 60
EDGE = 2
SEA, OPEN_EAST, FLOW_EAST, OPEN_NORTH, FLOW_NORTH, HALF_SEA, WIND, TURN = range(8)
KEEP, SPILL, IS_SEA = BLOCK, 2 * BLOCK, 2 * BLOCK


def upwind(courant, total, slope, bend_here, bend_ahead):
    bend = jnp.where(courant > 0.0, bend_here, bend_ahead)
    return courant * ((total - bend) - courant * (slope - courant * bend))


def pick_lanes(block, index):
    return jnp.take_along_axis(block, index, axis=1, mode="promise_in_bounds")


def tile_at(tile):
    return pl.ds(pl.multiple_of(tile * BLOCK, BLOCK), BLOCK)


def has(code, flag):
    return jnp.bitwise_and(code, flag) != 0


def pack_block(blocks, code, tile, out_ref, firsts, held):
    code = jnp.broadcast_to(code, (8, BLOCK))
    index = jnp.bitwise_and(code, BLOCK - 1)
    keep, spill = has(code, KEEP), has(code, SPILL)
    result = []
    for block, first, old in zip(blocks, firsts, held):
        moved = pick_lanes(block, index)
        merged = jnp.where(keep, moved, old)
        out_ref[pl.ds(first, 8), tile_at(tile)] = merged
        result.append(jnp.where(spill, moved, merged))
    return tuple(result)


def prepare_kernel(places, base_ref, speed_ref, sea_ref, east_ref, north_ref, wind_ref, turn_ref, cos_ref, sin_ref,
                   coef_ref, index_ref, place_ref, table_ref, speed_east_ref, speed_north_ref, field_ref, pick_ref):
    first_row, odd, first_freq = base_ref[0], base_ref[1], base_ref[2]
    all_rows, col_count = sea_ref.shape
    row_count = place_ref.shape[1]
    tiles = places // BLOCK
    sea = sea_ref[...].astype(jnp.float32)
    row = lax.broadcasted_iota(jnp.int32, sea.shape, 0)
    col = lax.broadcasted_iota(jnp.int32, sea.shape, 1)

    def next_row(field):
        return jnp.where(row == all_rows - 1, 0.0, pltpu.roll(field, all_rows - 1, 0))

    def next_col(field):
        return jnp.where(col == col_count - 1, 0.0, pltpu.roll(field, col_count - 1, 1))

    open_east, open_north = sea * next_row(sea), sea * next_col(sea)
    east, north = east_ref[...], north_ref[...]
    field_ref[SEA] = sea
    field_ref[OPEN_EAST] = open_east
    field_ref[FLOW_EAST] = open_east * (0.5 * (east + next_row(east)))
    field_ref[OPEN_NORTH] = open_north
    field_ref[FLOW_NORTH] = open_north * (0.5 * (north + next_col(north)))
    field_ref[HALF_SEA] = 0.5 * sea
    field_ref[WIND] = wind_ref[...]
    field_ref[TURN] = turn_ref[...]
    coef_ref[0:EDGE] = jnp.zeros((EDGE, 8, col_count), jnp.float32)
    coef_ref[EDGE + all_rows :] = jnp.zeros((EDGE, 8, col_count), jnp.float32)

    @pl.loop(0, all_rows // 8)
    def _(i):
        rows = field_ref[:, pl.ds(pl.multiple_of(8 * i, 8), 8), :]
        coef_ref[pl.ds(8 * i + EDGE, 8)] = jnp.swapaxes(rows, 0, 1)

    freqs = cos_ref.shape[0] // NTH
    for f in range(freqs):
        circle = slice(f * NTH, (f + 1) * NTH)
        speed_east_ref[circle, :] = cos_ref[circle, :] * speed_ref[first_freq + f]
        speed_north_ref[circle, :] = sin_ref[circle, :] * speed_ref[first_freq + f]

    bf16, f32 = jnp.bfloat16, jnp.float32
    tile_sea = sea_ref[pl.ds(pl.multiple_of(first_row, 8), row_count), :].astype(f32)
    square = (BLOCK, BLOCK)
    down, over = lax.broadcasted_iota(jnp.int32, square, 0), lax.broadcasted_iota(jnp.int32, square, 1)
    before = (down < over).astype(f32).astype(bf16)
    ones = jnp.ones(square, bf16)
    row_square = (row_count, row_count)
    above = lax.broadcasted_iota(jnp.int32, row_square, 1) < lax.broadcasted_iota(jnp.int32, row_square, 0)
    above = above.astype(f32).astype(bf16)
    parts = [tile_sea[:, :BLOCK], tile_sea[:, BLOCK:]]
    numbers = [jnp.dot(p.astype(bf16), ones, preferred_element_type=f32) for p in parts]
    in_row = numbers[0] + numbers[1]
    starts = [jnp.dot(above, in_row.astype(bf16), preferred_element_type=f32)]
    starts.append(starts[0] + numbers[0])
    total = jnp.sum(in_row, axis=0, keepdims=True).astype(jnp.int32)

    def turned_tile(tile):
        return jnp.where(tile >= tiles, tiles, jnp.bitwise_and(tile + odd * (tiles // 2), tiles - 1))

    columns = []
    for h in range(2):
        rank = jnp.dot(parts[h].astype(bf16), before, preferred_element_type=f32).astype(jnp.int32)
        start = starts[h].astype(jnp.int32)
        offset = jnp.bitwise_and(start, BLOCK - 1)
        keep = jnp.where(over[:row_count] >= offset, KEEP, 0)
        slot = jnp.bitwise_and(rank + offset, BLOCK - 1)
        is_sea = parts[h] > 0.0
        place_ref[h] = slot + keep + jnp.where(is_sea, IS_SEA, 0)
        slot = jnp.where(is_sea, slot, -1).astype(f32).T
        from_lane = down[:, :row_count].astype(f32)

        @pl.loop(0, BLOCK // 8)
        def _(i):
            found = []
            for k in range(8):
                lane = (8 * i + k).astype(f32)
                found.append(jnp.sum(jnp.where(slot == lane, from_lane, 0.0), axis=0, keepdims=True))
            pick_ref[pl.ds(pl.multiple_of(8 * i, 8), 8), :] = jnp.concatenate(found, axis=0)

        spill = jnp.where(offset + numbers[h].astype(jnp.int32) >= BLOCK, SPILL, 0)
        index_ref[h] = pick_ref[...].T.astype(jnp.int32) + keep + spill
        columns.append(turned_tile(lax.shift_right_logical(starts[h].T[0:8, :].astype(jnp.int32), 7)))
    row_id = lax.broadcasted_iota(jnp.int32, (8, row_count), 0)
    end_tile = jnp.where(
        jnp.bitwise_and(total, BLOCK - 1) == 0, tiles, turned_tile(lax.shift_right_logical(total, 7))
    )
    end_tile = jnp.broadcast_to(end_tile, (8, BLOCK))
    table_ref[...] = jnp.concatenate([jnp.where(row_id == 0, columns[0], columns[1]), end_tile], axis=1)


def propagate_kernel(part, late, pieces, base_ref, table_ref, energy_ref, halo_ref, coef_ref, index_ref, east_ref,
                     north_ref, *refs):
    refs = list(refs)
    with_fields = part == 0 and not late
    fields_ref = None if with_fields else refs.pop(0)
    seam_ref = refs.pop(0) if late else None
    if late:
        refs.pop(0)
    piece_refs = [refs.pop(0) for _ in range(2 * pieces)]
    sum_ref, full_ref = refs.pop(0), refs.pop(0)
    seam_out_ref = None if late else refs.pop(0)
    fields_out_ref = refs.pop(0) if with_fields else None
    energy_vmem, rows_ref, spread_ref, wide_ref, result_ref, strip_sems, out_sems = refs
    row_count, comp_count, col_count = rows_ref.shape
    strips = comp_count // 8
    sent_rows = piece_refs[0].shape[0]
    cells = result_ref.shape[1]
    first_row = base_ref[0]
    first_comp = pl.multiple_of((part + base_ref[1] * (1 - 2 * part)) * 2 * NTH + late * EARLY, 8)
    lane = lax.broadcasted_iota(jnp.int32, (8, BLOCK), 1)
    first_lane, last_lane = lane == 0, lane == BLOCK - 1
    third = 1.0 / 3.0

    def arrival(g):
        target = energy_vmem.at[pl.ds(pl.multiple_of(8 * g, 8), 8)]
        source = energy_ref.at[pl.ds(pl.multiple_of(first_comp + 8 * g, 8), 8)]
        return pltpu.make_async_copy(source, target, strip_sems.at[g])

    for g in range(strips):
        arrival(g).start()

    def halves(row):
        return row[:, :BLOCK], row[:, BLOCK:]

    @pl.loop(0, row_count + 2 * EDGE, unroll=4)
    def _(r):
        coef = coef_ref[first_row + r]
        for k in range(HALF_SEA + 1):
            spread_ref[r, k] = jnp.broadcast_to(coef[k : k + 1, :], coef.shape)

    def masked(row, at):
        return tuple(part * sea for part, sea in zip(halves(row), halves(spread_ref[at, SEA])))

    def cell_rows(first, fresh, state, east, north):
        here, ahead, slope_here, bend_here, flux_low = state
        count, sides = len(fresh), range(2)
        level = [here, ahead] + [masked(row, first + k + EDGE) for k, row in enumerate(fresh)]
        rows = range(count)
        coef = [[None] + [halves(spread_ref[first + k, f]) for f in range(1, HALF_SEA + 1)] for k in rows]
        one_right = [[pltpu.roll(part, BLOCK - 1, 1) for part in level[k]] for k in rows]
        right = [
            (jnp.where(last_lane, one[1], one[0]), jnp.where(last_lane, 0.0, one[1])) for one in one_right
        ]
        slope = [[right[k][h] - level[k][h] for h in sides] for k in rows]
        slope_roll = [[pltpu.roll(part, 1, 1) for part in slope[k]] for k in rows]
        bend = [
            (third * (slope[k][0] - jnp.where(first_lane, level[k][0], slope_roll[k][0])),
             third * (slope[k][1] - jnp.where(first_lane, slope_roll[k][0], slope_roll[k][1])))
            for k in rows
        ]
        bend_roll = [[pltpu.roll(part, BLOCK - 1, 1) for part in bend[k]] for k in rows]
        cross = []
        for k in rows:
            bend_right = (jnp.where(last_lane, bend_roll[k][1], bend_roll[k][0]), bend_roll[k][1])
            cross.append([
                upwind(north * coef[k][OPEN_NORTH][h] + coef[k][FLOW_NORTH][h], level[k][h] + right[k][h],
                       slope[k][h], bend[k][h], bend_right[h])
                for h in sides
            ])
        cross_roll = [[pltpu.roll(part, 1, 1) for part in cross[k]] for k in rows]
        slopes = [slope_here] + [tuple(level[k + 1][h] - level[k][h] for h in sides) for k in range(1, count + 1)]
        bends = [bend_here] + [
            tuple(third * (slopes[k][h] - slopes[k - 1][h]) for h in sides) for k in range(1, count + 1)
        ]
        flux = [flux_low]
        for k in rows:
            flux.append(tuple(
                upwind(east * coef[k][OPEN_EAST][h] + coef[k][FLOW_EAST][h], level[k][h] + level[k + 1][h],
                       slopes[k][h], bends[k][h], bends[k + 1][h])
                for h in sides
            ))
        done = []
        for k in rows:
            cross_low = (jnp.where(first_lane, cross_roll[k][1], cross_roll[k][0]),
                         jnp.where(first_lane, cross_roll[k][0], cross_roll[k][1]))
            done.append([
                coef[k][HALF_SEA][h] * (((level[k][h] + level[k][h]) + (flux[k][h] + cross_low[h]))
                                        - (flux[k + 1][h] + cross[k][h]))
                for h in sides
            ])
        return (level[count], level[count + 1], slopes[count], bends[count], flux[count]), done

    def store_row(row, local, parts):
        for h in range(2):
            rows_ref[row, local, h * BLOCK : (h + 1) * BLOCK] = parts[h]

    @pl.loop(0, strips)
    def _(g):
        arrival(g).wait()
        local = pl.ds(pl.multiple_of(g * 8, 8), 8)
        comps = pl.ds(pl.multiple_of(first_comp + g * 8, 8), 8)
        east, north = east_ref[comps, :], north_ref[comps, :]
        zero = (jnp.zeros((8, BLOCK), jnp.float32),) * 2
        here, ahead = masked(halo_ref[comps, 0, :], 0), masked(halo_ref[comps, 1, :], 1)
        state = (here, ahead, tuple(b - a for a, b in zip(here, ahead)), zero, zero)

        def eight(i, state):
            block = jnp.swapaxes(energy_vmem[local, pl.ds(pl.multiple_of(8 * i, 8), 8), :], 0, 1)
            for first in range(0, 8, BATCH):
                fresh = [block[first + k] for k in range(BATCH)]
                state, done = cell_rows(8 * i + first, fresh, state, east, north)
                for k in range(BATCH):
                    store_row(jnp.maximum(8 * i + first + k - EDGE, 0), local, done[k])
            return state

        state = lax.fori_loop(0, row_count // 8, eight, state)
        fresh = [halo_ref[comps, k, :] for k in range(EDGE)]
        state, done = cell_rows(row_count, fresh, state, east, north)
        for k in range(EDGE):
            store_row(row_count - EDGE + k, local, done[k])

    group_rows = [8 * n for n in range(strips + with_fields)]

    def pack_eight(i, held):
        codes = [index_ref[h, pl.ds(pl.multiple_of(8 * i, 8), 8), :] for h in range(2)]
        for k in range(8):
            row = 8 * i + k
            for h in range(2):
                lanes = slice(h * BLOCK, (h + 1) * BLOCK)
                blocks = [rows_ref[row, 8 * n : 8 * n + 8, lanes] for n in range(strips)]
                if with_fields:
                    blocks.append(coef_ref[first_row + EDGE + row, :, lanes])
                held = pack_block(blocks, codes[h][k : k + 1, :], table_ref[h, row], wide_ref, group_rows, held)
        return held

    empty = (jnp.zeros((8, BLOCK), jnp.float32),) * len(group_rows)
    held = lax.fori_loop(0, row_count // 8, pack_eight, empty)
    for first, block in zip(group_rows, held):
        wide_ref[pl.ds(first, 8), tile_at(table_ref[0, row_count])] = block
    if with_fields:
        fields_out_ref[...] = wide_ref[comp_count:, :cells]

    tile_width = 2 * BLOCK
    height = result_ref.shape[0]
    comp_row = lax.broadcasted_iota(jnp.int32, (height, tile_width), 0)
    start = height - NTH if late else 0
    end = start + NTH - 1
    mixed = slice(0, 8) if late else slice(height - 8, height)
    mixed_row = comp_row[mixed]
    in_circle = (mixed_row >= start) & (mixed_row <= end)

    @pl.loop(0, cells // tile_width, unroll=2)
    def _(i):
        source = pl.ds(pl.multiple_of(i * tile_width, tile_width), tile_width)
        level = wide_ref[:comp_count, source]
        if late:
            level = jnp.concatenate([seam_ref[:, source], level], axis=0)
        if with_fields:
            rate = wide_ref[comp_count + TURN : comp_count + TURN + 1, source]
        else:
            rate = fields_ref[TURN : TURN + 1, source]
        forward = jnp.maximum(rate, 0.0)
        backward = jnp.minimum(rate, 0.0)
        stay = (1.0 - forward) + backward
        above = pltpu.roll(level, height - 1, 0)
        below = pltpu.roll(level, 1, 0)

        def with_row(rolled, row, value):
            tile = slice(row - row % 8, row - row % 8 + 8)
            fixed = jnp.where(comp_row[tile] == row, value, rolled[tile])
            parts = [rolled[: tile.start], fixed, rolled[tile.stop :]]
            return jnp.concatenate([part for part in parts if part.shape[0]], axis=0)

        above = with_row(above, end, level[start : start + 1, :])
        below = with_row(below, start, level[end : end + 1, :])
        turned = stay * level - backward * above + forward * below
        partial = jnp.where(in_circle, turned[mixed], 0.0)
        for first in range(0, height, 8):
            rows = slice(first, first + 8)
            if first == mixed.start:
                result_ref[rows, source] = jnp.where(in_circle, turned[rows], level[rows])
            else:
                result_ref[rows, source] = turned[rows]
                partial += turned[rows]
        sum_ref[:, source] = jnp.sum(partial, axis=0, keepdims=True)

    if not late:
        seam_out_ref[...] = result_ref[sent_rows:, :]
    width = cells // (2 * pieces)
    copies = []
    for n, piece in enumerate(piece_refs):
        source = result_ref.at[:sent_rows, n * width : (n + 1) * width]
        copies.append(pltpu.make_async_copy(source, piece, out_sems.at[n]))
    rows = pl.ds(EARLY - 8 if late else 0, sent_rows)
    copies.append(pltpu.make_async_copy(result_ref.at[:sent_rows, :], full_ref.at[rows, :], out_sems.at[2 * pieces]))
    for copy in copies:
        copy.start()
    for copy in copies:
        copy.wait()


def interact_kernel(table_ref, spread_ref, coupling_ref, *refs):
    own_ref, back_0_ref, back_1_ref, delta_ref = refs[16:]
    window = [jnp.concatenate([refs[2 * j][...], refs[2 * j + 1][...]], axis=0) for j in range(8)]
    comps = window[0].shape[0]
    for j in range(1, 7):
        level = window[j]
        around = jnp.concatenate([window[j - 1], level, window[j + 1]], axis=0).astype(jnp.bfloat16)
        partner = jnp.dot(table_ref[j - 1], around, preferred_element_type=jnp.float32)
        rate = coupling_ref[(j - 1) * comps : j * comps, :] * level
        plus_part = weight_plus * level
        minus_part = weight_minus * level
        deltas = []
        for pair in range(2):
            plus = partner[2 * pair * comps : (2 * pair + 1) * comps, :]
            minus = partner[(2 * pair + 1) * comps : (2 * pair + 2) * comps, :]
            deltas.append(rate * (plus * (plus_part - (2.0 * weight_cross) * minus) + minus_part * minus))
        both = jnp.concatenate(deltas, axis=0).astype(jnp.bfloat16)
        delta_ref[(j - 1) * 2 * comps : j * 2 * comps, :] = both
        if 2 <= j <= 5:
            part = -2.0 * (deltas[0] + deltas[1])
            if j <= 3:
                own_ref[(j - 2) * comps : (j - 1) * comps, :] = part
            elif j == 4:
                back_1_ref[...] = part
            else:
                back_0_ref[...] = part
    spread = jnp.dot(spread_ref[...], delta_ref[...], preferred_element_type=jnp.float32)
    own_ref[...] += spread[: 2 * comps, :]
    back_1_ref[...] += spread[2 * comps : 3 * comps, :]
    back_0_ref[...] += spread[3 * comps :, :]


def finish_kernel(chunks, base_ref, table_ref, place_ref, mean_ref, fields_ref, growth_ref, damping_ref, *refs):
    turned_ref, own, back = refs[0], refs[1 : 1 + chunks], refs[1 + chunks : 1 + 2 * chunks]
    out_ref, wide_ref = refs[-2], refs[-1]
    width = own[0].shape[1]
    tiles = wide_ref.shape[1] // BLOCK
    tile_width = 2 * BLOCK
    growth = jnp.broadcast_to(growth_ref[...], (GROUP, tile_width))
    damping = jnp.broadcast_to(damping_ref[...], (GROUP, tile_width))
    for o in range(2 * chunks):
        extra = own[o] if o < chunks else back[o - chunks]

        @pl.loop(0, width // tile_width, unroll=2)
        def _(i):
            source = pl.ds(pl.multiple_of(i * tile_width, tile_width), tile_width)
            target = pl.ds(pl.multiple_of(o * width + i * tile_width, tile_width), tile_width)
            scale = 1.0 + growth * fields_ref[WIND : WIND + 1, target] - damping * mean_ref[0:1, target]
            wide_ref[:, target] = turned_ref[:, target] * scale + extra[:, source]

    @pl.loop(0, out_ref.shape[1] // 8)
    def _(i):
        codes = [place_ref[h, pl.ds(pl.multiple_of(8 * i, 8), 8), :] for h in range(2)]
        done = [[] for _ in range(GROUP // 8)]
        for r in range(8):
            parts = [[] for _ in range(GROUP // 8)]
            for h in range(2):
                code = jnp.broadcast_to(codes[h][r : r + 1, :], (8, BLOCK))
                index = jnp.bitwise_and(code, BLOCK - 1)
                keep, is_sea = has(code, KEEP), has(code, IS_SEA)
                tile = table_ref[h, 8 * i + r]
                first, second = jnp.minimum(tile, tiles - 1), jnp.bitwise_and(tile + 1, tiles - 1)
                for k in range(GROUP // 8):
                    rows = slice(8 * k, 8 * k + 8)
                    near = jnp.where(keep, wide_ref[rows, tile_at(first)], wide_ref[rows, tile_at(second)])
                    parts[k].append(jnp.where(is_sea, pick_lanes(near, index), 0.0))
            for k in range(GROUP // 8):
                done[k].append(jnp.concatenate(parts[k], axis=1))
        for k in range(GROUP // 8):
            out_ref[8 * k : 8 * k + 8, pl.ds(pl.multiple_of(8 * i, 8), 8), :] = jnp.swapaxes(jnp.stack(done[k]), 0, 1)


def params(limit):
    return pltpu.CompilerParams(vmem_limit_bytes=limit * MIB)


def after(value, *others):
    return lax.optimization_barrier((value,) + others)[0]


def packed_shards(energy, sea_mask, current_u, current_v, wind_forcing, refraction, group_speed, growth, damping,
                  coupling, dia_index):
    comp_count = lax.axis_size("comp")
    comp_pos = lax.axis_index("comp")
    tile_pos = lax.axis_index("tile")
    odd = lax.rem(comp_pos, 2)
    pair_pos = comp_pos // 2
    local_comps, row_count, col_count = energy.shape
    comps = local_comps // 2
    comp_total = NTH * NF
    first_row = tile_pos * row_count
    first_comp = comp_pos * local_comps
    cells = row_count * col_count // 2
    half = cells // 2
    width = half // CELL_CHUNKS
    f32, i32 = jnp.float32, jnp.int32
    base = jnp.stack([first_row, odd, comp_pos * (local_comps // NTH)]).astype(i32)

    edge_first = jnp.where(tile_pos == 0, row_count - EDGE, 0)
    edge_rows = lax.dynamic_slice_in_dim(energy, edge_first, EDGE, axis=1)
    halo_rows = lax.ppermute(edge_rows, "tile", [(0, 1), (1, 0)])

    all_rows = sea_mask.shape[0]
    angles = np.float32(2.0 * math.pi / NTH) * (np.arange(local_comps) % NTH).astype(np.float32)
    cosines = np.broadcast_to(np.cos(angles)[:, None], (local_comps, BLOCK)).astype(np.float32)
    sines = np.broadcast_to(np.sin(angles)[:, None], (local_comps, BLOCK)).astype(np.float32)
    vmem = pl.BlockSpec(memory_space=pltpu.VMEM)
    coef, index, place, table, speed_east, speed_north = pl.pallas_call(
        functools.partial(prepare_kernel, cells),
        grid_spec=pltpu.PrefetchScalarGridSpec(
            num_scalar_prefetch=2,
            grid=(),
            in_specs=[vmem] * 7,
            out_specs=[vmem] * 6,
            scratch_shapes=[pltpu.VMEM((8, all_rows, col_count), f32), pltpu.VMEM((BLOCK, row_count), f32)],
        ),
        out_shape=[
            jax.ShapeDtypeStruct((all_rows + 2 * EDGE, 8, col_count), f32),
            jax.ShapeDtypeStruct((2, row_count, BLOCK), i32),
            jax.ShapeDtypeStruct((2, row_count, BLOCK), i32),
            jax.ShapeDtypeStruct((8, 2 * BLOCK), i32),
            jax.ShapeDtypeStruct((local_comps, BLOCK), f32),
            jax.ShapeDtypeStruct((local_comps, BLOCK), f32),
        ],
        name="prepare",
        compiler_params=params(VMEM_MIB),
    )(base, group_speed, sea_mask, current_u, current_v, wind_forcing, refraction, cosines, sines)
    steps = comps // GROUP

    def group_at(part, base_ref):
        return (part + base_ref[1] * (1 - 2 * part)) * steps

    def whole(shape):
        return pl.BlockSpec(shape, lambda s, b, t: (0,) * len(shape))

    def column(part, lanes):
        return pl.BlockSpec((GROUP, lanes), lambda s, b, t: (group_at(part, b) + s, 0))

    def propagate(part, late, table, fields=None, seam=None, full=None):
        pieces = CELL_CHUNKS if part and late else 1
        comp_rows = comps - EARLY if late else EARLY
        sent_rows = comps - EARLY + 8 if late else EARLY - 8
        height = EARLY
        anywhere = pl.BlockSpec(memory_space=pl.ANY)
        with_fields = fields is None
        inputs = [energy, halo_rows, coef, index, speed_east, speed_north]
        in_specs = [anywhere] + [vmem] * 5
        aliases = {}
        if not with_fields:
            inputs.append(fields)
            in_specs.append(vmem)
        if late:
            inputs += [seam, full]
            in_specs += [vmem, anywhere]
            aliases = {len(inputs) + 1: 2 * pieces + 1}
        shapes = [(sent_rows, half // pieces)] * (2 * pieces) + [(1, cells), (comps, cells)]
        out_specs = [anywhere] * (2 * pieces) + [vmem, anywhere]
        if not late:
            shapes.append((8, cells))
            out_specs.append(vmem)
        if with_fields:
            shapes.append((8, cells))
            out_specs.append(vmem)
        outs = pl.pallas_call(
            functools.partial(propagate_kernel, part, late, pieces),
            grid_spec=pltpu.PrefetchScalarGridSpec(
                num_scalar_prefetch=2,
                grid=(),
                in_specs=in_specs,
                out_specs=out_specs,
                scratch_shapes=[
                    pltpu.VMEM((comp_rows, row_count, col_count), f32),
                    pltpu.VMEM((row_count, comp_rows, col_count), f32),
                    pltpu.VMEM((row_count + 2 * EDGE, HALF_SEA + 1, 8, col_count), f32),
                    pltpu.VMEM((comp_rows + (8 if with_fields else 0), cells + BLOCK), f32),
                    pltpu.VMEM((height, cells), f32),
                    pltpu.SemaphoreType.DMA((comp_rows // 8,)),
                    pltpu.SemaphoreType.DMA((2 * pieces + 1,)),
                ],
            ),
            out_shape=[jax.ShapeDtypeStruct(shape, f32) for shape in shapes],
            input_output_aliases=aliases,
            name="propagate_late" if late else "propagate_early",
            compiler_params=params(VMEM_MIB),
            cost_estimate=pl.CostEstimate(
                flops=60 * comp_rows * row_count * col_count, bytes_accessed=60 * MIB, transcendentals=0,
            ),
        )(base, table, *inputs)
        return list(outs[:pieces]), list(outs[pieces : 2 * pieces]), outs[2 * pieces :]

    pairs = [(i, i ^ 1) for i in range(comp_count)]
    apart = [(i, i - 2 if i % 2 == 0 else i + 2) for i in range(comp_count)]
    apart = [(a, b) for a, b in apart if 0 <= b < comp_count]
    across = [(b, a) for a, b in apart]
    chunk_range = range(CELL_CHUNKS)

    def send(pieces, route, waits):
        return [lax.ppermute(after(piece, *wait), "comp", route) for piece, wait in zip(pieces, waits)]

    stages = [(0, 0), (0, 1), (1, 0), (1, 1)]
    kept, sent, got, from_own, from_got, level_sums, full = {}, {}, {}, {}, {}, [], {}
    fields = seam = before = None
    part_table = table
    for stage in stages:
        part, late = stage
        kept[stage], sent[stage], extra = propagate(part, late, part_table, fields, seam, full.get(part))
        level_sums.append(extra[0])
        full[part] = extra[1]
        seam = None if late else extra[2]
        fields = extra[3] if fields is None else fields
        if stage == stages[-1]:
            break
        got[stage] = send(sent[stage], pairs, [[]])
        from_own[stage] = send(kept[stage], apart, [[]])
        waits = [from_got[before][0]] if stage == stages[2] else []
        from_got[stage] = send(got[stage], across, [waits])
        done = [extra[0]]
        if before is not None:
            done.append(got[before][0])
            if stage == stages[2]:
                done += [from_got[stages[0]][0], from_own[stages[1]][0]]
        part_table = after(table, *done)
        before = stage
    packed_fields = fields
    sums_0 = level_sums[0]

    sums = level_sums[0] + level_sums[1] + level_sums[2] + level_sums[3]
    partner_sums = lax.ppermute(sums, "comp", pairs)
    partner_sums = jnp.roll(partner_sums, half, axis=1)
    last, got_1, from_own_1 = stages[-1], [], []
    for c in chunk_range:
        waits = [got[before][0]] + ([got_1[c - 2]] if c >= 2 else []) + ([partner_sums] if c == 2 else [])
        got_1.append(lax.ppermute(after(sent[last][c], *waits), "comp", pairs))
        from_own_1.append(lax.ppermute(after(kept[last][c], from_own[before][0]), "comp", apart))
    got[last], from_own[last], from_got[last] = got_1, from_own_1, []
    sums = sums + partner_sums
    sums = sums_two = sums + lax.ppermute(sums, "comp", [(i, i ^ 2) for i in range(comp_count)])
    sums = sums + lax.ppermute(sums, "comp", [(i, i ^ 4) for i in range(comp_count)])
    mean_level = sums / comp_total

    dia_index, coupling, growth, damping, late_odd, late_pair, _ = lax.optimization_barrier(
        (dia_index, coupling, growth, damping, odd, pair_pos, sums_0)
    )
    own_growth = lax.dynamic_slice_in_dim(growth, first_comp, local_comps)[:, None]
    own_damping = lax.dynamic_slice_in_dim(damping, first_comp, local_comps)[:, None]
    chunk_first = [
        NTH * jnp.where(late_odd > 0, 8 * late_pair + 10 - 2 * j, 8 * late_pair - 4 + 2 * j) for j in range(8)
    ]
    margin = 8 * NTH
    dia_pad = jnp.pad(dia_index, ((0, 0), (margin, margin)), constant_values=-1)
    coupling_pad = jnp.pad(coupling, (margin, margin))
    own_ids = jnp.arange(comps)
    targets, rates = [], []
    for j in range(1, 7):
        targets.append(lax.dynamic_slice(dia_pad, (0, chunk_first[j] + margin), (4, comps)))
        rates.append(lax.dynamic_slice_in_dim(coupling_pad, chunk_first[j] + margin, comps))
    lookup = []
    for j in range(1, 7):
        ids = jnp.concatenate([chunk_first[j + d] + own_ids for d in (-1, 0, 1)])
        lookup.append((targets[j - 1].reshape(4 * comps)[:, None] == ids[None, :]).astype(jnp.bfloat16))
    lookup = jnp.stack(lookup)
    out_ids = jnp.concatenate([chunk_first[j] + own_ids for j in range(2, 6)])
    spread = []
    for j in range(1, 7):
        for pair in range(2):
            hits = [
                (out_ids[:, None] == targets[j - 1][2 * pair + q][None, :]).astype(f32) for q in range(2)
            ]
            spread.append(hits[0] + hits[1])
    spread = jnp.concatenate(spread, axis=1).astype(jnp.bfloat16)
    rates = jnp.concatenate(rates)[:, None]

    lanes = 512 if width % 512 == 0 else width
    own_parts, parts_0, parts_1 = [], [], []
    groups = [(from_got, 1), (from_got, 0), (kept, 0), (kept, 1), (got, 1), (got, 0), (from_own, 0), (from_own, 1)]
    for c in chunk_range:
        waits = [from_got[before][0]] + ([from_got[last][c - 2]] if c >= 2 else [])
        from_got[last].append(lax.ppermute(after(got_1[c], *waits), "comp", across))
        levels, level_specs = [], []
        for group, part in groups:
            for late in range(2):
                pieces = group[part, late]
                single = len(pieces) == 1
                levels.append(pieces[0 if single else c])
                skipped = c * (width // lanes) if single else 0
                level_specs.append(
                    pl.BlockSpec((levels[-1].shape[0], lanes), functools.partial(lambda n, s: (0, n + s), skipped))
                )
        own_part, part_0, part_1 = pl.pallas_call(
            interact_kernel,
            grid=(width // lanes,),
            in_specs=[
                pl.BlockSpec(lookup.shape, lambda s: (0, 0, 0)),
                pl.BlockSpec(spread.shape, lambda s: (0, 0)),
                pl.BlockSpec(rates.shape, lambda s: (0, 0)),
            ] + level_specs,
            out_specs=[pl.BlockSpec((n * comps, lanes), lambda s: (0, s)) for n in (2, 1, 1)],
            out_shape=[jax.ShapeDtypeStruct((n * comps, width), f32) for n in (2, 1, 1)],
            scratch_shapes=[pltpu.VMEM((12 * comps, lanes), jnp.bfloat16)],
            name="interact_cells",
            compiler_params=params(VMEM_MIB),
            cost_estimate=pl.CostEstimate(
                flops=2 * width * comps * comps * (6 * 12 + 48),
                bytes_accessed=20 * MIB, transcendentals=0,
            ),
        )(lookup, spread, rates, *levels)
        own_parts.append(own_part)
        parts_0.append(part_0)
        parts_1.append(part_1)

    def send_back(piece, *waits):
        return lax.ppermute(after(piece, *waits), "comp", pairs)

    back = [[None] * CELL_CHUNKS for _ in range(2)]
    back[0][0] = send_back(parts_0[0], got_1[2], sums_two)
    back[1][0] = send_back(parts_1[0], got_1[3])
    back[0][1] = send_back(parts_0[1], back[0][0], sums)
    back[0][2] = send_back(parts_0[2], back[1][0])
    back[0][3] = send_back(parts_0[3], back[0][1])
    for c in range(1, CELL_CHUNKS):
        back[1][c] = send_back(parts_1[c], back[0][2])

    def finish(part, so_far):
        piece = pl.BlockSpec((GROUP, width), lambda s, b, t: (s, 0))
        own_piece = pl.BlockSpec((GROUP, width), lambda s, b, t: (part * steps + s, 0))
        inputs = [place, mean_level, packed_fields, own_growth, own_damping]
        specs = [whole(place.shape), whole(mean_level.shape), whole(packed_fields.shape), column(part, 1),
                 column(part, 1)]
        inputs += [full[part]] + own_parts + back[part]
        specs.append(pl.BlockSpec((GROUP, cells), lambda s, b, t: (s, 0)))
        specs += [own_piece] * CELL_CHUNKS + [piece] * CELL_CHUNKS
        aliases = {}
        if so_far is not None:
            inputs.append(so_far)
            specs.append(pl.BlockSpec(memory_space=pl.ANY))
            aliases = {len(inputs) + 1: 0}
        return pl.pallas_call(
            functools.partial(finish_kernel, CELL_CHUNKS),
            grid_spec=pltpu.PrefetchScalarGridSpec(
                num_scalar_prefetch=2,
                grid=(steps,),
                in_specs=specs,
                out_specs=pl.BlockSpec((GROUP, row_count, col_count), lambda s, b, t: (group_at(part, b) + s, 0, 0)),
                scratch_shapes=[pltpu.VMEM((GROUP, cells), f32)],
            ),
            out_shape=jax.ShapeDtypeStruct(energy.shape, f32),
            input_output_aliases=aliases,
            name="finish_chunk",
            compiler_params=params(VMEM_MIB),
            cost_estimate=pl.CostEstimate(
                flops=20 * comps * row_count * col_count,
                bytes_accessed=100 * MIB, transcendentals=0,
            ),
        )(base, table, *inputs)

    return finish(1, finish(0, None))


def choose_shards(energy, *rest):
    local_comps, row_count, col_count = energy.shape
    fits = (
        local_comps == 4 * NTH and lax.axis_size("comp") == 8 and local_comps * 8 == NTH * NF
        and lax.axis_size("tile") == 2 and row_count == BLOCK and col_count == 2 * BLOCK
    )
    return packed_shards(energy, *rest) if fits else shards(energy, *rest)


def solution(mesh):
    placed = (
        P("comp", ("grp", "tile"), None),
        P("grp", None),
        P("grp", None),
        P("grp", None),
        P("grp", None),
        P("grp", None),
        P(),
        P(),
        P(),
        P(),
        P(),
    )
    return jax.shard_map(
        choose_shards,
        mesh=mesh,
        in_specs=placed,
        out_specs=P("comp", ("grp", "tile"), None),
        check_vma=False,
    )
```

```python
import functools
import math

import jax
import jax.numpy as jnp
import numpy as np
from jax import lax
from jax.experimental import pallas as pl
from jax.experimental.pallas import tpu as pltpu
from jax.sharding import PartitionSpec as P

NTH = 36
NF = 32


weight_plus = 0.4096
weight_minus = 3.1605
weight_cross = 1.2945


def with_halo(block, sides, width):
    for axis, dim in sides:
        count = lax.axis_size(axis)
        forward = [(i, i + 1) for i in range(count - 1)]
        backward = [(target, source) for source, target in forward]
        low = lax.ppermute(
            lax.slice_in_dim(block, block.shape[dim] - width, None, axis=dim), axis, forward
        )
        high = lax.ppermute(lax.slice_in_dim(block, 0, width, axis=dim), axis, backward)
        block = jnp.concatenate([low, block, high], axis=dim)
    return block


def quick_flux(far_left, left_cell, right_cell, far_right, courant):
    centre = 0.5 * (left_cell + right_cell) - 0.5 * courant * (right_cell - left_cell)
    curvature = (1.0 - courant * courant) / 6.0
    upward = centre - curvature * (right_cell - 2.0 * left_cell + far_left)
    downward = centre - curvature * (left_cell - 2.0 * right_cell + far_right)
    return courant * jnp.where(courant > 0.0, upward, downward)


def flux_change(padded, speed, current, sea_pad, axis):
    cell_count = padded.shape[axis] - 4

    def take_part(source, first, which_axis):
        return lax.slice_in_dim(source, first, first + cell_count + 1, axis=which_axis)

    face_current = 0.5 * (take_part(current, 0, axis - 1) + take_part(current, 1, axis - 1))
    courant = speed[:, None, None] + face_current[None]
    open_face = (take_part(sea_pad, 0, axis - 1) * take_part(sea_pad, 1, axis - 1))[None]
    face_flux = (
        quick_flux(
            take_part(padded, 0, axis),
            take_part(padded, 1, axis),
            take_part(padded, 2, axis),
            take_part(padded, 3, axis),
            courant,
        )
        * open_face
    )
    return lax.slice_in_dim(face_flux, 1, cell_count + 1, axis=axis) - lax.slice_in_dim(
        face_flux, 0, cell_count, axis=axis
    )


def source_terms(energy_block, wind, turning, growth, damping, coupling, lookup, spread):
    cell_count = energy_block.shape[1]
    spectrum = energy_block.reshape(NF, NTH, cell_count)
    turn_rate = turning[None, None, :]
    next_dir = jnp.roll(spectrum, -1, axis=1)
    forward = jnp.maximum(turn_rate, 0.0)
    backward = jnp.minimum(turn_rate, 0.0)
    upper_flux = forward * spectrum + backward * next_dir
    lower_flux = jnp.roll(upper_flux, 1, axis=1)
    turned = (spectrum - upper_flux + lower_flux).reshape(energy_block.shape)
    rounded = turned.astype(jnp.bfloat16)
    plus_first, minus_first, plus_second, minus_second = lookup(rounded)
    couple_rate = coupling[:, None]
    delta_first = couple_rate * (
        turned * turned * (weight_plus * plus_first + weight_minus * minus_first)
        - 2.0 * weight_cross * turned * plus_first * minus_first
    )
    delta_second = couple_rate * (
        turned * turned * (weight_plus * plus_second + weight_minus * minus_second)
        - 2.0 * weight_cross * turned * plus_second * minus_second
    )
    moved = spread(delta_first.astype(jnp.bfloat16), delta_second.astype(jnp.bfloat16))
    mean_level = jnp.sum(turned, axis=0) / energy_block.shape[0]
    return (
        turned
        + growth[:, None] * wind[None] * turned
        - damping[:, None] * mean_level[None] * turned
        - 2.0 * (delta_first + delta_second)
        + moved
    )


def shards(
    energy,
    sea_mask,
    current_u,
    current_v,
    wind_forcing,
    refraction,
    group_speed,
    growth,
    damping,
    coupling,
    dia_index,
):
    comp_count = lax.axis_size("comp")
    comp_pos = lax.axis_index("comp")
    tile_pos = lax.axis_index("tile")
    local_comps, row_count, col_count = energy.shape
    first_row = tile_pos * row_count
    first_comp = comp_pos * local_comps
    comp_total = NTH * NF
    angles = 2.0 * math.pi / NTH * (jnp.arange(comp_total) % NTH).astype(jnp.float32)
    speeds = jnp.repeat(group_speed, NTH)
    speed_east = lax.dynamic_slice_in_dim(speeds * jnp.cos(angles), first_comp, local_comps)
    speed_north = lax.dynamic_slice_in_dim(speeds * jnp.sin(angles), first_comp, local_comps)
    window = (row_count + 2, col_count + 2)
    sea_pad = lax.dynamic_slice(jnp.pad(sea_mask.astype(jnp.float32), 1), (first_row, 0), window)
    east_pad = lax.dynamic_slice(jnp.pad(current_u, 1), (first_row, 0), window)
    north_pad = lax.dynamic_slice(jnp.pad(current_v, 1), (first_row, 0), window)
    sea_tile = sea_pad[1:-1, 1:-1]
    masked = energy * sea_tile[None]
    padded_east = with_halo(masked, (("tile", 1),), 2)
    along_east = flux_change(padded_east, speed_east, east_pad[:, 1:-1], sea_pad[:, 1:-1], 1)
    along_north = flux_change(
        jnp.pad(masked, ((0, 0), (0, 0), (2, 2))),
        speed_north,
        north_pad[1:-1, :],
        sea_pad[1:-1, :],
        2,
    )
    propagated = (sea_tile[None] * (masked - along_east - along_north)).reshape(
        local_comps, row_count * col_count
    )
    tile_wind = lax.dynamic_slice(wind_forcing, (first_row, 0), (row_count, col_count)).reshape(-1)
    tile_turn = lax.dynamic_slice(refraction, (first_row, 0), (row_count, col_count)).reshape(-1)
    comp_ids = jnp.arange(comp_total)
    tables = [
        (dia_index[slot_row][:, None] == comp_ids[None, :]).astype(jnp.bfloat16)
        for slot_row in range(4)
    ]

    def lookup(rounded):
        return tuple(
            (
                jnp.dot(tables[slot_row], rounded, preferred_element_type=jnp.float32)
                for slot_row in range(4)
            )
        )

    def scatter_back(table, terms):
        return lax.dot_general(
            table, terms, (((0,), (0,)), ((), ())), preferred_element_type=jnp.float32
        )

    def spread(first_terms, second_terms):
        return (
            scatter_back(tables[0], first_terms)
            + scatter_back(tables[1], first_terms)
            + scatter_back(tables[2], second_terms)
            + scatter_back(tables[3], second_terms)
        )

    share_size = row_count * col_count // comp_count
    point_field = lax.all_to_all(propagated, "comp", split_axis=1, concat_axis=0, tiled=True)
    first_point = comp_pos * share_size
    own_wind = lax.dynamic_slice_in_dim(tile_wind, first_point, share_size)
    own_turn = lax.dynamic_slice_in_dim(tile_turn, first_point, share_size)
    result = source_terms(
        point_field, own_wind, own_turn, growth, damping, coupling, lookup, spread
    )
    returned_field = lax.all_to_all(result, "comp", split_axis=0, concat_axis=1, tiled=True)
    return returned_field.reshape(local_comps, row_count, col_count)


BLOCK = 128
GROUP = 24
EARLY = 40
BATCH = 4
CELL_CHUNKS = 4
MIB = 1024 * 1024
VMEM_MIB = 60
EDGE = 2
SEA, OPEN_EAST, FLOW_EAST, OPEN_NORTH, FLOW_NORTH, HALF_SEA, WIND, TURN = range(8)
KEEP, SPILL, IS_SEA = BLOCK, 2 * BLOCK, 2 * BLOCK


def upwind(courant, total, slope, bend_here, bend_ahead):
    bend = jnp.where(courant > 0.0, bend_here, bend_ahead)
    return courant * ((total - bend) - courant * (slope - courant * bend))


def pick_lanes(block, index):
    return jnp.take_along_axis(block, index, axis=1, mode="promise_in_bounds")


def tile_at(tile):
    return pl.ds(pl.multiple_of(tile * BLOCK, BLOCK), BLOCK)


def has(code, flag):
    return jnp.bitwise_and(code, flag) != 0


def pack_block(blocks, code, tile, out_ref, firsts, held):
    code = jnp.broadcast_to(code, (8, BLOCK))
    index = jnp.bitwise_and(code, BLOCK - 1)
    keep, spill = has(code, KEEP), has(code, SPILL)
    result = []
    for block, first, old in zip(blocks, firsts, held):
        moved = pick_lanes(block, index)
        merged = jnp.where(keep, moved, old)
        out_ref[pl.ds(first, 8), tile_at(tile)] = merged
        result.append(jnp.where(spill, moved, merged))
    return tuple(result)


def prepare_kernel(places, base_ref, speed_ref, sea_ref, east_ref, north_ref, wind_ref, turn_ref, cos_ref, sin_ref,
                   coef_ref, index_ref, place_ref, table_ref, speed_east_ref, speed_north_ref, field_ref, pick_ref):
    first_row, odd, first_freq = base_ref[0], base_ref[1], base_ref[2]
    all_rows, col_count = sea_ref.shape
    row_count = place_ref.shape[1]
    tiles = places // BLOCK
    sea = sea_ref[...].astype(jnp.float32)
    row = lax.broadcasted_iota(jnp.int32, sea.shape, 0)
    col = lax.broadcasted_iota(jnp.int32, sea.shape, 1)

    def next_row(field):
        return jnp.where(row == all_rows - 1, 0.0, pltpu.roll(field, all_rows - 1, 0))

    def next_col(field):
        return jnp.where(col == col_count - 1, 0.0, pltpu.roll(field, col_count - 1, 1))

    open_east, open_north = sea * next_row(sea), sea * next_col(sea)
    east, north = east_ref[...], north_ref[...]
    field_ref[SEA] = sea
    field_ref[OPEN_EAST] = open_east
    field_ref[FLOW_EAST] = open_east * (0.5 * (east + next_row(east)))
    field_ref[OPEN_NORTH] = open_north
    field_ref[FLOW_NORTH] = open_north * (0.5 * (north + next_col(north)))
    field_ref[HALF_SEA] = 0.5 * sea
    field_ref[WIND] = wind_ref[...]
    field_ref[TURN] = turn_ref[...]
    coef_ref[0:EDGE] = jnp.zeros((EDGE, 8, col_count), jnp.float32)
    coef_ref[EDGE + all_rows :] = jnp.zeros((EDGE, 8, col_count), jnp.float32)

    @pl.loop(0, all_rows // 8)
    def _(i):
        rows = field_ref[:, pl.ds(pl.multiple_of(8 * i, 8), 8), :]
        coef_ref[pl.ds(8 * i + EDGE, 8)] = jnp.swapaxes(rows, 0, 1)

    freqs = cos_ref.shape[0] // NTH
    for f in range(freqs):
        circle = slice(f * NTH, (f + 1) * NTH)
        speed_east_ref[circle, :] = cos_ref[circle, :] * speed_ref[first_freq + f]
        speed_north_ref[circle, :] = sin_ref[circle, :] * speed_ref[first_freq + f]

    bf16, f32 = jnp.bfloat16, jnp.float32
    tile_sea = sea_ref[pl.ds(pl.multiple_of(first_row, 8), row_count), :].astype(f32)
    square = (BLOCK, BLOCK)
    down, over = lax.broadcasted_iota(jnp.int32, square, 0), lax.broadcasted_iota(jnp.int32, square, 1)
    before = (down < over).astype(f32).astype(bf16)
    ones = jnp.ones(square, bf16)
    row_square = (row_count, row_count)
    above = lax.broadcasted_iota(jnp.int32, row_square, 1) < lax.broadcasted_iota(jnp.int32, row_square, 0)
    above = above.astype(f32).astype(bf16)
    parts = [tile_sea[:, :BLOCK], tile_sea[:, BLOCK:]]
    numbers = [jnp.dot(p.astype(bf16), ones, preferred_element_type=f32) for p in parts]
    in_row = numbers[0] + numbers[1]
    starts = [jnp.dot(above, in_row.astype(bf16), preferred_element_type=f32)]
    starts.append(starts[0] + numbers[0])
    total = jnp.sum(in_row, axis=0, keepdims=True).astype(jnp.int32)

    def turned_tile(tile):
        return jnp.where(tile >= tiles, tiles, jnp.bitwise_and(tile + odd * (tiles // 2), tiles - 1))

    columns = []
    for h in range(2):
        rank = jnp.dot(parts[h].astype(bf16), before, preferred_element_type=f32).astype(jnp.int32)
        start = starts[h].astype(jnp.int32)
        offset = jnp.bitwise_and(start, BLOCK - 1)
        keep = jnp.where(over[:row_count] >= offset, KEEP, 0)
        slot = jnp.bitwise_and(rank + offset, BLOCK - 1)
        is_sea = parts[h] > 0.0
        place_ref[h] = slot + keep + jnp.where(is_sea, IS_SEA, 0)
        slot = jnp.where(is_sea, slot, -1).astype(f32).T
        from_lane = down[:, :row_count].astype(f32)

        @pl.loop(0, BLOCK // 8)
        def _(i):
            found = []
            for k in range(8):
                lane = (8 * i + k).astype(f32)
                found.append(jnp.sum(jnp.where(slot == lane, from_lane, 0.0), axis=0, keepdims=True))
            pick_ref[pl.ds(pl.multiple_of(8 * i, 8), 8), :] = jnp.concatenate(found, axis=0)

        spill = jnp.where(offset + numbers[h].astype(jnp.int32) >= BLOCK, SPILL, 0)
        index_ref[h] = pick_ref[...].T.astype(jnp.int32) + keep + spill
        columns.append(turned_tile(lax.shift_right_logical(starts[h].T[0:8, :].astype(jnp.int32), 7)))
    row_id = lax.broadcasted_iota(jnp.int32, (8, row_count), 0)
    end_tile = jnp.where(
        jnp.bitwise_and(total, BLOCK - 1) == 0, tiles, turned_tile(lax.shift_right_logical(total, 7))
    )
    end_tile = jnp.broadcast_to(end_tile, (8, BLOCK))
    table_ref[...] = jnp.concatenate([jnp.where(row_id == 0, columns[0], columns[1]), end_tile], axis=1)


def propagate_kernel(part, late, pieces, base_ref, table_ref, energy_ref, halo_ref, coef_ref, index_ref, east_ref,
                     north_ref, *refs):
    refs = list(refs)
    with_fields = part == 0 and late == 0
    fields_ref = None if with_fields else refs.pop(0)
    seam_ref = refs.pop(0) if late else None
    if late:
        refs.pop(0)
    piece_refs = [refs.pop(0) for _ in range(2 * pieces)]
    sum_ref, full_ref = refs.pop(0), refs.pop(0)
    seam_out_ref = refs.pop(0) if late == 0 else None
    fields_out_ref = refs.pop(0) if with_fields else None
    energy_vmem, rows_ref, spread_ref, wide_ref, result_ref, strip_sems, out_sems = refs
    row_count, comp_count, col_count = rows_ref.shape
    strips = comp_count // 8
    sent_rows = piece_refs[0].shape[0]
    cells = result_ref.shape[1]
    first_row = base_ref[0]
    first_comp = pl.multiple_of((part + base_ref[1] * (1 - 2 * part)) * 2 * NTH + (EARLY if late else 0), 8)
    lane = lax.broadcasted_iota(jnp.int32, (8, BLOCK), 1)
    first_lane, last_lane = lane == 0, lane == BLOCK - 1
    third = 1.0 / 3.0

    def arrival(g):
        target = energy_vmem.at[pl.ds(pl.multiple_of(8 * g, 8), 8)]
        source = energy_ref.at[pl.ds(pl.multiple_of(first_comp + 8 * g, 8), 8)]
        return pltpu.make_async_copy(source, target, strip_sems.at[g])

    for g in range(strips):
        arrival(g).start()

    def halves(row):
        return row[:, :BLOCK], row[:, BLOCK:]

    @pl.loop(0, row_count + 2 * EDGE, unroll=4)
    def _(r):
        coef = coef_ref[first_row + r]
        for k in range(HALF_SEA + 1):
            spread_ref[r, k] = jnp.broadcast_to(coef[k : k + 1, :], coef.shape)

    def masked(row, at):
        return tuple(part * sea for part, sea in zip(halves(row), halves(spread_ref[at, SEA])))

    def cell_rows(first, fresh, state, east, north):
        here, ahead, slope_here, bend_here, flux_low = state
        count, sides = len(fresh), range(2)
        level = [here, ahead] + [masked(row, first + k + EDGE) for k, row in enumerate(fresh)]
        rows = range(count)
        coef = [[None] + [halves(spread_ref[first + k, f]) for f in range(1, HALF_SEA + 1)] for k in rows]
        one_right = [[pltpu.roll(part, BLOCK - 1, 1) for part in level[k]] for k in rows]
        right = [
            (jnp.where(last_lane, one[1], one[0]), jnp.where(last_lane, 0.0, one[1])) for one in one_right
        ]
        slope = [[right[k][h] - level[k][h] for h in sides] for k in rows]
        slope_roll = [[pltpu.roll(part, 1, 1) for part in slope[k]] for k in rows]
        bend = [
            (third * (slope[k][0] - jnp.where(first_lane, level[k][0], slope_roll[k][0])),
             third * (slope[k][1] - jnp.where(first_lane, slope_roll[k][0], slope_roll[k][1])))
            for k in rows
        ]
        bend_roll = [[pltpu.roll(part, BLOCK - 1, 1) for part in bend[k]] for k in rows]
        cross = []
        for k in rows:
            bend_right = (jnp.where(last_lane, bend_roll[k][1], bend_roll[k][0]), bend_roll[k][1])
            cross.append([
                upwind(north * coef[k][OPEN_NORTH][h] + coef[k][FLOW_NORTH][h], level[k][h] + right[k][h],
                       slope[k][h], bend[k][h], bend_right[h])
                for h in sides
            ])
        cross_roll = [[pltpu.roll(part, 1, 1) for part in cross[k]] for k in rows]
        slopes = [slope_here] + [tuple(level[k + 1][h] - level[k][h] for h in sides) for k in range(1, count + 1)]
        bends = [bend_here] + [
            tuple(third * (slopes[k][h] - slopes[k - 1][h]) for h in sides) for k in range(1, count + 1)
        ]
        flux = [flux_low]
        for k in rows:
            flux.append(tuple(
                upwind(east * coef[k][OPEN_EAST][h] + coef[k][FLOW_EAST][h], level[k][h] + level[k + 1][h],
                       slopes[k][h], bends[k][h], bends[k + 1][h])
                for h in sides
            ))
        done = []
        for k in rows:
            cross_low = (jnp.where(first_lane, cross_roll[k][1], cross_roll[k][0]),
                         jnp.where(first_lane, cross_roll[k][0], cross_roll[k][1]))
            done.append([
                coef[k][HALF_SEA][h] * (((level[k][h] + level[k][h]) + (flux[k][h] + cross_low[h]))
                                        - (flux[k + 1][h] + cross[k][h]))
                for h in sides
            ])
        return (level[count], level[count + 1], slopes[count], bends[count], flux[count]), done

    def store_row(row, local, parts):
        for h in range(2):
            rows_ref[row, local, h * BLOCK : (h + 1) * BLOCK] = parts[h]

    @pl.loop(0, strips)
    def _(g):
        arrival(g).wait()
        local = pl.ds(pl.multiple_of(g * 8, 8), 8)
        comps = pl.ds(pl.multiple_of(first_comp + g * 8, 8), 8)
        east, north = east_ref[comps, :], north_ref[comps, :]
        zero = (jnp.zeros((8, BLOCK), jnp.float32),) * 2
        here, ahead = masked(halo_ref[comps, 0, :], 0), masked(halo_ref[comps, 1, :], 1)
        state = (here, ahead, tuple(b - a for a, b in zip(here, ahead)), zero, zero)

        def eight(i, state):
            block = jnp.swapaxes(energy_vmem[local, pl.ds(pl.multiple_of(8 * i, 8), 8), :], 0, 1)
            for first in range(0, 8, BATCH):
                fresh = [block[first + k] for k in range(BATCH)]
                state, done = cell_rows(8 * i + first, fresh, state, east, north)
                for k in range(BATCH):
                    store_row(jnp.maximum(8 * i + first + k - EDGE, 0), local, done[k])
            return state

        state = lax.fori_loop(0, row_count // 8, eight, state)
        fresh = [halo_ref[comps, k, :] for k in range(EDGE)]
        state, done = cell_rows(row_count, fresh, state, east, north)
        for k in range(EDGE):
            store_row(row_count - EDGE + k, local, done[k])

    group_rows = [8 * n for n in range(strips + with_fields)]

    def pack_eight(i, held):
        codes = [index_ref[h, pl.ds(pl.multiple_of(8 * i, 8), 8), :] for h in range(2)]
        for k in range(8):
            row = 8 * i + k
            for h in range(2):
                lanes = slice(h * BLOCK, (h + 1) * BLOCK)
                blocks = [rows_ref[row, 8 * n : 8 * n + 8, lanes] for n in range(strips)]
                if with_fields:
                    blocks.append(coef_ref[first_row + EDGE + row, :, lanes])
                held = pack_block(blocks, codes[h][k : k + 1, :], table_ref[h, row], wide_ref, group_rows, held)
        return held

    empty = (jnp.zeros((8, BLOCK), jnp.float32),) * len(group_rows)
    held = lax.fori_loop(0, row_count // 8, pack_eight, empty)
    for first, block in zip(group_rows, held):
        wide_ref[pl.ds(first, 8), tile_at(table_ref[0, row_count])] = block
    if with_fields:
        fields_out_ref[...] = wide_ref[comp_count:, :cells]

    tile_width = 2 * BLOCK
    height = result_ref.shape[0]
    comp_row = lax.broadcasted_iota(jnp.int32, (height, tile_width), 0)
    starts = {0: [0], 1: [height - NTH], None: [0, NTH]}[late]
    mixed = {0: slice(height - 8, height), 1: slice(0, 8), None: slice(0, 0)}[late]
    in_circle = (comp_row[:8] + mixed.start >= starts[0]) & (comp_row[:8] + mixed.start < starts[0] + NTH)

    @pl.loop(0, cells // tile_width, unroll=2)
    def _(i):
        source = pl.ds(pl.multiple_of(i * tile_width, tile_width), tile_width)
        level = wide_ref[:comp_count, source]
        if late:
            level = jnp.concatenate([seam_ref[:, source], level], axis=0)
        if with_fields:
            rate = wide_ref[comp_count + TURN : comp_count + TURN + 1, source]
        else:
            rate = fields_ref[TURN : TURN + 1, source]
        forward = jnp.maximum(rate, 0.0)
        backward = jnp.minimum(rate, 0.0)
        stay = (1.0 - forward) + backward
        above = pltpu.roll(level, height - 1, 0)
        below = pltpu.roll(level, 1, 0)

        def with_row(rolled, row, value):
            tile = slice(row - row % 8, row - row % 8 + 8)
            fixed = jnp.where(comp_row[tile] == row, value, rolled[tile])
            parts = [rolled[: tile.start], fixed, rolled[tile.stop :]]
            return jnp.concatenate([part for part in parts if part.shape[0]], axis=0)

        for start in starts:
            end = start + NTH - 1
            above = with_row(above, end, level[start : start + 1, :])
            below = with_row(below, start, level[end : end + 1, :])
        turned = stay * level - backward * above + forward * below
        partial = jnp.zeros((8, tile_width), jnp.float32)
        for first in range(0, height, 8):
            rows = slice(first, first + 8)
            if rows == mixed:
                result_ref[rows, source] = jnp.where(in_circle, turned[rows], level[rows])
                partial += jnp.where(in_circle, turned[rows], 0.0)
            else:
                result_ref[rows, source] = turned[rows]
                partial += turned[rows]
        sum_ref[:, source] = jnp.sum(partial, axis=0, keepdims=True)

    if late == 0:
        seam_out_ref[...] = result_ref[sent_rows:, :]
    width = cells // (2 * pieces)
    copies = []
    for n, piece in enumerate(piece_refs):
        source = result_ref.at[:sent_rows, n * width : (n + 1) * width]
        copies.append(pltpu.make_async_copy(source, piece, out_sems.at[n]))
    rows = pl.ds(EARLY - 8 if late else 0, sent_rows)
    copies.append(pltpu.make_async_copy(result_ref.at[:sent_rows, :], full_ref.at[rows, :], out_sems.at[2 * pieces]))
    for copy in copies:
        copy.start()
    for copy in copies:
        copy.wait()


def interact_kernel(counts, table_ref, spread_ref, coupling_ref, *refs):
    own_ref, back_0_ref, back_1_ref, delta_ref = refs[sum(counts) :]
    window = []
    for j, count in enumerate(counts):
        first = sum(counts[:j])
        parts = [ref[...] for ref in refs[first : first + count]]
        window.append(parts[0] if count == 1 else jnp.concatenate(parts, axis=0))
    comps = window[0].shape[0]
    for j in range(1, 7):
        level = window[j]
        around = jnp.concatenate([window[j - 1], level, window[j + 1]], axis=0).astype(jnp.bfloat16)
        partner = jnp.dot(table_ref[j - 1], around, preferred_element_type=jnp.float32)
        rate = coupling_ref[(j - 1) * comps : j * comps, :] * level
        plus_part = weight_plus * level
        minus_part = weight_minus * level
        deltas = []
        for pair in range(2):
            plus = partner[2 * pair * comps : (2 * pair + 1) * comps, :]
            minus = partner[(2 * pair + 1) * comps : (2 * pair + 2) * comps, :]
            deltas.append(rate * (plus * (plus_part - (2.0 * weight_cross) * minus) + minus_part * minus))
        both = jnp.concatenate(deltas, axis=0).astype(jnp.bfloat16)
        delta_ref[(j - 1) * 2 * comps : j * 2 * comps, :] = both
        if 2 <= j <= 5:
            part = -2.0 * (deltas[0] + deltas[1])
            if j <= 3:
                own_ref[(j - 2) * comps : (j - 1) * comps, :] = part
            elif j == 4:
                back_1_ref[...] = part
            else:
                back_0_ref[...] = part
    spread = jnp.dot(spread_ref[...], delta_ref[...], preferred_element_type=jnp.float32)
    own_ref[...] += spread[: 2 * comps, :]
    back_1_ref[...] += spread[2 * comps : 3 * comps, :]
    back_0_ref[...] += spread[3 * comps :, :]


def finish_kernel(chunks, base_ref, table_ref, place_ref, mean_ref, fields_ref, growth_ref, damping_ref, *refs):
    turned_ref, own, back = refs[0], refs[1 : 1 + chunks], refs[1 + chunks : 1 + 2 * chunks]
    out_ref, wide_ref = refs[-2], refs[-1]
    width = own[0].shape[1]
    tiles = wide_ref.shape[1] // BLOCK
    tile_width = 2 * BLOCK
    growth = jnp.broadcast_to(growth_ref[...], (GROUP, tile_width))
    damping = jnp.broadcast_to(damping_ref[...], (GROUP, tile_width))
    for o in range(2 * chunks):
        extra = own[o] if o < chunks else back[o - chunks]

        @pl.loop(0, width // tile_width, unroll=2)
        def _(i):
            source = pl.ds(pl.multiple_of(i * tile_width, tile_width), tile_width)
            target = pl.ds(pl.multiple_of(o * width + i * tile_width, tile_width), tile_width)
            scale = 1.0 + growth * fields_ref[WIND : WIND + 1, target] - damping * mean_ref[0:1, target]
            wide_ref[:, target] = turned_ref[:, target] * scale + extra[:, source]

    @pl.loop(0, out_ref.shape[1] // 8)
    def _(i):
        codes = [place_ref[h, pl.ds(pl.multiple_of(8 * i, 8), 8), :] for h in range(2)]
        done = [[] for _ in range(GROUP // 8)]
        for r in range(8):
            parts = [[] for _ in range(GROUP // 8)]
            for h in range(2):
                code = jnp.broadcast_to(codes[h][r : r + 1, :], (8, BLOCK))
                index = jnp.bitwise_and(code, BLOCK - 1)
                keep, is_sea = has(code, KEEP), has(code, IS_SEA)
                tile = table_ref[h, 8 * i + r]
                first, second = jnp.minimum(tile, tiles - 1), jnp.bitwise_and(tile + 1, tiles - 1)
                for k in range(GROUP // 8):
                    rows = slice(8 * k, 8 * k + 8)
                    near = jnp.where(keep, wide_ref[rows, tile_at(first)], wide_ref[rows, tile_at(second)])
                    parts[k].append(jnp.where(is_sea, pick_lanes(near, index), 0.0))
            for k in range(GROUP // 8):
                done[k].append(jnp.concatenate(parts[k], axis=1))
        for k in range(GROUP // 8):
            out_ref[8 * k : 8 * k + 8, pl.ds(pl.multiple_of(8 * i, 8), 8), :] = jnp.swapaxes(jnp.stack(done[k]), 0, 1)


def params(limit):
    return pltpu.CompilerParams(vmem_limit_bytes=limit * MIB)


def after(value, *others):
    return lax.optimization_barrier((value,) + others)[0]


def packed_shards(energy, sea_mask, current_u, current_v, wind_forcing, refraction, group_speed, growth, damping,
                  coupling, dia_index):
    comp_count = lax.axis_size("comp")
    comp_pos = lax.axis_index("comp")
    tile_pos = lax.axis_index("tile")
    odd = lax.rem(comp_pos, 2)
    pair_pos = comp_pos // 2
    local_comps, row_count, col_count = energy.shape
    comps = local_comps // 2
    comp_total = NTH * NF
    first_row = tile_pos * row_count
    first_comp = comp_pos * local_comps
    cells = row_count * col_count // 2
    half = cells // 2
    width = half // CELL_CHUNKS
    f32, i32 = jnp.float32, jnp.int32
    base = jnp.stack([first_row, odd, comp_pos * (local_comps // NTH)]).astype(i32)

    edge_first = jnp.where(tile_pos == 0, row_count - EDGE, 0)
    edge_rows = lax.dynamic_slice_in_dim(energy, edge_first, EDGE, axis=1)
    halo_rows = lax.ppermute(edge_rows, "tile", [(0, 1), (1, 0)])

    all_rows = sea_mask.shape[0]
    angles = np.float32(2.0 * math.pi / NTH) * (np.arange(local_comps) % NTH).astype(np.float32)
    cosines = np.broadcast_to(np.cos(angles)[:, None], (local_comps, BLOCK)).astype(np.float32)
    sines = np.broadcast_to(np.sin(angles)[:, None], (local_comps, BLOCK)).astype(np.float32)
    vmem = pl.BlockSpec(memory_space=pltpu.VMEM)
    coef, index, place, table, speed_east, speed_north = pl.pallas_call(
        functools.partial(prepare_kernel, cells),
        grid_spec=pltpu.PrefetchScalarGridSpec(
            num_scalar_prefetch=2,
            grid=(),
            in_specs=[vmem] * 7,
            out_specs=[vmem] * 6,
            scratch_shapes=[pltpu.VMEM((8, all_rows, col_count), f32), pltpu.VMEM((BLOCK, row_count), f32)],
        ),
        out_shape=[
            jax.ShapeDtypeStruct((all_rows + 2 * EDGE, 8, col_count), f32),
            jax.ShapeDtypeStruct((2, row_count, BLOCK), i32),
            jax.ShapeDtypeStruct((2, row_count, BLOCK), i32),
            jax.ShapeDtypeStruct((8, 2 * BLOCK), i32),
            jax.ShapeDtypeStruct((local_comps, BLOCK), f32),
            jax.ShapeDtypeStruct((local_comps, BLOCK), f32),
        ],
        name="prepare",
        compiler_params=params(VMEM_MIB),
    )(base, group_speed, sea_mask, current_u, current_v, wind_forcing, refraction, cosines, sines)
    steps = comps // GROUP

    def group_at(part, base_ref):
        return (part + base_ref[1] * (1 - 2 * part)) * steps

    def whole(shape):
        return pl.BlockSpec(shape, lambda s, b, t: (0,) * len(shape))

    def column(part, lanes):
        return pl.BlockSpec((GROUP, lanes), lambda s, b, t: (group_at(part, b) + s, 0))

    def propagate(part, late, table, fields=None, seam=None, full=None):
        pieces = CELL_CHUNKS if part else 1
        comp_rows = {0: EARLY, 1: comps - EARLY, None: comps}[late]
        sent_rows = {0: EARLY - 8, 1: comps - EARLY + 8, None: comps}[late]
        height = comps if late is None else EARLY
        anywhere = pl.BlockSpec(memory_space=pl.ANY)
        with_fields = fields is None
        inputs = [energy, halo_rows, coef, index, speed_east, speed_north]
        in_specs = [anywhere] + [vmem] * 5
        aliases = {}
        if not with_fields:
            inputs.append(fields)
            in_specs.append(vmem)
        if late:
            inputs += [seam, full]
            in_specs += [vmem, anywhere]
            aliases = {len(inputs) + 1: 2 * pieces + 1}
        shapes = [(sent_rows, half // pieces)] * (2 * pieces) + [(1, cells), (comps, cells)]
        out_specs = [anywhere] * (2 * pieces) + [vmem, anywhere]
        if late == 0:
            shapes.append((8, cells))
            out_specs.append(vmem)
        if with_fields:
            shapes.append((8, cells))
            out_specs.append(vmem)
        outs = pl.pallas_call(
            functools.partial(propagate_kernel, part, late, pieces),
            grid_spec=pltpu.PrefetchScalarGridSpec(
                num_scalar_prefetch=2,
                grid=(),
                in_specs=in_specs,
                out_specs=out_specs,
                scratch_shapes=[
                    pltpu.VMEM((comp_rows, row_count, col_count), f32),
                    pltpu.VMEM((row_count, comp_rows, col_count), f32),
                    pltpu.VMEM((row_count + 2 * EDGE, HALF_SEA + 1, 8, col_count), f32),
                    pltpu.VMEM((comp_rows + (8 if with_fields else 0), cells + BLOCK), f32),
                    pltpu.VMEM((height, cells), f32),
                    pltpu.SemaphoreType.DMA((comp_rows // 8,)),
                    pltpu.SemaphoreType.DMA((2 * pieces + 1,)),
                ],
            ),
            out_shape=[jax.ShapeDtypeStruct(shape, f32) for shape in shapes],
            input_output_aliases=aliases,
            name={0: "propagate_early", 1: "propagate_late", None: "propagate_whole"}[late],
            compiler_params=params(VMEM_MIB),
            cost_estimate=pl.CostEstimate(
                flops=60 * comp_rows * row_count * col_count, bytes_accessed=60 * MIB, transcendentals=0,
            ),
        )(base, table, *inputs)
        return list(outs[:pieces]), list(outs[pieces : 2 * pieces]), outs[2 * pieces :]

    pairs = [(i, i ^ 1) for i in range(comp_count)]
    apart = [(i, i - 2 if i % 2 == 0 else i + 2) for i in range(comp_count)]
    apart = [(a, b) for a, b in apart if 0 <= b < comp_count]
    across = [(b, a) for a, b in apart]
    chunk_range = range(CELL_CHUNKS)

    def send(pieces, route, waits):
        return [lax.ppermute(after(piece, *wait), "comp", route) for piece, wait in zip(pieces, waits)]

    stages = [(0, 0), (0, 1), (1, None)]
    kept, sent, got, from_own, from_got, level_sums, full = {}, {}, {}, {}, {}, [], {}
    fields = seam = before = None
    part_table = table
    for stage in stages:
        part, late = stage
        kept[stage], sent[stage], extra = propagate(part, late, part_table, fields, seam, full.get(part))
        level_sums.append(extra[0])
        full[part] = extra[1]
        seam = extra[2] if late == 0 else None
        fields = extra[3] if fields is None else fields
        if stage == stages[-1]:
            break
        got[stage] = send(sent[stage], pairs, [[]])
        from_own[stage] = send(kept[stage], apart, [[]])
        waits = [from_got[before][0]] if before is not None else []
        from_got[stage] = send(got[stage], across, [waits])
        done = [extra[0]]
        if before is not None:
            done.append(got[before][0])
        part_table = after(table, *done)
        before = stage
    packed_fields = fields
    sums_0 = level_sums[0]

    sums = level_sums[0] + level_sums[1] + level_sums[2]
    partner_sums = lax.ppermute(sums, "comp", pairs)
    partner_sums = jnp.roll(partner_sums, half, axis=1)
    last, got_1, from_own_1 = stages[-1], [], []
    for c in chunk_range:
        waits = [got[before][0]] + ([got_1[c - 2]] if c >= 2 else []) + ([partner_sums] if c == 2 else [])
        got_1.append(lax.ppermute(after(sent[last][c], *waits), "comp", pairs))
        from_own_1.append(lax.ppermute(after(kept[last][c], from_own[before][0]), "comp", apart))
    got[last], from_own[last], from_got[last] = got_1, from_own_1, []
    sums = sums + partner_sums
    sums = sums_two = sums + lax.ppermute(sums, "comp", [(i, i ^ 2) for i in range(comp_count)])
    sums = sums + lax.ppermute(sums, "comp", [(i, i ^ 4) for i in range(comp_count)])
    mean_level = sums / comp_total

    dia_index, coupling, growth, damping, late_odd, late_pair, _ = lax.optimization_barrier(
        (dia_index, coupling, growth, damping, odd, pair_pos, sums_0)
    )
    own_growth = lax.dynamic_slice_in_dim(growth, first_comp, local_comps)[:, None]
    own_damping = lax.dynamic_slice_in_dim(damping, first_comp, local_comps)[:, None]
    chunk_first = [
        NTH * jnp.where(late_odd > 0, 8 * late_pair + 10 - 2 * j, 8 * late_pair - 4 + 2 * j) for j in range(8)
    ]
    margin = 8 * NTH
    dia_pad = jnp.pad(dia_index, ((0, 0), (margin, margin)), constant_values=-1)
    coupling_pad = jnp.pad(coupling, (margin, margin))
    own_ids = jnp.arange(comps)
    targets, rates = [], []
    for j in range(1, 7):
        targets.append(lax.dynamic_slice(dia_pad, (0, chunk_first[j] + margin), (4, comps)))
        rates.append(lax.dynamic_slice_in_dim(coupling_pad, chunk_first[j] + margin, comps))
    lookup = []
    for j in range(1, 7):
        ids = jnp.concatenate([chunk_first[j + d] + own_ids for d in (-1, 0, 1)])
        lookup.append((targets[j - 1].reshape(4 * comps)[:, None] == ids[None, :]).astype(jnp.bfloat16))
    lookup = jnp.stack(lookup)
    out_ids = jnp.concatenate([chunk_first[j] + own_ids for j in range(2, 6)])
    spread = []
    for j in range(1, 7):
        for pair in range(2):
            hits = [
                (out_ids[:, None] == targets[j - 1][2 * pair + q][None, :]).astype(f32) for q in range(2)
            ]
            spread.append(hits[0] + hits[1])
    spread = jnp.concatenate(spread, axis=1).astype(jnp.bfloat16)
    rates = jnp.concatenate(rates)[:, None]

    lanes = 512 if width % 512 == 0 else width
    own_parts, parts_0, parts_1 = [], [], []
    groups = [(from_got, 1), (from_got, 0), (kept, 0), (kept, 1), (got, 1), (got, 0), (from_own, 0), (from_own, 1)]
    for c in chunk_range:
        waits = [from_got[before][0]] + ([from_got[last][c - 2]] if c >= 2 else [])
        from_got[last].append(lax.ppermute(after(got_1[c], *waits), "comp", across))
        levels, level_specs, counts = [], [], []
        for group, part in groups:
            counts.append(1 if part else 2)
            for late in [None] if part else [0, 1]:
                pieces = group[part, late]
                single = len(pieces) == 1
                levels.append(pieces[0 if single else c])
                skipped = c * (width // lanes) if single else 0
                level_specs.append(
                    pl.BlockSpec((levels[-1].shape[0], lanes), functools.partial(lambda n, s: (0, n + s), skipped))
                )
        own_part, part_0, part_1 = pl.pallas_call(
            functools.partial(interact_kernel, tuple(counts)),
            grid=(width // lanes,),
            in_specs=[
                pl.BlockSpec(lookup.shape, lambda s: (0, 0, 0)),
                pl.BlockSpec(spread.shape, lambda s: (0, 0)),
                pl.BlockSpec(rates.shape, lambda s: (0, 0)),
            ] + level_specs,
            out_specs=[pl.BlockSpec((n * comps, lanes), lambda s: (0, s)) for n in (2, 1, 1)],
            out_shape=[jax.ShapeDtypeStruct((n * comps, width), f32) for n in (2, 1, 1)],
            scratch_shapes=[pltpu.VMEM((12 * comps, lanes), jnp.bfloat16)],
            name="interact_cells",
            compiler_params=params(VMEM_MIB),
            cost_estimate=pl.CostEstimate(
                flops=2 * width * comps * comps * (6 * 12 + 48),
                bytes_accessed=20 * MIB, transcendentals=0,
            ),
        )(lookup, spread, rates, *levels)
        own_parts.append(own_part)
        parts_0.append(part_0)
        parts_1.append(part_1)

    def send_back(piece, *waits):
        return lax.ppermute(after(piece, *waits), "comp", pairs)

    back = [[None] * CELL_CHUNKS for _ in range(2)]
    back[0][0] = send_back(parts_0[0], got_1[2], sums_two)
    back[1][0] = send_back(parts_1[0], got_1[3])
    back[0][1] = send_back(parts_0[1], back[0][0], sums)
    back[0][2] = send_back(parts_0[2], back[1][0])
    back[0][3] = send_back(parts_0[3], back[0][1])
    for c in range(1, CELL_CHUNKS):
        back[1][c] = send_back(parts_1[c], back[0][2])

    def finish(part, so_far):
        piece = pl.BlockSpec((GROUP, width), lambda s, b, t: (s, 0))
        own_piece = pl.BlockSpec((GROUP, width), lambda s, b, t: (part * steps + s, 0))
        inputs = [place, mean_level, packed_fields, own_growth, own_damping]
        specs = [whole(place.shape), whole(mean_level.shape), whole(packed_fields.shape), column(part, 1),
                 column(part, 1)]
        inputs += [full[part]] + own_parts + back[part]
        specs.append(pl.BlockSpec((GROUP, cells), lambda s, b, t: (s, 0)))
        specs += [own_piece] * CELL_CHUNKS + [piece] * CELL_CHUNKS
        aliases = {}
        if so_far is not None:
            inputs.append(so_far)
            specs.append(pl.BlockSpec(memory_space=pl.ANY))
            aliases = {len(inputs) + 1: 0}
        return pl.pallas_call(
            functools.partial(finish_kernel, CELL_CHUNKS),
            grid_spec=pltpu.PrefetchScalarGridSpec(
                num_scalar_prefetch=2,
                grid=(steps,),
                in_specs=specs,
                out_specs=pl.BlockSpec((GROUP, row_count, col_count), lambda s, b, t: (group_at(part, b) + s, 0, 0)),
                scratch_shapes=[pltpu.VMEM((GROUP, cells), f32)],
            ),
            out_shape=jax.ShapeDtypeStruct(energy.shape, f32),
            input_output_aliases=aliases,
            name="finish_chunk",
            compiler_params=params(VMEM_MIB),
            cost_estimate=pl.CostEstimate(
                flops=20 * comps * row_count * col_count,
                bytes_accessed=100 * MIB, transcendentals=0,
            ),
        )(base, table, *inputs)

    return finish(1, finish(0, None))


def choose_shards(energy, *rest):
    local_comps, row_count, col_count = energy.shape
    fits = (
        local_comps == 4 * NTH and lax.axis_size("comp") == 8 and local_comps * 8 == NTH * NF
        and lax.axis_size("tile") == 2 and row_count == BLOCK and col_count == 2 * BLOCK
    )
    return packed_shards(energy, *rest) if fits else shards(energy, *rest)


def solution(mesh):
    placed = (
        P("comp", ("grp", "tile"), None),
        P("grp", None),
        P("grp", None),
        P("grp", None),
        P("grp", None),
        P("grp", None),
        P(),
        P(),
        P(),
        P(),
        P(),
    )
    return jax.shard_map(
        choose_shards,
        mesh=mesh,
        in_specs=placed,
        out_specs=P("comp", ("grp", "tile"), None),
        check_vma=False,
    )
```

```python
import functools
import math

import jax
import jax.numpy as jnp
import numpy as np
from jax import lax
from jax.experimental import pallas as pl
from jax.experimental.pallas import tpu as pltpu
from jax.sharding import PartitionSpec as P

NTH = 36
NF = 32


weight_plus = 0.4096
weight_minus = 3.1605
weight_cross = 1.2945


def with_halo(block, sides, width):
    for axis, dim in sides:
        count = lax.axis_size(axis)
        forward = [(i, i + 1) for i in range(count - 1)]
        backward = [(target, source) for source, target in forward]
        low = lax.ppermute(
            lax.slice_in_dim(block, block.shape[dim] - width, None, axis=dim), axis, forward
        )
        high = lax.ppermute(lax.slice_in_dim(block, 0, width, axis=dim), axis, backward)
        block = jnp.concatenate([low, block, high], axis=dim)
    return block


def quick_flux(far_left, left_cell, right_cell, far_right, courant):
    centre = 0.5 * (left_cell + right_cell) - 0.5 * courant * (right_cell - left_cell)
    curvature = (1.0 - courant * courant) / 6.0
    upward = centre - curvature * (right_cell - 2.0 * left_cell + far_left)
    downward = centre - curvature * (left_cell - 2.0 * right_cell + far_right)
    return courant * jnp.where(courant > 0.0, upward, downward)


def flux_change(padded, speed, current, sea_pad, axis):
    cell_count = padded.shape[axis] - 4

    def take_part(source, first, which_axis):
        return lax.slice_in_dim(source, first, first + cell_count + 1, axis=which_axis)

    face_current = 0.5 * (take_part(current, 0, axis - 1) + take_part(current, 1, axis - 1))
    courant = speed[:, None, None] + face_current[None]
    open_face = (take_part(sea_pad, 0, axis - 1) * take_part(sea_pad, 1, axis - 1))[None]
    face_flux = (
        quick_flux(
            take_part(padded, 0, axis),
            take_part(padded, 1, axis),
            take_part(padded, 2, axis),
            take_part(padded, 3, axis),
            courant,
        )
        * open_face
    )
    return lax.slice_in_dim(face_flux, 1, cell_count + 1, axis=axis) - lax.slice_in_dim(
        face_flux, 0, cell_count, axis=axis
    )


def source_terms(energy_block, wind, turning, growth, damping, coupling, lookup, spread):
    cell_count = energy_block.shape[1]
    spectrum = energy_block.reshape(NF, NTH, cell_count)
    turn_rate = turning[None, None, :]
    next_dir = jnp.roll(spectrum, -1, axis=1)
    forward = jnp.maximum(turn_rate, 0.0)
    backward = jnp.minimum(turn_rate, 0.0)
    upper_flux = forward * spectrum + backward * next_dir
    lower_flux = jnp.roll(upper_flux, 1, axis=1)
    turned = (spectrum - upper_flux + lower_flux).reshape(energy_block.shape)
    rounded = turned.astype(jnp.bfloat16)
    plus_first, minus_first, plus_second, minus_second = lookup(rounded)
    couple_rate = coupling[:, None]
    delta_first = couple_rate * (
        turned * turned * (weight_plus * plus_first + weight_minus * minus_first)
        - 2.0 * weight_cross * turned * plus_first * minus_first
    )
    delta_second = couple_rate * (
        turned * turned * (weight_plus * plus_second + weight_minus * minus_second)
        - 2.0 * weight_cross * turned * plus_second * minus_second
    )
    moved = spread(delta_first.astype(jnp.bfloat16), delta_second.astype(jnp.bfloat16))
    mean_level = jnp.sum(turned, axis=0) / energy_block.shape[0]
    return (
        turned
        + growth[:, None] * wind[None] * turned
        - damping[:, None] * mean_level[None] * turned
        - 2.0 * (delta_first + delta_second)
        + moved
    )


def shards(
    energy,
    sea_mask,
    current_u,
    current_v,
    wind_forcing,
    refraction,
    group_speed,
    growth,
    damping,
    coupling,
    dia_index,
):
    comp_count = lax.axis_size("comp")
    comp_pos = lax.axis_index("comp")
    tile_pos = lax.axis_index("tile")
    local_comps, row_count, col_count = energy.shape
    first_row = tile_pos * row_count
    first_comp = comp_pos * local_comps
    comp_total = NTH * NF
    angles = 2.0 * math.pi / NTH * (jnp.arange(comp_total) % NTH).astype(jnp.float32)
    speeds = jnp.repeat(group_speed, NTH)
    speed_east = lax.dynamic_slice_in_dim(speeds * jnp.cos(angles), first_comp, local_comps)
    speed_north = lax.dynamic_slice_in_dim(speeds * jnp.sin(angles), first_comp, local_comps)
    window = (row_count + 2, col_count + 2)
    sea_pad = lax.dynamic_slice(jnp.pad(sea_mask.astype(jnp.float32), 1), (first_row, 0), window)
    east_pad = lax.dynamic_slice(jnp.pad(current_u, 1), (first_row, 0), window)
    north_pad = lax.dynamic_slice(jnp.pad(current_v, 1), (first_row, 0), window)
    sea_tile = sea_pad[1:-1, 1:-1]
    masked = energy * sea_tile[None]
    padded_east = with_halo(masked, (("tile", 1),), 2)
    along_east = flux_change(padded_east, speed_east, east_pad[:, 1:-1], sea_pad[:, 1:-1], 1)
    along_north = flux_change(
        jnp.pad(masked, ((0, 0), (0, 0), (2, 2))),
        speed_north,
        north_pad[1:-1, :],
        sea_pad[1:-1, :],
        2,
    )
    propagated = (sea_tile[None] * (masked - along_east - along_north)).reshape(
        local_comps, row_count * col_count
    )
    tile_wind = lax.dynamic_slice(wind_forcing, (first_row, 0), (row_count, col_count)).reshape(-1)
    tile_turn = lax.dynamic_slice(refraction, (first_row, 0), (row_count, col_count)).reshape(-1)
    comp_ids = jnp.arange(comp_total)
    tables = [
        (dia_index[slot_row][:, None] == comp_ids[None, :]).astype(jnp.bfloat16)
        for slot_row in range(4)
    ]

    def lookup(rounded):
        return tuple(
            (
                jnp.dot(tables[slot_row], rounded, preferred_element_type=jnp.float32)
                for slot_row in range(4)
            )
        )

    def scatter_back(table, terms):
        return lax.dot_general(
            table, terms, (((0,), (0,)), ((), ())), preferred_element_type=jnp.float32
        )

    def spread(first_terms, second_terms):
        return (
            scatter_back(tables[0], first_terms)
            + scatter_back(tables[1], first_terms)
            + scatter_back(tables[2], second_terms)
            + scatter_back(tables[3], second_terms)
        )

    share_size = row_count * col_count // comp_count
    point_field = lax.all_to_all(propagated, "comp", split_axis=1, concat_axis=0, tiled=True)
    first_point = comp_pos * share_size
    own_wind = lax.dynamic_slice_in_dim(tile_wind, first_point, share_size)
    own_turn = lax.dynamic_slice_in_dim(tile_turn, first_point, share_size)
    result = source_terms(
        point_field, own_wind, own_turn, growth, damping, coupling, lookup, spread
    )
    returned_field = lax.all_to_all(result, "comp", split_axis=0, concat_axis=1, tiled=True)
    return returned_field.reshape(local_comps, row_count, col_count)


BLOCK = 128
GROUP = 24
EARLY = 40
BATCH = 4
CELL_CHUNKS = 4
MIB = 1024 * 1024
VMEM_MIB = 60
EDGE = 2
SEA, OPEN_EAST, FLOW_EAST, OPEN_NORTH, FLOW_NORTH, HALF_SEA, WIND, TURN = range(8)
KEEP, SPILL, IS_SEA = BLOCK, 2 * BLOCK, 2 * BLOCK


def upwind(courant, total, slope, bend_here, bend_ahead):
    bend = jnp.where(courant > 0.0, bend_here, bend_ahead)
    return courant * ((total - bend) - courant * (slope - courant * bend))


def pick_lanes(block, index):
    return jnp.take_along_axis(block, index, axis=1, mode="promise_in_bounds")


def tile_at(tile):
    return pl.ds(pl.multiple_of(tile * BLOCK, BLOCK), BLOCK)


def has(code, flag):
    return jnp.bitwise_and(code, flag) != 0


def pack_block(blocks, code, tile, out_ref, firsts, held):
    code = jnp.broadcast_to(code, (8, BLOCK))
    index = jnp.bitwise_and(code, BLOCK - 1)
    keep, spill = has(code, KEEP), has(code, SPILL)
    result = []
    for block, first, old in zip(blocks, firsts, held):
        moved = pick_lanes(block, index)
        merged = jnp.where(keep, moved, old)
        out_ref[pl.ds(first, 8), tile_at(tile)] = merged
        result.append(jnp.where(spill, moved, merged))
    return tuple(result)


def prepare_kernel(places, base_ref, speed_ref, sea_ref, east_ref, north_ref, wind_ref, turn_ref, cos_ref, sin_ref,
                   coef_ref, index_ref, place_ref, table_ref, speed_east_ref, speed_north_ref, field_ref, pick_ref):
    first_row, odd, first_freq = base_ref[0], base_ref[1], base_ref[2]
    all_rows, col_count = sea_ref.shape
    row_count = place_ref.shape[1]
    tiles = places // BLOCK
    sea = sea_ref[...].astype(jnp.float32)
    row = lax.broadcasted_iota(jnp.int32, sea.shape, 0)
    col = lax.broadcasted_iota(jnp.int32, sea.shape, 1)

    def next_row(field):
        return jnp.where(row == all_rows - 1, 0.0, pltpu.roll(field, all_rows - 1, 0))

    def next_col(field):
        return jnp.where(col == col_count - 1, 0.0, pltpu.roll(field, col_count - 1, 1))

    open_east, open_north = sea * next_row(sea), sea * next_col(sea)
    east, north = east_ref[...], north_ref[...]
    field_ref[SEA] = sea
    field_ref[OPEN_EAST] = open_east
    field_ref[FLOW_EAST] = open_east * (0.5 * (east + next_row(east)))
    field_ref[OPEN_NORTH] = open_north
    field_ref[FLOW_NORTH] = open_north * (0.5 * (north + next_col(north)))
    field_ref[HALF_SEA] = 0.5 * sea
    field_ref[WIND] = wind_ref[...]
    field_ref[TURN] = turn_ref[...]
    coef_ref[0:EDGE] = jnp.zeros((EDGE, 8, col_count), jnp.float32)
    coef_ref[EDGE + all_rows :] = jnp.zeros((EDGE, 8, col_count), jnp.float32)

    @pl.loop(0, all_rows // 8)
    def _(i):
        rows = field_ref[:, pl.ds(pl.multiple_of(8 * i, 8), 8), :]
        coef_ref[pl.ds(8 * i + EDGE, 8)] = jnp.swapaxes(rows, 0, 1)

    freqs = cos_ref.shape[0] // NTH
    for f in range(freqs):
        circle = slice(f * NTH, (f + 1) * NTH)
        speed_east_ref[circle, :] = cos_ref[circle, :] * speed_ref[first_freq + f]
        speed_north_ref[circle, :] = sin_ref[circle, :] * speed_ref[first_freq + f]

    bf16, f32 = jnp.bfloat16, jnp.float32
    tile_sea = sea_ref[pl.ds(pl.multiple_of(first_row, 8), row_count), :].astype(f32)
    square = (BLOCK, BLOCK)
    down, over = lax.broadcasted_iota(jnp.int32, square, 0), lax.broadcasted_iota(jnp.int32, square, 1)
    before = (down < over).astype(f32).astype(bf16)
    ones = jnp.ones(square, bf16)
    row_square = (row_count, row_count)
    above = lax.broadcasted_iota(jnp.int32, row_square, 1) < lax.broadcasted_iota(jnp.int32, row_square, 0)
    above = above.astype(f32).astype(bf16)
    parts = [tile_sea[:, :BLOCK], tile_sea[:, BLOCK:]]
    numbers = [jnp.dot(p.astype(bf16), ones, preferred_element_type=f32) for p in parts]
    in_row = numbers[0] + numbers[1]
    starts = [jnp.dot(above, in_row.astype(bf16), preferred_element_type=f32)]
    starts.append(starts[0] + numbers[0])
    total = jnp.sum(in_row, axis=0, keepdims=True).astype(jnp.int32)

    def turned_tile(tile):
        return jnp.where(tile >= tiles, tiles, jnp.bitwise_and(tile + odd * (tiles // 2), tiles - 1))

    columns = []
    for h in range(2):
        rank = jnp.dot(parts[h].astype(bf16), before, preferred_element_type=f32).astype(jnp.int32)
        start = starts[h].astype(jnp.int32)
        offset = jnp.bitwise_and(start, BLOCK - 1)
        keep = jnp.where(over[:row_count] >= offset, KEEP, 0)
        slot = jnp.bitwise_and(rank + offset, BLOCK - 1)
        is_sea = parts[h] > 0.0
        place_ref[h] = slot + keep + jnp.where(is_sea, IS_SEA, 0)
        slot = jnp.where(is_sea, slot, -1).astype(f32).T
        from_lane = down[:, :row_count].astype(f32)

        @pl.loop(0, BLOCK // 8)
        def _(i):
            found = []
            for k in range(8):
                lane = (8 * i + k).astype(f32)
                found.append(jnp.sum(jnp.where(slot == lane, from_lane, 0.0), axis=0, keepdims=True))
            pick_ref[pl.ds(pl.multiple_of(8 * i, 8), 8), :] = jnp.concatenate(found, axis=0)

        spill = jnp.where(offset + numbers[h].astype(jnp.int32) >= BLOCK, SPILL, 0)
        index_ref[h] = pick_ref[...].T.astype(jnp.int32) + keep + spill
        columns.append(turned_tile(lax.shift_right_logical(starts[h].T[0:8, :].astype(jnp.int32), 7)))
    row_id = lax.broadcasted_iota(jnp.int32, (8, row_count), 0)
    end_tile = jnp.where(
        jnp.bitwise_and(total, BLOCK - 1) == 0, tiles, turned_tile(lax.shift_right_logical(total, 7))
    )
    end_tile = jnp.broadcast_to(end_tile, (8, BLOCK))
    table_ref[...] = jnp.concatenate([jnp.where(row_id == 0, columns[0], columns[1]), end_tile], axis=1)


def propagate_kernel(part, late, pieces, base_ref, table_ref, energy_ref, halo_ref, coef_ref, index_ref, east_ref,
                     north_ref, *refs):
    refs = list(refs)
    with_fields = part == 0 and late == 0
    fields_ref = None if with_fields else refs.pop(0)
    seam_ref = refs.pop(0) if late else None
    if late:
        refs.pop(0)
    piece_refs = [refs.pop(0) for _ in range(2 * pieces)]
    sum_ref, full_ref = refs.pop(0), refs.pop(0)
    seam_out_ref = refs.pop(0) if late == 0 else None
    fields_out_ref = refs.pop(0) if with_fields else None
    energy_vmem, rows_ref, spread_ref, wide_ref, result_ref, strip_sems, out_sems = refs
    row_count, comp_count, col_count = rows_ref.shape
    strips = comp_count // 8
    sent_rows = piece_refs[0].shape[0]
    cells = result_ref.shape[1]
    first_row = base_ref[0]
    first_comp = pl.multiple_of((part + base_ref[1] * (1 - 2 * part)) * 2 * NTH + (EARLY if late else 0), 8)
    lane = lax.broadcasted_iota(jnp.int32, (8, BLOCK), 1)
    first_lane, last_lane = lane == 0, lane == BLOCK - 1
    third = 1.0 / 3.0

    def arrival(g):
        target = energy_vmem.at[pl.ds(pl.multiple_of(8 * g, 8), 8)]
        source = energy_ref.at[pl.ds(pl.multiple_of(first_comp + 8 * g, 8), 8)]
        return pltpu.make_async_copy(source, target, strip_sems.at[g])

    for g in range(strips):
        arrival(g).start()

    def halves(row):
        return row[:, :BLOCK], row[:, BLOCK:]

    @pl.loop(0, row_count + 2 * EDGE, unroll=4)
    def _(r):
        coef = coef_ref[first_row + r]
        for k in range(HALF_SEA + 1):
            spread_ref[r, k] = jnp.broadcast_to(coef[k : k + 1, :], coef.shape)

    def masked(row, at):
        return tuple(part * sea for part, sea in zip(halves(row), halves(spread_ref[at, SEA])))

    def cell_rows(first, fresh, state, east, north):
        here, ahead, slope_here, bend_here, flux_low = state
        count, sides = len(fresh), range(2)
        level = [here, ahead] + [masked(row, first + k + EDGE) for k, row in enumerate(fresh)]
        rows = range(count)
        coef = [[None] + [halves(spread_ref[first + k, f]) for f in range(1, HALF_SEA + 1)] for k in rows]
        one_right = [[pltpu.roll(part, BLOCK - 1, 1) for part in level[k]] for k in rows]
        right = [
            (jnp.where(last_lane, one[1], one[0]), jnp.where(last_lane, 0.0, one[1])) for one in one_right
        ]
        slope = [[right[k][h] - level[k][h] for h in sides] for k in rows]
        slope_roll = [[pltpu.roll(part, 1, 1) for part in slope[k]] for k in rows]
        bend = [
            (third * (slope[k][0] - jnp.where(first_lane, level[k][0], slope_roll[k][0])),
             third * (slope[k][1] - jnp.where(first_lane, slope_roll[k][0], slope_roll[k][1])))
            for k in rows
        ]
        bend_roll = [[pltpu.roll(part, BLOCK - 1, 1) for part in bend[k]] for k in rows]
        cross = []
        for k in rows:
            bend_right = (jnp.where(last_lane, bend_roll[k][1], bend_roll[k][0]), bend_roll[k][1])
            cross.append([
                upwind(north * coef[k][OPEN_NORTH][h] + coef[k][FLOW_NORTH][h], level[k][h] + right[k][h],
                       slope[k][h], bend[k][h], bend_right[h])
                for h in sides
            ])
        cross_roll = [[pltpu.roll(part, 1, 1) for part in cross[k]] for k in rows]
        slopes = [slope_here] + [tuple(level[k + 1][h] - level[k][h] for h in sides) for k in range(1, count + 1)]
        bends = [bend_here] + [
            tuple(third * (slopes[k][h] - slopes[k - 1][h]) for h in sides) for k in range(1, count + 1)
        ]
        flux = [flux_low]
        for k in rows:
            flux.append(tuple(
                upwind(east * coef[k][OPEN_EAST][h] + coef[k][FLOW_EAST][h], level[k][h] + level[k + 1][h],
                       slopes[k][h], bends[k][h], bends[k + 1][h])
                for h in sides
            ))
        done = []
        for k in rows:
            cross_low = (jnp.where(first_lane, cross_roll[k][1], cross_roll[k][0]),
                         jnp.where(first_lane, cross_roll[k][0], cross_roll[k][1]))
            done.append([
                coef[k][HALF_SEA][h] * (((level[k][h] + level[k][h]) + (flux[k][h] + cross_low[h]))
                                        - (flux[k + 1][h] + cross[k][h]))
                for h in sides
            ])
        return (level[count], level[count + 1], slopes[count], bends[count], flux[count]), done

    def store_row(row, local, parts):
        for h in range(2):
            rows_ref[row, local, h * BLOCK : (h + 1) * BLOCK] = parts[h]

    @pl.loop(0, strips)
    def _(g):
        arrival(g).wait()
        local = pl.ds(pl.multiple_of(g * 8, 8), 8)
        comps = pl.ds(pl.multiple_of(first_comp + g * 8, 8), 8)
        east, north = east_ref[comps, :], north_ref[comps, :]
        zero = (jnp.zeros((8, BLOCK), jnp.float32),) * 2
        here, ahead = masked(halo_ref[comps, 0, :], 0), masked(halo_ref[comps, 1, :], 1)
        state = (here, ahead, tuple(b - a for a, b in zip(here, ahead)), zero, zero)

        def eight(i, state):
            block = jnp.swapaxes(energy_vmem[local, pl.ds(pl.multiple_of(8 * i, 8), 8), :], 0, 1)
            for first in range(0, 8, BATCH):
                fresh = [block[first + k] for k in range(BATCH)]
                state, done = cell_rows(8 * i + first, fresh, state, east, north)
                for k in range(BATCH):
                    store_row(jnp.maximum(8 * i + first + k - EDGE, 0), local, done[k])
            return state

        state = lax.fori_loop(0, row_count // 8, eight, state)
        fresh = [halo_ref[comps, k, :] for k in range(EDGE)]
        state, done = cell_rows(row_count, fresh, state, east, north)
        for k in range(EDGE):
            store_row(row_count - EDGE + k, local, done[k])

    group_rows = [8 * n for n in range(strips + with_fields)]

    def pack_eight(i, held):
        codes = [index_ref[h, pl.ds(pl.multiple_of(8 * i, 8), 8), :] for h in range(2)]
        for k in range(8):
            row = 8 * i + k
            for h in range(2):
                lanes = slice(h * BLOCK, (h + 1) * BLOCK)
                blocks = [rows_ref[row, 8 * n : 8 * n + 8, lanes] for n in range(strips)]
                if with_fields:
                    blocks.append(coef_ref[first_row + EDGE + row, :, lanes])
                held = pack_block(blocks, codes[h][k : k + 1, :], table_ref[h, row], wide_ref, group_rows, held)
        return held

    empty = (jnp.zeros((8, BLOCK), jnp.float32),) * len(group_rows)
    held = lax.fori_loop(0, row_count // 8, pack_eight, empty)
    for first, block in zip(group_rows, held):
        wide_ref[pl.ds(first, 8), tile_at(table_ref[0, row_count])] = block
    if with_fields:
        fields_out_ref[...] = wide_ref[comp_count:, :cells]

    tile_width = 2 * BLOCK
    height = result_ref.shape[0]
    comp_row = lax.broadcasted_iota(jnp.int32, (height, tile_width), 0)
    starts = {0: [0], 1: [height - NTH], None: [0, NTH]}[late]
    mixed = {0: slice(height - 8, height), 1: slice(0, 8), None: slice(0, 0)}[late]
    in_circle = (comp_row[:8] + mixed.start >= starts[0]) & (comp_row[:8] + mixed.start < starts[0] + NTH)

    @pl.loop(0, cells // tile_width, unroll=2)
    def _(i):
        source = pl.ds(pl.multiple_of(i * tile_width, tile_width), tile_width)
        level = wide_ref[:comp_count, source]
        if late:
            level = jnp.concatenate([seam_ref[:, source], level], axis=0)
        if with_fields:
            rate = wide_ref[comp_count + TURN : comp_count + TURN + 1, source]
        else:
            rate = fields_ref[TURN : TURN + 1, source]
        forward = jnp.maximum(rate, 0.0)
        backward = jnp.minimum(rate, 0.0)
        stay = (1.0 - forward) + backward
        above = pltpu.roll(level, height - 1, 0)
        below = pltpu.roll(level, 1, 0)

        def with_row(rolled, row, value):
            tile = slice(row - row % 8, row - row % 8 + 8)
            fixed = jnp.where(comp_row[tile] == row, value, rolled[tile])
            parts = [rolled[: tile.start], fixed, rolled[tile.stop :]]
            return jnp.concatenate([part for part in parts if part.shape[0]], axis=0)

        for start in starts:
            end = start + NTH - 1
            above = with_row(above, end, level[start : start + 1, :])
            below = with_row(below, start, level[end : end + 1, :])
        turned = stay * level - backward * above + forward * below
        partial = jnp.zeros((8, tile_width), jnp.float32)
        for first in range(0, height, 8):
            rows = slice(first, first + 8)
            if rows == mixed:
                result_ref[rows, source] = jnp.where(in_circle, turned[rows], level[rows])
                partial += jnp.where(in_circle, turned[rows], 0.0)
            else:
                result_ref[rows, source] = turned[rows]
                partial += turned[rows]
        sum_ref[:, source] = jnp.sum(partial, axis=0, keepdims=True)

    if late == 0:
        seam_out_ref[...] = result_ref[sent_rows:, :]
    width = cells // (2 * pieces)
    copies = []
    for n, piece in enumerate(piece_refs):
        source = result_ref.at[:sent_rows, n * width : (n + 1) * width]
        copies.append(pltpu.make_async_copy(source, piece, out_sems.at[n]))
    rows = pl.ds(EARLY - 8 if late else 0, sent_rows)
    copies.append(pltpu.make_async_copy(result_ref.at[:sent_rows, :], full_ref.at[rows, :], out_sems.at[2 * pieces]))
    for copy in copies:
        copy.start()
    for copy in copies:
        copy.wait()


def interact_kernel(counts, table_ref, spread_ref, coupling_ref, *refs):
    own_ref, back_0_ref, back_1_ref, delta_ref = refs[sum(counts) :]
    window = []
    for j, count in enumerate(counts):
        first = sum(counts[:j])
        parts = [ref[...] for ref in refs[first : first + count]]
        window.append(parts[0] if count == 1 else jnp.concatenate(parts, axis=0))
    comps = window[0].shape[0]
    for j in range(1, 7):
        level = window[j]
        around = jnp.concatenate([window[j - 1], level, window[j + 1]], axis=0).astype(jnp.bfloat16)
        partner = jnp.dot(table_ref[j - 1], around, preferred_element_type=jnp.float32)
        rate = coupling_ref[(j - 1) * comps : j * comps, :] * level
        plus_part = weight_plus * level
        minus_part = weight_minus * level
        deltas = []
        for pair in range(2):
            plus = partner[2 * pair * comps : (2 * pair + 1) * comps, :]
            minus = partner[(2 * pair + 1) * comps : (2 * pair + 2) * comps, :]
            deltas.append(rate * (plus * (plus_part - (2.0 * weight_cross) * minus) + minus_part * minus))
        both = jnp.concatenate(deltas, axis=0).astype(jnp.bfloat16)
        delta_ref[(j - 1) * 2 * comps : j * 2 * comps, :] = both
        if 2 <= j <= 5:
            part = -2.0 * (deltas[0] + deltas[1])
            if j <= 3:
                own_ref[(j - 2) * comps : (j - 1) * comps, :] = part
            elif j == 4:
                back_1_ref[...] = part
            else:
                back_0_ref[...] = part
    spread = jnp.dot(spread_ref[...], delta_ref[...], preferred_element_type=jnp.float32)
    own_ref[...] += spread[: 2 * comps, :]
    back_1_ref[...] += spread[2 * comps : 3 * comps, :]
    back_0_ref[...] += spread[3 * comps :, :]


def finish_kernel(chunks, base_ref, table_ref, place_ref, mean_ref, fields_ref, growth_ref, damping_ref, *refs):
    turned_ref, own, back = refs[0], refs[1 : 1 + chunks], refs[1 + chunks : 1 + 2 * chunks]
    out_ref, wide_ref = refs[-2], refs[-1]
    width = own[0].shape[1]
    tiles = wide_ref.shape[1] // BLOCK
    tile_width = 2 * BLOCK
    growth = jnp.broadcast_to(growth_ref[...], (GROUP, tile_width))
    damping = jnp.broadcast_to(damping_ref[...], (GROUP, tile_width))
    for o in range(2 * chunks):
        extra = own[o] if o < chunks else back[o - chunks]

        @pl.loop(0, width // tile_width, unroll=2)
        def _(i):
            source = pl.ds(pl.multiple_of(i * tile_width, tile_width), tile_width)
            target = pl.ds(pl.multiple_of(o * width + i * tile_width, tile_width), tile_width)
            scale = 1.0 + growth * fields_ref[WIND : WIND + 1, target] - damping * mean_ref[0:1, target]
            wide_ref[:, target] = turned_ref[:, target] * scale + extra[:, source]

    @pl.loop(0, out_ref.shape[1] // 8)
    def _(i):
        codes = [place_ref[h, pl.ds(pl.multiple_of(8 * i, 8), 8), :] for h in range(2)]
        done = [[] for _ in range(GROUP // 8)]
        for r in range(8):
            parts = [[] for _ in range(GROUP // 8)]
            for h in range(2):
                code = jnp.broadcast_to(codes[h][r : r + 1, :], (8, BLOCK))
                index = jnp.bitwise_and(code, BLOCK - 1)
                keep, is_sea = has(code, KEEP), has(code, IS_SEA)
                tile = table_ref[h, 8 * i + r]
                first, second = jnp.minimum(tile, tiles - 1), jnp.bitwise_and(tile + 1, tiles - 1)
                for k in range(GROUP // 8):
                    rows = slice(8 * k, 8 * k + 8)
                    near = jnp.where(keep, wide_ref[rows, tile_at(first)], wide_ref[rows, tile_at(second)])
                    parts[k].append(jnp.where(is_sea, pick_lanes(near, index), 0.0))
            for k in range(GROUP // 8):
                done[k].append(jnp.concatenate(parts[k], axis=1))
        for k in range(GROUP // 8):
            out_ref[8 * k : 8 * k + 8, pl.ds(pl.multiple_of(8 * i, 8), 8), :] = jnp.swapaxes(jnp.stack(done[k]), 0, 1)


def params(limit):
    return pltpu.CompilerParams(vmem_limit_bytes=limit * MIB)


def after(value, *others):
    return lax.optimization_barrier((value,) + others)[0]


def packed_shards(energy, sea_mask, current_u, current_v, wind_forcing, refraction, group_speed, growth, damping,
                  coupling, dia_index):
    comp_count = lax.axis_size("comp")
    comp_pos = lax.axis_index("comp")
    tile_pos = lax.axis_index("tile")
    odd = lax.rem(comp_pos, 2)
    pair_pos = comp_pos // 2
    local_comps, row_count, col_count = energy.shape
    comps = local_comps // 2
    comp_total = NTH * NF
    first_row = tile_pos * row_count
    first_comp = comp_pos * local_comps
    cells = row_count * col_count // 2
    half = cells // 2
    width = half // CELL_CHUNKS
    f32, i32 = jnp.float32, jnp.int32
    base = jnp.stack([first_row, odd, comp_pos * (local_comps // NTH)]).astype(i32)

    edge_first = jnp.where(tile_pos == 0, row_count - EDGE, 0)
    edge_rows = lax.dynamic_slice_in_dim(energy, edge_first, EDGE, axis=1)
    halo_rows = lax.ppermute(edge_rows, "tile", [(0, 1), (1, 0)])

    all_rows = sea_mask.shape[0]
    angles = np.float32(2.0 * math.pi / NTH) * (np.arange(local_comps) % NTH).astype(np.float32)
    cosines = np.broadcast_to(np.cos(angles)[:, None], (local_comps, BLOCK)).astype(np.float32)
    sines = np.broadcast_to(np.sin(angles)[:, None], (local_comps, BLOCK)).astype(np.float32)
    vmem = pl.BlockSpec(memory_space=pltpu.VMEM)
    coef, index, place, table, speed_east, speed_north = pl.pallas_call(
        functools.partial(prepare_kernel, cells),
        grid_spec=pltpu.PrefetchScalarGridSpec(
            num_scalar_prefetch=2,
            grid=(),
            in_specs=[vmem] * 7,
            out_specs=[vmem] * 6,
            scratch_shapes=[pltpu.VMEM((8, all_rows, col_count), f32), pltpu.VMEM((BLOCK, row_count), f32)],
        ),
        out_shape=[
            jax.ShapeDtypeStruct((all_rows + 2 * EDGE, 8, col_count), f32),
            jax.ShapeDtypeStruct((2, row_count, BLOCK), i32),
            jax.ShapeDtypeStruct((2, row_count, BLOCK), i32),
            jax.ShapeDtypeStruct((8, 2 * BLOCK), i32),
            jax.ShapeDtypeStruct((local_comps, BLOCK), f32),
            jax.ShapeDtypeStruct((local_comps, BLOCK), f32),
        ],
        name="prepare",
        compiler_params=params(VMEM_MIB),
    )(base, group_speed, sea_mask, current_u, current_v, wind_forcing, refraction, cosines, sines)
    steps = comps // GROUP

    def group_at(part, base_ref):
        return (part + base_ref[1] * (1 - 2 * part)) * steps

    def whole(shape):
        return pl.BlockSpec(shape, lambda s, b, t: (0,) * len(shape))

    def column(part, lanes):
        return pl.BlockSpec((GROUP, lanes), lambda s, b, t: (group_at(part, b) + s, 0))

    def propagate(part, late, table, fields=None, seam=None, full=None):
        pieces = CELL_CHUNKS if part else 1
        comp_rows = {0: EARLY, 1: comps - EARLY, None: comps}[late]
        sent_rows = {0: EARLY - 8, 1: comps - EARLY + 8, None: comps}[late]
        height = comps if late is None else EARLY
        anywhere = pl.BlockSpec(memory_space=pl.ANY)
        with_fields = fields is None
        inputs = [energy, halo_rows, coef, index, speed_east, speed_north]
        in_specs = [anywhere] + [vmem] * 5
        aliases = {}
        if not with_fields:
            inputs.append(fields)
            in_specs.append(vmem)
        if late:
            inputs += [seam, full]
            in_specs += [vmem, anywhere]
            aliases = {len(inputs) + 1: 2 * pieces + 1}
        shapes = [(sent_rows, half // pieces)] * (2 * pieces) + [(1, cells), (comps, cells)]
        out_specs = [anywhere] * (2 * pieces) + [vmem, anywhere]
        if late == 0:
            shapes.append((8, cells))
            out_specs.append(vmem)
        if with_fields:
            shapes.append((8, cells))
            out_specs.append(vmem)
        outs = pl.pallas_call(
            functools.partial(propagate_kernel, part, late, pieces),
            grid_spec=pltpu.PrefetchScalarGridSpec(
                num_scalar_prefetch=2,
                grid=(),
                in_specs=in_specs,
                out_specs=out_specs,
                scratch_shapes=[
                    pltpu.VMEM((comp_rows, row_count, col_count), f32),
                    pltpu.VMEM((row_count, comp_rows, col_count), f32),
                    pltpu.VMEM((row_count + 2 * EDGE, HALF_SEA + 1, 8, col_count), f32),
                    pltpu.VMEM((comp_rows + (8 if with_fields else 0), cells + BLOCK), f32),
                    pltpu.VMEM((height, cells), f32),
                    pltpu.SemaphoreType.DMA((comp_rows // 8,)),
                    pltpu.SemaphoreType.DMA((2 * pieces + 1,)),
                ],
            ),
            out_shape=[jax.ShapeDtypeStruct(shape, f32) for shape in shapes],
            input_output_aliases=aliases,
            name={0: "propagate_early", 1: "propagate_late", None: "propagate_whole"}[late],
            compiler_params=params(VMEM_MIB),
            cost_estimate=pl.CostEstimate(
                flops=60 * comp_rows * row_count * col_count, bytes_accessed=60 * MIB, transcendentals=0,
            ),
        )(base, table, *inputs)
        return list(outs[:pieces]), list(outs[pieces : 2 * pieces]), outs[2 * pieces :]

    pairs = [(i, i ^ 1) for i in range(comp_count)]
    apart = [(i, i - 2 if i % 2 == 0 else i + 2) for i in range(comp_count)]
    apart = [(a, b) for a, b in apart if 0 <= b < comp_count]
    across = [(b, a) for a, b in apart]
    chunk_range = range(CELL_CHUNKS)

    def send(pieces, route, waits):
        return [lax.ppermute(after(piece, *wait), "comp", route) for piece, wait in zip(pieces, waits)]

    stages = [(0, 0), (0, 1), (1, None)]
    kept, sent, got, from_own, from_got, level_sums, full = {}, {}, {}, {}, {}, [], {}
    fields = seam = before = None
    part_table = table
    for stage in stages:
        part, late = stage
        kept[stage], sent[stage], extra = propagate(part, late, part_table, fields, seam, full.get(part))
        level_sums.append(extra[0])
        full[part] = extra[1]
        seam = extra[2] if late == 0 else None
        fields = extra[3] if fields is None else fields
        if stage == stages[-1]:
            break
        got[stage] = send(sent[stage], pairs, [[]])
        from_own[stage] = send(kept[stage], apart, [[]])
        waits = [from_got[before][0]] if before is not None else []
        from_got[stage] = send(got[stage], across, [waits])
        done = [extra[0]]
        if before is not None:
            done.append(got[before][0])
        part_table = after(table, *done)
        before = stage
    packed_fields = fields
    sums_0 = level_sums[0]

    sums = level_sums[0] + level_sums[1] + level_sums[2]
    partner_sums = lax.ppermute(sums, "comp", pairs)
    partner_sums = jnp.roll(partner_sums, half, axis=1)
    last, got_1, from_own_1 = stages[-1], [], []
    for c in chunk_range:
        waits = [got[before][0]] + ([got_1[c - 2]] if c >= 2 else []) + ([partner_sums] if c == 2 else [])
        got_1.append(lax.ppermute(after(sent[last][c], *waits), "comp", pairs))
        from_own_1.append(lax.ppermute(after(kept[last][c], from_own[before][0]), "comp", apart))
    got[last], from_own[last], from_got[last] = got_1, from_own_1, []
    sums = sums + partner_sums
    sums = sums_two = sums + lax.ppermute(sums, "comp", [(i, i ^ 2) for i in range(comp_count)])
    sums = sums + lax.ppermute(sums, "comp", [(i, i ^ 4) for i in range(comp_count)])
    mean_level = sums / comp_total

    dia_index, coupling, growth, damping, late_odd, late_pair, _ = lax.optimization_barrier(
        (dia_index, coupling, growth, damping, odd, pair_pos, sums_0)
    )
    own_growth = lax.dynamic_slice_in_dim(growth, first_comp, local_comps)[:, None]
    own_damping = lax.dynamic_slice_in_dim(damping, first_comp, local_comps)[:, None]
    chunk_first = [
        NTH * jnp.where(late_odd > 0, 8 * late_pair + 10 - 2 * j, 8 * late_pair - 4 + 2 * j) for j in range(8)
    ]
    margin = 8 * NTH
    dia_pad = jnp.pad(dia_index, ((0, 0), (margin, margin)), constant_values=-1)
    coupling_pad = jnp.pad(coupling, (margin, margin))
    own_ids = jnp.arange(comps)
    targets, rates = [], []
    for j in range(1, 7):
        targets.append(lax.dynamic_slice(dia_pad, (0, chunk_first[j] + margin), (4, comps)))
        rates.append(lax.dynamic_slice_in_dim(coupling_pad, chunk_first[j] + margin, comps))
    lookup = []
    for j in range(1, 7):
        ids = jnp.concatenate([chunk_first[j + d] + own_ids for d in (-1, 0, 1)])
        lookup.append((targets[j - 1].reshape(4 * comps)[:, None] == ids[None, :]).astype(jnp.bfloat16))
    lookup = jnp.stack(lookup)
    out_ids = jnp.concatenate([chunk_first[j] + own_ids for j in range(2, 6)])
    spread = []
    for j in range(1, 7):
        for pair in range(2):
            hits = [
                (out_ids[:, None] == targets[j - 1][2 * pair + q][None, :]).astype(f32) for q in range(2)
            ]
            spread.append(hits[0] + hits[1])
    spread = jnp.concatenate(spread, axis=1).astype(jnp.bfloat16)
    rates = jnp.concatenate(rates)[:, None]

    lanes = 512 if width % 512 == 0 else width
    own_parts, parts_0, parts_1 = [], [], []
    groups = [(from_got, 1), (from_got, 0), (kept, 0), (kept, 1), (got, 1), (got, 0), (from_own, 0), (from_own, 1)]
    for c in chunk_range:
        waits = [from_got[before][0], from_own_1[c]] + ([from_got[last][c - 2]] if c >= 2 else [])
        from_got[last].append(lax.ppermute(after(got_1[c], *waits), "comp", across))
        levels, level_specs, counts = [], [], []
        for group, part in groups:
            counts.append(1 if part else 2)
            for late in [None] if part else [0, 1]:
                pieces = group[part, late]
                single = len(pieces) == 1
                levels.append(pieces[0 if single else c])
                skipped = c * (width // lanes) if single else 0
                level_specs.append(
                    pl.BlockSpec((levels[-1].shape[0], lanes), functools.partial(lambda n, s: (0, n + s), skipped))
                )
        own_part, part_0, part_1 = pl.pallas_call(
            functools.partial(interact_kernel, tuple(counts)),
            grid=(width // lanes,),
            in_specs=[
                pl.BlockSpec(lookup.shape, lambda s: (0, 0, 0)),
                pl.BlockSpec(spread.shape, lambda s: (0, 0)),
                pl.BlockSpec(rates.shape, lambda s: (0, 0)),
            ] + level_specs,
            out_specs=[pl.BlockSpec((n * comps, lanes), lambda s: (0, s)) for n in (2, 1, 1)],
            out_shape=[jax.ShapeDtypeStruct((n * comps, width), f32) for n in (2, 1, 1)],
            scratch_shapes=[pltpu.VMEM((12 * comps, lanes), jnp.bfloat16)],
            name="interact_cells",
            compiler_params=params(VMEM_MIB),
            cost_estimate=pl.CostEstimate(
                flops=2 * width * comps * comps * (6 * 12 + 48),
                bytes_accessed=20 * MIB, transcendentals=0,
            ),
        )(lookup, spread, rates, *levels)
        own_parts.append(own_part)
        parts_0.append(part_0)
        parts_1.append(part_1)

    def send_back(piece, *waits):
        return lax.ppermute(after(piece, *waits), "comp", pairs)

    back = [[None] * CELL_CHUNKS for _ in range(2)]
    back[0][0] = send_back(parts_0[0], got_1[2], sums_two)
    back[1][0] = send_back(parts_1[0], got_1[3])
    back[0][1] = send_back(parts_0[1], back[0][0], sums)
    back[0][2] = send_back(parts_0[2], back[1][0])
    back[0][3] = send_back(parts_0[3], back[0][1])
    for c in range(1, CELL_CHUNKS):
        back[1][c] = send_back(parts_1[c], back[0][2])

    def finish(part, so_far):
        piece = pl.BlockSpec((GROUP, width), lambda s, b, t: (s, 0))
        own_piece = pl.BlockSpec((GROUP, width), lambda s, b, t: (part * steps + s, 0))
        inputs = [place, mean_level, packed_fields, own_growth, own_damping]
        specs = [whole(place.shape), whole(mean_level.shape), whole(packed_fields.shape), column(part, 1),
                 column(part, 1)]
        inputs += [full[part]] + own_parts + back[part]
        specs.append(pl.BlockSpec((GROUP, cells), lambda s, b, t: (s, 0)))
        specs += [own_piece] * CELL_CHUNKS + [piece] * CELL_CHUNKS
        aliases = {}
        if so_far is not None:
            inputs.append(so_far)
            specs.append(pl.BlockSpec(memory_space=pl.ANY))
            aliases = {len(inputs) + 1: 0}
        return pl.pallas_call(
            functools.partial(finish_kernel, CELL_CHUNKS),
            grid_spec=pltpu.PrefetchScalarGridSpec(
                num_scalar_prefetch=2,
                grid=(steps,),
                in_specs=specs,
                out_specs=pl.BlockSpec((GROUP, row_count, col_count), lambda s, b, t: (group_at(part, b) + s, 0, 0)),
                scratch_shapes=[pltpu.VMEM((GROUP, cells), f32)],
            ),
            out_shape=jax.ShapeDtypeStruct(energy.shape, f32),
            input_output_aliases=aliases,
            name="finish_chunk",
            compiler_params=params(VMEM_MIB),
            cost_estimate=pl.CostEstimate(
                flops=20 * comps * row_count * col_count,
                bytes_accessed=100 * MIB, transcendentals=0,
            ),
        )(base, table, *inputs)

    return finish(1, finish(0, None))


def choose_shards(energy, *rest):
    local_comps, row_count, col_count = energy.shape
    fits = (
        local_comps == 4 * NTH and lax.axis_size("comp") == 8 and local_comps * 8 == NTH * NF
        and lax.axis_size("tile") == 2 and row_count == BLOCK and col_count == 2 * BLOCK
    )
    return packed_shards(energy, *rest) if fits else shards(energy, *rest)


def solution(mesh):
    placed = (
        P("comp", ("grp", "tile"), None),
        P("grp", None),
        P("grp", None),
        P("grp", None),
        P("grp", None),
        P("grp", None),
        P(),
        P(),
        P(),
        P(),
        P(),
    )
    return jax.shard_map(
        choose_shards,
        mesh=mesh,
        in_specs=placed,
        out_specs=P("comp", ("grp", "tile"), None),
        check_vma=False,
    )
```

```python
import functools
import math

import jax
import jax.numpy as jnp
import numpy as np
from jax import lax
from jax.experimental import pallas as pl
from jax.experimental.pallas import tpu as pltpu
from jax.sharding import PartitionSpec as P

NTH = 36
NF = 32


weight_plus = 0.4096
weight_minus = 3.1605
weight_cross = 1.2945


def with_halo(block, sides, width):
    for axis, dim in sides:
        count = lax.axis_size(axis)
        forward = [(i, i + 1) for i in range(count - 1)]
        backward = [(target, source) for source, target in forward]
        low = lax.ppermute(
            lax.slice_in_dim(block, block.shape[dim] - width, None, axis=dim), axis, forward
        )
        high = lax.ppermute(lax.slice_in_dim(block, 0, width, axis=dim), axis, backward)
        block = jnp.concatenate([low, block, high], axis=dim)
    return block


def quick_flux(far_left, left_cell, right_cell, far_right, courant):
    centre = 0.5 * (left_cell + right_cell) - 0.5 * courant * (right_cell - left_cell)
    curvature = (1.0 - courant * courant) / 6.0
    upward = centre - curvature * (right_cell - 2.0 * left_cell + far_left)
    downward = centre - curvature * (left_cell - 2.0 * right_cell + far_right)
    return courant * jnp.where(courant > 0.0, upward, downward)


def flux_change(padded, speed, current, sea_pad, axis):
    cell_count = padded.shape[axis] - 4

    def take_part(source, first, which_axis):
        return lax.slice_in_dim(source, first, first + cell_count + 1, axis=which_axis)

    face_current = 0.5 * (take_part(current, 0, axis - 1) + take_part(current, 1, axis - 1))
    courant = speed[:, None, None] + face_current[None]
    open_face = (take_part(sea_pad, 0, axis - 1) * take_part(sea_pad, 1, axis - 1))[None]
    face_flux = (
        quick_flux(
            take_part(padded, 0, axis),
            take_part(padded, 1, axis),
            take_part(padded, 2, axis),
            take_part(padded, 3, axis),
            courant,
        )
        * open_face
    )
    return lax.slice_in_dim(face_flux, 1, cell_count + 1, axis=axis) - lax.slice_in_dim(
        face_flux, 0, cell_count, axis=axis
    )


def source_terms(energy_block, wind, turning, growth, damping, coupling, lookup, spread):
    cell_count = energy_block.shape[1]
    spectrum = energy_block.reshape(NF, NTH, cell_count)
    turn_rate = turning[None, None, :]
    next_dir = jnp.roll(spectrum, -1, axis=1)
    forward = jnp.maximum(turn_rate, 0.0)
    backward = jnp.minimum(turn_rate, 0.0)
    upper_flux = forward * spectrum + backward * next_dir
    lower_flux = jnp.roll(upper_flux, 1, axis=1)
    turned = (spectrum - upper_flux + lower_flux).reshape(energy_block.shape)
    rounded = turned.astype(jnp.bfloat16)
    plus_first, minus_first, plus_second, minus_second = lookup(rounded)
    couple_rate = coupling[:, None]
    delta_first = couple_rate * (
        turned * turned * (weight_plus * plus_first + weight_minus * minus_first)
        - 2.0 * weight_cross * turned * plus_first * minus_first
    )
    delta_second = couple_rate * (
        turned * turned * (weight_plus * plus_second + weight_minus * minus_second)
        - 2.0 * weight_cross * turned * plus_second * minus_second
    )
    moved = spread(delta_first.astype(jnp.bfloat16), delta_second.astype(jnp.bfloat16))
    mean_level = jnp.sum(turned, axis=0) / energy_block.shape[0]
    return (
        turned
        + growth[:, None] * wind[None] * turned
        - damping[:, None] * mean_level[None] * turned
        - 2.0 * (delta_first + delta_second)
        + moved
    )


def shards(
    energy,
    sea_mask,
    current_u,
    current_v,
    wind_forcing,
    refraction,
    group_speed,
    growth,
    damping,
    coupling,
    dia_index,
):
    comp_count = lax.axis_size("comp")
    comp_pos = lax.axis_index("comp")
    tile_pos = lax.axis_index("tile")
    local_comps, row_count, col_count = energy.shape
    first_row = tile_pos * row_count
    first_comp = comp_pos * local_comps
    comp_total = NTH * NF
    angles = 2.0 * math.pi / NTH * (jnp.arange(comp_total) % NTH).astype(jnp.float32)
    speeds = jnp.repeat(group_speed, NTH)
    speed_east = lax.dynamic_slice_in_dim(speeds * jnp.cos(angles), first_comp, local_comps)
    speed_north = lax.dynamic_slice_in_dim(speeds * jnp.sin(angles), first_comp, local_comps)
    window = (row_count + 2, col_count + 2)
    sea_pad = lax.dynamic_slice(jnp.pad(sea_mask.astype(jnp.float32), 1), (first_row, 0), window)
    east_pad = lax.dynamic_slice(jnp.pad(current_u, 1), (first_row, 0), window)
    north_pad = lax.dynamic_slice(jnp.pad(current_v, 1), (first_row, 0), window)
    sea_tile = sea_pad[1:-1, 1:-1]
    masked = energy * sea_tile[None]
    padded_east = with_halo(masked, (("tile", 1),), 2)
    along_east = flux_change(padded_east, speed_east, east_pad[:, 1:-1], sea_pad[:, 1:-1], 1)
    along_north = flux_change(
        jnp.pad(masked, ((0, 0), (0, 0), (2, 2))),
        speed_north,
        north_pad[1:-1, :],
        sea_pad[1:-1, :],
        2,
    )
    propagated = (sea_tile[None] * (masked - along_east - along_north)).reshape(
        local_comps, row_count * col_count
    )
    tile_wind = lax.dynamic_slice(wind_forcing, (first_row, 0), (row_count, col_count)).reshape(-1)
    tile_turn = lax.dynamic_slice(refraction, (first_row, 0), (row_count, col_count)).reshape(-1)
    comp_ids = jnp.arange(comp_total)
    tables = [
        (dia_index[slot_row][:, None] == comp_ids[None, :]).astype(jnp.bfloat16)
        for slot_row in range(4)
    ]

    def lookup(rounded):
        return tuple(
            (
                jnp.dot(tables[slot_row], rounded, preferred_element_type=jnp.float32)
                for slot_row in range(4)
            )
        )

    def scatter_back(table, terms):
        return lax.dot_general(
            table, terms, (((0,), (0,)), ((), ())), preferred_element_type=jnp.float32
        )

    def spread(first_terms, second_terms):
        return (
            scatter_back(tables[0], first_terms)
            + scatter_back(tables[1], first_terms)
            + scatter_back(tables[2], second_terms)
            + scatter_back(tables[3], second_terms)
        )

    share_size = row_count * col_count // comp_count
    point_field = lax.all_to_all(propagated, "comp", split_axis=1, concat_axis=0, tiled=True)
    first_point = comp_pos * share_size
    own_wind = lax.dynamic_slice_in_dim(tile_wind, first_point, share_size)
    own_turn = lax.dynamic_slice_in_dim(tile_turn, first_point, share_size)
    result = source_terms(
        point_field, own_wind, own_turn, growth, damping, coupling, lookup, spread
    )
    returned_field = lax.all_to_all(result, "comp", split_axis=0, concat_axis=1, tiled=True)
    return returned_field.reshape(local_comps, row_count, col_count)


BLOCK = 128
GROUP = 24
EARLY = 40
BATCH = 4
CELL_CHUNKS = 4
MIB = 1024 * 1024
VMEM_MIB = 60
EDGE = 2
SEA, OPEN_EAST, FLOW_EAST, OPEN_NORTH, FLOW_NORTH, HALF_SEA, WIND, TURN = range(8)
KEEP, SPILL, IS_SEA = BLOCK, 2 * BLOCK, 2 * BLOCK


def upwind(courant, total, slope, bend_here, bend_ahead):
    bend = jnp.where(courant > 0.0, bend_here, bend_ahead)
    return courant * ((total - bend) - courant * (slope - courant * bend))


def pick_lanes(block, index):
    return jnp.take_along_axis(block, index, axis=1, mode="promise_in_bounds")


def tile_at(tile):
    return pl.ds(pl.multiple_of(tile * BLOCK, BLOCK), BLOCK)


def has(code, flag):
    return jnp.bitwise_and(code, flag) != 0


def pack_block(blocks, code, tile, out_ref, firsts, held):
    code = jnp.broadcast_to(code, (8, BLOCK))
    index = jnp.bitwise_and(code, BLOCK - 1)
    keep, spill = has(code, KEEP), has(code, SPILL)
    result = []
    for block, first, old in zip(blocks, firsts, held):
        moved = pick_lanes(block, index)
        merged = jnp.where(keep, moved, old)
        out_ref[pl.ds(first, 8), tile_at(tile)] = merged
        result.append(jnp.where(spill, moved, merged))
    return tuple(result)


def prepare_kernel(places, base_ref, speed_ref, sea_ref, east_ref, north_ref, wind_ref, turn_ref, cos_ref, sin_ref,
                   coef_ref, index_ref, place_ref, table_ref, speed_east_ref, speed_north_ref, field_ref, pick_ref):
    first_row, odd, first_freq = base_ref[0], base_ref[1], base_ref[2]
    all_rows, col_count = sea_ref.shape
    row_count = place_ref.shape[1]
    tiles = places // BLOCK
    sea = sea_ref[...].astype(jnp.float32)
    row = lax.broadcasted_iota(jnp.int32, sea.shape, 0)
    col = lax.broadcasted_iota(jnp.int32, sea.shape, 1)

    def next_row(field):
        return jnp.where(row == all_rows - 1, 0.0, pltpu.roll(field, all_rows - 1, 0))

    def next_col(field):
        return jnp.where(col == col_count - 1, 0.0, pltpu.roll(field, col_count - 1, 1))

    open_east, open_north = sea * next_row(sea), sea * next_col(sea)
    east, north = east_ref[...], north_ref[...]
    field_ref[SEA] = sea
    field_ref[OPEN_EAST] = open_east
    field_ref[FLOW_EAST] = open_east * (0.5 * (east + next_row(east)))
    field_ref[OPEN_NORTH] = open_north
    field_ref[FLOW_NORTH] = open_north * (0.5 * (north + next_col(north)))
    field_ref[HALF_SEA] = 0.5 * sea
    field_ref[WIND] = wind_ref[...]
    field_ref[TURN] = turn_ref[...]
    coef_ref[0:EDGE] = jnp.zeros((EDGE, 8, col_count), jnp.float32)
    coef_ref[EDGE + all_rows :] = jnp.zeros((EDGE, 8, col_count), jnp.float32)

    @pl.loop(0, all_rows // 8)
    def _(i):
        rows = field_ref[:, pl.ds(pl.multiple_of(8 * i, 8), 8), :]
        coef_ref[pl.ds(8 * i + EDGE, 8)] = jnp.swapaxes(rows, 0, 1)

    freqs = cos_ref.shape[0] // NTH
    for f in range(freqs):
        circle = slice(f * NTH, (f + 1) * NTH)
        speed_east_ref[circle, :] = cos_ref[circle, :] * speed_ref[first_freq + f]
        speed_north_ref[circle, :] = sin_ref[circle, :] * speed_ref[first_freq + f]

    bf16, f32 = jnp.bfloat16, jnp.float32
    tile_sea = sea_ref[pl.ds(pl.multiple_of(first_row, 8), row_count), :].astype(f32)
    square = (BLOCK, BLOCK)
    down, over = lax.broadcasted_iota(jnp.int32, square, 0), lax.broadcasted_iota(jnp.int32, square, 1)
    before = (down < over).astype(f32).astype(bf16)
    ones = jnp.ones(square, bf16)
    row_square = (row_count, row_count)
    above = lax.broadcasted_iota(jnp.int32, row_square, 1) < lax.broadcasted_iota(jnp.int32, row_square, 0)
    above = above.astype(f32).astype(bf16)
    parts = [tile_sea[:, :BLOCK], tile_sea[:, BLOCK:]]
    numbers = [jnp.dot(p.astype(bf16), ones, preferred_element_type=f32) for p in parts]
    in_row = numbers[0] + numbers[1]
    starts = [jnp.dot(above, in_row.astype(bf16), preferred_element_type=f32)]
    starts.append(starts[0] + numbers[0])
    total = jnp.sum(in_row, axis=0, keepdims=True).astype(jnp.int32)

    def turned_tile(tile):
        return jnp.where(tile >= tiles, tiles, jnp.bitwise_and(tile + odd * (tiles // 2), tiles - 1))

    columns = []
    for h in range(2):
        rank = jnp.dot(parts[h].astype(bf16), before, preferred_element_type=f32).astype(jnp.int32)
        start = starts[h].astype(jnp.int32)
        offset = jnp.bitwise_and(start, BLOCK - 1)
        keep = jnp.where(over[:row_count] >= offset, KEEP, 0)
        slot = jnp.bitwise_and(rank + offset, BLOCK - 1)
        is_sea = parts[h] > 0.0
        place_ref[h] = slot + keep + jnp.where(is_sea, IS_SEA, 0)
        slot = jnp.where(is_sea, slot, -1).astype(f32).T
        from_lane = down[:, :row_count].astype(f32)

        @pl.loop(0, BLOCK // 8)
        def _(i):
            found = []
            for k in range(8):
                lane = (8 * i + k).astype(f32)
                found.append(jnp.sum(jnp.where(slot == lane, from_lane, 0.0), axis=0, keepdims=True))
            pick_ref[pl.ds(pl.multiple_of(8 * i, 8), 8), :] = jnp.concatenate(found, axis=0)

        spill = jnp.where(offset + numbers[h].astype(jnp.int32) >= BLOCK, SPILL, 0)
        index_ref[h] = pick_ref[...].T.astype(jnp.int32) + keep + spill
        columns.append(turned_tile(lax.shift_right_logical(starts[h].T[0:8, :].astype(jnp.int32), 7)))
    row_id = lax.broadcasted_iota(jnp.int32, (8, row_count), 0)
    end_tile = jnp.where(
        jnp.bitwise_and(total, BLOCK - 1) == 0, tiles, turned_tile(lax.shift_right_logical(total, 7))
    )
    end_tile = jnp.broadcast_to(end_tile, (8, BLOCK))
    table_ref[...] = jnp.concatenate([jnp.where(row_id == 0, columns[0], columns[1]), end_tile], axis=1)


def propagate_kernel(part, late, pieces, base_ref, table_ref, energy_ref, halo_ref, coef_ref, index_ref, east_ref,
                     north_ref, *refs):
    refs = list(refs)
    with_fields = part == 0 and late == 0
    fields_ref = None if with_fields else refs.pop(0)
    seam_ref = refs.pop(0) if late else None
    if late:
        refs.pop(0)
    piece_refs = [refs.pop(0) for _ in range(2 * pieces)]
    sum_ref, full_ref = refs.pop(0), refs.pop(0)
    seam_out_ref = refs.pop(0) if late == 0 else None
    fields_out_ref = refs.pop(0) if with_fields else None
    energy_vmem, rows_ref, spread_ref, wide_ref, result_ref, strip_sems, out_sems = refs
    row_count, comp_count, col_count = rows_ref.shape
    strips = comp_count // 8
    sent_rows = piece_refs[0].shape[0]
    cells = result_ref.shape[1]
    first_row = base_ref[0]
    first_comp = pl.multiple_of((part + base_ref[1] * (1 - 2 * part)) * 2 * NTH + (EARLY if late else 0), 8)
    lane = lax.broadcasted_iota(jnp.int32, (8, BLOCK), 1)
    first_lane, last_lane = lane == 0, lane == BLOCK - 1
    third = 1.0 / 3.0

    def arrival(g):
        target = energy_vmem.at[pl.ds(pl.multiple_of(8 * g, 8), 8)]
        source = energy_ref.at[pl.ds(pl.multiple_of(first_comp + 8 * g, 8), 8)]
        return pltpu.make_async_copy(source, target, strip_sems.at[g])

    for g in range(strips):
        arrival(g).start()

    def halves(row):
        return row[:, :BLOCK], row[:, BLOCK:]

    @pl.loop(0, row_count + 2 * EDGE, unroll=4)
    def _(r):
        coef = coef_ref[first_row + r]
        for k in range(HALF_SEA + 1):
            spread_ref[r, k] = jnp.broadcast_to(coef[k : k + 1, :], coef.shape)

    def masked(row, at):
        return tuple(part * sea for part, sea in zip(halves(row), halves(spread_ref[at, SEA])))

    def cell_rows(first, fresh, state, east, north):
        here, ahead, slope_here, bend_here, flux_low = state
        count, sides = len(fresh), range(2)
        level = [here, ahead] + [masked(row, first + k + EDGE) for k, row in enumerate(fresh)]
        rows = range(count)
        coef = [[None] + [halves(spread_ref[first + k, f]) for f in range(1, HALF_SEA + 1)] for k in rows]
        one_right = [[pltpu.roll(part, BLOCK - 1, 1) for part in level[k]] for k in rows]
        right = [
            (jnp.where(last_lane, one[1], one[0]), jnp.where(last_lane, 0.0, one[1])) for one in one_right
        ]
        slope = [[right[k][h] - level[k][h] for h in sides] for k in rows]
        slope_roll = [[pltpu.roll(part, 1, 1) for part in slope[k]] for k in rows]
        bend = [
            (third * (slope[k][0] - jnp.where(first_lane, level[k][0], slope_roll[k][0])),
             third * (slope[k][1] - jnp.where(first_lane, slope_roll[k][0], slope_roll[k][1])))
            for k in rows
        ]
        bend_roll = [[pltpu.roll(part, BLOCK - 1, 1) for part in bend[k]] for k in rows]
        cross = []
        for k in rows:
            bend_right = (jnp.where(last_lane, bend_roll[k][1], bend_roll[k][0]), bend_roll[k][1])
            cross.append([
                upwind(north * coef[k][OPEN_NORTH][h] + coef[k][FLOW_NORTH][h], level[k][h] + right[k][h],
                       slope[k][h], bend[k][h], bend_right[h])
                for h in sides
            ])
        cross_roll = [[pltpu.roll(part, 1, 1) for part in cross[k]] for k in rows]
        slopes = [slope_here] + [tuple(level[k + 1][h] - level[k][h] for h in sides) for k in range(1, count + 1)]
        bends = [bend_here] + [
            tuple(third * (slopes[k][h] - slopes[k - 1][h]) for h in sides) for k in range(1, count + 1)
        ]
        flux = [flux_low]
        for k in rows:
            flux.append(tuple(
                upwind(east * coef[k][OPEN_EAST][h] + coef[k][FLOW_EAST][h], level[k][h] + level[k + 1][h],
                       slopes[k][h], bends[k][h], bends[k + 1][h])
                for h in sides
            ))
        done = []
        for k in rows:
            cross_low = (jnp.where(first_lane, cross_roll[k][1], cross_roll[k][0]),
                         jnp.where(first_lane, cross_roll[k][0], cross_roll[k][1]))
            done.append([
                coef[k][HALF_SEA][h] * (((level[k][h] + level[k][h]) + (flux[k][h] + cross_low[h]))
                                        - (flux[k + 1][h] + cross[k][h]))
                for h in sides
            ])
        return (level[count], level[count + 1], slopes[count], bends[count], flux[count]), done

    def store_row(row, local, parts):
        for h in range(2):
            rows_ref[row, local, h * BLOCK : (h + 1) * BLOCK] = parts[h]

    @pl.loop(0, strips)
    def _(g):
        arrival(g).wait()
        local = pl.ds(pl.multiple_of(g * 8, 8), 8)
        comps = pl.ds(pl.multiple_of(first_comp + g * 8, 8), 8)
        east, north = east_ref[comps, :], north_ref[comps, :]
        zero = (jnp.zeros((8, BLOCK), jnp.float32),) * 2
        here, ahead = masked(halo_ref[comps, 0, :], 0), masked(halo_ref[comps, 1, :], 1)
        state = (here, ahead, tuple(b - a for a, b in zip(here, ahead)), zero, zero)

        def eight(i, state):
            block = jnp.swapaxes(energy_vmem[local, pl.ds(pl.multiple_of(8 * i, 8), 8), :], 0, 1)
            for first in range(0, 8, BATCH):
                fresh = [block[first + k] for k in range(BATCH)]
                state, done = cell_rows(8 * i + first, fresh, state, east, north)
                for k in range(BATCH):
                    store_row(jnp.maximum(8 * i + first + k - EDGE, 0), local, done[k])
            return state

        state = lax.fori_loop(0, row_count // 8, eight, state)
        fresh = [halo_ref[comps, k, :] for k in range(EDGE)]
        state, done = cell_rows(row_count, fresh, state, east, north)
        for k in range(EDGE):
            store_row(row_count - EDGE + k, local, done[k])

    group_rows = [8 * n for n in range(strips + with_fields)]

    def pack_eight(i, held):
        codes = [index_ref[h, pl.ds(pl.multiple_of(8 * i, 8), 8), :] for h in range(2)]
        for k in range(8):
            row = 8 * i + k
            for h in range(2):
                lanes = slice(h * BLOCK, (h + 1) * BLOCK)
                blocks = [rows_ref[row, 8 * n : 8 * n + 8, lanes] for n in range(strips)]
                if with_fields:
                    blocks.append(coef_ref[first_row + EDGE + row, :, lanes])
                held = pack_block(blocks, codes[h][k : k + 1, :], table_ref[h, row], wide_ref, group_rows, held)
        return held

    empty = (jnp.zeros((8, BLOCK), jnp.float32),) * len(group_rows)
    held = lax.fori_loop(0, row_count // 8, pack_eight, empty)
    for first, block in zip(group_rows, held):
        wide_ref[pl.ds(first, 8), tile_at(table_ref[0, row_count])] = block
    if with_fields:
        fields_out_ref[...] = wide_ref[comp_count:, :cells]

    tile_width = 2 * BLOCK
    height = result_ref.shape[0]
    comp_row = lax.broadcasted_iota(jnp.int32, (height, tile_width), 0)
    starts = {0: [0], 1: [height - NTH], None: [0, NTH]}[late]
    mixed = {0: slice(height - 8, height), 1: slice(0, 8), None: slice(0, 0)}[late]
    in_circle = (comp_row[:8] + mixed.start >= starts[0]) & (comp_row[:8] + mixed.start < starts[0] + NTH)

    @pl.loop(0, cells // tile_width, unroll=2)
    def _(i):
        source = pl.ds(pl.multiple_of(i * tile_width, tile_width), tile_width)
        level = wide_ref[:comp_count, source]
        if late:
            level = jnp.concatenate([seam_ref[:, source], level], axis=0)
        if with_fields:
            rate = wide_ref[comp_count + TURN : comp_count + TURN + 1, source]
        else:
            rate = fields_ref[TURN : TURN + 1, source]
        forward = jnp.maximum(rate, 0.0)
        backward = jnp.minimum(rate, 0.0)
        stay = (1.0 - forward) + backward
        above = pltpu.roll(level, height - 1, 0)
        below = pltpu.roll(level, 1, 0)

        def with_row(rolled, row, value):
            tile = slice(row - row % 8, row - row % 8 + 8)
            fixed = jnp.where(comp_row[tile] == row, value, rolled[tile])
            parts = [rolled[: tile.start], fixed, rolled[tile.stop :]]
            return jnp.concatenate([part for part in parts if part.shape[0]], axis=0)

        for start in starts:
            end = start + NTH - 1
            above = with_row(above, end, level[start : start + 1, :])
            below = with_row(below, start, level[end : end + 1, :])
        turned = stay * level - backward * above + forward * below
        partial = jnp.zeros((8, tile_width), jnp.float32)
        for first in range(0, height, 8):
            rows = slice(first, first + 8)
            if rows == mixed:
                result_ref[rows, source] = jnp.where(in_circle, turned[rows], level[rows])
                partial += jnp.where(in_circle, turned[rows], 0.0)
            else:
                result_ref[rows, source] = turned[rows]
                partial += turned[rows]
        sum_ref[:, source] = jnp.sum(partial, axis=0, keepdims=True)

    if late == 0:
        seam_out_ref[...] = result_ref[sent_rows:, :]
    width = cells // (2 * pieces)
    copies = []
    for n, piece in enumerate(piece_refs):
        source = result_ref.at[:sent_rows, n * width : (n + 1) * width]
        copies.append(pltpu.make_async_copy(source, piece, out_sems.at[n]))
    rows = pl.ds(EARLY - 8 if late else 0, sent_rows)
    copies.append(pltpu.make_async_copy(result_ref.at[:sent_rows, :], full_ref.at[rows, :], out_sems.at[2 * pieces]))
    for copy in copies:
        copy.start()
    for copy in copies:
        copy.wait()


def interact_kernel(counts, table_ref, spread_ref, coupling_ref, *refs):
    own_ref, back_0_ref, back_1_ref, delta_ref = refs[sum(counts) :]
    window = []
    for j, count in enumerate(counts):
        first = sum(counts[:j])
        parts = [ref[...] for ref in refs[first : first + count]]
        window.append(parts[0] if count == 1 else jnp.concatenate(parts, axis=0))
    comps = window[0].shape[0]
    for j in range(1, 7):
        level = window[j]
        around = jnp.concatenate([window[j - 1], level, window[j + 1]], axis=0).astype(jnp.bfloat16)
        partner = jnp.dot(table_ref[j - 1], around, preferred_element_type=jnp.float32)
        rate = coupling_ref[(j - 1) * comps : j * comps, :] * level
        plus_part = weight_plus * level
        minus_part = weight_minus * level
        deltas = []
        for pair in range(2):
            plus = partner[2 * pair * comps : (2 * pair + 1) * comps, :]
            minus = partner[(2 * pair + 1) * comps : (2 * pair + 2) * comps, :]
            deltas.append(rate * (plus * (plus_part - (2.0 * weight_cross) * minus) + minus_part * minus))
        both = jnp.concatenate(deltas, axis=0).astype(jnp.bfloat16)
        delta_ref[(j - 1) * 2 * comps : j * 2 * comps, :] = both
        if 2 <= j <= 5:
            part = -2.0 * (deltas[0] + deltas[1])
            if j <= 3:
                own_ref[(j - 2) * comps : (j - 1) * comps, :] = part
            elif j == 4:
                back_1_ref[...] = part
            else:
                back_0_ref[...] = part
    spread = jnp.dot(spread_ref[...], delta_ref[...], preferred_element_type=jnp.float32)
    own_ref[...] += spread[: 2 * comps, :]
    back_1_ref[...] += spread[2 * comps : 3 * comps, :]
    back_0_ref[...] += spread[3 * comps :, :]


def finish_kernel(chunks, base_ref, table_ref, place_ref, mean_ref, fields_ref, growth_ref, damping_ref, *refs):
    turned_ref, own, back = refs[0], refs[1 : 1 + chunks], refs[1 + chunks : 1 + 2 * chunks]
    out_ref, wide_ref = refs[-2], refs[-1]
    width = own[0].shape[1]
    tiles = wide_ref.shape[1] // BLOCK
    tile_width = 2 * BLOCK
    growth = jnp.broadcast_to(growth_ref[...], (GROUP, tile_width))
    damping = jnp.broadcast_to(damping_ref[...], (GROUP, tile_width))
    for o in range(2 * chunks):
        extra = own[o] if o < chunks else back[o - chunks]

        @pl.loop(0, width // tile_width, unroll=2)
        def _(i):
            source = pl.ds(pl.multiple_of(i * tile_width, tile_width), tile_width)
            target = pl.ds(pl.multiple_of(o * width + i * tile_width, tile_width), tile_width)
            scale = 1.0 + growth * fields_ref[WIND : WIND + 1, target] - damping * mean_ref[0:1, target]
            wide_ref[:, target] = turned_ref[:, target] * scale + extra[:, source]

    @pl.loop(0, out_ref.shape[1] // 8)
    def _(i):
        codes = [place_ref[h, pl.ds(pl.multiple_of(8 * i, 8), 8), :] for h in range(2)]
        done = [[] for _ in range(GROUP // 8)]
        for r in range(8):
            parts = [[] for _ in range(GROUP // 8)]
            for h in range(2):
                code = jnp.broadcast_to(codes[h][r : r + 1, :], (8, BLOCK))
                index = jnp.bitwise_and(code, BLOCK - 1)
                keep, is_sea = has(code, KEEP), has(code, IS_SEA)
                tile = table_ref[h, 8 * i + r]
                first, second = jnp.minimum(tile, tiles - 1), jnp.bitwise_and(tile + 1, tiles - 1)
                for k in range(GROUP // 8):
                    rows = slice(8 * k, 8 * k + 8)
                    near = jnp.where(keep, wide_ref[rows, tile_at(first)], wide_ref[rows, tile_at(second)])
                    parts[k].append(jnp.where(is_sea, pick_lanes(near, index), 0.0))
            for k in range(GROUP // 8):
                done[k].append(jnp.concatenate(parts[k], axis=1))
        for k in range(GROUP // 8):
            out_ref[8 * k : 8 * k + 8, pl.ds(pl.multiple_of(8 * i, 8), 8), :] = jnp.swapaxes(jnp.stack(done[k]), 0, 1)


def params(limit):
    return pltpu.CompilerParams(vmem_limit_bytes=limit * MIB)


def after(value, *others):
    return lax.optimization_barrier((value,) + others)[0]


def packed_shards(energy, sea_mask, current_u, current_v, wind_forcing, refraction, group_speed, growth, damping,
                  coupling, dia_index):
    comp_count = lax.axis_size("comp")
    comp_pos = lax.axis_index("comp")
    tile_pos = lax.axis_index("tile")
    odd = lax.rem(comp_pos, 2)
    pair_pos = comp_pos // 2
    local_comps, row_count, col_count = energy.shape
    comps = local_comps // 2
    comp_total = NTH * NF
    first_row = tile_pos * row_count
    first_comp = comp_pos * local_comps
    cells = row_count * col_count // 2
    half = cells // 2
    width = half // CELL_CHUNKS
    f32, i32 = jnp.float32, jnp.int32
    base = jnp.stack([first_row, odd, comp_pos * (local_comps // NTH)]).astype(i32)

    edge_first = jnp.where(tile_pos == 0, row_count - EDGE, 0)
    edge_rows = lax.dynamic_slice_in_dim(energy, edge_first, EDGE, axis=1)
    halo_rows = lax.ppermute(edge_rows, "tile", [(0, 1), (1, 0)])

    all_rows = sea_mask.shape[0]
    angles = np.float32(2.0 * math.pi / NTH) * (np.arange(local_comps) % NTH).astype(np.float32)
    cosines = np.broadcast_to(np.cos(angles)[:, None], (local_comps, BLOCK)).astype(np.float32)
    sines = np.broadcast_to(np.sin(angles)[:, None], (local_comps, BLOCK)).astype(np.float32)
    vmem = pl.BlockSpec(memory_space=pltpu.VMEM)
    coef, index, place, table, speed_east, speed_north = pl.pallas_call(
        functools.partial(prepare_kernel, cells),
        grid_spec=pltpu.PrefetchScalarGridSpec(
            num_scalar_prefetch=2,
            grid=(),
            in_specs=[vmem] * 7,
            out_specs=[vmem] * 6,
            scratch_shapes=[pltpu.VMEM((8, all_rows, col_count), f32), pltpu.VMEM((BLOCK, row_count), f32)],
        ),
        out_shape=[
            jax.ShapeDtypeStruct((all_rows + 2 * EDGE, 8, col_count), f32),
            jax.ShapeDtypeStruct((2, row_count, BLOCK), i32),
            jax.ShapeDtypeStruct((2, row_count, BLOCK), i32),
            jax.ShapeDtypeStruct((8, 2 * BLOCK), i32),
            jax.ShapeDtypeStruct((local_comps, BLOCK), f32),
            jax.ShapeDtypeStruct((local_comps, BLOCK), f32),
        ],
        name="prepare",
        compiler_params=params(VMEM_MIB),
    )(base, group_speed, sea_mask, current_u, current_v, wind_forcing, refraction, cosines, sines)
    steps = comps // GROUP

    def group_at(part, base_ref):
        return (part + base_ref[1] * (1 - 2 * part)) * steps

    def whole(shape):
        return pl.BlockSpec(shape, lambda s, b, t: (0,) * len(shape))

    def column(part, lanes):
        return pl.BlockSpec((GROUP, lanes), lambda s, b, t: (group_at(part, b) + s, 0))

    def propagate(part, late, table, fields=None, seam=None, full=None):
        pieces = CELL_CHUNKS if part else 1
        comp_rows = {0: EARLY, 1: comps - EARLY, None: comps}[late]
        sent_rows = {0: EARLY - 8, 1: comps - EARLY + 8, None: comps}[late]
        height = comps if late is None else EARLY
        anywhere = pl.BlockSpec(memory_space=pl.ANY)
        with_fields = fields is None
        inputs = [energy, halo_rows, coef, index, speed_east, speed_north]
        in_specs = [anywhere] + [vmem] * 5
        aliases = {}
        if not with_fields:
            inputs.append(fields)
            in_specs.append(vmem)
        if late:
            inputs += [seam, full]
            in_specs += [vmem, anywhere]
            aliases = {len(inputs) + 1: 2 * pieces + 1}
        shapes = [(sent_rows, half // pieces)] * (2 * pieces) + [(1, cells), (comps, cells)]
        out_specs = [anywhere] * (2 * pieces) + [vmem, anywhere]
        if late == 0:
            shapes.append((8, cells))
            out_specs.append(vmem)
        if with_fields:
            shapes.append((8, cells))
            out_specs.append(vmem)
        outs = pl.pallas_call(
            functools.partial(propagate_kernel, part, late, pieces),
            grid_spec=pltpu.PrefetchScalarGridSpec(
                num_scalar_prefetch=2,
                grid=(),
                in_specs=in_specs,
                out_specs=out_specs,
                scratch_shapes=[
                    pltpu.VMEM((comp_rows, row_count, col_count), f32),
                    pltpu.VMEM((row_count, comp_rows, col_count), f32),
                    pltpu.VMEM((row_count + 2 * EDGE, HALF_SEA + 1, 8, col_count), f32),
                    pltpu.VMEM((comp_rows + (8 if with_fields else 0), cells + BLOCK), f32),
                    pltpu.VMEM((height, cells), f32),
                    pltpu.SemaphoreType.DMA((comp_rows // 8,)),
                    pltpu.SemaphoreType.DMA((2 * pieces + 1,)),
                ],
            ),
            out_shape=[jax.ShapeDtypeStruct(shape, f32) for shape in shapes],
            input_output_aliases=aliases,
            name={0: "propagate_early", 1: "propagate_late", None: "propagate_whole"}[late],
            compiler_params=params(VMEM_MIB),
            cost_estimate=pl.CostEstimate(
                flops=60 * comp_rows * row_count * col_count, bytes_accessed=60 * MIB, transcendentals=0,
            ),
        )(base, table, *inputs)
        return list(outs[:pieces]), list(outs[pieces : 2 * pieces]), outs[2 * pieces :]

    pairs = [(i, i ^ 1) for i in range(comp_count)]
    apart = [(i, i - 2 if i % 2 == 0 else i + 2) for i in range(comp_count)]
    apart = [(a, b) for a, b in apart if 0 <= b < comp_count]
    across = [(b, a) for a, b in apart]
    chunk_range = range(CELL_CHUNKS)

    def send(pieces, route, waits):
        return [lax.ppermute(after(piece, *wait), "comp", route) for piece, wait in zip(pieces, waits)]

    stages = [(0, 0), (0, 1), (1, None)]
    kept, sent, got, from_own, from_got, level_sums, full = {}, {}, {}, {}, {}, [], {}
    fields = seam = before = None
    part_table = table
    for stage in stages:
        part, late = stage
        kept[stage], sent[stage], extra = propagate(part, late, part_table, fields, seam, full.get(part))
        level_sums.append(extra[0])
        full[part] = extra[1]
        seam = extra[2] if late == 0 else None
        fields = extra[3] if fields is None else fields
        if stage == stages[-1]:
            break
        got[stage] = send(sent[stage], pairs, [[]])
        from_own[stage] = send(kept[stage], apart, [[]])
        waits = [from_got[before][0]] if before is not None else []
        from_got[stage] = send(got[stage], across, [waits])
        done = [extra[0]]
        if before is not None:
            done.append(got[before][0])
        part_table = after(table, *done)
        before = stage
    packed_fields = fields
    sums_0 = level_sums[0]

    sums = level_sums[0] + level_sums[1] + level_sums[2]
    partner_sums = lax.ppermute(sums, "comp", pairs)
    partner_sums = jnp.roll(partner_sums, half, axis=1)
    last, got_1, from_own_1 = stages[-1], [], []
    for c in chunk_range:
        waits = [got[before][0]] + ([got_1[c - 2]] if c >= 2 else []) + ([partner_sums] if c == 2 else [])
        got_1.append(lax.ppermute(after(sent[last][c], *waits), "comp", pairs))
        from_own_1.append(lax.ppermute(after(kept[last][c], from_own[before][0]), "comp", apart))
    got[last], from_own[last], from_got[last] = got_1, from_own_1, []

    dia_index, coupling, growth, damping, late_odd, late_pair, _ = lax.optimization_barrier(
        (dia_index, coupling, growth, damping, odd, pair_pos, sums_0)
    )
    own_growth = lax.dynamic_slice_in_dim(growth, first_comp, local_comps)[:, None]
    own_damping = lax.dynamic_slice_in_dim(damping, first_comp, local_comps)[:, None]
    chunk_first = [
        NTH * jnp.where(late_odd > 0, 8 * late_pair + 10 - 2 * j, 8 * late_pair - 4 + 2 * j) for j in range(8)
    ]
    margin = 8 * NTH
    dia_pad = jnp.pad(dia_index, ((0, 0), (margin, margin)), constant_values=-1)
    coupling_pad = jnp.pad(coupling, (margin, margin))
    own_ids = jnp.arange(comps)
    targets, rates = [], []
    for j in range(1, 7):
        targets.append(lax.dynamic_slice(dia_pad, (0, chunk_first[j] + margin), (4, comps)))
        rates.append(lax.dynamic_slice_in_dim(coupling_pad, chunk_first[j] + margin, comps))
    lookup = []
    for j in range(1, 7):
        ids = jnp.concatenate([chunk_first[j + d] + own_ids for d in (-1, 0, 1)])
        lookup.append((targets[j - 1].reshape(4 * comps)[:, None] == ids[None, :]).astype(jnp.bfloat16))
    lookup = jnp.stack(lookup)
    out_ids = jnp.concatenate([chunk_first[j] + own_ids for j in range(2, 6)])
    spread = []
    for j in range(1, 7):
        for pair in range(2):
            hits = [
                (out_ids[:, None] == targets[j - 1][2 * pair + q][None, :]).astype(f32) for q in range(2)
            ]
            spread.append(hits[0] + hits[1])
    spread = jnp.concatenate(spread, axis=1).astype(jnp.bfloat16)
    rates = jnp.concatenate(rates)[:, None]

    lanes = 512 if width % 512 == 0 else width
    own_parts, parts_0, parts_1 = [], [], []
    groups = [(from_got, 1), (from_got, 0), (kept, 0), (kept, 1), (got, 1), (got, 0), (from_own, 0), (from_own, 1)]
    for c in chunk_range:
        waits = [from_got[before][0], from_own_1[c]] + ([from_got[last][c - 2]] if c >= 2 else [])
        from_got[last].append(lax.ppermute(after(got_1[c], *waits), "comp", across))
        levels, level_specs, counts = [], [], []
        for group, part in groups:
            counts.append(1 if part else 2)
            for late in [None] if part else [0, 1]:
                pieces = group[part, late]
                single = len(pieces) == 1
                levels.append(pieces[0 if single else c])
                skipped = c * (width // lanes) if single else 0
                level_specs.append(
                    pl.BlockSpec((levels[-1].shape[0], lanes), functools.partial(lambda n, s: (0, n + s), skipped))
                )
        own_part, part_0, part_1 = pl.pallas_call(
            functools.partial(interact_kernel, tuple(counts)),
            grid=(width // lanes,),
            in_specs=[
                pl.BlockSpec(lookup.shape, lambda s: (0, 0, 0)),
                pl.BlockSpec(spread.shape, lambda s: (0, 0)),
                pl.BlockSpec(rates.shape, lambda s: (0, 0)),
            ] + level_specs,
            out_specs=[pl.BlockSpec((n * comps, lanes), lambda s: (0, s)) for n in (2, 1, 1)],
            out_shape=[jax.ShapeDtypeStruct((n * comps, width), f32) for n in (2, 1, 1)],
            scratch_shapes=[pltpu.VMEM((12 * comps, lanes), jnp.bfloat16)],
            name="interact_cells",
            compiler_params=params(VMEM_MIB),
            cost_estimate=pl.CostEstimate(
                flops=2 * width * comps * comps * (6 * 12 + 48),
                bytes_accessed=20 * MIB, transcendentals=0,
            ),
        )(lookup, spread, rates, *levels)
        own_parts.append(own_part)
        parts_0.append(part_0)
        parts_1.append(part_1)

    sums = sums + partner_sums
    sums = sums + lax.ppermute(after(sums, own_parts[0]), "comp", [(i, i ^ 2) for i in range(comp_count)])
    sums = sums + lax.ppermute(after(sums, own_parts[2]), "comp", [(i, i ^ 4) for i in range(comp_count)])
    mean_level = sums / comp_total

    def send_back(piece, *waits):
        return lax.ppermute(after(piece, *waits), "comp", pairs)

    back = [[None] * CELL_CHUNKS for _ in range(2)]
    back[0][0] = send_back(parts_0[0], got_1[2])
    back[1][0] = send_back(parts_1[0], got_1[3])
    back[0][1] = send_back(parts_0[1], back[0][0])
    back[0][2] = send_back(parts_0[2], back[1][0])
    back[0][3] = send_back(parts_0[3], back[0][1])
    for c in range(1, CELL_CHUNKS):
        back[1][c] = send_back(parts_1[c], back[0][2])

    def finish(part, so_far):
        piece = pl.BlockSpec((GROUP, width), lambda s, b, t: (s, 0))
        own_piece = pl.BlockSpec((GROUP, width), lambda s, b, t: (part * steps + s, 0))
        inputs = [place, mean_level, packed_fields, own_growth, own_damping]
        specs = [whole(place.shape), whole(mean_level.shape), whole(packed_fields.shape), column(part, 1),
                 column(part, 1)]
        inputs += [full[part]] + own_parts + back[part]
        specs.append(pl.BlockSpec((GROUP, cells), lambda s, b, t: (s, 0)))
        specs += [own_piece] * CELL_CHUNKS + [piece] * CELL_CHUNKS
        aliases = {}
        if so_far is not None:
            inputs.append(so_far)
            specs.append(pl.BlockSpec(memory_space=pl.ANY))
            aliases = {len(inputs) + 1: 0}
        return pl.pallas_call(
            functools.partial(finish_kernel, CELL_CHUNKS),
            grid_spec=pltpu.PrefetchScalarGridSpec(
                num_scalar_prefetch=2,
                grid=(steps,),
                in_specs=specs,
                out_specs=pl.BlockSpec((GROUP, row_count, col_count), lambda s, b, t: (group_at(part, b) + s, 0, 0)),
                scratch_shapes=[pltpu.VMEM((GROUP, cells), f32)],
            ),
            out_shape=jax.ShapeDtypeStruct(energy.shape, f32),
            input_output_aliases=aliases,
            name="finish_chunk",
            compiler_params=params(VMEM_MIB),
            cost_estimate=pl.CostEstimate(
                flops=20 * comps * row_count * col_count,
                bytes_accessed=100 * MIB, transcendentals=0,
            ),
        )(base, table, *inputs)

    return finish(1, finish(0, None))


def choose_shards(energy, *rest):
    local_comps, row_count, col_count = energy.shape
    fits = (
        local_comps == 4 * NTH and lax.axis_size("comp") == 8 and local_comps * 8 == NTH * NF
        and lax.axis_size("tile") == 2 and row_count == BLOCK and col_count == 2 * BLOCK
    )
    return packed_shards(energy, *rest) if fits else shards(energy, *rest)


def solution(mesh):
    placed = (
        P("comp", ("grp", "tile"), None),
        P("grp", None),
        P("grp", None),
        P("grp", None),
        P("grp", None),
        P("grp", None),
        P(),
        P(),
        P(),
        P(),
        P(),
    )
    return jax.shard_map(
        choose_shards,
        mesh=mesh,
        in_specs=placed,
        out_specs=P("comp", ("grp", "tile"), None),
        check_vma=False,
    )
```

```python
import functools
import math

import jax
import jax.numpy as jnp
import numpy as np
from jax import lax
from jax.experimental import pallas as pl
from jax.experimental.pallas import tpu as pltpu
from jax.sharding import PartitionSpec as P

NTH = 36
NF = 32


weight_plus = 0.4096
weight_minus = 3.1605
weight_cross = 1.2945


def with_halo(block, sides, width):
    for axis, dim in sides:
        count = lax.axis_size(axis)
        forward = [(i, i + 1) for i in range(count - 1)]
        backward = [(target, source) for source, target in forward]
        low = lax.ppermute(
            lax.slice_in_dim(block, block.shape[dim] - width, None, axis=dim), axis, forward
        )
        high = lax.ppermute(lax.slice_in_dim(block, 0, width, axis=dim), axis, backward)
        block = jnp.concatenate([low, block, high], axis=dim)
    return block


def quick_flux(far_left, left_cell, right_cell, far_right, courant):
    centre = 0.5 * (left_cell + right_cell) - 0.5 * courant * (right_cell - left_cell)
    curvature = (1.0 - courant * courant) / 6.0
    upward = centre - curvature * (right_cell - 2.0 * left_cell + far_left)
    downward = centre - curvature * (left_cell - 2.0 * right_cell + far_right)
    return courant * jnp.where(courant > 0.0, upward, downward)


def flux_change(padded, speed, current, sea_pad, axis):
    cell_count = padded.shape[axis] - 4

    def take_part(source, first, which_axis):
        return lax.slice_in_dim(source, first, first + cell_count + 1, axis=which_axis)

    face_current = 0.5 * (take_part(current, 0, axis - 1) + take_part(current, 1, axis - 1))
    courant = speed[:, None, None] + face_current[None]
    open_face = (take_part(sea_pad, 0, axis - 1) * take_part(sea_pad, 1, axis - 1))[None]
    face_flux = (
        quick_flux(
            take_part(padded, 0, axis),
            take_part(padded, 1, axis),
            take_part(padded, 2, axis),
            take_part(padded, 3, axis),
            courant,
        )
        * open_face
    )
    return lax.slice_in_dim(face_flux, 1, cell_count + 1, axis=axis) - lax.slice_in_dim(
        face_flux, 0, cell_count, axis=axis
    )


def source_terms(energy_block, wind, turning, growth, damping, coupling, lookup, spread):
    cell_count = energy_block.shape[1]
    spectrum = energy_block.reshape(NF, NTH, cell_count)
    turn_rate = turning[None, None, :]
    next_dir = jnp.roll(spectrum, -1, axis=1)
    forward = jnp.maximum(turn_rate, 0.0)
    backward = jnp.minimum(turn_rate, 0.0)
    upper_flux = forward * spectrum + backward * next_dir
    lower_flux = jnp.roll(upper_flux, 1, axis=1)
    turned = (spectrum - upper_flux + lower_flux).reshape(energy_block.shape)
    rounded = turned.astype(jnp.bfloat16)
    plus_first, minus_first, plus_second, minus_second = lookup(rounded)
    couple_rate = coupling[:, None]
    delta_first = couple_rate * (
        turned * turned * (weight_plus * plus_first + weight_minus * minus_first)
        - 2.0 * weight_cross * turned * plus_first * minus_first
    )
    delta_second = couple_rate * (
        turned * turned * (weight_plus * plus_second + weight_minus * minus_second)
        - 2.0 * weight_cross * turned * plus_second * minus_second
    )
    moved = spread(delta_first.astype(jnp.bfloat16), delta_second.astype(jnp.bfloat16))
    mean_level = jnp.sum(turned, axis=0) / energy_block.shape[0]
    return (
        turned
        + growth[:, None] * wind[None] * turned
        - damping[:, None] * mean_level[None] * turned
        - 2.0 * (delta_first + delta_second)
        + moved
    )


def shards(
    energy,
    sea_mask,
    current_u,
    current_v,
    wind_forcing,
    refraction,
    group_speed,
    growth,
    damping,
    coupling,
    dia_index,
):
    comp_count = lax.axis_size("comp")
    comp_pos = lax.axis_index("comp")
    tile_pos = lax.axis_index("tile")
    local_comps, row_count, col_count = energy.shape
    first_row = tile_pos * row_count
    first_comp = comp_pos * local_comps
    comp_total = NTH * NF
    angles = 2.0 * math.pi / NTH * (jnp.arange(comp_total) % NTH).astype(jnp.float32)
    speeds = jnp.repeat(group_speed, NTH)
    speed_east = lax.dynamic_slice_in_dim(speeds * jnp.cos(angles), first_comp, local_comps)
    speed_north = lax.dynamic_slice_in_dim(speeds * jnp.sin(angles), first_comp, local_comps)
    window = (row_count + 2, col_count + 2)
    sea_pad = lax.dynamic_slice(jnp.pad(sea_mask.astype(jnp.float32), 1), (first_row, 0), window)
    east_pad = lax.dynamic_slice(jnp.pad(current_u, 1), (first_row, 0), window)
    north_pad = lax.dynamic_slice(jnp.pad(current_v, 1), (first_row, 0), window)
    sea_tile = sea_pad[1:-1, 1:-1]
    masked = energy * sea_tile[None]
    padded_east = with_halo(masked, (("tile", 1),), 2)
    along_east = flux_change(padded_east, speed_east, east_pad[:, 1:-1], sea_pad[:, 1:-1], 1)
    along_north = flux_change(
        jnp.pad(masked, ((0, 0), (0, 0), (2, 2))),
        speed_north,
        north_pad[1:-1, :],
        sea_pad[1:-1, :],
        2,
    )
    propagated = (sea_tile[None] * (masked - along_east - along_north)).reshape(
        local_comps, row_count * col_count
    )
    tile_wind = lax.dynamic_slice(wind_forcing, (first_row, 0), (row_count, col_count)).reshape(-1)
    tile_turn = lax.dynamic_slice(refraction, (first_row, 0), (row_count, col_count)).reshape(-1)
    comp_ids = jnp.arange(comp_total)
    tables = [
        (dia_index[slot_row][:, None] == comp_ids[None, :]).astype(jnp.bfloat16)
        for slot_row in range(4)
    ]

    def lookup(rounded):
        return tuple(
            (
                jnp.dot(tables[slot_row], rounded, preferred_element_type=jnp.float32)
                for slot_row in range(4)
            )
        )

    def scatter_back(table, terms):
        return lax.dot_general(
            table, terms, (((0,), (0,)), ((), ())), preferred_element_type=jnp.float32
        )

    def spread(first_terms, second_terms):
        return (
            scatter_back(tables[0], first_terms)
            + scatter_back(tables[1], first_terms)
            + scatter_back(tables[2], second_terms)
            + scatter_back(tables[3], second_terms)
        )

    share_size = row_count * col_count // comp_count
    point_field = lax.all_to_all(propagated, "comp", split_axis=1, concat_axis=0, tiled=True)
    first_point = comp_pos * share_size
    own_wind = lax.dynamic_slice_in_dim(tile_wind, first_point, share_size)
    own_turn = lax.dynamic_slice_in_dim(tile_turn, first_point, share_size)
    result = source_terms(
        point_field, own_wind, own_turn, growth, damping, coupling, lookup, spread
    )
    returned_field = lax.all_to_all(result, "comp", split_axis=0, concat_axis=1, tiled=True)
    return returned_field.reshape(local_comps, row_count, col_count)


BLOCK = 128
GROUP = 24
EARLY = 40
BATCH = 2
CELL_CHUNKS = 4
MIB = 1024 * 1024
VMEM_MIB = 60
EDGE = 2
SEA, OPEN_EAST, FLOW_EAST, OPEN_NORTH, FLOW_NORTH, HALF_SEA, WIND, TURN = range(8)
KEEP, SPILL, IS_SEA = BLOCK, 2 * BLOCK, 2 * BLOCK


def upwind(courant, total, slope, bend_here, bend_ahead):
    bend = jnp.where(courant > 0.0, bend_here, bend_ahead)
    return courant * ((total - bend) - courant * (slope - courant * bend))


def pick_lanes(block, index):
    return jnp.take_along_axis(block, index, axis=1, mode="promise_in_bounds")


def tile_at(tile):
    return pl.ds(pl.multiple_of(tile * BLOCK, BLOCK), BLOCK)


def has(code, flag):
    return jnp.bitwise_and(code, flag) != 0


def pack_block(blocks, code, tile, out_ref, firsts, held):
    code = jnp.broadcast_to(code, (8, BLOCK))
    index = jnp.bitwise_and(code, BLOCK - 1)
    keep, spill = has(code, KEEP), has(code, SPILL)
    result = []
    for block, first, old in zip(blocks, firsts, held):
        moved = pick_lanes(block, index)
        merged = jnp.where(keep, moved, old)
        out_ref[pl.ds(first, 8), tile_at(tile)] = merged
        result.append(jnp.where(spill, moved, merged))
    return tuple(result)


def prepare_kernel(places, base_ref, speed_ref, sea_ref, east_ref, north_ref, wind_ref, turn_ref, cos_ref, sin_ref,
                   coef_ref, index_ref, place_ref, table_ref, speed_east_ref, speed_north_ref, field_ref, pick_ref):
    first_row, odd, first_freq = base_ref[0], base_ref[1], base_ref[2]
    all_rows, col_count = sea_ref.shape
    row_count = place_ref.shape[1]
    tiles = places // BLOCK
    sea = sea_ref[...].astype(jnp.float32)
    row = lax.broadcasted_iota(jnp.int32, sea.shape, 0)
    col = lax.broadcasted_iota(jnp.int32, sea.shape, 1)

    def next_row(field):
        return jnp.where(row == all_rows - 1, 0.0, pltpu.roll(field, all_rows - 1, 0))

    def next_col(field):
        return jnp.where(col == col_count - 1, 0.0, pltpu.roll(field, col_count - 1, 1))

    open_east, open_north = sea * next_row(sea), sea * next_col(sea)
    east, north = east_ref[...], north_ref[...]
    field_ref[SEA] = sea
    field_ref[OPEN_EAST] = open_east
    field_ref[FLOW_EAST] = open_east * (0.5 * (east + next_row(east)))
    field_ref[OPEN_NORTH] = open_north
    field_ref[FLOW_NORTH] = open_north * (0.5 * (north + next_col(north)))
    field_ref[HALF_SEA] = 0.5 * sea
    field_ref[WIND] = wind_ref[...]
    field_ref[TURN] = turn_ref[...]
    coef_ref[0:EDGE] = jnp.zeros((EDGE, 8, col_count), jnp.float32)
    coef_ref[EDGE + all_rows :] = jnp.zeros((EDGE, 8, col_count), jnp.float32)

    @pl.loop(0, all_rows // 8)
    def _(i):
        rows = field_ref[:, pl.ds(pl.multiple_of(8 * i, 8), 8), :]
        coef_ref[pl.ds(8 * i + EDGE, 8)] = jnp.swapaxes(rows, 0, 1)

    freqs = cos_ref.shape[0] // NTH
    for f in range(freqs):
        circle = slice(f * NTH, (f + 1) * NTH)
        speed_east_ref[circle, :] = cos_ref[circle, :] * speed_ref[first_freq + f]
        speed_north_ref[circle, :] = sin_ref[circle, :] * speed_ref[first_freq + f]

    bf16, f32 = jnp.bfloat16, jnp.float32
    tile_sea = sea_ref[pl.ds(pl.multiple_of(first_row, 8), row_count), :].astype(f32)
    square = (BLOCK, BLOCK)
    down, over = lax.broadcasted_iota(jnp.int32, square, 0), lax.broadcasted_iota(jnp.int32, square, 1)
    before = (down < over).astype(f32).astype(bf16)
    ones = jnp.ones(square, bf16)
    row_square = (row_count, row_count)
    above = lax.broadcasted_iota(jnp.int32, row_square, 1) < lax.broadcasted_iota(jnp.int32, row_square, 0)
    above = above.astype(f32).astype(bf16)
    parts = [tile_sea[:, :BLOCK], tile_sea[:, BLOCK:]]
    numbers = [jnp.dot(p.astype(bf16), ones, preferred_element_type=f32) for p in parts]
    in_row = numbers[0] + numbers[1]
    starts = [jnp.dot(above, in_row.astype(bf16), preferred_element_type=f32)]
    starts.append(starts[0] + numbers[0])
    total = jnp.sum(in_row, axis=0, keepdims=True).astype(jnp.int32)

    def turned_tile(tile):
        return jnp.where(tile >= tiles, tiles, jnp.bitwise_and(tile + odd * (tiles // 2), tiles - 1))

    columns = []
    for h in range(2):
        rank = jnp.dot(parts[h].astype(bf16), before, preferred_element_type=f32).astype(jnp.int32)
        start = starts[h].astype(jnp.int32)
        offset = jnp.bitwise_and(start, BLOCK - 1)
        keep = jnp.where(over[:row_count] >= offset, KEEP, 0)
        slot = jnp.bitwise_and(rank + offset, BLOCK - 1)
        is_sea = parts[h] > 0.0
        place_ref[h] = slot + keep + jnp.where(is_sea, IS_SEA, 0)
        slot = jnp.where(is_sea, slot, -1).astype(f32).T
        from_lane = down[:, :row_count].astype(f32)

        @pl.loop(0, BLOCK // 8)
        def _(i):
            found = []
            for k in range(8):
                lane = (8 * i + k).astype(f32)
                found.append(jnp.sum(jnp.where(slot == lane, from_lane, 0.0), axis=0, keepdims=True))
            pick_ref[pl.ds(pl.multiple_of(8 * i, 8), 8), :] = jnp.concatenate(found, axis=0)

        spill = jnp.where(offset + numbers[h].astype(jnp.int32) >= BLOCK, SPILL, 0)
        index_ref[h] = pick_ref[...].T.astype(jnp.int32) + keep + spill
        columns.append(turned_tile(lax.shift_right_logical(starts[h].T[0:8, :].astype(jnp.int32), 7)))
    row_id = lax.broadcasted_iota(jnp.int32, (8, row_count), 0)
    end_tile = jnp.where(
        jnp.bitwise_and(total, BLOCK - 1) == 0, tiles, turned_tile(lax.shift_right_logical(total, 7))
    )
    end_tile = jnp.broadcast_to(end_tile, (8, BLOCK))
    table_ref[...] = jnp.concatenate([jnp.where(row_id == 0, columns[0], columns[1]), end_tile], axis=1)


def propagate_kernel(part, late, pieces, base_ref, table_ref, energy_ref, halo_ref, coef_ref, index_ref, east_ref,
                     north_ref, *refs):
    refs = list(refs)
    with_fields = part == 0 and late == 0
    fields_ref = None if with_fields else refs.pop(0)
    seam_ref = refs.pop(0) if late else None
    if late:
        refs.pop(0)
    piece_refs = [refs.pop(0) for _ in range(2 * pieces)]
    sum_ref, full_ref = refs.pop(0), refs.pop(0)
    seam_out_ref = refs.pop(0) if late == 0 else None
    fields_out_ref = refs.pop(0) if with_fields else None
    energy_vmem, rows_ref, spread_ref, wide_ref, result_ref, strip_sems, out_sems = refs
    row_count, comp_count, col_count = rows_ref.shape
    strips = comp_count // 8
    sent_rows = piece_refs[0].shape[0]
    cells = result_ref.shape[1]
    first_row = base_ref[0]
    first_comp = pl.multiple_of((part + base_ref[1] * (1 - 2 * part)) * 2 * NTH + (EARLY if late else 0), 8)
    lane = lax.broadcasted_iota(jnp.int32, (8, BLOCK), 1)
    first_lane, last_lane = lane == 0, lane == BLOCK - 1
    third = 1.0 / 3.0

    def arrival(g):
        target = energy_vmem.at[pl.ds(pl.multiple_of(8 * g, 8), 8)]
        source = energy_ref.at[pl.ds(pl.multiple_of(first_comp + 8 * g, 8), 8)]
        return pltpu.make_async_copy(source, target, strip_sems.at[g])

    for g in range(strips):
        arrival(g).start()

    def halves(row):
        return row[:, :BLOCK], row[:, BLOCK:]

    @pl.loop(0, row_count + 2 * EDGE, unroll=4)
    def _(r):
        coef = coef_ref[first_row + r]
        for k in range(HALF_SEA + 1):
            spread_ref[r, k] = jnp.broadcast_to(coef[k : k + 1, :], coef.shape)

    def masked(row, at):
        return tuple(part * sea for part, sea in zip(halves(row), halves(spread_ref[at, SEA])))

    def cell_rows(first, fresh, state, east, north):
        here, ahead, slope_here, bend_here, flux_low = state
        count, sides = len(fresh), range(2)
        level = [here, ahead] + [masked(row, first + k + EDGE) for k, row in enumerate(fresh)]
        rows = range(count)
        coef = [[None] + [halves(spread_ref[first + k, f]) for f in range(1, HALF_SEA + 1)] for k in rows]
        one_right = [[pltpu.roll(part, BLOCK - 1, 1) for part in level[k]] for k in rows]
        right = [
            (jnp.where(last_lane, one[1], one[0]), jnp.where(last_lane, 0.0, one[1])) for one in one_right
        ]
        slope = [[right[k][h] - level[k][h] for h in sides] for k in rows]
        slope_roll = [[pltpu.roll(part, 1, 1) for part in slope[k]] for k in rows]
        bend = [
            (third * (slope[k][0] - jnp.where(first_lane, level[k][0], slope_roll[k][0])),
             third * (slope[k][1] - jnp.where(first_lane, slope_roll[k][0], slope_roll[k][1])))
            for k in rows
        ]
        bend_roll = [[pltpu.roll(part, BLOCK - 1, 1) for part in bend[k]] for k in rows]
        cross = []
        for k in rows:
            bend_right = (jnp.where(last_lane, bend_roll[k][1], bend_roll[k][0]), bend_roll[k][1])
            cross.append([
                upwind(north * coef[k][OPEN_NORTH][h] + coef[k][FLOW_NORTH][h], level[k][h] + right[k][h],
                       slope[k][h], bend[k][h], bend_right[h])
                for h in sides
            ])
        cross_roll = [[pltpu.roll(part, 1, 1) for part in cross[k]] for k in rows]
        slopes = [slope_here] + [tuple(level[k + 1][h] - level[k][h] for h in sides) for k in range(1, count + 1)]
        bends = [bend_here] + [
            tuple(third * (slopes[k][h] - slopes[k - 1][h]) for h in sides) for k in range(1, count + 1)
        ]
        flux = [flux_low]
        for k in rows:
            flux.append(tuple(
                upwind(east * coef[k][OPEN_EAST][h] + coef[k][FLOW_EAST][h], level[k][h] + level[k + 1][h],
                       slopes[k][h], bends[k][h], bends[k + 1][h])
                for h in sides
            ))
        done = []
        for k in rows:
            cross_low = (jnp.where(first_lane, cross_roll[k][1], cross_roll[k][0]),
                         jnp.where(first_lane, cross_roll[k][0], cross_roll[k][1]))
            done.append([
                coef[k][HALF_SEA][h] * (((level[k][h] + level[k][h]) + (flux[k][h] + cross_low[h]))
                                        - (flux[k + 1][h] + cross[k][h]))
                for h in sides
            ])
        return (level[count], level[count + 1], slopes[count], bends[count], flux[count]), done

    def store_row(row, local, parts):
        for h in range(2):
            rows_ref[row, local, h * BLOCK : (h + 1) * BLOCK] = parts[h]

    @pl.loop(0, strips)
    def _(g):
        arrival(g).wait()
        local = pl.ds(pl.multiple_of(g * 8, 8), 8)
        comps = pl.ds(pl.multiple_of(first_comp + g * 8, 8), 8)
        east, north = east_ref[comps, :], north_ref[comps, :]
        zero = (jnp.zeros((8, BLOCK), jnp.float32),) * 2
        here, ahead = masked(halo_ref[comps, 0, :], 0), masked(halo_ref[comps, 1, :], 1)
        state = (here, ahead, tuple(b - a for a, b in zip(here, ahead)), zero, zero)

        def eight(i, state):
            block = jnp.swapaxes(energy_vmem[local, pl.ds(pl.multiple_of(8 * i, 8), 8), :], 0, 1)
            for first in range(0, 8, BATCH):
                fresh = [block[first + k] for k in range(BATCH)]
                state, done = cell_rows(8 * i + first, fresh, state, east, north)
                for k in range(BATCH):
                    store_row(jnp.maximum(8 * i + first + k - EDGE, 0), local, done[k])
            return state

        state = lax.fori_loop(0, row_count // 8, eight, state)
        fresh = [halo_ref[comps, k, :] for k in range(EDGE)]
        state, done = cell_rows(row_count, fresh, state, east, north)
        for k in range(EDGE):
            store_row(row_count - EDGE + k, local, done[k])

    group_rows = [8 * n for n in range(strips + with_fields)]

    def pack_eight(i, held):
        codes = [index_ref[h, pl.ds(pl.multiple_of(8 * i, 8), 8), :] for h in range(2)]
        for k in range(8):
            row = 8 * i + k
            for h in range(2):
                lanes = slice(h * BLOCK, (h + 1) * BLOCK)
                blocks = [rows_ref[row, 8 * n : 8 * n + 8, lanes] for n in range(strips)]
                if with_fields:
                    blocks.append(coef_ref[first_row + EDGE + row, :, lanes])
                held = pack_block(blocks, codes[h][k : k + 1, :], table_ref[h, row], wide_ref, group_rows, held)
        return held

    empty = (jnp.zeros((8, BLOCK), jnp.float32),) * len(group_rows)
    held = lax.fori_loop(0, row_count // 8, pack_eight, empty)
    for first, block in zip(group_rows, held):
        wide_ref[pl.ds(first, 8), tile_at(table_ref[0, row_count])] = block
    if with_fields:
        fields_out_ref[...] = wide_ref[comp_count:, :cells]

    tile_width = 2 * BLOCK
    height = result_ref.shape[0]
    comp_row = lax.broadcasted_iota(jnp.int32, (height, tile_width), 0)
    starts = {0: [0], 1: [height - NTH], None: [0, NTH]}[late]
    mixed = {0: slice(height - 8, height), 1: slice(0, 8), None: slice(0, 0)}[late]
    in_circle = (comp_row[:8] + mixed.start >= starts[0]) & (comp_row[:8] + mixed.start < starts[0] + NTH)

    @pl.loop(0, cells // tile_width, unroll=2)
    def _(i):
        source = pl.ds(pl.multiple_of(i * tile_width, tile_width), tile_width)
        level = wide_ref[:comp_count, source]
        if late:
            level = jnp.concatenate([seam_ref[:, source], level], axis=0)
        if with_fields:
            rate = wide_ref[comp_count + TURN : comp_count + TURN + 1, source]
        else:
            rate = fields_ref[TURN : TURN + 1, source]
        forward = jnp.maximum(rate, 0.0)
        backward = jnp.minimum(rate, 0.0)
        stay = (1.0 - forward) + backward
        above = pltpu.roll(level, height - 1, 0)
        below = pltpu.roll(level, 1, 0)

        def with_row(rolled, row, value):
            tile = slice(row - row % 8, row - row % 8 + 8)
            fixed = jnp.where(comp_row[tile] == row, value, rolled[tile])
            parts = [rolled[: tile.start], fixed, rolled[tile.stop :]]
            return jnp.concatenate([part for part in parts if part.shape[0]], axis=0)

        for start in starts:
            end = start + NTH - 1
            above = with_row(above, end, level[start : start + 1, :])
            below = with_row(below, start, level[end : end + 1, :])
        turned = stay * level - backward * above + forward * below
        partial = jnp.zeros((8, tile_width), jnp.float32)
        for first in range(0, height, 8):
            rows = slice(first, first + 8)
            if rows == mixed:
                result_ref[rows, source] = jnp.where(in_circle, turned[rows], level[rows])
                partial += jnp.where(in_circle, turned[rows], 0.0)
            else:
                result_ref[rows, source] = turned[rows]
                partial += turned[rows]
        sum_ref[:, source] = jnp.sum(partial, axis=0, keepdims=True)

    if late == 0:
        seam_out_ref[...] = result_ref[sent_rows:, :]
    width = cells // (2 * pieces)
    copies = []
    for n, piece in enumerate(piece_refs):
        source = result_ref.at[:sent_rows, n * width : (n + 1) * width]
        copies.append(pltpu.make_async_copy(source, piece, out_sems.at[n]))
    rows = pl.ds(EARLY - 8 if late else 0, sent_rows)
    copies.append(pltpu.make_async_copy(result_ref.at[:sent_rows, :], full_ref.at[rows, :], out_sems.at[2 * pieces]))
    for copy in copies:
        copy.start()
    for copy in copies:
        copy.wait()


def interact_kernel(counts, table_ref, spread_ref, coupling_ref, *refs):
    own_ref, back_0_ref, back_1_ref, delta_ref = refs[sum(counts) :]
    window = []
    for j, count in enumerate(counts):
        first = sum(counts[:j])
        parts = [ref[...] for ref in refs[first : first + count]]
        window.append(parts[0] if count == 1 else jnp.concatenate(parts, axis=0))
    comps = window[0].shape[0]
    for j in range(1, 7):
        level = window[j]
        around = jnp.concatenate([window[j - 1], level, window[j + 1]], axis=0).astype(jnp.bfloat16)
        partner = jnp.dot(table_ref[j - 1], around, preferred_element_type=jnp.float32)
        rate = coupling_ref[(j - 1) * comps : j * comps, :] * level
        plus_part = weight_plus * level
        minus_part = weight_minus * level
        deltas = []
        for pair in range(2):
            plus = partner[2 * pair * comps : (2 * pair + 1) * comps, :]
            minus = partner[(2 * pair + 1) * comps : (2 * pair + 2) * comps, :]
            deltas.append(rate * (plus * (plus_part - (2.0 * weight_cross) * minus) + minus_part * minus))
        both = jnp.concatenate(deltas, axis=0).astype(jnp.bfloat16)
        delta_ref[(j - 1) * 2 * comps : j * 2 * comps, :] = both
        if 2 <= j <= 5:
            part = -2.0 * (deltas[0] + deltas[1])
            if j <= 3:
                own_ref[(j - 2) * comps : (j - 1) * comps, :] = part
            elif j == 4:
                back_1_ref[...] = part
            else:
                back_0_ref[...] = part
    spread = jnp.dot(spread_ref[...], delta_ref[...], preferred_element_type=jnp.float32)
    own_ref[...] += spread[: 2 * comps, :]
    back_1_ref[...] += spread[2 * comps : 3 * comps, :]
    back_0_ref[...] += spread[3 * comps :, :]


def finish_kernel(chunks, base_ref, table_ref, place_ref, mean_ref, fields_ref, growth_ref, damping_ref, *refs):
    turned_ref, own, back = refs[0], refs[1 : 1 + chunks], refs[1 + chunks : 1 + 2 * chunks]
    out_ref, wide_ref = refs[-2], refs[-1]
    width = own[0].shape[1]
    tiles = wide_ref.shape[1] // BLOCK
    tile_width = 2 * BLOCK
    growth = jnp.broadcast_to(growth_ref[...], (GROUP, tile_width))
    damping = jnp.broadcast_to(damping_ref[...], (GROUP, tile_width))
    for o in range(2 * chunks):
        extra = own[o] if o < chunks else back[o - chunks]

        @pl.loop(0, width // tile_width, unroll=2)
        def _(i):
            source = pl.ds(pl.multiple_of(i * tile_width, tile_width), tile_width)
            target = pl.ds(pl.multiple_of(o * width + i * tile_width, tile_width), tile_width)
            scale = 1.0 + growth * fields_ref[WIND : WIND + 1, target] - damping * mean_ref[0:1, target]
            wide_ref[:, target] = turned_ref[:, target] * scale + extra[:, source]

    @pl.loop(0, out_ref.shape[1] // 8)
    def _(i):
        codes = [place_ref[h, pl.ds(pl.multiple_of(8 * i, 8), 8), :] for h in range(2)]
        done = [[] for _ in range(GROUP // 8)]
        for r in range(8):
            parts = [[] for _ in range(GROUP // 8)]
            for h in range(2):
                code = jnp.broadcast_to(codes[h][r : r + 1, :], (8, BLOCK))
                index = jnp.bitwise_and(code, BLOCK - 1)
                keep, is_sea = has(code, KEEP), has(code, IS_SEA)
                tile = table_ref[h, 8 * i + r]
                first, second = jnp.minimum(tile, tiles - 1), jnp.bitwise_and(tile + 1, tiles - 1)
                for k in range(GROUP // 8):
                    rows = slice(8 * k, 8 * k + 8)
                    near = jnp.where(keep, wide_ref[rows, tile_at(first)], wide_ref[rows, tile_at(second)])
                    parts[k].append(jnp.where(is_sea, pick_lanes(near, index), 0.0))
            for k in range(GROUP // 8):
                done[k].append(jnp.concatenate(parts[k], axis=1))
        for k in range(GROUP // 8):
            out_ref[8 * k : 8 * k + 8, pl.ds(pl.multiple_of(8 * i, 8), 8), :] = jnp.swapaxes(jnp.stack(done[k]), 0, 1)


def params(limit):
    return pltpu.CompilerParams(vmem_limit_bytes=limit * MIB)


def after(value, *others):
    return lax.optimization_barrier((value,) + others)[0]


def packed_shards(energy, sea_mask, current_u, current_v, wind_forcing, refraction, group_speed, growth, damping,
                  coupling, dia_index):
    comp_count = lax.axis_size("comp")
    comp_pos = lax.axis_index("comp")
    tile_pos = lax.axis_index("tile")
    odd = lax.rem(comp_pos, 2)
    pair_pos = comp_pos // 2
    local_comps, row_count, col_count = energy.shape
    comps = local_comps // 2
    comp_total = NTH * NF
    first_row = tile_pos * row_count
    first_comp = comp_pos * local_comps
    cells = row_count * col_count // 2
    half = cells // 2
    width = half // CELL_CHUNKS
    f32, i32 = jnp.float32, jnp.int32
    base = jnp.stack([first_row, odd, comp_pos * (local_comps // NTH)]).astype(i32)

    edge_first = jnp.where(tile_pos == 0, row_count - EDGE, 0)
    edge_rows = lax.dynamic_slice_in_dim(energy, edge_first, EDGE, axis=1)
    halo_rows = lax.ppermute(edge_rows, "tile", [(0, 1), (1, 0)])

    all_rows = sea_mask.shape[0]
    angles = np.float32(2.0 * math.pi / NTH) * (np.arange(local_comps) % NTH).astype(np.float32)
    cosines = np.broadcast_to(np.cos(angles)[:, None], (local_comps, BLOCK)).astype(np.float32)
    sines = np.broadcast_to(np.sin(angles)[:, None], (local_comps, BLOCK)).astype(np.float32)
    vmem = pl.BlockSpec(memory_space=pltpu.VMEM)
    coef, index, place, table, speed_east, speed_north = pl.pallas_call(
        functools.partial(prepare_kernel, cells),
        grid_spec=pltpu.PrefetchScalarGridSpec(
            num_scalar_prefetch=2,
            grid=(),
            in_specs=[vmem] * 7,
            out_specs=[vmem] * 6,
            scratch_shapes=[pltpu.VMEM((8, all_rows, col_count), f32), pltpu.VMEM((BLOCK, row_count), f32)],
        ),
        out_shape=[
            jax.ShapeDtypeStruct((all_rows + 2 * EDGE, 8, col_count), f32),
            jax.ShapeDtypeStruct((2, row_count, BLOCK), i32),
            jax.ShapeDtypeStruct((2, row_count, BLOCK), i32),
            jax.ShapeDtypeStruct((8, 2 * BLOCK), i32),
            jax.ShapeDtypeStruct((local_comps, BLOCK), f32),
            jax.ShapeDtypeStruct((local_comps, BLOCK), f32),
        ],
        name="prepare",
        compiler_params=params(VMEM_MIB),
    )(base, group_speed, sea_mask, current_u, current_v, wind_forcing, refraction, cosines, sines)
    steps = comps // GROUP

    def group_at(part, base_ref):
        return (part + base_ref[1] * (1 - 2 * part)) * steps

    def whole(shape):
        return pl.BlockSpec(shape, lambda s, b, t: (0,) * len(shape))

    def column(part, lanes):
        return pl.BlockSpec((GROUP, lanes), lambda s, b, t: (group_at(part, b) + s, 0))

    def propagate(part, late, table, fields=None, seam=None, full=None):
        pieces = CELL_CHUNKS if part else 1
        comp_rows = {0: EARLY, 1: comps - EARLY, None: comps}[late]
        sent_rows = {0: EARLY - 8, 1: comps - EARLY + 8, None: comps}[late]
        height = comps if late is None else EARLY
        anywhere = pl.BlockSpec(memory_space=pl.ANY)
        with_fields = fields is None
        inputs = [energy, halo_rows, coef, index, speed_east, speed_north]
        in_specs = [anywhere] + [vmem] * 5
        aliases = {}
        if not with_fields:
            inputs.append(fields)
            in_specs.append(vmem)
        if late:
            inputs += [seam, full]
            in_specs += [vmem, anywhere]
            aliases = {len(inputs) + 1: 2 * pieces + 1}
        shapes = [(sent_rows, half // pieces)] * (2 * pieces) + [(1, cells), (comps, cells)]
        out_specs = [anywhere] * (2 * pieces) + [vmem, anywhere]
        if late == 0:
            shapes.append((8, cells))
            out_specs.append(vmem)
        if with_fields:
            shapes.append((8, cells))
            out_specs.append(vmem)
        outs = pl.pallas_call(
            functools.partial(propagate_kernel, part, late, pieces),
            grid_spec=pltpu.PrefetchScalarGridSpec(
                num_scalar_prefetch=2,
                grid=(),
                in_specs=in_specs,
                out_specs=out_specs,
                scratch_shapes=[
                    pltpu.VMEM((comp_rows, row_count, col_count), f32),
                    pltpu.VMEM((row_count, comp_rows, col_count), f32),
                    pltpu.VMEM((row_count + 2 * EDGE, HALF_SEA + 1, 8, col_count), f32),
                    pltpu.VMEM((comp_rows + (8 if with_fields else 0), cells + BLOCK), f32),
                    pltpu.VMEM((height, cells), f32),
                    pltpu.SemaphoreType.DMA((comp_rows // 8,)),
                    pltpu.SemaphoreType.DMA((2 * pieces + 1,)),
                ],
            ),
            out_shape=[jax.ShapeDtypeStruct(shape, f32) for shape in shapes],
            input_output_aliases=aliases,
            name={0: "propagate_early", 1: "propagate_late", None: "propagate_whole"}[late],
            compiler_params=params(VMEM_MIB),
            cost_estimate=pl.CostEstimate(
                flops=60 * comp_rows * row_count * col_count, bytes_accessed=60 * MIB, transcendentals=0,
            ),
        )(base, table, *inputs)
        return list(outs[:pieces]), list(outs[pieces : 2 * pieces]), outs[2 * pieces :]

    pairs = [(i, i ^ 1) for i in range(comp_count)]
    apart = [(i, i - 2 if i % 2 == 0 else i + 2) for i in range(comp_count)]
    apart = [(a, b) for a, b in apart if 0 <= b < comp_count]
    across = [(b, a) for a, b in apart]
    chunk_range = range(CELL_CHUNKS)

    def send(pieces, route, waits):
        return [lax.ppermute(after(piece, *wait), "comp", route) for piece, wait in zip(pieces, waits)]

    stages = [(0, 0), (0, 1), (1, None)]
    kept, sent, got, from_own, from_got, level_sums, full = {}, {}, {}, {}, {}, [], {}
    fields = seam = before = None
    part_table = table
    for stage in stages:
        part, late = stage
        kept[stage], sent[stage], extra = propagate(part, late, part_table, fields, seam, full.get(part))
        level_sums.append(extra[0])
        full[part] = extra[1]
        seam = extra[2] if late == 0 else None
        fields = extra[3] if fields is None else fields
        if stage == stages[-1]:
            break
        got[stage] = send(sent[stage], pairs, [[]])
        from_own[stage] = send(kept[stage], apart, [[]])
        waits = [from_got[before][0]] if before is not None else []
        from_got[stage] = send(got[stage], across, [waits])
        done = [extra[0]]
        if before is not None:
            done.append(got[before][0])
        part_table = after(table, *done)
        before = stage
    packed_fields = fields
    sums_0 = level_sums[0]

    sums = level_sums[0] + level_sums[1] + level_sums[2]
    partner_sums = lax.ppermute(sums, "comp", pairs)
    partner_sums = jnp.roll(partner_sums, half, axis=1)
    last, got_1, from_own_1 = stages[-1], [], []
    for c in chunk_range:
        waits = [got[before][0]] + ([got_1[c - 2]] if c >= 2 else []) + ([partner_sums] if c == 2 else [])
        got_1.append(lax.ppermute(after(sent[last][c], *waits), "comp", pairs))
        from_own_1.append(lax.ppermute(after(kept[last][c], from_own[before][0]), "comp", apart))
    got[last], from_own[last], from_got[last] = got_1, from_own_1, []
    sums = sums + partner_sums
    sums = sums_two = sums + lax.ppermute(sums, "comp", [(i, i ^ 2) for i in range(comp_count)])
    sums = sums + lax.ppermute(sums, "comp", [(i, i ^ 4) for i in range(comp_count)])
    mean_level = sums / comp_total

    dia_index, coupling, growth, damping, late_odd, late_pair, _ = lax.optimization_barrier(
        (dia_index, coupling, growth, damping, odd, pair_pos, sums_0)
    )
    own_growth = lax.dynamic_slice_in_dim(growth, first_comp, local_comps)[:, None]
    own_damping = lax.dynamic_slice_in_dim(damping, first_comp, local_comps)[:, None]
    chunk_first = [
        NTH * jnp.where(late_odd > 0, 8 * late_pair + 10 - 2 * j, 8 * late_pair - 4 + 2 * j) for j in range(8)
    ]
    margin = 8 * NTH
    dia_pad = jnp.pad(dia_index, ((0, 0), (margin, margin)), constant_values=-1)
    coupling_pad = jnp.pad(coupling, (margin, margin))
    own_ids = jnp.arange(comps)
    targets, rates = [], []
    for j in range(1, 7):
        targets.append(lax.dynamic_slice(dia_pad, (0, chunk_first[j] + margin), (4, comps)))
        rates.append(lax.dynamic_slice_in_dim(coupling_pad, chunk_first[j] + margin, comps))
    lookup = []
    for j in range(1, 7):
        ids = jnp.concatenate([chunk_first[j + d] + own_ids for d in (-1, 0, 1)])
        lookup.append((targets[j - 1].reshape(4 * comps)[:, None] == ids[None, :]).astype(jnp.bfloat16))
    lookup = jnp.stack(lookup)
    out_ids = jnp.concatenate([chunk_first[j] + own_ids for j in range(2, 6)])
    spread = []
    for j in range(1, 7):
        for pair in range(2):
            hits = [
                (out_ids[:, None] == targets[j - 1][2 * pair + q][None, :]).astype(f32) for q in range(2)
            ]
            spread.append(hits[0] + hits[1])
    spread = jnp.concatenate(spread, axis=1).astype(jnp.bfloat16)
    rates = jnp.concatenate(rates)[:, None]

    lanes = 512 if width % 512 == 0 else width
    own_parts, parts_0, parts_1 = [], [], []
    groups = [(from_got, 1), (from_got, 0), (kept, 0), (kept, 1), (got, 1), (got, 0), (from_own, 0), (from_own, 1)]
    for c in chunk_range:
        waits = [from_got[before][0], from_own_1[c]] + ([from_got[last][c - 2]] if c >= 2 else [])
        from_got[last].append(lax.ppermute(after(got_1[c], *waits), "comp", across))
        levels, level_specs, counts = [], [], []
        for group, part in groups:
            counts.append(1 if part else 2)
            for late in [None] if part else [0, 1]:
                pieces = group[part, late]
                single = len(pieces) == 1
                levels.append(pieces[0 if single else c])
                skipped = c * (width // lanes) if single else 0
                level_specs.append(
                    pl.BlockSpec((levels[-1].shape[0], lanes), functools.partial(lambda n, s: (0, n + s), skipped))
                )
        own_part, part_0, part_1 = pl.pallas_call(
            functools.partial(interact_kernel, tuple(counts)),
            grid=(width // lanes,),
            in_specs=[
                pl.BlockSpec(lookup.shape, lambda s: (0, 0, 0)),
                pl.BlockSpec(spread.shape, lambda s: (0, 0)),
                pl.BlockSpec(rates.shape, lambda s: (0, 0)),
            ] + level_specs,
            out_specs=[pl.BlockSpec((n * comps, lanes), lambda s: (0, s)) for n in (2, 1, 1)],
            out_shape=[jax.ShapeDtypeStruct((n * comps, width), f32) for n in (2, 1, 1)],
            scratch_shapes=[pltpu.VMEM((12 * comps, lanes), jnp.bfloat16)],
            name="interact_cells",
            compiler_params=params(VMEM_MIB),
            cost_estimate=pl.CostEstimate(
                flops=2 * width * comps * comps * (6 * 12 + 48),
                bytes_accessed=20 * MIB, transcendentals=0,
            ),
        )(lookup, spread, rates, *levels)
        own_parts.append(own_part)
        parts_0.append(part_0)
        parts_1.append(part_1)

    def send_back(piece, *waits):
        return lax.ppermute(after(piece, *waits), "comp", pairs)

    back = [[None] * CELL_CHUNKS for _ in range(2)]
    back[0][0] = send_back(parts_0[0], got_1[2], sums_two)
    back[1][0] = send_back(parts_1[0], got_1[3])
    back[0][1] = send_back(parts_0[1], back[0][0], sums)
    back[0][2] = send_back(parts_0[2], back[1][0])
    back[0][3] = send_back(parts_0[3], back[0][1])
    for c in range(1, CELL_CHUNKS):
        back[1][c] = send_back(parts_1[c], back[0][2])

    def finish(part, so_far):
        piece = pl.BlockSpec((GROUP, width), lambda s, b, t: (s, 0))
        own_piece = pl.BlockSpec((GROUP, width), lambda s, b, t: (part * steps + s, 0))
        inputs = [place, mean_level, packed_fields, own_growth, own_damping]
        specs = [whole(place.shape), whole(mean_level.shape), whole(packed_fields.shape), column(part, 1),
                 column(part, 1)]
        inputs += [full[part]] + own_parts + back[part]
        specs.append(pl.BlockSpec((GROUP, cells), lambda s, b, t: (s, 0)))
        specs += [own_piece] * CELL_CHUNKS + [piece] * CELL_CHUNKS
        aliases = {}
        if so_far is not None:
            inputs.append(so_far)
            specs.append(pl.BlockSpec(memory_space=pl.ANY))
            aliases = {len(inputs) + 1: 0}
        return pl.pallas_call(
            functools.partial(finish_kernel, CELL_CHUNKS),
            grid_spec=pltpu.PrefetchScalarGridSpec(
                num_scalar_prefetch=2,
                grid=(steps,),
                in_specs=specs,
                out_specs=pl.BlockSpec((GROUP, row_count, col_count), lambda s, b, t: (group_at(part, b) + s, 0, 0)),
                scratch_shapes=[pltpu.VMEM((GROUP, cells), f32)],
            ),
            out_shape=jax.ShapeDtypeStruct(energy.shape, f32),
            input_output_aliases=aliases,
            name="finish_chunk",
            compiler_params=params(VMEM_MIB),
            cost_estimate=pl.CostEstimate(
                flops=20 * comps * row_count * col_count,
                bytes_accessed=100 * MIB, transcendentals=0,
            ),
        )(base, table, *inputs)

    return finish(1, finish(0, None))


def choose_shards(energy, *rest):
    local_comps, row_count, col_count = energy.shape
    fits = (
        local_comps == 4 * NTH and lax.axis_size("comp") == 8 and local_comps * 8 == NTH * NF
        and lax.axis_size("tile") == 2 and row_count == BLOCK and col_count == 2 * BLOCK
    )
    return packed_shards(energy, *rest) if fits else shards(energy, *rest)


def solution(mesh):
    placed = (
        P("comp", ("grp", "tile"), None),
        P("grp", None),
        P("grp", None),
        P("grp", None),
        P("grp", None),
        P("grp", None),
        P(),
        P(),
        P(),
        P(),
        P(),
    )
    return jax.shard_map(
        choose_shards,
        mesh=mesh,
        in_specs=placed,
        out_specs=P("comp", ("grp", "tile"), None),
        check_vma=False,
    )
```
